32 devices in a mesh: fsdp: 4 (over y, x), tensor: 8 (over z, core).
Axes of the slice: x: 2, y: 2, z: 4, core: 2. Of those that a mesh axis runs over, the one named last changes fastest.
Arguments:
- tokens: bfloat16 [2, 4, 1024, 2048], P(None, 'fsdp', 'tensor'), may hold values from -6 to 6
- lengths: int32 [2, 4], P(None, 'fsdp'), may hold values from 256 to 1024, as said below
- routes: int32 [2, 4, 1024, 4], P(None, 'fsdp'), may hold values from 0 to 7, all different within a row; in each aligned block of 128 rows (0 to 127, 128 to 255, ..., all dimensions but the last counted through in order) at most 96 rows name the same one
- norm1_gain: bfloat16 [2048], P(('fsdp', 'tensor')), may hold values from 0.5 to 1.5
- w_query: bfloat16 [2048, 2048], P('fsdp', 'tensor'), may hold values from -0.125 to 0.125
- w_key: bfloat16 [2048, 2048], P('fsdp', 'tensor'), may hold values from -0.125 to 0.125
- w_value: bfloat16 [2048, 2048], P('fsdp', 'tensor'), may hold values from -0.125 to 0.125
- b_query: bfloat16 [16, 128], P('tensor', 'fsdp'), may hold values from -3 to 3
- b_key: bfloat16 [16, 128], P('tensor', 'fsdp'), may hold values from -3 to 3
- b_value: bfloat16 [16, 128], P('tensor', 'fsdp'), may hold values from -3 to 3
- w_out: bfloat16 [2048, 2048], P('tensor', 'fsdp'), may hold values from -1.5 to 1.5
- norm2_gain: bfloat16 [2048], P(('fsdp', 'tensor')), may hold values from 0.5 to 1.5
- router: bfloat16 [2048, 8], P(('fsdp', 'tensor')), may hold values from -0.25 to 0.25
- shared_gate_vec: bfloat16 [2048], P(('fsdp', 'tensor')), may hold values from -0.125 to 0.125
- shared_gate: bfloat16 [2048, 5632], P('fsdp', 'tensor'), may hold values from -0.125 to 0.125
- shared_up: bfloat16 [2048, 5632], P('fsdp', 'tensor'), may hold values from -0.125 to 0.125
- shared_down: bfloat16 [5632, 2048], P('tensor', 'fsdp'), may hold values from -0.625 to 0.625
- expert_gate: bfloat16 [8, 2048, 1408], P('tensor', 'fsdp'), may hold values from -0.125 to 0.125
- expert_up: bfloat16 [8, 2048, 1408], P('tensor', 'fsdp'), may hold values from -0.125 to 0.125
- expert_down: bfloat16 [8, 1408, 2048], P('tensor', None, 'fsdp'), may hold values from -1.25 to 1.25
- cotangent: bfloat16 [2, 4, 1024, 2048], P(None, 'fsdp', 'tensor'), may hold values from -6 to 6
Outputs:
- layer_out: bfloat16 [2, 4, 1024, 2048], P(None, 'fsdp', 'tensor')
- grad_tokens: bfloat16 [2, 4, 1024, 2048], P(None, 'fsdp', 'tensor')
- grad_norm1_gain: float32 [2048], P(('fsdp', 'tensor'))
- grad_w_query: float32 [2048, 2048], P('fsdp', 'tensor')
- grad_w_key: float32 [2048, 2048], P('fsdp', 'tensor')
- grad_w_value: float32 [2048, 2048], P('fsdp', 'tensor')
- grad_b_query: float32 [16, 128], P('tensor', 'fsdp')
- grad_b_key: float32 [16, 128], P('tensor', 'fsdp')
- grad_b_value: float32 [16, 128], P('tensor', 'fsdp')
- grad_w_out: float32 [2048, 2048], P('tensor', 'fsdp')
- grad_norm2_gain: float32 [2048], P(('fsdp', 'tensor'))
- grad_router: float32 [2048, 8], P(('fsdp', 'tensor'))
- grad_shared_gate_vec: float32 [2048], P(('fsdp', 'tensor'))
- grad_shared_gate: float32 [2048, 5632], P('fsdp', 'tensor')
- grad_shared_up: float32 [2048, 5632], P('fsdp', 'tensor')
- grad_shared_down: float32 [5632, 2048], P('tensor', 'fsdp')
- grad_expert_gate: float32 [8, 2048, 1408], P('tensor', 'fsdp')
- grad_expert_up: float32 [8, 2048, 1408], P('tensor', 'fsdp')
- grad_expert_down: float32 [8, 1408, 2048], P('tensor', None, 'fsdp')
The draws below stay inside these ranges and needn't reach their ends.
Inputs may be any that keep to these rules, and one draw needn't show every extreme that they name: `lengths`: one sequence of every draw has exactly 1024 valid tokens. `routes`: each row names 4 different experts; among the 128 rows of one device within a sequence no expert is named by more than 96 rows, and in every draw some expert is named by exactly 96 of them.
All inputs are finite; a program needn't handle non-finite values.
Results may differ from the reference program's by a relative error of at most 0.03.
The reference program's roundings to bfloat16 on the way count: a program that leaves them out, or rounds other values in their place, can miss the bound.
Values may be sent and summed in bfloat16 or wider, within the bound.
A program may use at most 320 MiB of HBM per device.

```python
import math
import jax
import jax.numpy as jnp
import numpy as np
from jax import lax

D = 2048
HEADS = 16
HD = 128
FF_E = 1408
FF_S = 5632
TOP = 4
MICRO = 2
EXPERTS = 8
BATCH = 4
SEQLEN = 1024
TOK_LOC = 128
CAP = 96
SLOTS = 768


def draw_lengths(key, part):
    first_key, second_key, third_key = jax.random.split(key, 3)
    drawn = jax.random.randint(first_key, (MICRO, BATCH), SEQLEN // 4, SEQLEN + 1)
    pick_micro = jax.random.randint(second_key, (), 0, MICRO)
    pick_batch = jax.random.randint(third_key, (), 0, BATCH)
    chosen = (jnp.arange(MICRO)[:, None] == pick_micro) & (jnp.arange(BATCH)[None, :] == pick_batch)
    return jnp.where(chosen, SEQLEN, drawn).astype(jnp.int32)


def levels(own_key, dims, shards, least, largest):
    loudness, own = 1.0, jax.random.fold_in(own_key, 6)
    for axis_at, shards_of in shards:
        draws = jnp.exp(jax.random.uniform(jax.random.fold_in(own, axis_at), (shards_of,), jnp.float32, least / len(shards), largest / len(shards)))
        loudness = loudness * jnp.repeat(draws, dims[axis_at] // shards_of).reshape([-1 if axis == axis_at else 1 for axis in range(len(dims))])
    return loudness


def deal_out(own_key, own, number, rows, count, top, bound, skew):
    order = jax.random.permutation(own_key, count)
    crowded, common = shares(count, rows * top, bound, skew, True), shares(count, rows * top, bound, skew, False)
    places = jnp.arange(count)

    def named(sizes, offset_by):
        used = int((sizes > 0).sum())
        fixed = max(1, used // 4)
        moved = fixed + (places - fixed + offset_by * (used - fixed)) % max(1, count - fixed)
        return jnp.zeros((count,), jnp.int32).at[order[jnp.where(places < fixed, places, moved)]].set(jnp.asarray(sizes, jnp.int32))

    sizes = jnp.where(number % 4 == 0, named(crowded, number // 4), named(common, number - number // 4 - 1))
    mixed = jax.random.permutation(jax.random.fold_in(own, 3), count)
    donor, taker = mixed[0:count // 2 * 2:2], mixed[1:count // 2 * 2:2]
    room = jnp.minimum(sizes[donor] - 1, bound - sizes[taker]) // 2
    room = jnp.where((donor == order[0]) | (taker == order[0]) | (sizes[taker] == 0), 0, jnp.maximum(room, 0))
    moved = jax.random.randint(jax.random.fold_in(own, 4), (count // 2,), 0, 1 << 20) % (room + 1)
    sizes = sizes.at[donor].add(-moved).at[taker].add(moved)
    items = jnp.searchsorted(jnp.cumsum(sizes), jnp.arange(rows * top), side="right").astype(jnp.int32)
    listing = items.reshape(top, rows).T
    listing = listing[jax.random.permutation(jax.random.fold_in(own, 1), rows)]
    offset_by = jax.random.randint(jax.random.fold_in(own, 2), (rows, 1), 0, top)
    return jnp.take_along_axis(listing, (jnp.arange(top)[None, :] + offset_by) % top, axis=1)


def shares(count, total, bound, lean, full):
    loads = [(1 << 20) // math.isqrt(standing ** lean) + 1 for standing in range(1, count + 1)]
    largest = bound if full else min(bound, max(-(-total // count), total * loads[0] // sum(loads)))
    least = 1 if total - largest >= count - 1 else 0
    counts, rest = [largest] + [least] * (count - 1), total - largest - least * (count - 1)
    while rest > 0:
        free = [i for i in range(1, count) if counts[i] < largest] or [i for i in range(1, count) if counts[i] < bound]
        mass, left = sum([loads[i] for i in free]), rest
        for i in free:
            addition = min(bound - counts[i], max(1, left * loads[i] // mass), rest)
            counts[i] = counts[i] + addition
            rest = rest - addition
    return np.array(counts)


def normal_values(key, shape, deviation, limit, cuts=(), kind=jnp.bfloat16):
    level = levels(key, shape, cuts, -0.22, 0.18) if cuts else 1.0
    entries = jax.random.normal(key, shape, jnp.float32) * deviation * level
    return jnp.minimum(jnp.maximum(entries, -limit), limit).astype(kind)


def setup_inputs(seed: int = 0) -> dict:
    streams_of = jax.random.split(jax.random.key(seed), 22)
    tokens = normal_values(streams_of[0], (MICRO, BATCH, SEQLEN, D), 1.0, 6.0, ((1, 4), (2, 8)))
    lengths = draw_lengths(jax.random.fold_in(streams_of[21], 71), 0)
    routes_keys = jax.random.split(jax.random.fold_in(streams_of[2], 1), MICRO * BATCH * SEQLEN // TOK_LOC)
    routes_turns = jax.random.permutation(jax.random.fold_in(streams_of[2], 3), MICRO * BATCH * SEQLEN // TOK_LOC)
    routes = jax.vmap(lambda own, number: deal_out(jax.random.fold_in(streams_of[2], 2), own, number, TOK_LOC, EXPERTS, TOP, CAP, 2))(routes_keys, routes_turns).reshape((MICRO, BATCH, SEQLEN, TOP))
    norm1_gain = jnp.clip(1.0 + 0.1 * jax.random.normal(streams_of[3], (D,), jnp.float32), 0.5, 1.5).astype(jnp.bfloat16)
    w_query = normal_values(streams_of[4], (D, HEADS * HD), D ** -0.5, 0.125, ((0, 4), (1, 8)))
    w_key = normal_values(streams_of[5], (D, HEADS * HD), D ** -0.5, 0.125, ((0, 4), (1, 8)))
    w_value = normal_values(streams_of[6], (D, HEADS * HD), D ** -0.5, 0.125, ((0, 4), (1, 8)))
    b_query = normal_values(streams_of[7], (HEADS, HD), 0.5, 3.0, ((0, 8), (1, 4)))
    b_key = normal_values(streams_of[8], (HEADS, HD), 0.5, 3.0, ((0, 8), (1, 4)))
    b_value = normal_values(streams_of[9], (HEADS, HD), 0.5, 3.0, ((0, 8), (1, 4)))
    w_out = normal_values(streams_of[10], (HEADS * HD, D), (HD // 8) ** -0.5, 1.5, ((0, 8), (1, 4)))
    norm2_gain = jnp.clip(1.0 + 0.1 * jax.random.normal(streams_of[11], (D,), jnp.float32), 0.5, 1.5).astype(jnp.bfloat16)
    router = normal_values(streams_of[12], (D, EXPERTS), (D // 4) ** -0.5, 0.25, ((0, 32),))
    shared_gate_vec = normal_values(streams_of[13], (D,), D ** -0.5, 0.125, ((0, 32),))
    shared_gate = normal_values(streams_of[14], (D, FF_S), D ** -0.5, 0.125, ((0, 4), (1, 8)))
    shared_up = normal_values(streams_of[15], (D, FF_S), D ** -0.5, 0.125, ((0, 4), (1, 8)))
    shared_down = normal_values(streams_of[16], (FF_S, D), (max(1, FF_S // 64)) ** -0.5, 0.625, ((0, 8), (1, 4)))
    expert_gate = normal_values(streams_of[17], (EXPERTS, D, FF_E), D ** -0.5, 0.125, ((0, 8), (1, 4)))
    expert_up = normal_values(streams_of[18], (EXPERTS, D, FF_E), D ** -0.5, 0.125, ((0, 8), (1, 4)))
    expert_down = normal_values(streams_of[19], (EXPERTS, FF_E, D), (max(1, FF_E // 64)) ** -0.5, 1.25, ((0, 8), (2, 4)))
    cotangent = normal_values(streams_of[20], (MICRO, BATCH, SEQLEN, D), 1.0, 6.0, ((1, 4), (2, 8)))
    return dict(tokens=tokens, lengths=lengths, routes=routes, norm1_gain=norm1_gain, w_query=w_query, w_key=w_key, w_value=w_value, b_query=b_query, b_key=b_key, b_value=b_value, w_out=w_out, norm2_gain=norm2_gain, router=router, shared_gate_vec=shared_gate_vec, shared_gate=shared_gate, shared_up=shared_up, shared_down=shared_down, expert_gate=expert_gate, expert_up=expert_up, expert_down=expert_down, cotangent=cotangent)


@jax.custom_vjp
def low(v):
    return lax.optimization_barrier(v.astype(jnp.bfloat16)).astype(jnp.float32)

@jax.custom_vjp
def low_back(v):
    return v

def low_keep(v):
    return (low(v), None)

def low_pass(kept, grad):
    return (grad,)

def back_keep(v):
    return (v, None)

def back_low(kept, grad):
    return (low(grad),)
low.defvjp(low_keep, low_pass)
low_back.defvjp(back_keep, back_low)
EPSILON = 1e-06
ROPE_BASE = 1000000.0
HIGHEST = lax.Precision.HIGHEST

def matmul_hi(left, right):
    return jnp.dot(left, right, precision=HIGHEST)

def rms_norm(values, gain):
    return values * lax.rsqrt(lax.optimization_barrier(jnp.mean(values * values, axis=-1, keepdims=True)) + EPSILON) * gain

def rotary(values, positions):
    half_dim = values.shape[-1] // 2
    frequency = ROPE_BASE ** (-(2.0 * jnp.arange(half_dim, dtype=jnp.float32)) / values.shape[-1])
    angles = positions.astype(jnp.float32)[:, None] * frequency[None, :]
    cosine_part = jnp.cos(angles)[:, None, :]
    sine_part = jnp.sin(angles)[:, None, :]
    first_half = values[..., :half_dim]
    second_half = values[..., half_dim:]
    return jnp.concatenate([first_half * cosine_part - second_half * sine_part, second_half * cosine_part + first_half * sine_part], axis=-1)

def attention(query_rows, key_rows, values, length):
    seq_len = query_rows.shape[0]
    block_len = min(512, seq_len)
    score_scale = query_rows.shape[-1] ** (-0.5)
    key_pos = jnp.arange(seq_len, dtype=jnp.int32)
    starts = jnp.arange(seq_len // block_len, dtype=jnp.int32) * block_len

    def one_block(first_row):
        query_block = lax.dynamic_slice_in_dim(query_rows, first_row, block_len, 0)
        raw_scores = jnp.einsum('qhd,khd->hqk', query_block, key_rows, precision=HIGHEST)
        scores = low_back(raw_scores) * score_scale
        row_pos = first_row + jnp.arange(block_len, dtype=jnp.int32)
        allowed = (key_pos[None, :] <= row_pos[:, None]) & (key_pos[None, :] < length)
        scores = jnp.where(allowed[None], scores, -1e+30)
        weights = jax.nn.softmax(scores, axis=-1)
        return jnp.einsum('hqk,khd->qhd', low(weights), values, precision=HIGHEST)
    blocks_out = lax.map(jax.checkpoint(one_block), starts)
    return blocks_out.reshape(seq_len, query_rows.shape[1], query_rows.shape[2])

def pick_slots(route_rows, expert_id, slot_total):
    chosen = jnp.any(route_rows == expert_id, axis=1)
    rank_of = jnp.cumsum(chosen.astype(jnp.int32)) - 1
    target = jnp.where(chosen, rank_of, slot_total).astype(jnp.int32)
    token_ids = jnp.arange(route_rows.shape[0], dtype=jnp.int32)
    slot_index = jnp.zeros((slot_total,), jnp.int32).at[target].set(token_ids, mode='drop')
    filled = jnp.sum(chosen.astype(jnp.int32))
    slot_used = (jnp.arange(slot_total, dtype=jnp.int32) < filled).astype(jnp.float32)
    return (slot_index, slot_used)

def expert_mix(normed_two, route_rows, router_probs, expert_gate, expert_up, expert_down):

    def one_expert(running, expert_id):
        slot_index, slot_used = pick_slots(route_rows, expert_id, SLOTS)
        inputs = normed_two[slot_index]
        gate_act = low_back(matmul_hi(inputs, expert_gate[expert_id]))
        up_act = low_back(matmul_hi(inputs, expert_up[expert_id]))
        hidden = low(jax.nn.silu(gate_act) * up_act)
        result = low_back(matmul_hi(hidden, expert_down[expert_id]))
        slot_weight = router_probs[slot_index, expert_id] * slot_used
        return (running.at[slot_index].add(slot_weight[:, None] * result), None)
    mixed_sum, unused = lax.scan(jax.checkpoint(one_expert), jnp.zeros(normed_two.shape, jnp.float32), jnp.arange(EXPERTS, dtype=jnp.int32))
    return mixed_sum

def layer_step(params, sequence, length, route_rows):
    norm1_gain, w_query, w_key, w_value, b_query, b_key, b_value, w_out, norm2_gain, router, shared_gate_vec, shared_gate, shared_up, shared_down, expert_gate, expert_up, expert_down = params
    seq_len = sequence.shape[0]
    positions = jnp.arange(seq_len, dtype=jnp.int32)
    normed = low(rms_norm(sequence, norm1_gain))
    query_pre = low_back(matmul_hi(normed, w_query) + b_query.reshape(-1)).reshape(seq_len, HEADS, HD)
    key_pre = low_back(matmul_hi(normed, w_key) + b_key.reshape(-1)).reshape(seq_len, HEADS, HD)
    query_rows = low(rotary(query_pre, positions))
    key_rows = low(rotary(key_pre, positions))
    values = low(low_back(matmul_hi(normed, w_value) + b_value.reshape(-1))).reshape(seq_len, HEADS, HD)
    mixed_heads = low(low_back(attention(query_rows, key_rows, values, length))).reshape(seq_len, HEADS * HD)
    attended = low_back(matmul_hi(mixed_heads, w_out))
    hidden_one = sequence + attended
    normed_two = low(rms_norm(hidden_one, norm2_gain))
    router_probs = jax.nn.softmax(matmul_hi(normed_two, router), axis=-1)
    shared_scale = jax.nn.sigmoid(matmul_hi(normed_two, shared_gate_vec))
    gate_act = low_back(matmul_hi(normed_two, shared_gate))
    up_act = low_back(matmul_hi(normed_two, shared_up))
    shared_hidden = low(jax.nn.silu(gate_act) * up_act)
    shared_result = low_back(matmul_hi(shared_hidden, shared_down))
    expert_sum = expert_mix(normed_two, route_rows, router_probs, expert_gate, expert_up, expert_down)
    inside = (positions < length).astype(jnp.float32)
    return inside[:, None] * (hidden_one + expert_sum + shared_scale[:, None] * shared_result)

def reference(tokens, lengths, routes, norm1_gain, w_query, w_key, w_value, b_query, b_key, b_value, w_out, norm2_gain, router, shared_gate_vec, shared_gate, shared_up, shared_down, expert_gate, expert_up, expert_down, cotangent):
    weights = tuple((item.astype(jnp.float32) for item in (norm1_gain, w_query, w_key, w_value, b_query, b_key, b_value, w_out, norm2_gain, router, shared_gate_vec, shared_gate, shared_up, shared_down, expert_gate, expert_up, expert_down)))
    flat_tokens = tokens.reshape(MICRO * BATCH, SEQLEN, D).astype(jnp.float32)
    flat_lengths = lengths.reshape(MICRO * BATCH)
    flat_routes = routes.reshape(MICRO * BATCH, SEQLEN, TOP)

    def forward(params, inputs):

        def sequence_step(carried, element):
            sequence, length, route_rows = element
            return (carried, layer_step(params, sequence, length, route_rows))
        unused, outputs = lax.scan(jax.checkpoint(sequence_step), jnp.zeros((), jnp.float32), (inputs, flat_lengths, flat_routes))
        return outputs
    outputs, pullback = jax.vjp(forward, weights, flat_tokens)
    grads_w, grad_in = pullback(cotangent.reshape(MICRO * BATCH, SEQLEN, D).astype(jnp.float32))
    return (outputs.reshape(tokens.shape).astype(jnp.bfloat16), grad_in.reshape(tokens.shape).astype(jnp.bfloat16), grads_w[0], grads_w[1], grads_w[2], grads_w[3], grads_w[4], grads_w[5], grads_w[6], grads_w[7], grads_w[8], grads_w[9], grads_w[10], grads_w[11], grads_w[12], grads_w[13], grads_w[14], grads_w[15], grads_w[16])
```

```python
import functools

import jax
import jax.numpy as jnp
from jax import lax
from jax.experimental import pallas as pl
from jax.experimental.pallas import tpu as pltpu
from jax.sharding import PartitionSpec as P

HD = 128
EPSILON = 1e-06
ROPE_BASE = 1000000.0
BF = jnp.bfloat16
F32 = jnp.float32
QB = 256


def dot(left, right, left_dims, right_dims):
    return lax.dot_general(
        left, right, ((left_dims, right_dims), ((), ())), preferred_element_type=F32
    )


def normalize(values):
    inverse = lax.rsqrt(jnp.mean(values * values, axis=-1, keepdims=True) + EPSILON)
    return (values * inverse, inverse)


def norm_back(grad_normed, unit, inverse, gain):
    grad_unit = grad_normed * gain
    grad_values = inverse * (grad_unit - unit * jnp.mean(grad_unit * unit, axis=-1, keepdims=True))
    return (grad_values, jnp.sum(grad_normed * unit, axis=0))


def line_pairs(size, chips):
    return [(2 * z + c, 2 * (z + size) + c) for z in chips for c in range(2)]


def swap_cores(values, ranks):
    return lax.ppermute(values, "tensor", [(t, t ^ 1) for t in range(ranks)])


def gather_rows(block, ranks):
    chips = ranks // 2
    rank = lax.axis_index("tensor")
    chip, core = rank // 2, rank % 2
    pieces = []
    upward = downward = block
    for step in range(1, chips):
        upward = lax.ppermute(upward, "tensor", line_pairs(1, range(step - 1, chips - 1)))
        downward = lax.ppermute(downward, "tensor", line_pairs(-1, range(1, chips - step + 1)))
        from_below, from_above = chip >= step, chip < chips - step
        if 2 * step > chips - 1:
            place = jnp.where(from_below, chip - step, jnp.where(from_above, chip + step, chip))
            pieces.append((jnp.where(from_below, upward, downward), place))
        else:
            pieces.append((upward, jnp.where(from_below, chip - step, chip)))
            pieces.append((downward, jnp.where(from_above, chip + step, chip)))
    pieces.append((block, chip))
    whole = jnp.zeros((chips, 2) + block.shape, block.dtype)
    rest = (0,) * block.ndim
    for piece, place in pieces:
        whole = lax.dynamic_update_slice(whole, piece[None, None], (place, core) + rest)
        other = swap_cores(piece, ranks)
        whole = lax.dynamic_update_slice(whole, other[None, None], (place, 1 - core) + rest)
    return whole.reshape((ranks * block.shape[0],) + block.shape[1:])


def scatter_rows(partial, ranks):
    chips = ranks // 2
    rank = lax.axis_index("tensor")
    chip, core = rank // 2, rank % 2
    rows = partial.shape[0] // ranks
    halves = partial.reshape(chips, 2, rows, -1)
    kept = lax.dynamic_index_in_dim(halves, core, 1, False)
    given = lax.dynamic_index_in_dim(halves, 1 - core, 1, False)
    both = kept.astype(F32) + swap_cores(given, ranks).astype(F32)
    narrow = both.astype(BF)

    def pick(index):
        return lax.dynamic_index_in_dim(narrow, jnp.clip(index, 0, chips - 1), 0, False)

    upward = pick(chip + chips - 1)
    downward = pick(chip - chips + 1)
    for step in range(1, chips):
        upward = lax.ppermute(upward, "tensor", line_pairs(1, range(0, step)))
        downward = lax.ppermute(downward, "tensor", line_pairs(-1, range(chips - step, chips)))
        if step < chips - 1:
            following = chips - step - 1
            upward = (upward.astype(F32) + pick(chip + following).astype(F32)).astype(BF)
            downward = (downward.astype(F32) + pick(chip - following).astype(F32)).astype(BF)
    own = lax.dynamic_index_in_dim(both, chip, 0, False)
    return own + upward.astype(F32) + downward.astype(F32)


def rope_tables(seq_len):
    half = HD // 2
    frequency = ROPE_BASE ** (-(2.0 * jnp.arange(half, dtype=F32)) / HD)
    angles = jnp.arange(seq_len, dtype=F32)[:, None] * frequency[None, :]
    cosine, sine = jnp.cos(angles), jnp.sin(angles)
    return (
        jnp.concatenate([cosine, cosine], axis=1),
        jnp.concatenate([-sine, sine], axis=1),
    )


def swap_halves(values):
    half = HD // 2
    return jnp.concatenate([values[:, half:], values[:, :half]], axis=1)


def block_weights(query, keys, first_row, length):
    scores = dot(query, keys, (1,), (1,)) * (HD ** (-0.5))
    rows = first_row + lax.broadcasted_iota(jnp.int32, scores.shape, 0)
    cols = lax.broadcasted_iota(jnp.int32, scores.shape, 1)
    scores = jnp.where((cols <= rows) & (cols < length), scores, -1e30)
    exps = jnp.exp(scores - jnp.max(scores, axis=1, keepdims=True))
    return exps / jnp.sum(exps, axis=1, keepdims=True)


def attend_kernel(heads, length_ref, pre_ref, bias_ref, cos_ref, sin_ref, qkv_ref, out_ref):
    seq_len = pre_ref.shape[0]
    length = length_ref[0]
    for head in range(heads):
        for which in range(3):
            at = (which * heads + head) * HD
            for row in range(0, seq_len, QB):
                part = pre_ref[row : row + QB, at : at + HD] + bias_ref[:, at : at + HD]
                if which < 2:
                    part = (
                        part * cos_ref[row : row + QB, :]
                        + swap_halves(part) * sin_ref[row : row + QB, :]
                    )
                qkv_ref[row : row + QB, at : at + HD] = part.astype(BF)
        q_at, k_at, v_at = (head * HD, (heads + head) * HD, (2 * heads + head) * HD)
        for row in range(0, seq_len, QB):
            end = row + QB
            weights = block_weights(
                qkv_ref[row:end, q_at : q_at + HD], qkv_ref[:end, k_at : k_at + HD], row, length
            )
            mixed = dot(weights.astype(BF), qkv_ref[:end, v_at : v_at + HD], (1,), (0,))
            out_ref[row:end, q_at : q_at + HD] = mixed.astype(BF)


def attend_back_kernel(
    heads, length_ref, qkv_ref, grad_ref, cos_ref, sin_ref, out_ref, sums_ref, key_acc, value_acc
):
    seq_len = qkv_ref.shape[0]
    length = length_ref[0]
    scale = HD ** (-0.5)
    for head in range(heads):
        q_at, k_at, v_at = (head * HD, (heads + head) * HD, (2 * heads + head) * HD)
        key_acc[...] = jnp.zeros_like(key_acc)
        value_acc[...] = jnp.zeros_like(value_acc)
        q_sum = jnp.zeros((1, HD), F32)
        for row in range(0, seq_len, QB):
            end = row + QB
            query = qkv_ref[row:end, q_at : q_at + HD]
            keys = qkv_ref[:end, k_at : k_at + HD]
            grad = grad_ref[row:end, q_at : q_at + HD]
            weights = block_weights(query, keys, row, length)
            grad_weights = dot(grad, qkv_ref[:end, v_at : v_at + HD], (1,), (1,))
            inner = jnp.sum(weights * grad_weights, axis=1, keepdims=True)
            grad_scores = (scale * weights * (grad_weights - inner)).astype(BF)
            turned = dot(grad_scores, keys, (1,), (0,))
            grad_query = (
                turned * cos_ref[row:end, :] - swap_halves(turned) * sin_ref[row:end, :]
            ).astype(BF)
            out_ref[row:end, q_at : q_at + HD] = grad_query
            q_sum = q_sum + jnp.sum(grad_query.astype(F32), axis=0, keepdims=True)
            key_acc[:end, :] += dot(grad_scores, query, (0,), (0,))
            value_acc[:end, :] += dot(weights.astype(BF), grad, (0,), (0,))
        k_sum = jnp.zeros((1, HD), F32)
        v_sum = jnp.zeros((1, HD), F32)
        for row in range(0, seq_len, QB):
            end = row + QB
            turned = key_acc[row:end, :]
            grad_key = (
                turned * cos_ref[row:end, :] - swap_halves(turned) * sin_ref[row:end, :]
            ).astype(BF)
            grad_value = value_acc[row:end, :].astype(BF)
            out_ref[row:end, k_at : k_at + HD] = grad_key
            out_ref[row:end, v_at : v_at + HD] = grad_value
            k_sum = k_sum + jnp.sum(grad_key.astype(F32), axis=0, keepdims=True)
            v_sum = v_sum + jnp.sum(grad_value.astype(F32), axis=0, keepdims=True)
        sums_ref[:, q_at : q_at + HD] = q_sum
        sums_ref[:, k_at : k_at + HD] = k_sum
        sums_ref[:, v_at : v_at + HD] = v_sum


def in_vmem(count):
    return [pl.BlockSpec(memory_space=pltpu.VMEM)] * count


def attend(length, pre, bias, cosine, sine):
    seq_len, width = pre.shape
    heads = width // (3 * HD)
    return pl.pallas_call(
        functools.partial(attend_kernel, heads),
        out_shape=(
            jax.ShapeDtypeStruct((seq_len, width), BF),
            jax.ShapeDtypeStruct((seq_len, heads * HD), BF),
        ),
        in_specs=[pl.BlockSpec(memory_space=pltpu.SMEM)] + in_vmem(4),
        out_specs=tuple(in_vmem(2)),
        compiler_params=pltpu.CompilerParams(vmem_limit_bytes=32 << 20),
        cost_estimate=pl.CostEstimate(
            flops=3 * heads * HD * seq_len * seq_len,
            bytes_accessed=10 * seq_len * width,
            transcendentals=heads * seq_len * seq_len,
        ),
    )(length, pre, bias, cosine, sine)


def attend_back(length, qkv, grad, cosine, sine):
    seq_len, width = qkv.shape
    heads = width // (3 * HD)
    return pl.pallas_call(
        functools.partial(attend_back_kernel, heads),
        out_shape=(
            jax.ShapeDtypeStruct((seq_len, width), BF),
            jax.ShapeDtypeStruct((1, width), F32),
        ),
        in_specs=[pl.BlockSpec(memory_space=pltpu.SMEM)] + in_vmem(4),
        out_specs=tuple(in_vmem(2)),
        scratch_shapes=[pltpu.VMEM((seq_len, HD), F32), pltpu.VMEM((seq_len, HD), F32)],
        compiler_params=pltpu.CompilerParams(vmem_limit_bytes=32 << 20),
        cost_estimate=pl.CostEstimate(
            flops=8 * heads * HD * seq_len * seq_len,
            bytes_accessed=8 * seq_len * width,
            transcendentals=heads * seq_len * seq_len,
        ),
    )(length, qkv, grad, cosine, sine)


def local(
    tokens,
    lengths,
    routes,
    norm1_gain,
    w_query,
    w_key,
    w_value,
    b_query,
    b_key,
    b_value,
    w_out,
    norm2_gain,
    router,
    shared_gate_vec,
    shared_gate,
    shared_up,
    shared_down,
    expert_gate,
    expert_up,
    expert_down,
    cotangent,
):
    ranks = lax.axis_size("tensor")
    groups = lax.axis_size("fsdp")
    rank = lax.axis_index("tensor")
    micros, _, rows, width = tokens.shape
    seq_len = rows * ranks
    heads = w_query.shape[1] // HD
    span = heads * HD
    experts = ranks * expert_gate.shape[0]
    shared_units = shared_gate.shape[1]
    own_first = rank * rows
    positions = jnp.arange(seq_len, dtype=jnp.int32)
    local_pos = own_first + jnp.arange(rows, dtype=jnp.int32)

    per_device = norm1_gain.shape[0]
    small = jnp.concatenate(
        [
            norm1_gain,
            norm2_gain,
            shared_gate_vec,
            router.reshape(-1),
            b_query.reshape(-1),
            b_key.reshape(-1),
            b_value.reshape(-1),
        ]
    )
    small_all = lax.all_gather(small, ("fsdp", "tensor"), axis=0, tiled=False)
    gain_one = small_all[:, :per_device].reshape(-1).astype(F32)
    gain_two = small_all[:, per_device : 2 * per_device].reshape(-1).astype(F32)
    gate_vec = small_all[:, 2 * per_device : 3 * per_device].reshape(-1)
    bias_at = per_device * (3 + experts)
    router_full = small_all[:, 3 * per_device : bias_at].reshape(width, experts)
    router_wide = jnp.concatenate([router_full, gate_vec[:, None]], axis=1)
    own_bias = lax.dynamic_index_in_dim(
        small_all.reshape(groups, ranks, -1), rank, 1, False
    )[:, bias_at:].reshape(groups, 3, heads, HD // groups)
    bias = own_bias.transpose(1, 2, 0, 3).reshape(1, 3 * span).astype(F32)

    qkv_w = lax.all_gather(
        jnp.concatenate([w_query, w_key, w_value], axis=1), "fsdp", axis=0, tiled=True
    )
    out_w = lax.all_gather(w_out, "fsdp", axis=1, tiled=True)
    gate_w = lax.all_gather(
        jnp.concatenate([shared_gate, expert_gate[0]], axis=1), "fsdp", axis=0, tiled=True
    )
    up_w = lax.all_gather(
        jnp.concatenate([shared_up, expert_up[0]], axis=1), "fsdp", axis=0, tiled=True
    )
    down_w = lax.all_gather(
        jnp.concatenate([shared_down, expert_down[0]], axis=0), "fsdp", axis=1, tiled=True
    )

    cosine, sine = rope_tables(seq_len)
    token_rows = [gather_rows(tokens[m, 0], ranks) for m in range(micros)]
    grads_own = []
    for m in range(micros):
        inside = (local_pos < lengths[m, 0])[:, None]
        grads_own.append(jnp.where(inside, cotangent[m, 0], jnp.zeros((), BF)))
    grad_rows = [gather_rows(grads_own[m], ranks) for m in range(micros)]

    saved = []
    layer_outs = []
    for m in range(micros):
        length = lengths[m]
        normed_one = (normalize(token_rows[m].astype(F32))[0] * gain_one).astype(BF)
        pre = dot(normed_one, qkv_w, (1,), (0,))
        qkv, mixed = attend(length, pre, bias, cosine, sine)
        attended = scatter_rows(dot(mixed, out_w, (1,), (0,)).astype(BF), ranks)
        hidden = tokens[m, 0].astype(F32) + attended
        unit_two, inverse_two = normalize(hidden)
        rows_two = gather_rows((unit_two * gain_two).astype(BF), ranks)
        saved.append((normed_one, qkv, mixed, hidden, rows_two))

    ffn = []
    for m in range(micros):
        normed_one, qkv, mixed, hidden, rows_two = saved[m]
        logits = dot(rows_two, router_wide, (1,), (0,))
        probs = jax.nn.softmax(logits[:, :experts], axis=-1)
        shared_scale = jax.nn.sigmoid(logits[:, experts:])
        chosen = jnp.any(routes[m, 0] == rank, axis=1, keepdims=True)
        own_expert = (jnp.arange(experts, dtype=jnp.int32) == rank)[None, :]
        prob = jnp.sum(jnp.where(own_expert, probs, 0.0), axis=1, keepdims=True)
        expert_scale = jnp.where(chosen, prob, 0.0)
        is_shared = (jnp.arange(gate_w.shape[1]) < shared_units)[None, :]
        scale = jnp.where(is_shared, shared_scale, expert_scale)
        gate_act = dot(rows_two, gate_w, (1,), (0,))
        up_act = dot(rows_two, up_w, (1,), (0,))
        sigmoid = jax.nn.sigmoid(gate_act)
        unit_hidden = (gate_act * sigmoid * up_act).astype(BF)
        scaled = (scale * unit_hidden.astype(F32)).astype(BF)
        moved = scatter_rows(dot(scaled, down_w, (1,), (0,)).astype(BF), ranks)
        inside = (local_pos < lengths[m, 0]).astype(F32)[:, None]
        layer_outs.append((inside * (hidden + moved)).astype(BF))
        back = dot(grad_rows[m], down_w, (1,), (1,))
        product = unit_hidden.astype(F32) * back
        shared_grad = jnp.sum(jnp.where(is_shared, product, 0.0), axis=1, keepdims=True)
        expert_grad = jnp.sum(jnp.where(is_shared, 0.0, product), axis=1, keepdims=True)
        grad_hidden = scale * back
        grad_gate = (grad_hidden * up_act * sigmoid * (1.0 + gate_act * (1.0 - sigmoid))).astype(BF)
        grad_up = (grad_hidden * gate_act * sigmoid).astype(BF)
        expert_grad = jnp.where(chosen, expert_grad, 0.0)
        grad_logits = probs * (jnp.where(own_expert, expert_grad, 0.0) - expert_grad * prob)
        grad_gate_logit = shared_grad * shared_scale * (1.0 - shared_scale)
        grad_wide = jnp.concatenate([grad_logits, grad_gate_logit], axis=1).astype(BF)
        partial = (
            dot(grad_gate, gate_w, (1,), (1,))
            + dot(grad_up, up_w, (1,), (1,))
            + dot(grad_wide, router_wide, (1,), (1,))
        )
        ffn.append((scaled, grad_gate, grad_up, grad_wide, scatter_rows(partial.astype(BF), ranks)))

    rows_both = jnp.concatenate([saved[m][4] for m in range(micros)], axis=0)
    total_down = dot(
        jnp.concatenate([ffn[m][0] for m in range(micros)], axis=0),
        jnp.concatenate(grad_rows, axis=0),
        (0,),
        (0,),
    )
    total_gate = dot(rows_both, jnp.concatenate([ffn[m][1] for m in range(micros)], axis=0), (0,), (0,))
    total_up = dot(rows_both, jnp.concatenate([ffn[m][2] for m in range(micros)], axis=0), (0,), (0,))
    total_wide = dot(rows_both, jnp.concatenate([ffn[m][3] for m in range(micros)], axis=0), (0,), (0,))
    down_g = lax.psum_scatter(total_down.astype(BF), "fsdp", scatter_dimension=1, tiled=True)
    gate_g = lax.psum_scatter(total_gate.astype(BF), "fsdp", scatter_dimension=0, tiled=True)
    up_g = lax.psum_scatter(total_up.astype(BF), "fsdp", scatter_dimension=0, tiled=True)

    grad_gain_two = jnp.zeros((width,), F32)
    backs = []
    for m in range(micros):
        normed_one, qkv, mixed, hidden, rows_two = saved[m]
        unit_two, inverse_two = normalize(hidden)
        grad_hidden, gain_part = norm_back(ffn[m][4], unit_two, inverse_two, gain_two)
        grad_gain_two = grad_gain_two + gain_part
        grad_hidden = grad_hidden + grads_own[m].astype(F32)
        attn_grad = gather_rows(grad_hidden.astype(BF), ranks)
        backs.append((grad_hidden, attn_grad))

    grad_gain_one = jnp.zeros((width,), F32)
    bias_sums = jnp.zeros((1, 3 * span), F32)
    grad_qkvs = []
    input_grads = []
    for m in range(micros):
        normed_one, qkv, mixed, hidden, rows_two = saved[m]
        grad_hidden, attn_grad = backs[m]
        grad_mixed = dot(attn_grad, out_w, (1,), (1,)).astype(BF)
        grad_qkv, sums = attend_back(lengths[m], qkv, grad_mixed, cosine, sine)
        bias_sums = bias_sums + sums
        grad_qkvs.append(grad_qkv)
        grad_normed = scatter_rows(dot(grad_qkv, qkv_w, (1,), (1,)).astype(BF), ranks)
        unit_one, inverse_one = normalize(tokens[m, 0].astype(F32))
        grad_inputs, gain_part = norm_back(grad_normed, unit_one, inverse_one, gain_one)
        grad_gain_one = grad_gain_one + gain_part
        input_grads.append((grad_inputs + grad_hidden).astype(BF))

    total_out = dot(
        jnp.concatenate([saved[m][2] for m in range(micros)], axis=0),
        jnp.concatenate([backs[m][1] for m in range(micros)], axis=0),
        (0,),
        (0,),
    )
    total_qkv = dot(
        jnp.concatenate([saved[m][0] for m in range(micros)], axis=0),
        jnp.concatenate(grad_qkvs, axis=0),
        (0,),
        (0,),
    )
    out_g = lax.psum_scatter(total_out.astype(BF), "fsdp", scatter_dimension=1, tiled=True).astype(F32)
    qkv_g = lax.psum_scatter(total_qkv.astype(BF), "fsdp", scatter_dimension=0, tiled=True).astype(F32)

    early = jnp.concatenate([grad_gain_two[:, None], total_wide], axis=1)
    early = lax.psum_scatter(early, ("fsdp", "tensor"), scatter_dimension=0, tiled=True)
    slots = (jnp.arange(ranks, dtype=jnp.int32) == rank).astype(F32)[:, None]
    late = jnp.concatenate([grad_gain_one, (slots * bias_sums).reshape(-1)])
    late = lax.psum(late, ("fsdp", "tensor"))
    place = lax.axis_index("fsdp") * ranks + rank
    gain_one_g = lax.dynamic_slice_in_dim(late, place * per_device, per_device, 0)
    bias_g = lax.dynamic_slice_in_dim(late, width + rank * 3 * span, 3 * span, 0)
    part = HD // groups
    bias_g = lax.dynamic_slice_in_dim(
        bias_g.reshape(3, heads, HD), lax.axis_index("fsdp") * part, part, 2
    )

    return (
        jnp.stack(layer_outs)[:, None],
        jnp.stack(input_grads)[:, None],
        gain_one_g,
        qkv_g[:, :span],
        qkv_g[:, span : 2 * span],
        qkv_g[:, 2 * span :],
        bias_g[0],
        bias_g[1],
        bias_g[2],
        out_g,
        early[:, 0],
        early[:, 1 : 1 + experts],
        early[:, 1 + experts],
        gate_g[:, :shared_units].astype(F32),
        up_g[:, :shared_units].astype(F32),
        down_g[:shared_units].astype(F32),
        gate_g[None, :, shared_units:].astype(F32),
        up_g[None, :, shared_units:].astype(F32),
        down_g[None, shared_units:].astype(F32),
    )


def solution(mesh):
    in_specs = (
        P(None, "fsdp", "tensor", None),
        P(None, "fsdp"),
        P(None, "fsdp", None, None),
        P(("fsdp", "tensor")),
        P("fsdp", "tensor"),
        P("fsdp", "tensor"),
        P("fsdp", "tensor"),
        P("tensor", "fsdp"),
        P("tensor", "fsdp"),
        P("tensor", "fsdp"),
        P("tensor", "fsdp"),
        P(("fsdp", "tensor")),
        P(("fsdp", "tensor"), None),
        P(("fsdp", "tensor")),
        P("fsdp", "tensor"),
        P("fsdp", "tensor"),
        P("tensor", "fsdp"),
        P("tensor", "fsdp", None),
        P("tensor", "fsdp", None),
        P("tensor", None, "fsdp"),
        P(None, "fsdp", "tensor", None),
    )
    out_specs = (
        P(None, "fsdp", "tensor", None),
        P(None, "fsdp", "tensor", None),
        P(("fsdp", "tensor")),
        P("fsdp", "tensor"),
        P("fsdp", "tensor"),
        P("fsdp", "tensor"),
        P("tensor", "fsdp"),
        P("tensor", "fsdp"),
        P("tensor", "fsdp"),
        P("tensor", "fsdp"),
        P(("fsdp", "tensor")),
        P(("fsdp", "tensor"), None),
        P(("fsdp", "tensor")),
        P("fsdp", "tensor"),
        P("fsdp", "tensor"),
        P("tensor", "fsdp"),
        P("tensor", "fsdp", None),
        P("tensor", "fsdp", None),
        P("tensor", None, "fsdp"),
    )
    return jax.shard_map(local, mesh=mesh, in_specs=in_specs, out_specs=out_specs, check_vma=False)
```

```python
import functools

import jax
import jax.numpy as jnp
from jax import lax
from jax.experimental import pallas as pl
from jax.experimental.layout import Layout, with_layout_constraint
from jax.experimental.pallas import tpu as pltpu
from jax.sharding import PartitionSpec as P

HD = 128
EPSILON = 1e-06
ROPE_BASE = 1000000.0
BF = jnp.bfloat16
F32 = jnp.float32
MESH = pl.DeviceIdType.MESH
QB = 256
LANES = 128
CHUNKS = 2
STRIP = 16
ROW_BLOCK = 256
VMEM_BYTES = 60 << 20


def dot(left, right, left_dims, right_dims):
    return lax.dot_general(
        left, right, ((left_dims, right_dims), ((), ())), preferred_element_type=F32
    )


def normalize(values):
    inverse = lax.rsqrt(jnp.mean(values * values, axis=-1, keepdims=True) + EPSILON)
    return (values * inverse, inverse)


def norm_back(grad_normed, unit, inverse, gain):
    grad_unit = grad_normed * gain
    grad_values = inverse * (grad_unit - unit * jnp.mean(grad_unit * unit, axis=-1, keepdims=True))
    return (grad_values, jnp.sum(grad_normed * unit, axis=0))


def after(value, *others):
    return lax.optimization_barrier((value,) + others)[0]


def remote(src, dst, sems, at, target):
    return pltpu.make_async_remote_copy(
        src_ref=src,
        dst_ref=dst,
        send_sem=sems[0].at[at],
        recv_sem=sems[1].at[at],
        device_id={"tensor": target},
        device_id_type=MESH,
    )


class Place:
    def __init__(self, ranks):
        rank = lax.axis_index("tensor")
        self.chips = ranks // 2
        self.chip, self.core = rank // 2, rank % 2
        self.partner = rank + 1 - 2 * self.core
        self.above, self.below = rank + 2, rank - 2
        self.not_top = self.chip < self.chips - 1
        self.not_bottom = self.chip > 0

    def meet(self):
        barrier = pltpu.get_barrier_semaphore()

        def greet(target):
            pl.semaphore_signal(barrier, 1, device_id={"tensor": target}, device_id_type=MESH)

        greet(self.partner)
        pl.when(self.not_top)(lambda: greet(self.above))
        pl.when(self.not_bottom)(lambda: greet(self.below))
        peers = 1 + self.not_top.astype(jnp.int32) + self.not_bottom.astype(jnp.int32)
        pl.semaphore_wait(barrier, peers)


def gather_scratch(ranks):
    chips = ranks // 2
    pair = [pltpu.SemaphoreType.DMA((chips, CHUNKS))] * 2
    cross = [pltpu.SemaphoreType.DMA((2 * chips, CHUNKS))] * 2
    return [pltpu.SemaphoreType.DMA] + pair + pair + cross


def gather_steps(place, block, whole, local_sem, up_s, up_r, down_s, down_r, cross_s, cross_r):
    chips, chip, core = place.chips, place.chip, place.core
    rows = block.shape[0]
    part = rows // CHUNKS
    up, down, cross = (up_s, up_r), (down_s, down_r), (cross_s, cross_r)

    def at(owner, chunk):
        first = pl.multiple_of((2 * owner + core) * rows + chunk * part, part)
        return whole.at[pl.ds(first, part)]

    def theirs(owner, chunk):
        first = pl.multiple_of((2 * owner + 1 - core) * rows + chunk * part, part)
        return whole.at[pl.ds(first, part)]

    def own(chunk):
        return block.at[pl.ds(chunk * part, part)]

    def upward(step, chunk):
        source = own(chunk) if step == 0 else at(chip - step, chunk)
        return remote(source, at(chip - step, chunk), up, (step, chunk), place.above)

    def downward(step, chunk):
        source = own(chunk) if step == 0 else at(chip + step, chunk)
        return remote(source, at(chip + step, chunk), down, (step, chunk), place.below)

    def across(slot, owner, chunk):
        source = own(chunk) if slot == 0 else at(owner, chunk)
        return remote(source, at(owner, chunk), cross, (slot, chunk), place.partner)

    def arrived(slot, owner, chunk):
        return remote(theirs(owner, chunk), theirs(owner, chunk), cross, (slot, chunk), place.partner)

    def arrived_up(step, chunk):
        return remote(at(chip - step, chunk), at(chip - step, chunk), up, (step - 1, chunk), place.above)

    def arrived_down(step, chunk):
        return remote(at(chip + step, chunk), at(chip + step, chunk), down, (step - 1, chunk), place.below)

    both = range(CHUNKS)

    def mine():
        first = pl.multiple_of((2 * chip + core) * rows, rows)
        return pltpu.make_async_copy(block, whole.at[pl.ds(first, rows)], local_sem)

    for chunk in both:
        pl.when(place.not_top)(lambda: upward(0, chunk).start())
        pl.when(place.not_bottom)(lambda: downward(0, chunk).start())
    for chunk in both:
        across(0, chip, chunk).start()
    mine().start()
    yield
    for step in range(1, chips):
        for chunk in both:

            @pl.when(chip >= step)
            def _():
                arrived_up(step, chunk).wait_recv()
                pl.when(place.not_top)(lambda: upward(step, chunk).start())
                across(2 * step - 1, chip - step, chunk).start()

            @pl.when(chip < chips - step)
            def _():
                arrived_down(step, chunk).wait_recv()
                pl.when(place.not_bottom)(lambda: downward(step, chunk).start())
                across(2 * step, chip + step, chunk).start()

        yield
    mine().wait()
    for step in range(chips):
        for chunk in both:
            if step == 0:
                arrived(0, chip, chunk).wait_recv()
                across(0, chip, chunk).wait_send()
            else:

                @pl.when(chip >= step)
                def _():
                    arrived(2 * step - 1, chip - step, chunk).wait_recv()
                    across(2 * step - 1, chip - step, chunk).wait_send()

                @pl.when(chip < chips - step)
                def _():
                    arrived(2 * step, chip + step, chunk).wait_recv()
                    across(2 * step, chip + step, chunk).wait_send()

            @pl.when(place.not_top & (chip >= step))
            def _():
                upward(step, chunk).wait_send()

            @pl.when(place.not_bottom & (chip < chips - step))
            def _():
                downward(step, chunk).wait_send()


def scatter_scratch(ranks, rows, width):
    chips = ranks // 2
    line = [pltpu.SemaphoreType.DMA((chips, CHUNKS))] * 2
    buffers = [pltpu.VMEM((chips, rows, width), BF)] * 5
    return buffers + [pltpu.SemaphoreType.DMA((chips,))] + line * 3


def scatter_steps(
    place, partial, total, kept, pair, held, up_in, down_in, keep_sem,
    up_s, up_r, down_s, down_r, cross_s, cross_r,
):
    chips, chip, core = place.chips, place.chip, place.core
    rows = total.shape[0]
    part = rows // CHUNKS
    up, down, cross = (up_s, up_r), (down_s, down_r), (cross_s, cross_r)
    both = range(CHUNKS)

    def keep(k):
        first = pl.multiple_of((2 * k + core) * rows, rows)
        return pltpu.make_async_copy(partial.at[pl.ds(first, rows)], kept.at[k], keep_sem.at[k])

    def across(k, chunk):
        first = pl.multiple_of((2 * k + 1 - core) * rows + chunk * part, part)
        return remote(
            partial.at[pl.ds(first, part)],
            pair.at[k, pl.ds(chunk * part, part)],
            cross,
            (k, chunk),
            place.partner,
        )

    def upward(step, k, chunk):
        cut = pl.ds(chunk * part, part)
        return remote(held.at[k, cut], up_in.at[step, cut], up, (step, chunk), place.above)

    def downward(step, k, chunk):
        cut = pl.ds(chunk * part, part)
        return remote(held.at[k, cut], down_in.at[step, cut], down, (step, chunk), place.below)

    def add(k, chunk, target, others):
        def strip(i, carry):
            cut = pl.ds(chunk * part + i * STRIP, STRIP)
            value = kept[k, cut].astype(F32) + pair[k, cut].astype(F32)
            for ref, slot in others:
                value = value + ref[slot, cut].astype(F32)
            if target is None:
                total[cut] = value
            else:
                target[k, cut] = value.astype(BF)
            return carry

        lax.fori_loop(0, part // STRIP, strip, 0)

    order = []
    for i in range(chips):
        for k in (chips - 1 - i, i):
            if k not in order:
                order.append(k)
    for k in order:
        keep(k).start()
        for chunk in both:
            across(k, chunk).start()
    yield
    for step in range(1, chips):
        for chunk in both:

            @pl.when(place.not_top & (chip <= step - 1))
            def _():
                k = chip + chips - step
                if chunk == 0:
                    keep(k).wait()
                across(k, chunk).wait_recv()

                @pl.when(place.not_bottom)
                def _():
                    upward(step - 1, k, chunk).wait_recv()
                    add(k, chunk, held, [(up_in, step - 1)])

                pl.when(jnp.logical_not(place.not_bottom))(lambda: add(k, chunk, held, []))
                upward(step, k, chunk).start()

            @pl.when(place.not_bottom & (chip >= chips - step))
            def _():
                k = chip - (chips - step)
                if chunk == 0:
                    keep(k).wait()
                across(k, chunk).wait_recv()

                @pl.when(place.not_top)
                def _():
                    downward(step - 1, k, chunk).wait_recv()
                    add(k, chunk, held, [(down_in, step - 1)])

                pl.when(jnp.logical_not(place.not_top))(lambda: add(k, chunk, held, []))
                downward(step, k, chunk).start()

        yield
    keep(chip).wait()
    last = chips - 1
    for chunk in both:
        across(chip, chunk).wait_recv()

        @pl.when(place.not_top & place.not_bottom)
        def _():
            upward(last, chip, chunk).wait_recv()
            downward(last, chip, chunk).wait_recv()
            add(chip, chunk, None, [(up_in, last), (down_in, last)])

        @pl.when(jnp.logical_not(place.not_top))
        def _():
            upward(last, chip, chunk).wait_recv()
            add(chip, chunk, None, [(up_in, last)])

        @pl.when(jnp.logical_not(place.not_bottom))
        def _():
            downward(last, chip, chunk).wait_recv()
            add(chip, chunk, None, [(down_in, last)])

    for chunk in both:
        for k in range(chips):
            across(k, chunk).wait_send()
        for step in range(1, chips):

            @pl.when(place.not_top & (chip <= step - 1))
            def _():
                upward(step, chip + chips - step, chunk).wait_send()

            @pl.when(place.not_bottom & (chip >= chips - step))
            def _():
                downward(step, chip - (chips - step), chunk).wait_send()


GATHER_REFS, SCATTER_REFS = 7, 12


class Transfers:
    def __init__(self, ranks, ident, blocks=(), partials=(), needed=()):
        self.ranks, self.ident = ranks, ident
        self.blocks, self.partials = list(blocks), list(partials)
        self.inputs = self.blocks + self.partials + list(needed)
        self.moves = len(self.blocks) + len(self.partials)
        self.shapes, self.out_specs, self.scratch = [], [], []
        anywhere = pl.BlockSpec(memory_space=pl.ANY)
        self.in_specs = [anywhere] * len(self.inputs)
        for block in self.blocks:
            self.shapes.append(
                jax.ShapeDtypeStruct((ranks * block.shape[0], block.shape[1]), BF)
            )
            self.out_specs.append(anywhere)
            self.scratch += gather_scratch(ranks)
        for partial in self.partials:
            rows, width = partial.shape[0] // ranks, partial.shape[1]
            self.shapes.append(jax.ShapeDtypeStruct((rows, width), F32))
            self.out_specs.append(pl.BlockSpec(memory_space=pltpu.VMEM))
            self.scratch += scatter_scratch(ranks, rows, width)

    def params(self):
        if not self.moves:
            return pltpu.CompilerParams(vmem_limit_bytes=VMEM_BYTES)
        return pltpu.CompilerParams(
            collective_id=self.ident, has_side_effects=True, vmem_limit_bytes=VMEM_BYTES
        )

    def begin(self, inputs, outputs, scratch):
        if not self.moves:
            return lambda: False
        place = Place(self.ranks)
        scratch = list(scratch)
        running = []
        for i in range(self.moves):
            gathers = i < len(self.blocks)
            count = GATHER_REFS if gathers else SCATTER_REFS
            taken, scratch = scratch[:count], scratch[count:]
            steps = gather_steps if gathers else scatter_steps
            running.append(steps(place, inputs[i], outputs[i], *taken))
        state = {"met": False, "running": running}

        def phase():
            if not state["met"]:
                place.meet()
                state["met"] = True
            still = []
            for steps in state["running"]:
                if next(steps, True) is None:
                    still.append(steps)
            state["running"] = still
            return bool(still)

        return phase


def finish(phase):
    while phase():
        pass


def exchange_kernel(transfers, *refs):
    count, moves = len(transfers.inputs), transfers.moves
    finish(transfers.begin(refs[:moves], refs[count : count + moves], refs[count + moves :]))


def exchange(ranks, ident, blocks=(), partials=(), needed=()):
    transfers = Transfers(ranks, ident, blocks, partials, needed)
    return pl.pallas_call(
        functools.partial(exchange_kernel, transfers),
        out_shape=tuple(transfers.shapes),
        in_specs=transfers.in_specs,
        out_specs=tuple(transfers.out_specs),
        scratch_shapes=transfers.scratch,
        compiler_params=transfers.params(),
    )(*transfers.inputs)


def beside(phase, at, grid_steps, work):
    step = pl.program_id(0)
    for when in at:
        pl.when(step == when)(lambda: phase() and None)
    work()
    pl.when(step == grid_steps - 1)(lambda: finish(phase))


def spread_kernel(groups, ranks, reduces, value_ref, *refs):
    out_ref, landing, send_sem, recv_sem, own_sem = refs[-5:]
    devices = groups * ranks
    me = lax.axis_index("fsdp") * ranks + lax.axis_index("tensor")
    barrier = pltpu.get_barrier_semaphore()

    def name(device):
        return {"fsdp": device // ranks, "tensor": device % ranks}

    def greet(i, carry):
        target = lax.rem(me + i, devices)
        pl.semaphore_signal(barrier, 1, device_id=name(target), device_id_type=MESH)
        return carry

    lax.fori_loop(1, devices, greet, 0)
    pl.semaphore_wait(barrier, devices - 1)

    def copy(i):
        target = lax.rem(me + i, devices)
        return pltpu.make_async_remote_copy(
            src_ref=value_ref.at[target] if reduces else value_ref.at[0],
            dst_ref=landing.at[me],
            send_sem=send_sem.at[i],
            recv_sem=recv_sem.at[i],
            device_id=name(target),
            device_id_type=MESH,
        )

    def arrival(i):
        source = lax.rem(me - i + devices, devices)
        return pltpu.make_async_remote_copy(
            src_ref=landing.at[source],
            dst_ref=landing.at[source],
            send_sem=send_sem.at[i],
            recv_sem=recv_sem.at[i],
            device_id=name(source),
            device_id_type=MESH,
        )

    def send(i, carry):
        copy(i).start()
        return carry

    def receive(i, carry):
        arrival(i).wait_recv()
        copy(i).wait_send()
        return carry

    own = pltpu.make_async_copy(
        value_ref.at[me] if reduces else value_ref.at[0], landing.at[me], own_sem
    )
    own.start()
    lax.fori_loop(1, devices, send, 0)
    lax.fori_loop(1, devices, receive, 0)
    own.wait()
    if reduces:
        out_ref[...] = jnp.sum(landing[...], axis=0)
    else:
        out_ref[...] = landing[...]


def spread(groups, ranks, ident, values, reduces, needed=()):
    devices = groups * ranks
    tail = values.shape[1:]
    vmem = pl.BlockSpec(memory_space=pltpu.VMEM)
    return pl.pallas_call(
        functools.partial(spread_kernel, groups, ranks, reduces),
        out_shape=jax.ShapeDtypeStruct(tail if reduces else (devices,) + tail, values.dtype),
        in_specs=[vmem] + [pl.BlockSpec(memory_space=pl.ANY)] * len(needed),
        out_specs=vmem,
        scratch_shapes=[
            pltpu.VMEM((devices,) + tail, values.dtype),
            pltpu.SemaphoreType.DMA((devices,)),
            pltpu.SemaphoreType.DMA((devices,)),
            pltpu.SemaphoreType.DMA,
        ],
        compiler_params=pltpu.CompilerParams(collective_id=ident, has_side_effects=True),
    )(values, *needed)


def ffn_kernel(transfers, at, grid_steps, first, *refs):
    refs = list(refs)

    def take(count):
        taken = refs[:count]
        del refs[:count]
        return taken

    rows_ref, grad_ref, scale_ref, w_ref = take(4)
    before = () if first else take(2)
    sent = take(len(transfers.inputs))
    hidden_ref, gate_ref, up_ref, out_ref, back_ref, dots_ref = take(6)
    landed = take(transfers.moves)
    phase = transfers.begin(sent, landed, refs)

    def work():
        groups, _, depth, units = w_ref.shape
        gate_w, up_w, down_w = [w_ref[:, i].reshape(groups * depth, units) for i in range(3)]
        rows, grad, scale = rows_ref[...], grad_ref[...], scale_ref[...]
        gate_act = dot(rows, gate_w, (1,), (0,))
        up_act = dot(rows, up_w, (1,), (0,))
        back = dot(grad, down_w, (1,), (0,))
        sigmoid = 1.0 / (1.0 + jnp.exp(-gate_act))
        silu = gate_act * sigmoid
        hidden = (silu * up_act).astype(BF).astype(F32)
        dots_ref[...] = jnp.sum(hidden * back, axis=1, keepdims=True)
        scaled = (scale * hidden).astype(BF)
        hidden_ref[...] = scaled
        grad_hidden = scale * back
        grad_gate = (grad_hidden * up_act * (sigmoid * (1.0 + gate_act * (1.0 - sigmoid)))).astype(BF)
        gate_ref[...] = grad_gate
        grad_up = (grad_hidden * silu).astype(BF)
        up_ref[...] = grad_up
        moved = dot(scaled, down_w, (1,), (1,))
        turned = dot(grad_gate, gate_w, (1,), (1,)) + dot(grad_up, up_w, (1,), (1,))
        if not first:
            moved = moved + before[0][...].astype(F32)
            turned = turned + before[1][...].astype(F32)
        out_ref[...] = moved.astype(BF)
        back_ref[...] = turned.astype(BF)

    beside(phase, at, grid_steps, work)


def ffn(rows, grads, scale, weights, before, transfers, at=()):
    count, width = rows.shape
    units = weights.shape[3]
    first = before is None
    steps = count // ROW_BLOCK

    def block(size):
        return pl.BlockSpec((ROW_BLOCK, size), lambda i: (i, 0))

    whole = pl.BlockSpec(weights.shape, lambda i: (0, 0, 0, 0), pipeline_mode=pl.Buffered(1))
    given = [] if first else list(before)
    narrow = [jax.ShapeDtypeStruct((count, units), BF)] * 3
    wide = [jax.ShapeDtypeStruct((count, width), BF)] * 2
    dots = [jax.ShapeDtypeStruct((count, 1), F32)]
    results = pl.pallas_call(
        functools.partial(ffn_kernel, transfers, at, steps, first),
        grid=(steps,),
        in_specs=[block(width), block(width), block(1), whole]
        + [block(width)] * len(given)
        + transfers.in_specs,
        out_specs=tuple(
            [block(units)] * 3 + [block(width)] * 2 + [block(1)] + transfers.out_specs
        ),
        out_shape=tuple(narrow + wide + dots + transfers.shapes),
        scratch_shapes=transfers.scratch,
        compiler_params=transfers.params(),
        cost_estimate=pl.CostEstimate(
            flops=12 * count * width * units,
            bytes_accessed=2 * (3 * width * units + 4 * count * width + 3 * count * units),
            transcendentals=count * units,
        ),
    )(rows, grads, scale, weights, *given, *transfers.inputs)
    return results[:3], results[3:5], results[5], results[6:]


def ffn_grads_kernel(transfers, at, grid_steps, micros, *refs):
    refs = list(refs)

    def take(count):
        taken = refs[:count]
        del refs[:count]
        return taken

    per_micro = [take(5) for _ in range(micros)]
    sent = take(len(transfers.inputs))
    (out_ref,) = take(1)
    landed = take(transfers.moves)
    phase = transfers.begin(sent, landed, refs)

    def work():
        for which, left in ((0, 0), (1, 0), (2, 1)):
            total = None
            for one in per_micro:
                product = dot(one[left][...], one[2 + which][...], (0,), (0,))
                total = product if total is None else total + product
            out_ref[0, which] = total.astype(BF)

    beside(phase, at, grid_steps, work)


def ffn_grads(groups, per_micro, transfers, at=()):
    count, width = per_micro[0][0].shape
    units = per_micro[0][2].shape[1]
    depth = width // groups
    columns = pl.BlockSpec((count, depth), lambda i: (0, i))
    whole = pl.BlockSpec((count, units), lambda i: (0, 0), pipeline_mode=pl.Buffered(1))
    results = pl.pallas_call(
        functools.partial(ffn_grads_kernel, transfers, at, groups, len(per_micro)),
        grid=(groups,),
        in_specs=[columns, columns, whole, whole, whole] * len(per_micro) + transfers.in_specs,
        out_specs=tuple(
            [pl.BlockSpec((1, 3, depth, units), lambda i: (i, 0, 0, 0))] + transfers.out_specs
        ),
        out_shape=tuple(
            [jax.ShapeDtypeStruct((groups, 3, depth, units), BF)] + transfers.shapes
        ),
        scratch_shapes=transfers.scratch,
        compiler_params=transfers.params(),
        cost_estimate=pl.CostEstimate(
            flops=6 * len(per_micro) * count * width * units,
            bytes_accessed=2 * len(per_micro) * (2 * count * width + 3 * count * units)
            + 6 * width * units,
            transcendentals=0,
        ),
    )(*[array for one in per_micro for array in one], *transfers.inputs)
    return results[0], results[1:]


def rope_tables(seq_len):
    half = HD // 2
    frequency = ROPE_BASE ** (-(2.0 * jnp.arange(half, dtype=F32)) / HD)
    angles = jnp.arange(seq_len, dtype=F32)[:, None] * frequency[None, :]
    cosine, sine = jnp.cos(angles), jnp.sin(angles)
    return (
        jnp.concatenate([cosine, cosine], axis=1),
        jnp.concatenate([-sine, sine], axis=1),
    )


def swap_halves(values):
    half = HD // 2
    return jnp.concatenate([values[:, half:], values[:, :half]], axis=1)


def block_weights(query, keys, first_row, length):
    scores = dot(query, keys, (1,), (1,)) * (HD ** (-0.5))
    rows = first_row + lax.broadcasted_iota(jnp.int32, scores.shape, 0)
    cols = lax.broadcasted_iota(jnp.int32, scores.shape, 1)
    scores = jnp.where((cols <= rows) & (cols < length), scores, -1e30)
    exps = jnp.exp(scores - jnp.max(scores, axis=1, keepdims=True))
    return exps / jnp.sum(exps, axis=1, keepdims=True)


def attend_kernel(heads, length_ref, pre_ref, bias_ref, cos_ref, sin_ref, qkv_ref, out_ref):
    seq_len = pre_ref.shape[0]
    length = length_ref[0]
    for head in range(heads):
        for which in range(3):
            at = (which * heads + head) * HD
            for row in range(0, seq_len, QB):
                part = pre_ref[row : row + QB, at : at + HD] + bias_ref[:, at : at + HD]
                if which < 2:
                    part = (
                        part * cos_ref[row : row + QB, :]
                        + swap_halves(part) * sin_ref[row : row + QB, :]
                    )
                qkv_ref[row : row + QB, at : at + HD] = part.astype(BF)
        q_at, k_at, v_at = (head * HD, (heads + head) * HD, (2 * heads + head) * HD)
        for row in range(0, seq_len, QB):
            end = row + QB
            weights = block_weights(
                qkv_ref[row:end, q_at : q_at + HD], qkv_ref[:end, k_at : k_at + HD], row, length
            )
            mixed = dot(weights.astype(BF), qkv_ref[:end, v_at : v_at + HD], (1,), (0,))
            out_ref[row:end, q_at : q_at + HD] = mixed.astype(BF)


def attend_back_kernel(
    heads, length_ref, qkv_ref, grad_ref, cos_ref, sin_ref, out_ref, sums_ref, key_acc, value_acc
):
    seq_len = qkv_ref.shape[0]
    length = length_ref[0]
    scale = HD ** (-0.5)
    for head in range(heads):
        q_at, k_at, v_at = (head * HD, (heads + head) * HD, (2 * heads + head) * HD)
        key_acc[...] = jnp.zeros_like(key_acc)
        value_acc[...] = jnp.zeros_like(value_acc)
        q_sum = jnp.zeros((1, HD), F32)
        for row in range(0, seq_len, QB):
            end = row + QB
            query = qkv_ref[row:end, q_at : q_at + HD]
            keys = qkv_ref[:end, k_at : k_at + HD]
            grad = grad_ref[row:end, q_at : q_at + HD]
            weights = block_weights(query, keys, row, length)
            grad_weights = dot(grad, qkv_ref[:end, v_at : v_at + HD], (1,), (1,))
            inner = jnp.sum(weights * grad_weights, axis=1, keepdims=True)
            grad_scores = (scale * weights * (grad_weights - inner)).astype(BF)
            turned = dot(grad_scores, keys, (1,), (0,))
            grad_query = (
                turned * cos_ref[row:end, :] - swap_halves(turned) * sin_ref[row:end, :]
            ).astype(BF)
            out_ref[row:end, q_at : q_at + HD] = grad_query
            q_sum = q_sum + jnp.sum(grad_query.astype(F32), axis=0, keepdims=True)
            key_acc[:end, :] += dot(grad_scores, query, (0,), (0,))
            value_acc[:end, :] += dot(weights.astype(BF), grad, (0,), (0,))
        k_sum = jnp.zeros((1, HD), F32)
        v_sum = jnp.zeros((1, HD), F32)
        for row in range(0, seq_len, QB):
            end = row + QB
            turned = key_acc[row:end, :]
            grad_key = (
                turned * cos_ref[row:end, :] - swap_halves(turned) * sin_ref[row:end, :]
            ).astype(BF)
            grad_value = value_acc[row:end, :].astype(BF)
            out_ref[row:end, k_at : k_at + HD] = grad_key
            out_ref[row:end, v_at : v_at + HD] = grad_value
            k_sum = k_sum + jnp.sum(grad_key.astype(F32), axis=0, keepdims=True)
            v_sum = v_sum + jnp.sum(grad_value.astype(F32), axis=0, keepdims=True)
        sums_ref[:, q_at : q_at + HD] = q_sum
        sums_ref[:, k_at : k_at + HD] = k_sum
        sums_ref[:, v_at : v_at + HD] = v_sum


def in_vmem(count):
    return [pl.BlockSpec(memory_space=pltpu.VMEM)] * count


def attend(length, pre, bias, cosine, sine):
    seq_len, width = pre.shape
    heads = width // (3 * HD)
    return pl.pallas_call(
        functools.partial(attend_kernel, heads),
        out_shape=(
            jax.ShapeDtypeStruct((seq_len, width), BF),
            jax.ShapeDtypeStruct((seq_len, heads * HD), BF),
        ),
        in_specs=[pl.BlockSpec(memory_space=pltpu.SMEM)] + in_vmem(4),
        out_specs=tuple(in_vmem(2)),
        compiler_params=pltpu.CompilerParams(vmem_limit_bytes=32 << 20),
        cost_estimate=pl.CostEstimate(
            flops=3 * heads * HD * seq_len * seq_len,
            bytes_accessed=10 * seq_len * width,
            transcendentals=heads * seq_len * seq_len,
        ),
    )(length, pre, bias, cosine, sine)


def attend_back(length, qkv, grad, cosine, sine):
    seq_len, width = qkv.shape
    heads = width // (3 * HD)
    return pl.pallas_call(
        functools.partial(attend_back_kernel, heads),
        out_shape=(
            jax.ShapeDtypeStruct((seq_len, width), BF),
            jax.ShapeDtypeStruct((1, width), F32),
        ),
        in_specs=[pl.BlockSpec(memory_space=pltpu.SMEM)] + in_vmem(4),
        out_specs=tuple(in_vmem(2)),
        scratch_shapes=[pltpu.VMEM((seq_len, HD), F32), pltpu.VMEM((seq_len, HD), F32)],
        compiler_params=pltpu.CompilerParams(vmem_limit_bytes=32 << 20),
        cost_estimate=pl.CostEstimate(
            flops=8 * heads * HD * seq_len * seq_len,
            bytes_accessed=8 * seq_len * width,
            transcendentals=heads * seq_len * seq_len,
        ),
    )(length, qkv, grad, cosine, sine)


def padded(values, axis):
    size = values.shape[axis]
    more = -size % LANES
    if not more:
        return values
    return jnp.pad(values, [(0, more if i == axis else 0) for i in range(values.ndim)])


def packed(values, kind):
    tile = LANES * (16 if kind == BF else 8)
    values = values.astype(kind)
    return padded_to(values, -(-values.shape[-1] // tile) * tile)


def padded_to(values, size):
    more = size - values.shape[-1]
    return jnp.pad(values, [(0, 0)] * (values.ndim - 1) + [(0, more)])


def local(
    tokens,
    lengths,
    routes,
    norm1_gain,
    w_query,
    w_key,
    w_value,
    b_query,
    b_key,
    b_value,
    w_out,
    norm2_gain,
    router,
    shared_gate_vec,
    shared_gate,
    shared_up,
    shared_down,
    expert_gate,
    expert_up,
    expert_down,
    cotangent,
):
    ranks = lax.axis_size("tensor")
    groups = lax.axis_size("fsdp")
    rank = lax.axis_index("tensor")
    micros, _, rows, width = tokens.shape
    seq_len = rows * ranks
    heads = w_query.shape[1] // HD
    span = heads * HD
    experts = ranks * expert_gate.shape[0]
    shared_units = shared_gate.shape[1]
    expert_units = expert_gate.shape[2]
    cut = expert_units // (2 * LANES) * LANES
    own_first = rank * rows
    local_pos = own_first + jnp.arange(rows, dtype=jnp.int32)

    per_device = norm1_gain.shape[0]
    small = jnp.concatenate(
        [
            norm1_gain,
            norm2_gain,
            shared_gate_vec,
            router.reshape(-1),
            b_query.reshape(-1),
            b_key.reshape(-1),
            b_value.reshape(-1),
        ]
    )
    small_all = spread(groups, ranks, 1, packed(small, BF).reshape(1, -1, LANES), False)
    small_all = small_all.reshape(groups * ranks, -1)
    gain_one = small_all[:, :per_device].reshape(-1).astype(F32)
    gain_two = small_all[:, per_device : 2 * per_device].reshape(-1).astype(F32)
    gate_vec = small_all[:, 2 * per_device : 3 * per_device].reshape(-1)
    bias_at = per_device * (3 + experts)
    router_full = small_all[:, 3 * per_device : bias_at].reshape(width, experts)
    router_wide = jnp.concatenate([router_full, gate_vec[:, None]], axis=1)
    own_bias = lax.dynamic_index_in_dim(
        small_all.reshape(groups, ranks, -1), rank, 1, False
    )[:, bias_at : small.shape[0]].reshape(groups, 3, heads, HD // groups)
    bias = own_bias.transpose(1, 2, 0, 3).reshape(1, 3 * span).astype(F32)

    attn_w = lax.all_gather(
        jnp.concatenate([w_query, w_key, w_value, w_out.T], axis=1), "fsdp", axis=0, tiled=True
    )
    qkv_w, out_w = attn_w[:, : 3 * span], attn_w[:, 3 * span :]
    ranges = [
        (shared_gate, shared_up, shared_down),
        (expert_gate[0, :, :cut], expert_up[0, :, :cut], expert_down[0, :cut]),
        (expert_gate[0, :, cut:], expert_up[0, :, cut:], expert_down[0, cut:]),
    ]
    weights = [
        lax.all_gather(
            jnp.stack([padded(gate, 1), padded(up, 1), padded(down.T, 1)]), "fsdp", axis=0
        )
        for gate, up, down in ranges
    ]

    cosine, sine = rope_tables(seq_len)
    idle = Transfers(ranks, 0)
    token_own = [tokens[m, 0] for m in range(micros)]
    grads_own = []
    for m in range(micros):
        inside = (local_pos < lengths[m, 0])[:, None]
        grads_own.append(jnp.where(inside, cotangent[m, 0], jnp.zeros((), BF)))

    def attention(m, token_rows):
        normed = (normalize(token_rows.astype(F32))[0] * gain_one).astype(BF)
        pre = dot(normed, qkv_w, (1,), (0,))
        qkv, mixed = attend(lengths[m], pre, bias, cosine, sine)
        return normed, qkv, mixed, dot(mixed, out_w, (1,), (1,)).astype(BF)

    def second_norm(m, attended):
        hidden = token_own[m].astype(F32) + attended
        unit, inverse = normalize(hidden)
        return hidden, unit, inverse, (unit * gain_two).astype(BF)

    def routing(m, rows_two):
        logits = dot(rows_two, router_wide, (1,), (0,))
        probs = jax.nn.softmax(logits[:, :experts], axis=-1)
        shared_scale = jax.nn.sigmoid(logits[:, experts:])
        chosen = jnp.any(routes[m, 0] == rank, axis=1, keepdims=True)
        own_expert = (jnp.arange(experts, dtype=jnp.int32) == rank)[None, :]
        prob = jnp.sum(jnp.where(own_expert, probs, 0.0), axis=1, keepdims=True)
        return probs, shared_scale, chosen, own_expert, prob, jnp.where(chosen, prob, 0.0)

    def routing_back(route, dots):
        probs, shared_scale, chosen, own_expert, prob, _ = route
        expert_grad = jnp.where(chosen, dots[1] + dots[2], 0.0)
        grad_logits = probs * (jnp.where(own_expert, expert_grad, 0.0) - expert_grad * prob)
        grad_gate_logit = dots[0] * shared_scale * (1.0 - shared_scale)
        return jnp.concatenate([grad_logits, grad_gate_logit], axis=1).astype(BF)

    def second_norm_back(m, state, summed):
        grad_hidden, gain_part = norm_back(summed, state[1], state[2], gain_two)
        grad_hidden = grad_hidden + grads_own[m].astype(F32)
        return grad_hidden, grad_hidden.astype(BF), gain_part

    def attention_back(m, state, rows_grad):
        grad_mixed = dot(rows_grad, out_w, (1,), (0,)).astype(BF)
        grad_qkv, sums = attend_back(lengths[m], state[1], grad_mixed, cosine, sine)
        return grad_qkv, sums, dot(grad_qkv, qkv_w, (1,), (1,)).astype(BF)

    def first_norm_back(m, grad_hidden, summed):
        unit, inverse = normalize(token_own[m].astype(F32))
        grad_inputs, gain_part = norm_back(summed, unit, inverse, gain_one)
        return (grad_inputs + grad_hidden).astype(BF), gain_part

    def finished(m, hidden, moved):
        inside = (local_pos < lengths[m, 0]).astype(F32)[:, None]
        return (inside * (hidden + moved)).astype(BF)

    start = after(token_own[0], small_all)
    rows_a, grad_a = exchange(ranks, 2, [start, grads_own[0]])
    att_a = attention(0, rows_a)
    rows_b, sum_a = exchange(ranks, 3, [token_own[1]], [att_a[3]])
    att_b = attention(1, rows_b)
    norm_a = second_norm(0, sum_a)
    two_a, sum_b = exchange(ranks, 4, [norm_a[3]], [att_b[3]])
    norm_b = second_norm(1, sum_b)
    route_a = routing(0, two_a)

    def scale_of(route, which):
        return route[1] if which == 0 else route[5]

    act = {}
    dots_a, dots_b = [], []
    act[0, 0], acc_a, dots, (two_b,) = ffn(
        two_a, grad_a, scale_of(route_a, 0), weights[0], None, Transfers(ranks, 5, [norm_b[3]]), (0, 2, 3)
    )
    dots_a.append(dots)
    act[1, 0], acc_a, dots, (grad_b,) = ffn(
        two_a, grad_a, scale_of(route_a, 1), weights[1], acc_a, Transfers(ranks, 6, [grads_own[1]]), (0, 2, 3)
    )
    dots_a.append(dots)
    route_b = routing(1, two_b)
    acc_b = None
    for which in range(2):
        act[which, 1], acc_b, dots, _ = ffn(
            two_b, grad_b, scale_of(route_b, which), weights[which], acc_b, idle
        )
        dots_b.append(dots)

    def grads_of(which, transfers, at=()):
        per_micro = []
        for rows_two, grads, key in ((two_a, grad_a, 0), (two_b, grad_b, 1)):
            scaled, gate, up = act[which, key]
            per_micro.append((rows_two, grads, gate, up, scaled))
        return ffn_grads(groups, per_micro, transfers, at)

    def over_groups(grads):
        flat = grads.reshape(-1, grads.shape[-1])
        summed = lax.psum_scatter(flat, "fsdp", scatter_dimension=0, tiled=True)
        return with_layout_constraint(summed, Layout((0, 1))).reshape(grads.shape[1:])

    grads_0, _ = grads_of(0, idle)
    range_0 = over_groups(grads_0)
    scale_a = after(scale_of(route_a, 2), grads_0)
    act[2, 0], acc_a, dots, _ = ffn(two_a, grad_a, scale_a, weights[2], acc_a, idle)
    dots_a.append(dots)
    wide_a = routing_back(route_a, dots_a)
    back_a = (acc_a[1].astype(F32) + dot(wide_a, router_wide, (1,), (1,))).astype(BF)
    grads_1, (down_a,) = grads_of(1, Transfers(ranks, 7, [], [back_a]), (0, 2))
    range_1 = over_groups(grads_1)
    hid_a, send_a, gain_part_a = second_norm_back(0, norm_a, down_a)
    act[2, 1], acc_b, dots, (datt_a,) = ffn(
        two_b, grad_b, scale_of(route_b, 2), weights[2], acc_b, Transfers(ranks, 8, [send_a]), (0, 2, 3)
    )
    dots_b.append(dots)
    wide_b = routing_back(route_b, dots_b)
    back_b = (acc_b[1].astype(F32) + dot(wide_b, router_wide, (1,), (1,))).astype(BF)
    grad_qkv_a, sums_a, first_a = attention_back(0, att_a, datt_a)
    grads_2, (down_b, one_a) = grads_of(
        2, Transfers(ranks, 9, [], [back_b, first_a], [range_0]), (0, 2)
    )
    range_2 = over_groups(grads_2)
    hid_b, send_b, gain_part_b = second_norm_back(1, norm_b, down_b)
    datt_b, moved_a = exchange(ranks, 10, [send_b], [acc_a[0]], [range_1])
    grad_qkv_b, sums_b, first_b = attention_back(1, att_b, datt_b)
    one_b, moved_b = exchange(ranks, 11, [], [first_b, acc_b[0]], [range_2])

    def over_micros(left_a, right_a, left_b, right_b):
        return (dot(left_a, right_a, (0,), (0,)) + dot(left_b, right_b, (0,), (0,))).astype(BF)

    attn_g = jnp.concatenate(
        [
            over_micros(att_a[0], grad_qkv_a, att_b[0], grad_qkv_b),
            over_micros(datt_a, att_a[2], datt_b, att_b[2]),
        ],
        axis=1,
    )
    attn_g = lax.psum_scatter(attn_g, "fsdp", scatter_dimension=0, tiled=True).astype(F32)

    grad_in_a, one_part_a = first_norm_back(0, hid_a, one_a)
    grad_in_b, one_part_b = first_norm_back(1, hid_b, one_b)

    devices = groups * ranks
    total_wide = dot(two_a, wide_a, (0,), (0,)) + dot(two_b, wide_b, (0,), (0,))
    bias_part = (sums_a + sums_b).reshape(3, heads, groups, HD // groups).transpose(2, 0, 1, 3)
    bias_part = bias_part.reshape(groups, 1, -1)
    own_rank = (jnp.arange(ranks, dtype=jnp.int32) == rank).astype(F32)[None, :, None]
    parts = jnp.concatenate(
        [
            (one_part_a + one_part_b).reshape(devices, -1),
            (gain_part_a + gain_part_b).reshape(devices, -1),
            total_wide.reshape(devices, -1),
            (bias_part * own_rank).reshape(devices, -1),
        ],
        axis=1,
    )
    shares = spread(groups, ranks, 12, packed(parts, F32).reshape(devices, -1, LANES), True)
    shares = shares.reshape(-1)
    wide_g = shares[2 * per_device : (3 + experts) * per_device].reshape(per_device, experts + 1)
    bias_g = shares[bias_at : parts.shape[1]].reshape(3, heads, HD // groups)

    def plain(which):
        return [which[i].astype(F32) for i in range(3)]

    shared_g, low_g, high_g = plain(range_0), plain(range_1), plain(range_2)
    return (
        jnp.stack([finished(0, norm_a[0], moved_a), finished(1, norm_b[0], moved_b)])[:, None],
        jnp.stack([grad_in_a, grad_in_b])[:, None],
        shares[:per_device],
        attn_g[:, :span],
        attn_g[:, span : 2 * span],
        attn_g[:, 2 * span : 3 * span],
        bias_g[0],
        bias_g[1],
        bias_g[2],
        attn_g[:, 3 * span :].T,
        shares[per_device : 2 * per_device],
        wide_g[:, :experts],
        wide_g[:, experts],
        shared_g[0][:, :shared_units],
        shared_g[1][:, :shared_units],
        shared_g[2][:, :shared_units].T,
        jnp.concatenate([low_g[0], high_g[0]], axis=1)[None],
        jnp.concatenate([low_g[1], high_g[1]], axis=1)[None],
        jnp.concatenate([low_g[2].T, high_g[2].T], axis=0)[None],
    )


def solution(mesh):
    in_specs = (
        P(None, "fsdp", "tensor", None),
        P(None, "fsdp"),
        P(None, "fsdp", None, None),
        P(("fsdp", "tensor")),
        P("fsdp", "tensor"),
        P("fsdp", "tensor"),
        P("fsdp", "tensor"),
        P("tensor", "fsdp"),
        P("tensor", "fsdp"),
        P("tensor", "fsdp"),
        P("tensor", "fsdp"),
        P(("fsdp", "tensor")),
        P(("fsdp", "tensor"), None),
        P(("fsdp", "tensor")),
        P("fsdp", "tensor"),
        P("fsdp", "tensor"),
        P("tensor", "fsdp"),
        P("tensor", "fsdp", None),
        P("tensor", "fsdp", None),
        P("tensor", None, "fsdp"),
        P(None, "fsdp", "tensor", None),
    )
    out_specs = (
        P(None, "fsdp", "tensor", None),
        P(None, "fsdp", "tensor", None),
        P(("fsdp", "tensor")),
        P("fsdp", "tensor"),
        P("fsdp", "tensor"),
        P("fsdp", "tensor"),
        P("tensor", "fsdp"),
        P("tensor", "fsdp"),
        P("tensor", "fsdp"),
        P("tensor", "fsdp"),
        P(("fsdp", "tensor")),
        P(("fsdp", "tensor"), None),
        P(("fsdp", "tensor")),
        P("fsdp", "tensor"),
        P("fsdp", "tensor"),
        P("tensor", "fsdp"),
        P("tensor", "fsdp", None),
        P("tensor", "fsdp", None),
        P("tensor", None, "fsdp"),
    )
    return jax.shard_map(local, mesh=mesh, in_specs=in_specs, out_specs=out_specs, check_vma=False)
```

```python
import functools

import jax
import jax.numpy as jnp
from jax import lax
from jax.experimental import pallas as pl
from jax.experimental.layout import Layout, with_layout_constraint
from jax.experimental.pallas import tpu as pltpu
from jax.sharding import PartitionSpec as P

HD = 128
EPSILON = 1e-06
ROPE_BASE = 1000000.0
BF = jnp.bfloat16
F32 = jnp.float32
MESH = pl.DeviceIdType.MESH
QB = 256
LANES = 128
CHUNKS = 2
STRIP = 16
ROW_BLOCK = 256
VMEM_BYTES = 60 << 20


def dot(left, right, left_dims, right_dims):
    return lax.dot_general(
        left, right, ((left_dims, right_dims), ((), ())), preferred_element_type=F32
    )


def normalize(values):
    inverse = lax.rsqrt(jnp.mean(values * values, axis=-1, keepdims=True) + EPSILON)
    return (values * inverse, inverse)


def norm_back(grad_normed, unit, inverse, gain):
    grad_unit = grad_normed * gain
    grad_values = inverse * (grad_unit - unit * jnp.mean(grad_unit * unit, axis=-1, keepdims=True))
    return (grad_values, jnp.sum(grad_normed * unit, axis=0))


def after(value, *others):
    return lax.optimization_barrier((value,) + others)[0]


def remote(src, dst, sems, at, target):
    return pltpu.make_async_remote_copy(
        src_ref=src,
        dst_ref=dst,
        send_sem=sems[0].at[at],
        recv_sem=sems[1].at[at],
        device_id={"tensor": target},
        device_id_type=MESH,
    )


def gather_scratch(ranks):
    chips = ranks // 2
    pair = [pltpu.SemaphoreType.DMA((chips, CHUNKS))] * 2
    cross = [pltpu.SemaphoreType.DMA((2 * chips, CHUNKS))] * 2
    return [pltpu.SemaphoreType.DMA] + pair + pair + cross


def gather_steps(place, block, whole, local_sem, up_s, up_r, down_s, down_r, cross_s, cross_r):
    chips, chip, core = place.chips, place.chip, place.core
    rows = block.shape[0]
    part = rows // CHUNKS
    up, down, cross = (up_s, up_r), (down_s, down_r), (cross_s, cross_r)

    def at(owner, chunk):
        first = pl.multiple_of((2 * owner + core) * rows + chunk * part, part)
        return whole.at[pl.ds(first, part)]

    def theirs(owner, chunk):
        first = pl.multiple_of((2 * owner + 1 - core) * rows + chunk * part, part)
        return whole.at[pl.ds(first, part)]

    def own(chunk):
        return block.at[pl.ds(chunk * part, part)]

    def upward(step, chunk):
        source = own(chunk) if step == 0 else at(chip - step, chunk)
        return remote(source, at(chip - step, chunk), up, (step, chunk), place.above)

    def downward(step, chunk):
        source = own(chunk) if step == 0 else at(chip + step, chunk)
        return remote(source, at(chip + step, chunk), down, (step, chunk), place.below)

    def across(slot, owner, chunk):
        source = own(chunk) if slot == 0 else at(owner, chunk)
        return remote(source, at(owner, chunk), cross, (slot, chunk), place.partner)

    def arrived(slot, owner, chunk):
        return remote(theirs(owner, chunk), theirs(owner, chunk), cross, (slot, chunk), place.partner)

    def arrived_up(step, chunk):
        return remote(at(chip - step, chunk), at(chip - step, chunk), up, (step - 1, chunk), place.above)

    def arrived_down(step, chunk):
        return remote(at(chip + step, chunk), at(chip + step, chunk), down, (step - 1, chunk), place.below)

    both = range(CHUNKS)

    def mine():
        first = pl.multiple_of((2 * chip + core) * rows, rows)
        return pltpu.make_async_copy(block, whole.at[pl.ds(first, rows)], local_sem)

    for chunk in both:
        pl.when(place.not_top)(lambda: upward(0, chunk).start())
        pl.when(place.not_bottom)(lambda: downward(0, chunk).start())
    for chunk in both:
        across(0, chip, chunk).start()
    mine().start()
    yield
    for step in range(1, chips):
        for chunk in both:

            @pl.when(chip >= step)
            def _():
                arrived_up(step, chunk).wait_recv()
                pl.when(place.not_top)(lambda: upward(step, chunk).start())
                across(2 * step - 1, chip - step, chunk).start()

            @pl.when(chip < chips - step)
            def _():
                arrived_down(step, chunk).wait_recv()
                pl.when(place.not_bottom)(lambda: downward(step, chunk).start())
                across(2 * step, chip + step, chunk).start()

        yield
    mine().wait()
    for step in range(chips):
        for chunk in both:
            if step == 0:
                arrived(0, chip, chunk).wait_recv()
                across(0, chip, chunk).wait_send()
            else:

                @pl.when(chip >= step)
                def _():
                    arrived(2 * step - 1, chip - step, chunk).wait_recv()
                    across(2 * step - 1, chip - step, chunk).wait_send()

                @pl.when(chip < chips - step)
                def _():
                    arrived(2 * step, chip + step, chunk).wait_recv()
                    across(2 * step, chip + step, chunk).wait_send()

            @pl.when(place.not_top & (chip >= step))
            def _():
                upward(step, chunk).wait_send()

            @pl.when(place.not_bottom & (chip < chips - step))
            def _():
                downward(step, chunk).wait_send()


def scatter_scratch(ranks, rows, width):
    chips = ranks // 2
    line = [pltpu.SemaphoreType.DMA((chips, CHUNKS))] * 2
    buffers = [pltpu.VMEM((chips, rows, width), BF)] * 5
    return buffers + [pltpu.SemaphoreType.DMA((chips,))] + line * 3


def scatter_steps(
    place, partial, total, kept, pair, held, up_in, down_in, keep_sem,
    up_s, up_r, down_s, down_r, cross_s, cross_r,
):
    chips, chip, core = place.chips, place.chip, place.core
    rows = total.shape[0]
    part = rows // CHUNKS
    up, down, cross = (up_s, up_r), (down_s, down_r), (cross_s, cross_r)
    both = range(CHUNKS)

    def keep(k):
        first = pl.multiple_of((2 * k + core) * rows, rows)
        return pltpu.make_async_copy(partial.at[pl.ds(first, rows)], kept.at[k], keep_sem.at[k])

    def across(k, chunk):
        first = pl.multiple_of((2 * k + 1 - core) * rows + chunk * part, part)
        return remote(
            partial.at[pl.ds(first, part)],
            pair.at[k, pl.ds(chunk * part, part)],
            cross,
            (k, chunk),
            place.partner,
        )

    def upward(step, k, chunk):
        cut = pl.ds(chunk * part, part)
        return remote(held.at[k, cut], up_in.at[step, cut], up, (step, chunk), place.above)

    def downward(step, k, chunk):
        cut = pl.ds(chunk * part, part)
        return remote(held.at[k, cut], down_in.at[step, cut], down, (step, chunk), place.below)

    def add(k, chunk, target, others):
        def strip(i, carry):
            cut = pl.ds(chunk * part + i * STRIP, STRIP)
            value = kept[k, cut].astype(F32) + pair[k, cut].astype(F32)
            for ref, slot in others:
                value = value + ref[slot, cut].astype(F32)
            if target is None:
                total[cut] = value
            else:
                target[k, cut] = value.astype(BF)
            return carry

        lax.fori_loop(0, part // STRIP, strip, 0)

    order = []
    for i in range(chips):
        for k in (chips - 1 - i, i):
            if k not in order:
                order.append(k)
    for k in order:
        keep(k).start()
        for chunk in both:
            across(k, chunk).start()
    yield
    for step in range(1, chips):
        for chunk in both:

            @pl.when(place.not_top & (chip <= step - 1))
            def _():
                k = chip + chips - step
                if chunk == 0:
                    keep(k).wait()
                across(k, chunk).wait_recv()

                @pl.when(place.not_bottom)
                def _():
                    upward(step - 1, k, chunk).wait_recv()
                    add(k, chunk, held, [(up_in, step - 1)])

                pl.when(jnp.logical_not(place.not_bottom))(lambda: add(k, chunk, held, []))
                upward(step, k, chunk).start()

            @pl.when(place.not_bottom & (chip >= chips - step))
            def _():
                k = chip - (chips - step)
                if chunk == 0:
                    keep(k).wait()
                across(k, chunk).wait_recv()

                @pl.when(place.not_top)
                def _():
                    downward(step - 1, k, chunk).wait_recv()
                    add(k, chunk, held, [(down_in, step - 1)])

                pl.when(jnp.logical_not(place.not_top))(lambda: add(k, chunk, held, []))
                downward(step, k, chunk).start()

        yield
    keep(chip).wait()
    last = chips - 1
    for chunk in both:
        across(chip, chunk).wait_recv()

        @pl.when(place.not_top & place.not_bottom)
        def _():
            upward(last, chip, chunk).wait_recv()
            downward(last, chip, chunk).wait_recv()
            add(chip, chunk, None, [(up_in, last), (down_in, last)])

        @pl.when(jnp.logical_not(place.not_top))
        def _():
            upward(last, chip, chunk).wait_recv()
            add(chip, chunk, None, [(up_in, last)])

        @pl.when(jnp.logical_not(place.not_bottom))
        def _():
            downward(last, chip, chunk).wait_recv()
            add(chip, chunk, None, [(down_in, last)])

    for chunk in both:
        for k in range(chips):
            across(k, chunk).wait_send()
        for step in range(1, chips):

            @pl.when(place.not_top & (chip <= step - 1))
            def _():
                upward(step, chip + chips - step, chunk).wait_send()

            @pl.when(place.not_bottom & (chip >= chips - step))
            def _():
                downward(step, chip - (chips - step), chunk).wait_send()


class Place:
    def __init__(self, ranks, groups):
        rank, group = lax.axis_index("tensor"), lax.axis_index("fsdp")
        self.ranks, self.groups = ranks, groups
        self.chips = ranks // 2
        self.chip, self.core = rank // 2, rank % 2
        self.partner = rank + 1 - 2 * self.core
        self.above, self.below = rank + 2, rank - 2
        self.not_top = self.chip < self.chips - 1
        self.not_bottom = self.chip > 0
        self.rank, self.group = rank, group
        self.device = group * ranks + rank
        near, far = group % 2, group // 2
        self.beside = 2 * far + 1 - near
        self.across = 2 * (1 - far) + near
        self.opposite = 2 * (1 - far) + 1 - near
        self.square = groups == 4

    def name(self, device):
        return {"fsdp": device // self.ranks, "tensor": device % self.ranks}

    def meet(self, line, cross, everyone):
        barrier = pltpu.get_barrier_semaphore()

        def greet(name):
            pl.semaphore_signal(barrier, 1, device_id=name, device_id_type=MESH)

        if everyone:
            devices = self.groups * self.ranks

            def one(i, carry):
                greet(self.name(lax.rem(self.device + i, devices)))
                return carry

            lax.fori_loop(1, devices, one, 0)
            pl.semaphore_wait(barrier, devices - 1)
            return
        peers = 0
        if line:
            greet({"tensor": self.partner})
            pl.when(self.not_top)(lambda: greet({"tensor": self.above}))
            pl.when(self.not_bottom)(lambda: greet({"tensor": self.below}))
            peers = 1 + self.not_top.astype(jnp.int32) + self.not_bottom.astype(jnp.int32)
        if cross and self.square:
            greet({"fsdp": self.beside})
            greet({"fsdp": self.across})
            peers = peers + 2
        elif cross:
            for i in range(1, self.groups):
                greet({"fsdp": lax.rem(self.group + i, self.groups)})
            peers = peers + self.groups - 1
        pl.semaphore_wait(barrier, peers)


def to_group(src, dst, send, recv, at, target):
    return pltpu.make_async_remote_copy(
        src_ref=src,
        dst_ref=dst,
        send_sem=send.at[at],
        recv_sem=recv.at[at],
        device_id={"fsdp": target},
        device_id_type=MESH,
    )


def cross_gather_steps(place, block, whole, own_sem, send, recv):
    group = place.group
    half = block.shape[0] // 2

    def own():
        return pltpu.make_async_copy(block, whole.at[group], own_sem)

    if not place.square:

        def direct(i):
            target = lax.rem(group + i, place.groups)
            return to_group(block, whole.at[group], send, recv, i - 1, target)

        own().start()
        for i in range(1, place.groups):
            direct(i).start()
        yield
        own().wait()
        for i in range(1, place.groups):
            source = lax.rem(group - i + place.groups, place.groups)
            to_group(block, whole.at[source], send, recv, i - 1, source).wait_recv()
            direct(i).wait_send()
        return

    def near(at):
        return to_group(block, whole.at[group], send, recv, at, (place.beside, place.across)[at])

    def came(at):
        source = (place.beside, place.across)[at]
        return to_group(whole.at[source], whole.at[source], send, recv, at, source)

    def forward(at):
        source, target = ((place.beside, place.across), (place.across, place.beside))[at]
        piece = whole.at[source, pl.ds(at * half, half)]
        return to_group(piece, piece, send, recv, 2 + at, target)

    def far(at):
        piece = whole.at[place.opposite, pl.ds(at * half, half)]
        return to_group(piece, piece, send, recv, 2 + at, place.opposite)

    for at in range(2):
        near(at).start()
    own().start()
    yield
    for at in range(2):
        came(at).wait_recv()
        forward(at).start()
    yield
    yield
    own().wait()
    for at in range(2):
        far(at).wait_recv()
        near(at).wait_send()
        forward(at).wait_send()


def cross_scatter_steps(place, partial, total, mine, near_in, far_in, own_sem, send, recv):
    group = place.group
    rows = total.shape[0]
    half = rows // 2

    def own():
        return pltpu.make_async_copy(partial, mine, own_sem)

    def loop(count, body):
        def strip(i, carry):
            body(pl.ds(i * STRIP, STRIP))
            return carry

        lax.fori_loop(0, count // STRIP, strip, 0)

    if not place.square:

        def direct(i):
            target = lax.rem(group + i, place.groups)
            return to_group(partial.at[target], near_in.at[group], send, recv, i - 1, target)

        own().start()
        for i in range(1, place.groups):
            direct(i).start()
        yield
        own().wait()
        for i in range(1, place.groups):
            source = lax.rem(group - i + place.groups, place.groups)
            to_group(partial.at[source], near_in.at[source], send, recv, i - 1, source).wait_recv()

        def everything(cut):
            value = mine[group, cut].astype(F32)
            for i in range(1, place.groups):
                value = value + near_in[lax.rem(group + i, place.groups), cut].astype(F32)
            total[cut] = value

        loop(rows, everything)
        for i in range(1, place.groups):
            direct(i).wait_send()
        return

    def first(at):
        target = (place.beside, place.across)[at]
        piece = partial.at[place.opposite, pl.ds(at * half, half)]
        return to_group(piece, far_in.at[at], send, recv, at, target)

    def second(at):
        target = (place.beside, place.across)[at]
        return to_group(mine.at[target], near_in.at[at], send, recv, 2 + at, target)

    own().start()
    for at in range(2):
        first(at).start()
    yield
    own().wait()
    for at in range(2):
        target = (place.across, place.beside)[at]
        first(at).wait_recv()

        def join(cut, at=at, target=target):
            place_in = pl.ds(at * half + cut.start, STRIP)
            value = mine[target, place_in].astype(F32) + far_in[at, cut].astype(F32)
            mine[target, place_in] = value.astype(BF)

        loop(half, join)
        second(1 - at).start()
    yield
    yield
    for at in range(2):
        second(at).wait_recv()

    def everything(cut):
        value = mine[group, cut].astype(F32) + near_in[0, cut].astype(F32)
        total[cut] = value + near_in[1, cut].astype(F32)

    loop(rows, everything)
    for at in range(2):
        first(at).wait_send()
        second(at).wait_send()


def spread_steps(place, value, everyone, own_sem, send, recv):
    devices = place.groups * place.ranks
    me = place.device

    def copy(i):
        target = lax.rem(me + i, devices)
        return pltpu.make_async_remote_copy(
            src_ref=value,
            dst_ref=everyone.at[me],
            send_sem=send.at[i],
            recv_sem=recv.at[i],
            device_id=place.name(target),
            device_id_type=MESH,
        )

    def arrival(i):
        source = lax.rem(me - i + devices, devices)
        return pltpu.make_async_remote_copy(
            src_ref=everyone.at[source],
            dst_ref=everyone.at[source],
            send_sem=send.at[i],
            recv_sem=recv.at[i],
            device_id=place.name(source),
            device_id_type=MESH,
        )

    def start(i, carry):
        copy(i).start()
        return carry

    def finish_one(i, carry):
        arrival(i).wait_recv()
        copy(i).wait_send()
        return carry

    def own():
        return pltpu.make_async_copy(value, everyone.at[me], own_sem)

    own().start()
    lax.fori_loop(1, devices, start, 0)
    yield
    yield
    yield
    own().wait()
    lax.fori_loop(1, devices, finish_one, 0)


DMA = pltpu.SemaphoreType.DMA


class Transfers:
    def __init__(self, mesh_size, ident=0, moves=(), needed=()):
        self.ranks, self.groups = mesh_size
        self.ident = ident
        self.kinds = [kind for kind, _ in moves]
        self.inputs = [array for _, array in moves] + list(needed)
        self.moves = len(self.kinds)
        anywhere = pl.BlockSpec(memory_space=pl.ANY)
        vmem = pl.BlockSpec(memory_space=pltpu.VMEM)
        self.in_specs = [anywhere] * len(self.inputs)
        self.shapes, self.out_specs, self.scratch, self.counts = [], [], [], []
        for kind, array in moves:
            shape, spec = array.shape, anywhere
            if kind == "gather":
                shape, dtype = (self.ranks * shape[0], shape[1]), BF
                scratch = gather_scratch(self.ranks)
            elif kind == "scatter":
                shape, dtype, spec = (shape[0] // self.ranks, shape[1]), F32, vmem
                scratch = scatter_scratch(self.ranks, *shape)
            elif kind == "cross_gather":
                shape, dtype = (self.groups,) + shape, BF
                scratch = [DMA, DMA((max(4, self.groups),)), DMA((max(4, self.groups),))]
            elif kind == "cross_scatter":
                rest = shape[1:]
                square = self.groups == 4
                near = (2 if square else self.groups,) + rest
                scratch = [
                    pltpu.VMEM(shape, BF),
                    pltpu.VMEM(near, BF),
                    pltpu.VMEM((2, rest[0] // 2) + rest[1:], BF),
                    DMA,
                    DMA((max(4, self.groups),)),
                    DMA((max(4, self.groups),)),
                ]
                shape, dtype, spec = rest, F32, vmem
            else:
                devices = self.ranks * self.groups
                shape, dtype = (devices,) + shape, array.dtype
                scratch = [DMA, DMA((devices,)), DMA((devices,))]
            self.shapes.append(jax.ShapeDtypeStruct(shape, dtype))
            self.out_specs.append(spec)
            self.scratch += scratch
            self.counts.append(len(scratch))

    def params(self):
        if not self.moves:
            return pltpu.CompilerParams(vmem_limit_bytes=VMEM_BYTES)
        return pltpu.CompilerParams(
            collective_id=self.ident, has_side_effects=True, vmem_limit_bytes=VMEM_BYTES
        )

    def begin(self, inputs, outputs, scratch):
        if not self.moves:
            return lambda: False
        steps_of = {
            "gather": gather_steps,
            "scatter": scatter_steps,
            "cross_gather": cross_gather_steps,
            "cross_scatter": cross_scatter_steps,
            "spread": spread_steps,
        }
        place = Place(self.ranks, self.groups)
        scratch = list(scratch)
        running = []
        for i, kind in enumerate(self.kinds):
            taken, scratch = scratch[: self.counts[i]], scratch[self.counts[i] :]
            running.append((kind, steps_of[kind](place, inputs[i], outputs[i], *taken)))
        state = {"met": False, "running": running}

        def phase():
            first = not state["met"]
            if first:
                kinds = set(self.kinds)
                place.meet(
                    bool(kinds & {"gather", "scatter"}),
                    bool(kinds & {"cross_gather", "cross_scatter"}),
                    "spread" in kinds,
                )
                state["met"] = True
            still = []
            for kind, steps in state["running"]:
                if next(steps, True) is None:
                    still.append((kind, steps))
            if first:
                for kind, steps in still:
                    if kind == "scatter":
                        next(steps)
            state["running"] = still
            return bool(still)

        return phase


def finish(phase):
    while phase():
        pass


def exchange_kernel(transfers, *refs):
    count, moves = len(transfers.inputs), transfers.moves
    finish(transfers.begin(refs[:moves], refs[count : count + moves], refs[count + moves :]))


def exchange(mesh_size, ident, moves, needed=()):
    transfers = Transfers(mesh_size, ident, moves, needed)
    return pl.pallas_call(
        functools.partial(exchange_kernel, transfers),
        out_shape=tuple(transfers.shapes),
        in_specs=transfers.in_specs,
        out_specs=tuple(transfers.out_specs),
        scratch_shapes=transfers.scratch,
        compiler_params=transfers.params(),
    )(*transfers.inputs)


def beside(phase, at, grid_steps, work):
    step = pl.program_id(0)
    for when in at:
        pl.when(step == when)(lambda: phase() and None)
    work()
    pl.when(step == grid_steps - 1)(lambda: finish(phase))


def share_kernel(mesh_size, value_ref, out_ref, landing, send, recv, own_sem):
    ranks, groups = mesh_size
    place = Place(ranks, groups)
    place.meet(False, False, True)
    devices, me = groups * ranks, place.device

    def copy(i):
        target = lax.rem(me + i, devices)
        return pltpu.make_async_remote_copy(
            src_ref=value_ref.at[target],
            dst_ref=landing.at[me],
            send_sem=send.at[i],
            recv_sem=recv.at[i],
            device_id=place.name(target),
            device_id_type=MESH,
        )

    def arrival(i):
        source = lax.rem(me - i + devices, devices)
        return pltpu.make_async_remote_copy(
            src_ref=landing.at[source],
            dst_ref=landing.at[source],
            send_sem=send.at[i],
            recv_sem=recv.at[i],
            device_id=place.name(source),
            device_id_type=MESH,
        )

    def start(i, carry):
        copy(i).start()
        return carry

    def finish_one(i, carry):
        arrival(i).wait_recv()
        copy(i).wait_send()
        return carry

    own = pltpu.make_async_copy(value_ref.at[me], landing.at[me], own_sem)
    own.start()
    lax.fori_loop(1, devices, start, 0)
    lax.fori_loop(1, devices, finish_one, 0)
    own.wait()
    out_ref[...] = jnp.sum(landing[...], axis=0)


def share(mesh_size, ident, values):
    vmem = pl.BlockSpec(memory_space=pltpu.VMEM)
    devices = values.shape[0]
    return pl.pallas_call(
        functools.partial(share_kernel, mesh_size),
        out_shape=jax.ShapeDtypeStruct(values.shape[1:], values.dtype),
        in_specs=[vmem],
        out_specs=vmem,
        scratch_shapes=[pltpu.VMEM(values.shape, values.dtype), DMA((devices,)), DMA((devices,)), DMA],
        compiler_params=pltpu.CompilerParams(collective_id=ident, has_side_effects=True),
    )(values)


def column(values, at):
    lanes = lax.broadcasted_iota(jnp.int32, values.shape, 1)
    return jnp.sum(jnp.where(lanes == at, values, 0.0), axis=1, keepdims=True)


def route_kernel(experts, rows_ref, router_ref, routes_ref, out_ref):
    rank = lax.axis_index("tensor")
    logits = dot(rows_ref[...], router_ref[...], (1,), (0,))
    lanes = lax.broadcasted_iota(jnp.int32, logits.shape, 1)
    inside = lanes < experts
    top = jnp.max(jnp.where(inside, logits, -1e30), axis=1, keepdims=True)
    exps = jnp.where(inside, jnp.exp(jnp.where(inside, logits, top) - top), 0.0)
    probs = exps / jnp.sum(exps, axis=1, keepdims=True)
    gate = jax.nn.sigmoid(column(logits, experts))
    named = jnp.where(routes_ref[...] == rank, 1.0, 0.0)
    chosen = jnp.max(named, axis=1, keepdims=True)
    prob = column(probs, rank)
    out = jnp.where(lanes == experts, gate, probs)
    out = jnp.where(lanes == experts + 1, chosen * prob, out)
    out = jnp.where(lanes == experts + 2, chosen, out)
    out_ref[...] = jnp.where(lanes == experts + 3, prob, out)


def routing(experts, rows, router, routes):
    count, width = rows.shape
    return pl.pallas_call(
        functools.partial(route_kernel, experts),
        grid=(count // ROW_BLOCK,),
        in_specs=[
            pl.BlockSpec((ROW_BLOCK, width), lambda i: (i, 0)),
            pl.BlockSpec(router.shape, lambda i: (0, 0)),
            pl.BlockSpec((ROW_BLOCK, routes.shape[1]), lambda i: (i, 0)),
        ],
        out_specs=pl.BlockSpec((ROW_BLOCK, LANES), lambda i: (i, 0)),
        out_shape=jax.ShapeDtypeStruct((count, LANES), F32),
        cost_estimate=pl.CostEstimate(
            flops=2 * count * width * LANES, bytes_accessed=2 * count * width, transcendentals=0
        ),
    )(rows, router, routes)


def routing_back(experts, route, shared_dot, expert_dot):
    rank = lax.axis_index("tensor")
    lanes = lax.broadcasted_iota(jnp.int32, route.shape, 1)
    gate, chosen, prob = [column(route, experts + i) for i in (0, 2, 3)]
    expert_grad = chosen * expert_dot
    logits = route * (jnp.where(lanes == rank, expert_grad, 0.0) - expert_grad * prob)
    gate_logit = shared_dot * gate * (1.0 - gate)
    return jnp.where(lanes < experts, logits, jnp.where(lanes == experts, gate_logit, 0.0))


def ffn_kernel(transfers, at, grid_steps, experts, kind, *refs):
    refs = list(refs)

    def take(count):
        taken = refs[:count]
        del refs[:count]
        return taken

    first, last = kind == "first", kind == "last"
    rows_ref, grad_ref, route_ref, w_ref = take(4)
    before = () if first else take(3)
    router_ref = take(1)[0] if last else None
    sent = take(len(transfers.inputs))
    hidden_ref, gate_ref, up_ref, out_ref, back_ref, dots_ref = take(6)
    landed = take(transfers.moves)
    w_vmem, w_sem = take(2)
    phase = transfers.begin(sent, landed, refs)
    step = pl.program_id(0)

    def weights():
        return pltpu.make_async_copy(w_ref, w_vmem, w_sem)

    pl.when(step == 0)(lambda: weights().start())

    def work():
        pl.when(step == 0)(lambda: weights().wait())
        groups, _, depth, units = w_vmem.shape
        gate_w, up_w, down_w = [w_vmem[:, i].reshape(groups * depth, units) for i in range(3)]
        rows, grad, route = rows_ref[...], grad_ref[...], route_ref[...]
        scale = column(route, experts if first else experts + 1)
        gate_act = dot(rows, gate_w, (1,), (0,))
        up_act = dot(rows, up_w, (1,), (0,))
        back = dot(grad, down_w, (1,), (0,))
        sigmoid = 1.0 / (1.0 + jnp.exp(-gate_act))
        silu = gate_act * sigmoid
        hidden = (silu * up_act).astype(BF).astype(F32)
        dots = jnp.sum(hidden * back, axis=1, keepdims=True)
        scaled = (scale * hidden).astype(BF)
        hidden_ref[...] = scaled
        grad_hidden = scale * back
        grad_gate = (grad_hidden * up_act * (sigmoid * (1.0 + gate_act * (1.0 - sigmoid)))).astype(BF)
        gate_ref[...] = grad_gate
        grad_up = (grad_hidden * silu).astype(BF)
        up_ref[...] = grad_up
        moved = dot(scaled, down_w, (1,), (1,))
        turned = dot(grad_gate, gate_w, (1,), (1,)) + dot(grad_up, up_w, (1,), (1,))
        lanes = lax.broadcasted_iota(jnp.int32, route.shape, 1)
        if first:
            dots_ref[...] = jnp.where(lanes == 0, dots, 0.0)
        else:
            moved = moved + before[0][...].astype(F32)
            turned = turned + before[1][...].astype(F32)
            earlier = before[2][...]
            if last:
                wide = routing_back(experts, route, column(earlier, 0), column(earlier, 1) + dots)
                wide = wide.astype(BF)
                dots_ref[...] = wide
                turned = turned + dot(wide, router_ref[...], (1,), (1,))
            else:
                dots_ref[...] = earlier + jnp.where(lanes == 1, dots, 0.0)
        out_ref[...] = moved.astype(BF)
        back_ref[...] = turned.astype(BF)

    beside(phase, at, grid_steps, work)


def ffn(experts, kind, rows, grads, route, weights, before, router, transfers, at=()):
    count, width = rows.shape
    units = weights.shape[3]
    first, last = kind == "first", kind == "last"
    steps = count // ROW_BLOCK

    def block(size):
        return pl.BlockSpec((ROW_BLOCK, size), lambda i: (i, 0))

    given = [] if first else list(before)
    given_specs = [] if first else [block(width), block(width), block(LANES)]
    if last:
        given.append(router)
        given_specs.append(
            pl.BlockSpec(router.shape, lambda i: (0, 0), pipeline_mode=pl.Buffered(1))
        )
    narrow = [jax.ShapeDtypeStruct((count, units), BF)] * 3
    wide = [jax.ShapeDtypeStruct((count, width), BF)] * 2
    dots = [jax.ShapeDtypeStruct((count, LANES), BF if last else F32)]
    results = pl.pallas_call(
        functools.partial(ffn_kernel, transfers, at, steps, experts, kind),
        grid=(steps,),
        in_specs=[block(width), block(width), block(LANES), pl.BlockSpec(memory_space=pl.ANY)]
        + given_specs
        + transfers.in_specs,
        out_specs=tuple(
            [block(units)] * 3 + [block(width)] * 2 + [block(LANES)] + transfers.out_specs
        ),
        out_shape=tuple(narrow + wide + dots + transfers.shapes),
        scratch_shapes=[pltpu.VMEM(weights.shape, BF), DMA] + transfers.scratch,
        compiler_params=transfers.params(),
        cost_estimate=pl.CostEstimate(
            flops=12 * count * width * units,
            bytes_accessed=2 * (3 * width * units + 4 * count * width + 3 * count * units),
            transcendentals=count * units,
        ),
    )(rows, grads, route, weights, *given, *transfers.inputs)
    return results[:3], results[3:6], results[6:]


def ffn_grads_kernel(transfers, at, grid_steps, micros, last, *refs):
    refs = list(refs)

    def take(count):
        taken = refs[:count]
        del refs[:count]
        return taken

    per_micro = [take(6 if last else 5) for _ in range(micros)]
    sent = take(len(transfers.inputs))
    out_ref = take(1)[0]
    wide_ref = take(1)[0] if last else None
    landed = take(transfers.moves)
    phase = transfers.begin(sent, landed, refs)

    def summed(left, right):
        total = None
        for one in per_micro:
            product = dot(one[left][...], one[right][...], (0,), (0,))
            total = product if total is None else total + product
        return total

    def work():
        for which, left in ((0, 0), (1, 0), (2, 1)):
            out_ref[0, which] = summed(left, 2 + which).astype(BF)
        if last:
            wide_ref[...] = summed(0, 5)

    beside(phase, at, grid_steps, work)


def ffn_grads(groups, per_micro, transfers, at=()):
    count, width = per_micro[0][0].shape
    units = per_micro[0][2].shape[1]
    last = len(per_micro[0]) == 6
    depth = width // groups
    columns = pl.BlockSpec((count, depth), lambda i: (0, i))

    def whole(size):
        return pl.BlockSpec((count, size), lambda i: (0, 0), pipeline_mode=pl.Buffered(1))

    shapes = [jax.ShapeDtypeStruct((groups, 3, depth, units), BF)]
    specs = [pl.BlockSpec((1, 3, depth, units), lambda i: (i, 0, 0, 0))]
    taken = [columns, columns] + [whole(units)] * 3
    if last:
        taken.append(whole(LANES))
        shapes.append(jax.ShapeDtypeStruct((width, LANES), F32))
        specs.append(pl.BlockSpec((depth, LANES), lambda i: (i, 0)))
    results = pl.pallas_call(
        functools.partial(ffn_grads_kernel, transfers, at, groups, len(per_micro), last),
        grid=(groups,),
        in_specs=taken * len(per_micro) + transfers.in_specs,
        out_specs=tuple(specs + transfers.out_specs),
        out_shape=tuple(shapes + transfers.shapes),
        scratch_shapes=transfers.scratch,
        compiler_params=transfers.params(),
        cost_estimate=pl.CostEstimate(
            flops=6 * len(per_micro) * count * width * units,
            bytes_accessed=2 * len(per_micro) * (2 * count * width + 3 * count * units)
            + 6 * width * units,
            transcendentals=0,
        ),
    )(*[array for one in per_micro for array in one], *transfers.inputs)
    return results[: len(shapes)], results[len(shapes) :]


def attention_grads_kernel(micros, *refs):
    out_ref = refs[-1]
    span = refs[2].shape[1]
    totals = [None, None]
    for m in range(micros):
        one = refs[4 * m : 4 * m + 4]
        for which in range(2):
            product = dot(one[which][...], one[2 + which][...], (0,), (0,))
            totals[which] = product if totals[which] is None else totals[which] + product
    out_ref[0, :, :span] = totals[0].astype(BF)
    out_ref[0, :, span:] = totals[1].astype(BF)


def attention_grads(groups, per_micro, needed):
    count, width = per_micro[0][0].shape
    depth = width // groups
    spans = [per_micro[0][i].shape[1] for i in (2, 3)]
    columns = pl.BlockSpec((count, depth), lambda i: (0, i))
    whole = [
        pl.BlockSpec((count, size), lambda i: (0, 0), pipeline_mode=pl.Buffered(1)) for size in spans
    ]
    kernel = functools.partial(attention_grads_kernel, len(per_micro))
    return pl.pallas_call(
        kernel,
        grid=(groups,),
        in_specs=([columns, columns] + whole) * len(per_micro)
        + [pl.BlockSpec(memory_space=pl.ANY)] * len(needed),
        out_specs=pl.BlockSpec((1, depth, sum(spans)), lambda i: (i, 0, 0)),
        out_shape=jax.ShapeDtypeStruct((groups, depth, sum(spans)), BF),
        compiler_params=pltpu.CompilerParams(vmem_limit_bytes=VMEM_BYTES),
        cost_estimate=pl.CostEstimate(
            flops=2 * len(per_micro) * count * width * sum(spans),
            bytes_accessed=8 * len(per_micro) * count * width,
            transcendentals=0,
        ),
    )(*[array for one in per_micro for array in one], *needed)


def rope_tables(seq_len):
    half = HD // 2
    frequency = ROPE_BASE ** (-(2.0 * jnp.arange(half, dtype=F32)) / HD)
    angles = jnp.arange(seq_len, dtype=F32)[:, None] * frequency[None, :]
    cosine, sine = jnp.cos(angles), jnp.sin(angles)
    return (
        jnp.concatenate([cosine, cosine], axis=1),
        jnp.concatenate([-sine, sine], axis=1),
    )


def swap_halves(values):
    half = HD // 2
    return jnp.concatenate([values[:, half:], values[:, :half]], axis=1)


def block_weights(query, keys, first_row, length):
    scores = dot(query, keys, (1,), (1,)) * (HD ** (-0.5))
    rows = first_row + lax.broadcasted_iota(jnp.int32, scores.shape, 0)
    cols = lax.broadcasted_iota(jnp.int32, scores.shape, 1)
    scores = jnp.where((cols <= rows) & (cols < length), scores, -1e30)
    exps = jnp.exp(scores - jnp.max(scores, axis=1, keepdims=True))
    return exps / jnp.sum(exps, axis=1, keepdims=True)


def attend_kernel(heads, length_ref, pre_ref, bias_ref, cos_ref, sin_ref, qkv_ref, out_ref):
    seq_len = pre_ref.shape[0]
    length = length_ref[0]
    for head in range(heads):
        for which in range(3):
            at = (which * heads + head) * HD
            for row in range(0, seq_len, QB):
                part = pre_ref[row : row + QB, at : at + HD] + bias_ref[:, at : at + HD]
                if which < 2:
                    part = (
                        part * cos_ref[row : row + QB, :]
                        + swap_halves(part) * sin_ref[row : row + QB, :]
                    )
                qkv_ref[row : row + QB, at : at + HD] = part.astype(BF)
        q_at, k_at, v_at = (head * HD, (heads + head) * HD, (2 * heads + head) * HD)
        for row in range(0, seq_len, QB):
            end = row + QB
            weights = block_weights(
                qkv_ref[row:end, q_at : q_at + HD], qkv_ref[:end, k_at : k_at + HD], row, length
            )
            mixed = dot(weights.astype(BF), qkv_ref[:end, v_at : v_at + HD], (1,), (0,))
            out_ref[row:end, q_at : q_at + HD] = mixed.astype(BF)


def attend_back_kernel(
    heads, length_ref, qkv_ref, grad_ref, cos_ref, sin_ref, out_ref, sums_ref, key_acc, value_acc
):
    seq_len = qkv_ref.shape[0]
    length = length_ref[0]
    scale = HD ** (-0.5)
    for head in range(heads):
        q_at, k_at, v_at = (head * HD, (heads + head) * HD, (2 * heads + head) * HD)
        key_acc[...] = jnp.zeros_like(key_acc)
        value_acc[...] = jnp.zeros_like(value_acc)
        q_sum = jnp.zeros((1, HD), F32)
        for row in range(0, seq_len, QB):
            end = row + QB
            query = qkv_ref[row:end, q_at : q_at + HD]
            keys = qkv_ref[:end, k_at : k_at + HD]
            grad = grad_ref[row:end, q_at : q_at + HD]
            weights = block_weights(query, keys, row, length)
            grad_weights = dot(grad, qkv_ref[:end, v_at : v_at + HD], (1,), (1,))
            inner = jnp.sum(weights * grad_weights, axis=1, keepdims=True)
            grad_scores = (scale * weights * (grad_weights - inner)).astype(BF)
            turned = dot(grad_scores, keys, (1,), (0,))
            grad_query = (
                turned * cos_ref[row:end, :] - swap_halves(turned) * sin_ref[row:end, :]
            ).astype(BF)
            out_ref[row:end, q_at : q_at + HD] = grad_query
            q_sum = q_sum + jnp.sum(grad_query.astype(F32), axis=0, keepdims=True)
            key_acc[:end, :] += dot(grad_scores, query, (0,), (0,))
            value_acc[:end, :] += dot(weights.astype(BF), grad, (0,), (0,))
        k_sum = jnp.zeros((1, HD), F32)
        v_sum = jnp.zeros((1, HD), F32)
        for row in range(0, seq_len, QB):
            end = row + QB
            turned = key_acc[row:end, :]
            grad_key = (
                turned * cos_ref[row:end, :] - swap_halves(turned) * sin_ref[row:end, :]
            ).astype(BF)
            grad_value = value_acc[row:end, :].astype(BF)
            out_ref[row:end, k_at : k_at + HD] = grad_key
            out_ref[row:end, v_at : v_at + HD] = grad_value
            k_sum = k_sum + jnp.sum(grad_key.astype(F32), axis=0, keepdims=True)
            v_sum = v_sum + jnp.sum(grad_value.astype(F32), axis=0, keepdims=True)
        sums_ref[:, q_at : q_at + HD] = q_sum
        sums_ref[:, k_at : k_at + HD] = k_sum
        sums_ref[:, v_at : v_at + HD] = v_sum


def in_vmem(count):
    return [pl.BlockSpec(memory_space=pltpu.VMEM)] * count


def attend(length, pre, bias, cosine, sine):
    seq_len, width = pre.shape
    heads = width // (3 * HD)
    return pl.pallas_call(
        functools.partial(attend_kernel, heads),
        out_shape=(
            jax.ShapeDtypeStruct((seq_len, width), BF),
            jax.ShapeDtypeStruct((seq_len, heads * HD), BF),
        ),
        in_specs=[pl.BlockSpec(memory_space=pltpu.SMEM)] + in_vmem(4),
        out_specs=tuple(in_vmem(2)),
        compiler_params=pltpu.CompilerParams(vmem_limit_bytes=32 << 20),
        cost_estimate=pl.CostEstimate(
            flops=3 * heads * HD * seq_len * seq_len,
            bytes_accessed=10 * seq_len * width,
            transcendentals=heads * seq_len * seq_len,
        ),
    )(length, pre, bias, cosine, sine)


def attend_back(length, qkv, grad, cosine, sine):
    seq_len, width = qkv.shape
    heads = width // (3 * HD)
    return pl.pallas_call(
        functools.partial(attend_back_kernel, heads),
        out_shape=(
            jax.ShapeDtypeStruct((seq_len, width), BF),
            jax.ShapeDtypeStruct((1, width), F32),
        ),
        in_specs=[pl.BlockSpec(memory_space=pltpu.SMEM)] + in_vmem(4),
        out_specs=tuple(in_vmem(2)),
        scratch_shapes=[pltpu.VMEM((seq_len, HD), F32), pltpu.VMEM((seq_len, HD), F32)],
        compiler_params=pltpu.CompilerParams(vmem_limit_bytes=32 << 20),
        cost_estimate=pl.CostEstimate(
            flops=8 * heads * HD * seq_len * seq_len,
            bytes_accessed=8 * seq_len * width,
            transcendentals=heads * seq_len * seq_len,
        ),
    )(length, qkv, grad, cosine, sine)


def padded(values, axis):
    size = values.shape[axis]
    more = -size % LANES
    if not more:
        return values
    return jnp.pad(values, [(0, more if i == axis else 0) for i in range(values.ndim)])


def packed(values, kind):
    tile = LANES * (16 if kind == BF else 8)
    values = values.astype(kind)
    return padded_to(values, -(-values.shape[-1] // tile) * tile)


def padded_to(values, size):
    more = size - values.shape[-1]
    return jnp.pad(values, [(0, 0)] * (values.ndim - 1) + [(0, more)])


def local(
    tokens,
    lengths,
    routes,
    norm1_gain,
    w_query,
    w_key,
    w_value,
    b_query,
    b_key,
    b_value,
    w_out,
    norm2_gain,
    router,
    shared_gate_vec,
    shared_gate,
    shared_up,
    shared_down,
    expert_gate,
    expert_up,
    expert_down,
    cotangent,
):
    ranks = lax.axis_size("tensor")
    groups = lax.axis_size("fsdp")
    rank = lax.axis_index("tensor")
    micros, _, rows, width = tokens.shape
    seq_len = rows * ranks
    heads = w_query.shape[1] // HD
    span = heads * HD
    experts = ranks * expert_gate.shape[0]
    shared_units = shared_gate.shape[1]
    expert_units = expert_gate.shape[2]
    cut = expert_units // (2 * LANES) * LANES
    own_first = rank * rows
    local_pos = own_first + jnp.arange(rows, dtype=jnp.int32)

    per_device = norm1_gain.shape[0]
    small = jnp.concatenate(
        [
            norm1_gain,
            norm2_gain,
            shared_gate_vec,
            router.reshape(-1),
            b_query.reshape(-1),
            b_key.reshape(-1),
            b_value.reshape(-1),
        ]
    )
    attn_own = jnp.concatenate([w_query, w_key, w_value, w_out.T], axis=1)
    mesh_size = (ranks, groups)
    grads_own = []
    for m in range(micros):
        inside = (local_pos < lengths[m, 0])[:, None]
        grads_own.append(jnp.where(inside, cotangent[m, 0], jnp.zeros((), BF)))
    token_own = [tokens[m, 0] for m in range(micros)]
    rows_a, grad_a, attn_w, small_all = exchange(
        mesh_size,
        2,
        [
            ("gather", token_own[0]),
            ("gather", grads_own[0]),
            ("cross_gather", attn_own),
            ("spread", packed(small, BF).reshape(-1, LANES)),
        ],
    )
    attn_w = attn_w.reshape(width, -1)
    qkv_w, out_w = attn_w[:, : 3 * span], attn_w[:, 3 * span :]
    small_all = small_all.reshape(groups * ranks, -1)
    gain_one = small_all[:, :per_device].reshape(-1).astype(F32)
    gain_two = small_all[:, per_device : 2 * per_device].reshape(-1).astype(F32)
    gate_vec = small_all[:, 2 * per_device : 3 * per_device].reshape(-1)
    bias_at = per_device * (3 + experts)
    router_full = small_all[:, 3 * per_device : bias_at].reshape(width, experts)
    router_wide = padded_to(jnp.concatenate([router_full, gate_vec[:, None]], axis=1), LANES)
    own_bias = lax.dynamic_index_in_dim(
        small_all.reshape(groups, ranks, -1), rank, 1, False
    )[:, bias_at : small.shape[0]].reshape(groups, 3, heads, HD // groups)
    bias = own_bias.transpose(1, 2, 0, 3).reshape(1, 3 * span).astype(F32)

    ranges = [
        (shared_gate, shared_up, shared_down),
        (expert_gate[0, :, :cut], expert_up[0, :, :cut], expert_down[0, :cut]),
        (expert_gate[0, :, cut:], expert_up[0, :, cut:], expert_down[0, cut:]),
    ]
    weights = [
        lax.all_gather(
            jnp.stack([padded(gate, 1), padded(up, 1), padded(down.T, 1)]), "fsdp", axis=0
        )
        for gate, up, down in ranges
    ]

    cosine, sine = rope_tables(seq_len)
    idle = Transfers(mesh_size)

    def attention(m, token_rows):
        normed = (normalize(token_rows.astype(F32))[0] * gain_one).astype(BF)
        pre = dot(normed, qkv_w, (1,), (0,))
        qkv, mixed = attend(lengths[m], pre, bias, cosine, sine)
        return normed, qkv, mixed, dot(mixed, out_w, (1,), (1,)).astype(BF)

    def second_norm(m, attended):
        hidden = token_own[m].astype(F32) + attended
        unit, inverse = normalize(hidden)
        return hidden, unit, inverse, (unit * gain_two).astype(BF)

    def second_norm_back(m, state, summed):
        grad_hidden, gain_part = norm_back(summed, state[1], state[2], gain_two)
        grad_hidden = grad_hidden + grads_own[m].astype(F32)
        return grad_hidden, grad_hidden.astype(BF), gain_part

    def attention_back(m, state, rows_grad):
        grad_mixed = dot(rows_grad, out_w, (1,), (0,)).astype(BF)
        grad_qkv, sums = attend_back(lengths[m], state[1], grad_mixed, cosine, sine)
        return grad_qkv, sums, dot(grad_qkv, qkv_w, (1,), (1,)).astype(BF)

    def first_norm_back(m, grad_hidden, summed):
        unit, inverse = normalize(token_own[m].astype(F32))
        grad_inputs, gain_part = norm_back(summed, unit, inverse, gain_one)
        return (grad_inputs + grad_hidden).astype(BF), gain_part

    def finished(m, hidden, moved):
        inside = (local_pos < lengths[m, 0]).astype(F32)[:, None]
        return (inside * (hidden + moved)).astype(BF)

    att_a = attention(0, rows_a)
    rows_b, sum_a = exchange(
        mesh_size, 3, [("gather", token_own[1]), ("scatter", att_a[3])]
    )
    att_b = attention(1, rows_b)
    norm_a = second_norm(0, sum_a)
    two_a, sum_b = exchange(mesh_size, 4, [("gather", norm_a[3]), ("scatter", att_b[3])])
    norm_b = second_norm(1, sum_b)

    def moving(ident, *moves, needed=()):
        return Transfers(mesh_size, ident, moves, needed)

    def over_groups(grads):
        flat = grads.reshape(-1, grads.shape[-1])
        summed = lax.psum_scatter(flat, "fsdp", scatter_dimension=0, tiled=True)
        return with_layout_constraint(summed, Layout((0, 1))).reshape(grads.shape[1:])

    def grads_of(which, transfers, at=()):
        per_micro = []
        for key in range(micros):
            rows_two, grads = ((two_a, grad_a), (two_b, grad_b))[key]
            scaled, gate, up = act[which, key]
            more = [(acc_a, acc_b)[key][2]] if which == 2 else []
            per_micro.append([rows_two, grads, gate, up, scaled] + more)
        return ffn_grads(groups, per_micro, transfers, at)

    act = {}
    part = functools.partial(ffn, experts)
    route_a = routing(experts, two_a, router_wide, routes[0, 0])
    act[0, 0], acc_a, (two_b,) = part(
        "first", two_a, grad_a, route_a, weights[0], None, None,
        moving(5, ("gather", norm_b[3])), (0, 2),
    )
    act[1, 0], acc_a, (grad_b,) = part(
        "next", two_a, grad_a, route_a, weights[1], acc_a, None,
        moving(6, ("gather", grads_own[1])), (0, 2),
    )
    route_b = routing(experts, two_b, router_wide, routes[1, 0])
    act[0, 1], acc_b, _ = part("first", two_b, grad_b, route_b, weights[0], None, None, idle)
    (grads_0,), _ = grads_of(0, idle)
    range_0 = over_groups(grads_0)
    act[2, 0], acc_a, _ = part(
        "last", two_a, grad_a, route_a, weights[2], acc_a, router_wide, moving(0, needed=[grads_0])
    )
    act[1, 1], acc_b, (down_a,) = part(
        "next", two_b, grad_b, route_b, weights[1], acc_b, None,
        moving(7, ("scatter", acc_a[1])), (0, 2),
    )
    hid_a, send_a, gain_part_a = second_norm_back(0, norm_a, down_a)
    act[2, 1], acc_b, (datt_a, moved_a) = part(
        "last", two_b, grad_b, route_b, weights[2], acc_b, router_wide,
        moving(8, ("gather", send_a), ("scatter", acc_a[0])), (0, 2),
    )
    (grads_1,), (down_b,) = grads_of(
        1, moving(9, ("scatter", acc_b[1]), needed=[range_0]), (0, 2)
    )
    range_1 = over_groups(grads_1)
    hid_b, send_b, gain_part_b = second_norm_back(1, norm_b, down_b)
    grad_qkv_a, sums_a, first_a = attention_back(0, att_a, datt_a)
    (grads_2, total_wide), (datt_b, one_a, moved_b) = grads_of(
        2,
        moving(10, ("gather", send_b), ("scatter", first_a), ("scatter", acc_b[0])),
        (0, 2),
    )
    range_2 = over_groups(grads_2)
    grad_qkv_b, sums_b, first_b = attention_back(1, att_b, datt_b)
    attn_parts = attention_grads(
        groups,
        [
            (att_a[0], datt_a, grad_qkv_a, att_a[2]),
            (att_b[0], datt_b, grad_qkv_b, att_b[2]),
        ],
        [range_1],
    )
    one_b, attn_g = exchange(
        mesh_size, 11, [("scatter", first_b), ("cross_scatter", attn_parts)]
    )

    grad_in_a, one_part_a = first_norm_back(0, hid_a, one_a)
    grad_in_b, one_part_b = first_norm_back(1, hid_b, one_b)

    devices = groups * ranks
    bias_part = (sums_a + sums_b).reshape(3, heads, groups, HD // groups).transpose(2, 0, 1, 3)
    bias_part = bias_part.reshape(groups, 1, -1)
    own_rank = (jnp.arange(ranks, dtype=jnp.int32) == rank).astype(F32)[None, :, None]
    parts = jnp.concatenate(
        [
            (one_part_a + one_part_b).reshape(devices, -1),
            (gain_part_a + gain_part_b).reshape(devices, -1),
            total_wide[:, : experts + 1].reshape(devices, -1),
            (bias_part * own_rank).reshape(devices, -1),
        ],
        axis=1,
    )
    shares = share(mesh_size, 12, packed(parts, F32).reshape(devices, -1, LANES))
    shares = shares.reshape(-1)
    wide_g = shares[2 * per_device : (3 + experts) * per_device].reshape(per_device, experts + 1)
    bias_g = shares[bias_at : parts.shape[1]].reshape(3, heads, HD // groups)

    def plain(which):
        return [which[i].astype(F32) for i in range(3)]

    shared_g, low_g, high_g = plain(range_0), plain(range_1), plain(range_2)
    return (
        jnp.stack([finished(0, norm_a[0], moved_a), finished(1, norm_b[0], moved_b)])[:, None],
        jnp.stack([grad_in_a, grad_in_b])[:, None],
        shares[:per_device],
        attn_g[:, :span],
        attn_g[:, span : 2 * span],
        attn_g[:, 2 * span : 3 * span],
        bias_g[0],
        bias_g[1],
        bias_g[2],
        attn_g[:, 3 * span :].T,
        shares[per_device : 2 * per_device],
        wide_g[:, :experts],
        wide_g[:, experts],
        shared_g[0][:, :shared_units],
        shared_g[1][:, :shared_units],
        shared_g[2][:, :shared_units].T,
        jnp.concatenate([low_g[0], high_g[0]], axis=1)[None],
        jnp.concatenate([low_g[1], high_g[1]], axis=1)[None],
        jnp.concatenate([low_g[2].T, high_g[2].T], axis=0)[None],
    )


def solution(mesh):
    in_specs = (
        P(None, "fsdp", "tensor", None),
        P(None, "fsdp"),
        P(None, "fsdp", None, None),
        P(("fsdp", "tensor")),
        P("fsdp", "tensor"),
        P("fsdp", "tensor"),
        P("fsdp", "tensor"),
        P("tensor", "fsdp"),
        P("tensor", "fsdp"),
        P("tensor", "fsdp"),
        P("tensor", "fsdp"),
        P(("fsdp", "tensor")),
        P(("fsdp", "tensor"), None),
        P(("fsdp", "tensor")),
        P("fsdp", "tensor"),
        P("fsdp", "tensor"),
        P("tensor", "fsdp"),
        P("tensor", "fsdp", None),
        P("tensor", "fsdp", None),
        P("tensor", None, "fsdp"),
        P(None, "fsdp", "tensor", None),
    )
    out_specs = (
        P(None, "fsdp", "tensor", None),
        P(None, "fsdp", "tensor", None),
        P(("fsdp", "tensor")),
        P("fsdp", "tensor"),
        P("fsdp", "tensor"),
        P("fsdp", "tensor"),
        P("tensor", "fsdp"),
        P("tensor", "fsdp"),
        P("tensor", "fsdp"),
        P("tensor", "fsdp"),
        P(("fsdp", "tensor")),
        P(("fsdp", "tensor"), None),
        P(("fsdp", "tensor")),
        P("fsdp", "tensor"),
        P("fsdp", "tensor"),
        P("tensor", "fsdp"),
        P("tensor", "fsdp", None),
        P("tensor", "fsdp", None),
        P("tensor", None, "fsdp"),
    )
    return jax.shard_map(local, mesh=mesh, in_specs=in_specs, out_specs=out_specs, check_vma=False)
```

```python
import functools

import jax
import jax.numpy as jnp
import numpy as np
from jax import lax
from jax.experimental import pallas as pl
from jax.experimental.layout import Layout, with_layout_constraint
from jax.experimental.pallas import tpu as pltpu
from jax.sharding import PartitionSpec as P

HD = 128
EPSILON = 1e-06
ROPE_BASE = 1000000.0
BF = jnp.bfloat16
F32 = jnp.float32
MESH = pl.DeviceIdType.MESH
QB = 256
LANES = 128
CHUNKS = 2
STRIP = 16
ROW_BLOCK = 256
VMEM_BYTES = 60 << 20


def dot(left, right, left_dims, right_dims):
    return lax.dot_general(
        left, right, ((left_dims, right_dims), ((), ())), preferred_element_type=F32
    )


def normalize(values):
    inverse = lax.rsqrt(jnp.mean(values * values, axis=-1, keepdims=True) + EPSILON)
    return (values * inverse, inverse)


def norm_back(grad_normed, unit, inverse, gain):
    grad_unit = grad_normed * gain
    grad_values = inverse * (grad_unit - unit * jnp.mean(grad_unit * unit, axis=-1, keepdims=True))
    return (grad_values, jnp.sum(grad_normed * unit, axis=0))


def remote(src, dst, sems, at, target):
    return pltpu.make_async_remote_copy(
        src_ref=src,
        dst_ref=dst,
        send_sem=sems[0].at[at],
        recv_sem=sems[1].at[at],
        device_id={"tensor": target},
        device_id_type=MESH,
    )


def gather_scratch(ranks):
    chips = ranks // 2
    pair = [pltpu.SemaphoreType.DMA((chips, CHUNKS))] * 2
    cross = [pltpu.SemaphoreType.DMA((2 * chips, CHUNKS))] * 2
    return [pltpu.SemaphoreType.DMA] + pair + pair + cross


def gather_steps(place, block, whole, local_sem, up_s, up_r, down_s, down_r, cross_s, cross_r):
    chips, chip, core = place.chips, place.chip, place.core
    rows = block.shape[0]
    part = rows // CHUNKS
    up, down, cross = (up_s, up_r), (down_s, down_r), (cross_s, cross_r)

    def at(owner, chunk):
        first = pl.multiple_of((2 * owner + core) * rows + chunk * part, part)
        return whole.at[pl.ds(first, part)]

    def theirs(owner, chunk):
        first = pl.multiple_of((2 * owner + 1 - core) * rows + chunk * part, part)
        return whole.at[pl.ds(first, part)]

    def own(chunk):
        return block.at[pl.ds(chunk * part, part)]

    def upward(step, chunk):
        source = own(chunk) if step == 0 else at(chip - step, chunk)
        return remote(source, at(chip - step, chunk), up, (step, chunk), place.above)

    def downward(step, chunk):
        source = own(chunk) if step == 0 else at(chip + step, chunk)
        return remote(source, at(chip + step, chunk), down, (step, chunk), place.below)

    def across(slot, owner, chunk):
        source = own(chunk) if slot == 0 else at(owner, chunk)
        return remote(source, at(owner, chunk), cross, (slot, chunk), place.partner)

    def arrived(slot, owner, chunk):
        return remote(theirs(owner, chunk), theirs(owner, chunk), cross, (slot, chunk), place.partner)

    def arrived_up(step, chunk):
        return remote(at(chip - step, chunk), at(chip - step, chunk), up, (step - 1, chunk), place.above)

    def arrived_down(step, chunk):
        return remote(at(chip + step, chunk), at(chip + step, chunk), down, (step - 1, chunk), place.below)

    both = range(CHUNKS)

    def mine():
        first = pl.multiple_of((2 * chip + core) * rows, rows)
        return pltpu.make_async_copy(block, whole.at[pl.ds(first, rows)], local_sem)

    def begin():
        for chunk in both:
            pl.when(place.not_top)(lambda: upward(0, chunk).start())
            pl.when(place.not_bottom)(lambda: downward(0, chunk).start())
        for chunk in both:
            across(0, chip, chunk).start()
        mine().start()

    def hop(step, chunk):
        @pl.when(chip >= step)
        def _():
            arrived_up(step, chunk).wait_recv()
            pl.when(place.not_top)(lambda: upward(step, chunk).start())
            across(2 * step - 1, chip - step, chunk).start()

        @pl.when(chip < chips - step)
        def _():
            arrived_down(step, chunk).wait_recv()
            pl.when(place.not_bottom)(lambda: downward(step, chunk).start())
            across(2 * step, chip + step, chunk).start()

    def end():
        mine().wait()
        for step in range(chips):
            for chunk in both:
                if step == 0:
                    arrived(0, chip, chunk).wait_recv()
                    across(0, chip, chunk).wait_send()
                else:

                    @pl.when(chip >= step)
                    def _():
                        arrived(2 * step - 1, chip - step, chunk).wait_recv()
                        across(2 * step - 1, chip - step, chunk).wait_send()

                    @pl.when(chip < chips - step)
                    def _():
                        arrived(2 * step, chip + step, chunk).wait_recv()
                        across(2 * step, chip + step, chunk).wait_send()

                @pl.when(place.not_top & (chip >= step))
                def _():
                    upward(step, chunk).wait_send()

                @pl.when(place.not_bottom & (chip < chips - step))
                def _():
                    downward(step, chunk).wait_send()

    hops = [functools.partial(hop, step, chunk) for step in range(1, chips) for chunk in both]
    return [begin] + hops + [end]


def scatter_scratch(ranks, rows, width):
    chips = ranks // 2
    line = [pltpu.SemaphoreType.DMA((chips, CHUNKS))] * 2
    buffers = [pltpu.VMEM((chips, rows, width), BF)] * 5
    return buffers + [pltpu.SemaphoreType.DMA((chips,))] + line * 3


def scatter_steps(
    place, partial, total, kept, pair, held, up_in, down_in, keep_sem,
    up_s, up_r, down_s, down_r, cross_s, cross_r,
):
    chips, chip, core = place.chips, place.chip, place.core
    rows = total.shape[0]
    part = rows // CHUNKS
    up, down, cross = (up_s, up_r), (down_s, down_r), (cross_s, cross_r)
    both = range(CHUNKS)

    def keep(k):
        first = pl.multiple_of((2 * k + core) * rows, rows)
        return pltpu.make_async_copy(partial.at[pl.ds(first, rows)], kept.at[k], keep_sem.at[k])

    def across(k, chunk):
        first = pl.multiple_of((2 * k + 1 - core) * rows + chunk * part, part)
        return remote(
            partial.at[pl.ds(first, part)],
            pair.at[k, pl.ds(chunk * part, part)],
            cross,
            (k, chunk),
            place.partner,
        )

    def upward(step, k, chunk):
        cut = pl.ds(chunk * part, part)
        return remote(held.at[k, cut], up_in.at[step, cut], up, (step, chunk), place.above)

    def downward(step, k, chunk):
        cut = pl.ds(chunk * part, part)
        return remote(held.at[k, cut], down_in.at[step, cut], down, (step, chunk), place.below)

    def add(k, chunk, target, others):
        def strip(i, carry):
            cut = pl.ds(chunk * part + i * STRIP, STRIP)
            value = kept[k, cut].astype(F32) + pair[k, cut].astype(F32)
            for ref, slot in others:
                value = value + ref[slot, cut].astype(F32)
            if target is None:
                total[cut] = value
            else:
                target[k, cut] = value.astype(BF)
            return carry

        lax.fori_loop(0, part // STRIP, strip, 0)

    order = []
    for i in range(chips):
        for k in (chips - 1 - i, i):
            if k not in order:
                order.append(k)
    def begin():
        for k in order:
            keep(k).start()
            for chunk in both:
                across(k, chunk).start()

    def hop(step, chunk):
        @pl.when(place.not_top & (chip <= step - 1))
        def _():
            k = chip + chips - step
            if chunk == 0:
                keep(k).wait()
            across(k, chunk).wait_recv()

            @pl.when(place.not_bottom)
            def _():
                upward(step - 1, k, chunk).wait_recv()
                add(k, chunk, held, [(up_in, step - 1)])

            pl.when(jnp.logical_not(place.not_bottom))(lambda: add(k, chunk, held, []))
            upward(step, k, chunk).start()

        @pl.when(place.not_bottom & (chip >= chips - step))
        def _():
            k = chip - (chips - step)
            if chunk == 0:
                keep(k).wait()
            across(k, chunk).wait_recv()

            @pl.when(place.not_top)
            def _():
                downward(step - 1, k, chunk).wait_recv()
                add(k, chunk, held, [(down_in, step - 1)])

            pl.when(jnp.logical_not(place.not_top))(lambda: add(k, chunk, held, []))
            downward(step, k, chunk).start()

    last = chips - 1

    def add_last(chunk):
        if chunk == 0:
            keep(chip).wait()
        across(chip, chunk).wait_recv()

        @pl.when(place.not_top & place.not_bottom)
        def _():
            upward(last, chip, chunk).wait_recv()
            downward(last, chip, chunk).wait_recv()
            add(chip, chunk, None, [(up_in, last), (down_in, last)])

        @pl.when(jnp.logical_not(place.not_top))
        def _():
            upward(last, chip, chunk).wait_recv()
            add(chip, chunk, None, [(up_in, last)])

        @pl.when(jnp.logical_not(place.not_bottom))
        def _():
            downward(last, chip, chunk).wait_recv()
            add(chip, chunk, None, [(down_in, last)])

    def end():
        for chunk in both:
            for k in range(chips):
                across(k, chunk).wait_send()
            for step in range(1, chips):

                @pl.when(place.not_top & (chip <= step - 1))
                def _():
                    upward(step, chip + chips - step, chunk).wait_send()

                @pl.when(place.not_bottom & (chip >= chips - step))
                def _():
                    downward(step, chip - (chips - step), chunk).wait_send()

    def first():
        begin()
        for chunk in both:
            hop(1, chunk)

    hops = [functools.partial(hop, step, chunk) for step in range(2, chips) for chunk in both]
    return [first] + hops + [functools.partial(add_last, chunk) for chunk in both] + [end]


class Place:
    def __init__(self, ranks, groups):
        rank, group = lax.axis_index("tensor"), lax.axis_index("fsdp")
        self.ranks, self.groups = ranks, groups
        self.chips = ranks // 2
        self.chip, self.core = rank // 2, rank % 2
        self.partner = rank + 1 - 2 * self.core
        self.above, self.below = rank + 2, rank - 2
        self.not_top = self.chip < self.chips - 1
        self.not_bottom = self.chip > 0
        self.rank, self.group = rank, group
        self.device = group * ranks + rank
        near, far = group % 2, group // 2
        self.beside = 2 * far + 1 - near
        self.across = 2 * (1 - far) + near
        self.opposite = 2 * (1 - far) + 1 - near
        self.square = groups == 4

    def name(self, device):
        return {"fsdp": device // self.ranks, "tensor": device % self.ranks}

    def meet(self, line, cross, everyone):
        barrier = pltpu.get_barrier_semaphore()

        def greet(name):
            pl.semaphore_signal(barrier, 1, device_id=name, device_id_type=MESH)

        if everyone:
            devices = self.groups * self.ranks

            def one(i, carry):
                greet(self.name(lax.rem(self.device + i, devices)))
                return carry

            lax.fori_loop(1, devices, one, 0)
            pl.semaphore_wait(barrier, devices - 1)
            return
        peers = 0
        if line:
            greet({"tensor": self.partner})
            pl.when(self.not_top)(lambda: greet({"tensor": self.above}))
            pl.when(self.not_bottom)(lambda: greet({"tensor": self.below}))
            peers = 1 + self.not_top.astype(jnp.int32) + self.not_bottom.astype(jnp.int32)
        if cross and self.square:
            greet({"fsdp": self.beside})
            greet({"fsdp": self.across})
            peers = peers + 2
        elif cross:
            for i in range(1, self.groups):
                greet({"fsdp": lax.rem(self.group + i, self.groups)})
            peers = peers + self.groups - 1
        pl.semaphore_wait(barrier, peers)


def to_group(src, dst, send, recv, at, target):
    return pltpu.make_async_remote_copy(
        src_ref=src,
        dst_ref=dst,
        send_sem=send.at[at],
        recv_sem=recv.at[at],
        device_id={"fsdp": target},
        device_id_type=MESH,
    )


def cross_gather_steps(place, block, whole, own_sem, send, recv):
    group = place.group
    half = block.shape[0] // 2

    def own():
        return pltpu.make_async_copy(block, whole.at[group], own_sem)

    if not place.square:

        def direct(i):
            target = lax.rem(group + i, place.groups)
            return to_group(block, whole.at[group], send, recv, i - 1, target)

        def begin_direct():
            own().start()
            for i in range(1, place.groups):
                direct(i).start()

        def end_direct():
            own().wait()
            for i in range(1, place.groups):
                source = lax.rem(group - i + place.groups, place.groups)
                to_group(block, whole.at[source], send, recv, i - 1, source).wait_recv()
                direct(i).wait_send()

        return [begin_direct, end_direct]

    def near(at):
        return to_group(block, whole.at[group], send, recv, at, (place.beside, place.across)[at])

    def came(at):
        source = (place.beside, place.across)[at]
        return to_group(whole.at[source], whole.at[source], send, recv, at, source)

    def forward(at):
        source, target = ((place.beside, place.across), (place.across, place.beside))[at]
        piece = whole.at[source, pl.ds(at * half, half)]
        return to_group(piece, piece, send, recv, 2 + at, target)

    def far(at):
        piece = whole.at[place.opposite, pl.ds(at * half, half)]
        return to_group(piece, piece, send, recv, 2 + at, place.opposite)

    def begin():
        for at in range(2):
            near(at).start()
        own().start()

    def pass_on():
        for at in range(2):
            came(at).wait_recv()
            forward(at).start()

    def end():
        own().wait()
        for at in range(2):
            far(at).wait_recv()
            near(at).wait_send()
            forward(at).wait_send()

    return [begin] + [nothing] * 5 + [pass_on, end]


def cross_scatter_steps(place, partial, total, mine, near_in, far_in, own_sem, send, recv):
    group = place.group
    rows = total.shape[0]
    half = rows // 2

    def own():
        return pltpu.make_async_copy(partial, mine, own_sem)

    def loop(count, body):
        def strip(i, carry):
            body(pl.ds(i * STRIP, STRIP))
            return carry

        lax.fori_loop(0, count // STRIP, strip, 0)

    if not place.square:

        def direct(i):
            target = lax.rem(group + i, place.groups)
            return to_group(partial.at[target], near_in.at[group], send, recv, i - 1, target)

        def begin_direct():
            own().start()
            for i in range(1, place.groups):
                direct(i).start()

        def sum_direct(cut):
            value = mine[group, cut].astype(F32)
            for i in range(1, place.groups):
                value = value + near_in[lax.rem(group + i, place.groups), cut].astype(F32)
            total[cut] = value

        def end_direct():
            own().wait()
            for i in range(1, place.groups):
                source = lax.rem(group - i + place.groups, place.groups)
                piece = partial.at[source]
                to_group(piece, near_in.at[source], send, recv, i - 1, source).wait_recv()
            loop(rows, sum_direct)
            for i in range(1, place.groups):
                direct(i).wait_send()

        return [begin_direct, end_direct]

    def first(at):
        target = (place.beside, place.across)[at]
        piece = partial.at[place.opposite, pl.ds(at * half, half)]
        return to_group(piece, far_in.at[at], send, recv, at, target)

    def second(at):
        target = (place.beside, place.across)[at]
        return to_group(mine.at[target], near_in.at[at], send, recv, 2 + at, target)

    def begin():
        own().start()
        for at in range(2):
            first(at).start()

    def join():
        own().wait()
        for at in range(2):
            target = (place.across, place.beside)[at]
            first(at).wait_recv()

            def one(cut, at=at, target=target):
                place_in = pl.ds(at * half + cut.start, STRIP)
                value = mine[target, place_in].astype(F32) + far_in[at, cut].astype(F32)
                mine[target, place_in] = value.astype(BF)

            loop(half, one)
            second(1 - at).start()

    def everything(cut):
        value = mine[group, cut].astype(F32) + near_in[0, cut].astype(F32)
        total[cut] = value + near_in[1, cut].astype(F32)

    def end():
        for at in range(2):
            second(at).wait_recv()
        loop(rows, everything)
        for at in range(2):
            first(at).wait_send()
            second(at).wait_send()

    return [begin, nothing, join, nothing, nothing, end]


def everyone_steps(place, piece_for, landing, own_sem, send, recv):
    devices = place.groups * place.ranks
    me = place.device

    def copy(i):
        target = lax.rem(me + i, devices)
        return pltpu.make_async_remote_copy(
            src_ref=piece_for(target),
            dst_ref=landing.at[me],
            send_sem=send.at[i],
            recv_sem=recv.at[i],
            device_id=place.name(target),
            device_id_type=MESH,
        )

    def arrival(i):
        source = lax.rem(me - i + devices, devices)
        return pltpu.make_async_remote_copy(
            src_ref=landing.at[source],
            dst_ref=landing.at[source],
            send_sem=send.at[i],
            recv_sem=recv.at[i],
            device_id=place.name(source),
            device_id_type=MESH,
        )

    def start(i, carry):
        copy(i).start()
        return carry

    def finish_one(i, carry):
        arrival(i).wait_recv()
        copy(i).wait_send()
        return carry

    def own():
        return pltpu.make_async_copy(piece_for(me), landing.at[me], own_sem)

    def begin():
        own().start()
        lax.fori_loop(1, devices, start, 0)

    def end():
        own().wait()
        lax.fori_loop(1, devices, finish_one, 0)

    return [begin, nothing, end]


def spread_steps(place, value, everyone, own_sem, send, recv):
    return everyone_steps(place, lambda target: value, everyone, own_sem, send, recv)


def share_steps(place, values, total, landing, own_sem, send, recv):
    phases = everyone_steps(place, lambda target: values.at[target], landing, own_sem, send, recv)

    def add_up():
        total[...] = jnp.sum(landing[...], axis=0)

    return phases + [add_up]


DMA = pltpu.SemaphoreType.DMA


class Transfers:
    def __init__(self, mesh_size, ident=0, moves=(), needed=()):
        self.ranks, self.groups = mesh_size
        self.ident = ident
        self.kinds = [move[0] for move in moves]
        self.parts = [move[2] if len(move) > 2 else None for move in moves]
        self.inputs = [move[1] for move in moves] + list(needed)
        self.moves = len(self.kinds)
        anywhere = pl.BlockSpec(memory_space=pl.ANY)
        vmem = pl.BlockSpec(memory_space=pltpu.VMEM)
        self.in_specs = [anywhere] * len(self.inputs)
        self.shapes, self.out_specs, self.scratch, self.counts = [], [], [], []
        for kind, array, *part in moves:
            shape, spec = array.shape[len(part[0]) :] if part else array.shape, anywhere
            if kind == "gather":
                shape, dtype = (self.ranks * shape[0], shape[1]), BF
                scratch = gather_scratch(self.ranks)
            elif kind == "scatter":
                shape, dtype, spec = (shape[0] // self.ranks, shape[1]), F32, vmem
                scratch = scatter_scratch(self.ranks, *shape)
            elif kind == "cross_gather":
                shape, dtype = (self.groups,) + shape, BF
                scratch = [DMA, DMA((max(4, self.groups),)), DMA((max(4, self.groups),))]
            elif kind == "cross_scatter":
                rest = shape[1:]
                square = self.groups == 4
                near = (2 if square else self.groups,) + rest
                scratch = [
                    pltpu.VMEM(shape, BF),
                    pltpu.VMEM(near, BF),
                    pltpu.VMEM((2, rest[0] // 2) + rest[1:], BF),
                    DMA,
                    DMA((max(4, self.groups),)),
                    DMA((max(4, self.groups),)),
                ]
                shape, dtype, spec = rest, F32, vmem
            elif kind == "share":
                devices = self.ranks * self.groups
                scratch = [pltpu.VMEM(shape, F32), DMA, DMA((devices,)), DMA((devices,))]
                shape, dtype, spec = shape[1:], F32, vmem
            else:
                devices = self.ranks * self.groups
                shape, dtype = (devices,) + shape, array.dtype
                scratch = [DMA, DMA((devices,)), DMA((devices,))]
            self.shapes.append(jax.ShapeDtypeStruct(shape, dtype))
            self.out_specs.append(spec)
            self.scratch += scratch
            self.counts.append(len(scratch))

    def params(self):
        if not self.moves:
            return pltpu.CompilerParams(vmem_limit_bytes=VMEM_BYTES)
        return pltpu.CompilerParams(
            collective_id=self.ident, has_side_effects=True, vmem_limit_bytes=VMEM_BYTES
        )

    def begin(self, inputs, outputs, scratch):
        if not self.moves:
            return []
        steps_of = {
            "gather": gather_steps,
            "scatter": scatter_steps,
            "cross_gather": cross_gather_steps,
            "cross_scatter": cross_scatter_steps,
            "spread": spread_steps,
            "share": share_steps,
        }
        place = Place(self.ranks, self.groups)
        scratch = list(scratch)
        lines = []
        for i, kind in enumerate(self.kinds):
            taken, scratch = scratch[: self.counts[i]], scratch[self.counts[i] :]
            given = inputs[i] if self.parts[i] is None else inputs[i].at[self.parts[i]]
            lines.append(steps_of[kind](place, given, outputs[i], *taken))

        def phase(number):
            if number == 0:
                kinds = set(self.kinds)
                place.meet(
                    bool(kinds & {"gather", "scatter"}),
                    bool(kinds & {"cross_gather", "cross_scatter"}),
                    bool(kinds & {"spread", "share"}),
                )
            for steps in lines:
                if number < len(steps):
                    steps[number]()

        return [functools.partial(phase, i) for i in range(max(map(len, lines)))]


def nothing():
    pass


def run_all(phases):
    for phase in phases:
        phase()


def exchange_kernel(transfers, *refs):
    count, moves = len(transfers.inputs), transfers.moves
    run_all(transfers.begin(refs[:moves], refs[count : count + moves], refs[count + moves :]))


def exchange(mesh_size, ident, moves, needed=()):
    transfers = Transfers(mesh_size, ident, moves, needed)
    return pl.pallas_call(
        functools.partial(exchange_kernel, transfers),
        out_shape=tuple(transfers.shapes),
        in_specs=transfers.in_specs,
        out_specs=tuple(transfers.out_specs),
        scratch_shapes=transfers.scratch,
        compiler_params=transfers.params(),
    )(*transfers.inputs)


def beside(phases, at, grid_steps, parts):
    step = pl.program_id(0)
    state = None
    for number, part in enumerate(parts):
        for phase, (when, ahead_of) in zip(phases, at):
            if ahead_of == number:
                pl.when(step == when)(phase)
        state = part(state)
    if phases:
        pl.when(step == grid_steps - 1)(lambda: run_all(phases[len(at) :]))


def column(values, at):
    lanes = lax.broadcasted_iota(jnp.int32, values.shape, 1)
    return jnp.sum(jnp.where(lanes == at, values, 0.0), axis=1, keepdims=True)


def routing(experts, length, first_row, rows, router, routes):
    rank = lax.axis_index("tensor")
    logits = dot(rows, router, (1,), (0,))
    lanes = lax.broadcasted_iota(jnp.int32, logits.shape, 1)
    inside = lanes < experts
    top = jnp.max(jnp.where(inside, logits, -1e30), axis=1, keepdims=True)
    exps = jnp.where(inside, jnp.exp(jnp.where(inside, logits, top) - top), 0.0)
    probs = exps / jnp.sum(exps, axis=1, keepdims=True)
    position = first_row + lax.broadcasted_iota(jnp.int32, (rows.shape[0], 1), 0)
    valid = jnp.where(position < length, 1.0, 0.0)
    gate = valid * jax.nn.sigmoid(column(logits, experts))
    chosen = valid * jnp.max(jnp.where(routes == rank, 1.0, 0.0), axis=1, keepdims=True)
    prob = column(probs, rank)
    out = jnp.where(lanes == experts, gate, probs)
    out = jnp.where(lanes == experts + 1, chosen * prob, out)
    out = jnp.where(lanes == experts + 2, chosen, out)
    return jnp.where(lanes == experts + 3, prob, out)


def routing_back(experts, route, shared_dot, expert_dot):
    rank = lax.axis_index("tensor")
    lanes = lax.broadcasted_iota(jnp.int32, route.shape, 1)
    gate, chosen, prob = [column(route, experts + i) for i in (0, 2, 3)]
    expert_grad = chosen * expert_dot
    logits = route * (jnp.where(lanes == rank, expert_grad, 0.0) - expert_grad * prob)
    gate_logit = shared_dot * gate * (1.0 - gate)
    return jnp.where(lanes < experts, logits, jnp.where(lanes == experts, gate_logit, 0.0))


def ffn_kernel(transfers, at, grid_steps, experts, kind, *refs):
    refs = list(refs)

    def take(count):
        taken = refs[:count]
        del refs[:count]
        return taken

    first, last = kind == "first", kind == "last"
    rows_ref, grad_ref, route_ref, w_ref = take(4)
    before = take(1) if first else take(3)
    router_ref = take(1)[0] if first or last else None
    sent = take(len(transfers.inputs))
    hidden_ref, gate_ref, up_ref, out_ref, back_ref, dots_ref = take(6)
    if first:
        made_ref = take(1)[0]
    landed = take(transfers.moves)
    w_vmem, w_sem = take(2)
    phases = transfers.begin(sent, landed, refs)
    step = pl.program_id(0)

    def weights():
        return pltpu.make_async_copy(w_ref, w_vmem, w_sem)

    pl.when(step == 0)(lambda: weights().start())

    def hidden_part(_):
        pl.when(step == 0)(lambda: weights().wait())
        groups, _, depth, units = w_vmem.shape
        gate_w, up_w, down_w = [w_vmem[:, i].reshape(groups * depth, units) for i in range(3)]
        rows, grad = rows_ref[...], grad_ref[...]
        if first:
            length = before[0][0]
            route = routing(experts, length, step * ROW_BLOCK, rows, router_ref[...], route_ref[...])
            made_ref[...] = route
        else:
            route = route_ref[...]
        scale = column(route, experts if first else experts + 1)
        gate_act = dot(rows, gate_w, (1,), (0,))
        up_act = dot(rows, up_w, (1,), (0,))
        back = dot(grad, down_w, (1,), (0,))
        sigmoid = 1.0 / (1.0 + jnp.exp(-gate_act))
        silu = gate_act * sigmoid
        hidden = (silu * up_act).astype(BF).astype(F32)
        dots = jnp.sum(hidden * back, axis=1, keepdims=True)
        scaled = (scale * hidden).astype(BF)
        hidden_ref[...] = scaled
        grad_hidden = scale * back
        grad_gate = (grad_hidden * up_act * (sigmoid * (1.0 + gate_act * (1.0 - sigmoid)))).astype(BF)
        gate_ref[...] = grad_gate
        grad_up = (grad_hidden * silu).astype(BF)
        up_ref[...] = grad_up
        return gate_w, up_w, down_w, scaled, grad_gate, grad_up, route, dots

    def outer_part(state):
        gate_w, up_w, down_w, scaled, grad_gate, grad_up, route, dots = state
        moved = dot(scaled, down_w, (1,), (1,))
        turned = dot(grad_gate, gate_w, (1,), (1,)) + dot(grad_up, up_w, (1,), (1,))
        lanes = lax.broadcasted_iota(jnp.int32, route.shape, 1)
        if first:
            dots_ref[...] = jnp.where(lanes == 0, dots, 0.0)
        else:
            moved = moved + before[0][...].astype(F32)
            turned = turned + before[1][...].astype(F32)
            earlier = before[2][...]
            if last:
                wide = routing_back(experts, route, column(earlier, 0), column(earlier, 1) + dots)
                wide = wide.astype(BF)
                dots_ref[...] = wide
                turned = turned + dot(wide, router_ref[...], (1,), (1,))
            else:
                dots_ref[...] = earlier + jnp.where(lanes == 1, dots, 0.0)
        out_ref[...] = moved.astype(BF)
        back_ref[...] = turned.astype(BF)

    beside(phases, at, grid_steps, [hidden_part, outer_part])


def ffn(experts, kind, rows, grads, route, weights, before, router, transfers, at=()):
    count, width = rows.shape
    units = weights.shape[3]
    first, last = kind == "first", kind == "last"
    steps = count // ROW_BLOCK

    def block(size):
        return pl.BlockSpec((ROW_BLOCK, size), lambda i: (i, 0))

    given = list(before)
    given_specs = [block(width), block(width), block(LANES)]
    if first:
        given_specs = [pl.BlockSpec(memory_space=pltpu.SMEM)]
    if first or last:
        given.append(router)
        given_specs.append(
            pl.BlockSpec(router.shape, lambda i: (0, 0), pipeline_mode=pl.Buffered(1))
        )
    narrow = [jax.ShapeDtypeStruct((count, units), BF)] * 3
    wide = [jax.ShapeDtypeStruct((count, width), BF)] * 2
    dots = [jax.ShapeDtypeStruct((count, LANES), BF if last else F32)]
    dots += [jax.ShapeDtypeStruct((count, LANES), F32)] * first
    results = pl.pallas_call(
        functools.partial(ffn_kernel, transfers, at, steps, experts, kind),
        grid=(steps,),
        in_specs=[block(width), block(width), block(route.shape[1]), pl.BlockSpec(memory_space=pl.ANY)]
        + given_specs
        + transfers.in_specs,
        out_specs=tuple(
            [block(units)] * 3
            + [block(width)] * 2
            + [block(LANES)] * len(dots)
            + transfers.out_specs
        ),
        out_shape=tuple(narrow + wide + dots + transfers.shapes),
        scratch_shapes=[pltpu.VMEM(weights.shape, BF), DMA] + transfers.scratch,
        compiler_params=transfers.params(),
        cost_estimate=pl.CostEstimate(
            flops=12 * count * width * units,
            bytes_accessed=2 * (3 * width * units + 4 * count * width + 3 * count * units),
            transcendentals=count * units,
        ),
    )(rows, grads, route, weights, *given, *transfers.inputs)
    made = 5 + len(dots)
    return results[:3], results[3:made], results[made:]


def ffn_grads_kernel(transfers, at, grid_steps, micros, last, *refs):
    refs = list(refs)

    def take(count):
        taken = refs[:count]
        del refs[:count]
        return taken

    per_micro = [take(6 if last else 5) for _ in range(micros)]
    sent = take(len(transfers.inputs))
    out_ref = take(1)[0]
    wide_ref = take(1)[0] if last else None
    landed = take(transfers.moves)
    phases = transfers.begin(sent, landed, refs)

    def summed(left, right):
        total = None
        for one in per_micro:
            product = dot(one[left][...], one[right][...], (0,), (0,))
            total = product if total is None else total + product
        return total

    def one_product(which):
        def part(_):
            out_ref[0, which] = summed((0, 0, 1)[which], 2 + which).astype(BF)
            if last and which == 2:
                wide_ref[...] = summed(0, 5)

        return part

    beside(phases, at, grid_steps, [one_product(which) for which in range(3)])


def ffn_grads(groups, per_micro, transfers, at=()):
    count, width = per_micro[0][0].shape
    units = per_micro[0][2].shape[1]
    last = len(per_micro[0]) == 6
    depth = width // groups
    columns = pl.BlockSpec((count, depth), lambda i: (0, i))

    def whole(size):
        return pl.BlockSpec((count, size), lambda i: (0, 0), pipeline_mode=pl.Buffered(1))

    shapes = [jax.ShapeDtypeStruct((groups, 3, depth, units), BF)]
    specs = [pl.BlockSpec((1, 3, depth, units), lambda i: (i, 0, 0, 0))]
    taken = [columns, columns] + [whole(units)] * 3
    if last:
        taken.append(whole(LANES))
        shapes.append(jax.ShapeDtypeStruct((width, LANES), F32))
        specs.append(pl.BlockSpec((depth, LANES), lambda i: (i, 0)))
    results = pl.pallas_call(
        functools.partial(ffn_grads_kernel, transfers, at, groups, len(per_micro), last),
        grid=(groups,),
        in_specs=taken * len(per_micro) + transfers.in_specs,
        out_specs=tuple(specs + transfers.out_specs),
        out_shape=tuple(shapes + transfers.shapes),
        scratch_shapes=transfers.scratch,
        compiler_params=transfers.params(),
        cost_estimate=pl.CostEstimate(
            flops=6 * len(per_micro) * count * width * units,
            bytes_accessed=2 * len(per_micro) * (2 * count * width + 3 * count * units)
            + 6 * width * units,
            transcendentals=0,
        ),
    )(*[array for one in per_micro for array in one], *transfers.inputs)
    return results[: len(shapes)], results[len(shapes) :]


def attention_grads_kernel(transfers, grid_steps, micros, *refs):
    refs = list(refs)

    def take(count):
        taken = refs[:count]
        del refs[:count]
        return taken

    per_micro = [take(4) for _ in range(micros)]
    sent = take(len(transfers.inputs))
    out_ref = take(1)[0]
    landed = take(transfers.moves)
    phases = transfers.begin(sent, landed, refs)

    def work(_):
        span = per_micro[0][2].shape[1]
        totals = [None, None]
        for one in per_micro:
            for which in range(2):
                product = dot(one[which][...], one[2 + which][...], (0,), (0,))
                totals[which] = product if totals[which] is None else totals[which] + product
        out_ref[0, :, :span] = totals[0].astype(BF)
        out_ref[0, :, span:] = totals[1].astype(BF)

    beside(phases, [(0, 0)], grid_steps, [work])


def attention_grads(groups, per_micro, transfers):
    count, width = per_micro[0][0].shape
    depth = width // groups
    spans = [per_micro[0][i].shape[1] for i in (2, 3)]
    columns = pl.BlockSpec((count, depth), lambda i: (0, i))
    whole = [
        pl.BlockSpec((count, size), lambda i: (0, 0), pipeline_mode=pl.Buffered(1)) for size in spans
    ]
    results = pl.pallas_call(
        functools.partial(attention_grads_kernel, transfers, groups, len(per_micro)),
        grid=(groups,),
        in_specs=([columns, columns] + whole) * len(per_micro) + transfers.in_specs,
        out_specs=tuple(
            [pl.BlockSpec((1, depth, sum(spans)), lambda i: (i, 0, 0))] + transfers.out_specs
        ),
        out_shape=tuple(
            [jax.ShapeDtypeStruct((groups, depth, sum(spans)), BF)] + transfers.shapes
        ),
        scratch_shapes=transfers.scratch,
        compiler_params=transfers.params(),
        cost_estimate=pl.CostEstimate(
            flops=2 * len(per_micro) * count * width * sum(spans),
            bytes_accessed=8 * len(per_micro) * count * width,
            transcendentals=0,
        ),
    )(*[array for one in per_micro for array in one], *transfers.inputs)
    return results[0], results[1:]


def pack_kernel(cut, gate_ref, up_ref, down_ref, *refs):
    low_ref, high_ref = refs[-2:]
    for out_ref, part in ((low_ref, slice(0, cut)), (high_ref, slice(cut, None))):
        out_ref[0] = gate_ref[0, :, part]
        out_ref[1] = up_ref[0, :, part]
        out_ref[2] = down_ref[0, part, :].T


def pack(cut, gate, up, down, needed):
    _, depth, units = gate.shape
    vmem = pl.BlockSpec(memory_space=pltpu.VMEM)
    return pl.pallas_call(
        functools.partial(pack_kernel, cut),
        in_specs=[vmem] * 3 + [pl.BlockSpec(memory_space=pl.ANY)] * len(needed),
        out_specs=(vmem, vmem),
        out_shape=tuple(
            jax.ShapeDtypeStruct((3, depth, size), BF) for size in (cut, units - cut)
        ),
        compiler_params=pltpu.CompilerParams(vmem_limit_bytes=VMEM_BYTES),
        cost_estimate=pl.CostEstimate(flops=0, bytes_accessed=12 * depth * units, transcendentals=0),
    )(gate, up, down, *needed)


def unpack_kernel(turned, *refs):
    count = len(refs) - 3
    for which, out_ref in enumerate(refs[count:]):
        first = 0
        for ref in refs[:count]:
            values = ref[which].astype(F32)
            if turned[which]:
                values = values.T
                size = min(values.shape[0], out_ref.shape[0] - first)
                out_ref[first : first + size, :] = values[:size]
            else:
                size = min(values.shape[1], out_ref.shape[1] - first)
                out_ref[:, first : first + size] = values[:, :size]
            first += size


def unpack(ranges, units, turned):
    depth = ranges[0].shape[1]
    vmem = pl.BlockSpec(memory_space=pltpu.VMEM)
    return pl.pallas_call(
        functools.partial(unpack_kernel, turned),
        in_specs=[vmem] * len(ranges),
        out_specs=(vmem,) * 3,
        out_shape=tuple(
            jax.ShapeDtypeStruct((units, depth) if turn else (depth, units), F32) for turn in turned
        ),
        compiler_params=pltpu.CompilerParams(vmem_limit_bytes=VMEM_BYTES),
        cost_estimate=pl.CostEstimate(flops=0, bytes_accessed=18 * depth * units, transcendentals=0),
    )(*ranges)


def rope_tables(seq_len):
    half = HD // 2
    frequency = np.float32(ROPE_BASE) ** (-(2.0 * np.arange(half, dtype=np.float32)) / HD)
    angles = np.arange(seq_len, dtype=np.float32)[:, None] * frequency[None, :].astype(np.float32)
    cosine, sine = np.cos(angles.astype(np.float64)), np.sin(angles.astype(np.float64))
    return (
        jnp.asarray(np.concatenate([cosine, cosine], axis=1).astype(np.float32)),
        jnp.asarray(np.concatenate([-sine, sine], axis=1).astype(np.float32)),
    )


def swap_halves(values):
    half = HD // 2
    return jnp.concatenate([values[:, half:], values[:, :half]], axis=1)


def block_weights(query, keys, first_row, length):
    scores = dot(query, keys, (1,), (1,)) * (HD ** (-0.5))
    rows = first_row + lax.broadcasted_iota(jnp.int32, scores.shape, 0)
    cols = lax.broadcasted_iota(jnp.int32, scores.shape, 1)
    scores = jnp.where((cols <= rows) & (cols < length), scores, -1e30)
    exps = jnp.exp(scores - jnp.max(scores, axis=1, keepdims=True))
    return exps / jnp.sum(exps, axis=1, keepdims=True)


def attend_kernel(heads, transfers, *refs):
    refs = list(refs)

    def take(count):
        taken = refs[:count]
        del refs[:count]
        return taken

    length_ref, x_ref, gain_ref, w_ref, bias_ref, cos_ref, sin_ref = take(7)
    sent = take(len(transfers.inputs))
    normed_ref, qkv_ref, mixed_ref, out_ref = take(4)
    landed = take(transfers.moves)
    rows_vmem, out_vmem, in_sem, normed_sem, out_sem = take(5)
    phases = transfers.begin(sent, landed, refs)
    seq_len, width = x_ref.shape
    groups, depth, columns = w_ref.shape
    span = heads * HD
    length = length_ref[0]
    blocks = [pl.ds(row, QB) for row in range(0, seq_len, QB)]

    def fetch(i):
        return pltpu.make_async_copy(x_ref.at[blocks[i]], rows_vmem.at[blocks[i]], in_sem.at[i])

    def keep(i):
        return pltpu.make_async_copy(rows_vmem.at[blocks[i]], normed_ref.at[blocks[i]], normed_sem.at[i])

    def give(i):
        return pltpu.make_async_copy(out_vmem.at[blocks[i]], out_ref.at[blocks[i]], out_sem.at[i])

    for i in range(len(blocks)):
        fetch(i).start()
    run_all(phases[:1])
    weights = w_ref[...].reshape(groups * depth, columns)
    qkv_w, out_w = weights[:, : 3 * span], weights[:, 3 * span :]
    for i in range(len(blocks)):
        row, end = i * QB, (i + 1) * QB
        if i >= 2:
            run_all(phases[i - 1 : i])
        fetch(i).wait()
        values = rows_vmem[row:end, :].astype(F32)
        normed = (normalize(values)[0] * gain_ref[...]).astype(BF)
        rows_vmem[row:end, :] = normed
        keep(i).start()
        pre = dot(normed, qkv_w, (1,), (0,)) + bias_ref[...]
        cosine, sine = cos_ref[row:end, :], sin_ref[row:end, :]
        for at in range(0, 3 * span, HD):
            part = pre[:, at : at + HD]
            if at < 2 * span:
                part = part * cosine + swap_halves(part) * sine
            qkv_ref[row:end, at : at + HD] = part.astype(BF)
        for head in range(heads):
            q_at, k_at, v_at = (head * HD, span + head * HD, 2 * span + head * HD)
            shares = block_weights(
                qkv_ref[row:end, q_at : q_at + HD], qkv_ref[:end, k_at : k_at + HD], row, length
            )
            mixed = dot(shares.astype(BF), qkv_ref[:end, v_at : v_at + HD], (1,), (0,))
            mixed_ref[row:end, q_at : q_at + HD] = mixed.astype(BF)
        out_vmem[row:end, :] = dot(mixed_ref[row:end, :], out_w, (1,), (1,)).astype(BF)
        give(i).start()
    run_all(phases[max(1, len(blocks) - 1) :])
    for i in range(len(blocks)):
        keep(i).wait()
        give(i).wait()


def attend_back_kernel(heads, transfers, *refs):
    refs = list(refs)

    def take(count):
        taken = refs[:count]
        del refs[:count]
        return taken

    length_ref, datt_ref, w_ref, qkv_ref, cos_ref, sin_ref = take(6)
    sent = take(len(transfers.inputs))
    turned_ref, sums_ref, out_ref = take(3)
    landed = take(transfers.moves)
    rows_vmem, out_vmem, grad_vmem, key_acc, value_acc, in_sem, out_sem = take(7)
    phases = transfers.begin(sent, landed, refs)
    run_all(phases[:1])
    seq_len, width = datt_ref.shape
    groups, depth, columns = w_ref.shape
    span = heads * HD
    length = length_ref[0]
    scale = HD ** (-0.5)
    blocks = [pl.ds(row, QB) for row in range(0, seq_len, QB)]

    def fetch(i):
        return pltpu.make_async_copy(datt_ref.at[blocks[i]], rows_vmem.at[blocks[i]], in_sem.at[i])

    def give(i):
        return pltpu.make_async_copy(out_vmem.at[blocks[i]], out_ref.at[blocks[i]], out_sem.at[i])

    for i in range(len(blocks)):
        fetch(i).start()
    weights = w_ref[...].reshape(groups * depth, columns)
    qkv_w, out_w = weights[:, : 3 * span], weights[:, 3 * span :]
    key_acc[...] = jnp.zeros_like(key_acc)
    value_acc[...] = jnp.zeros_like(value_acc)
    query_sums = [jnp.zeros((1, HD), F32) for _ in range(heads)]
    for i in range(len(blocks)):
        row, end = i * QB, (i + 1) * QB
        fetch(i).wait()
        grad_vmem[row:end, :] = dot(rows_vmem[row:end, :], out_w, (1,), (0,)).astype(BF)
        for head in range(heads):
            q_at, k_at, v_at = (head * HD, span + head * HD, 2 * span + head * HD)
            query = qkv_ref[row:end, q_at : q_at + HD]
            keys = qkv_ref[:end, k_at : k_at + HD]
            grad = grad_vmem[row:end, q_at : q_at + HD]
            shares = block_weights(query, keys, row, length)
            grad_shares = dot(grad, qkv_ref[:end, v_at : v_at + HD], (1,), (1,))
            inner = jnp.sum(shares * grad_shares, axis=1, keepdims=True)
            grad_scores = (scale * shares * (grad_shares - inner)).astype(BF)
            turned = dot(grad_scores, keys, (1,), (0,))
            grad_query = (
                turned * cos_ref[row:end, :] - swap_halves(turned) * sin_ref[row:end, :]
            ).astype(BF)
            turned_ref[row:end, q_at : q_at + HD] = grad_query
            query_sums[head] += jnp.sum(grad_query.astype(F32), axis=0, keepdims=True)
            key_acc[:end, q_at : q_at + HD] += dot(grad_scores, query, (0,), (0,))
            value_acc[:end, q_at : q_at + HD] += dot(shares.astype(BF), grad, (0,), (0,))
    key_sums = [jnp.zeros((1, HD), F32) for _ in range(heads)]
    value_sums = [jnp.zeros((1, HD), F32) for _ in range(heads)]
    for i in range(len(blocks)):
        row, end = i * QB, (i + 1) * QB
        for head in range(heads):
            q_at, k_at, v_at = (head * HD, span + head * HD, 2 * span + head * HD)
            turned = key_acc[row:end, q_at : q_at + HD]
            grad_key = (
                turned * cos_ref[row:end, :] - swap_halves(turned) * sin_ref[row:end, :]
            ).astype(BF)
            grad_value = value_acc[row:end, q_at : q_at + HD].astype(BF)
            turned_ref[row:end, k_at : k_at + HD] = grad_key
            turned_ref[row:end, v_at : v_at + HD] = grad_value
            key_sums[head] += jnp.sum(grad_key.astype(F32), axis=0, keepdims=True)
            value_sums[head] += jnp.sum(grad_value.astype(F32), axis=0, keepdims=True)
        out_vmem[row:end, :] = dot(turned_ref[row:end, :], qkv_w, (1,), (1,)).astype(BF)
        give(i).start()
    for at, sums in enumerate(query_sums + key_sums + value_sums):
        sums_ref[:, at * HD : (at + 1) * HD] = sums
    for i in range(len(blocks)):
        give(i).wait()
    run_all(phases[1:])


def in_vmem(count):
    return [pl.BlockSpec(memory_space=pltpu.VMEM)] * count


def attend(length, rows, gain, weights, bias, cosine, sine, transfers):
    seq_len, width = rows.shape
    span = weights.shape[2] // 4
    heads, blocks = span // HD, seq_len // QB
    anywhere = pl.BlockSpec(memory_space=pl.ANY)
    results = pl.pallas_call(
        functools.partial(attend_kernel, heads, transfers),
        out_shape=tuple(
            [
                jax.ShapeDtypeStruct((seq_len, width), BF),
                jax.ShapeDtypeStruct((seq_len, 3 * span), BF),
                jax.ShapeDtypeStruct((seq_len, span), BF),
                jax.ShapeDtypeStruct((seq_len, width), BF),
            ]
            + transfers.shapes
        ),
        in_specs=[pl.BlockSpec(memory_space=pltpu.SMEM), anywhere] + in_vmem(5) + transfers.in_specs,
        out_specs=tuple([anywhere] + in_vmem(2) + [anywhere] + transfers.out_specs),
        scratch_shapes=[pltpu.VMEM((seq_len, width), BF)] * 2
        + [DMA((blocks,))] * 3
        + transfers.scratch,
        compiler_params=transfers.params(),
        cost_estimate=pl.CostEstimate(
            flops=8 * seq_len * width * span + 3 * span * seq_len * seq_len,
            bytes_accessed=8 * seq_len * width,
            transcendentals=heads * seq_len * seq_len,
        ),
    )(length, rows, gain, weights, bias, cosine, sine, *transfers.inputs)
    return results[:4], results[4:]


def attend_back(length, rows, weights, qkv, cosine, sine, transfers):
    seq_len, width = rows.shape
    span = weights.shape[2] // 4
    heads, blocks = span // HD, seq_len // QB
    anywhere = pl.BlockSpec(memory_space=pl.ANY)
    results = pl.pallas_call(
        functools.partial(attend_back_kernel, heads, transfers),
        out_shape=tuple(
            [
                jax.ShapeDtypeStruct((seq_len, 3 * span), BF),
                jax.ShapeDtypeStruct((1, 3 * span), F32),
                jax.ShapeDtypeStruct((seq_len, width), BF),
            ]
            + transfers.shapes
        ),
        in_specs=[pl.BlockSpec(memory_space=pltpu.SMEM), anywhere] + in_vmem(4) + transfers.in_specs,
        out_specs=tuple(in_vmem(2) + [anywhere] + transfers.out_specs),
        scratch_shapes=[pltpu.VMEM((seq_len, width), BF)] * 2
        + [pltpu.VMEM((seq_len, span), BF)]
        + [pltpu.VMEM((seq_len, span), F32)] * 2
        + [DMA((blocks,))] * 2
        + transfers.scratch,
        compiler_params=transfers.params(),
        cost_estimate=pl.CostEstimate(
            flops=8 * seq_len * width * span + 8 * span * seq_len * seq_len,
            bytes_accessed=8 * seq_len * width,
            transcendentals=heads * seq_len * seq_len,
        ),
    )(length, rows, weights, qkv, cosine, sine, *transfers.inputs)
    return results[:3], results[3:]


def padded(values, axis):
    size = values.shape[axis]
    more = -size % LANES
    if not more:
        return values
    return jnp.pad(values, [(0, more if i == axis else 0) for i in range(values.ndim)])


def packed(values, kind):
    tile = LANES * (16 if kind == BF else 8)
    values = values.astype(kind)
    return padded_to(values, -(-values.shape[-1] // tile) * tile)


def padded_to(values, size):
    more = size - values.shape[-1]
    return jnp.pad(values, [(0, 0)] * (values.ndim - 1) + [(0, more)])


def local(
    tokens,
    lengths,
    routes,
    norm1_gain,
    w_query,
    w_key,
    w_value,
    b_query,
    b_key,
    b_value,
    w_out,
    norm2_gain,
    router,
    shared_gate_vec,
    shared_gate,
    shared_up,
    shared_down,
    expert_gate,
    expert_up,
    expert_down,
    cotangent,
):
    ranks = lax.axis_size("tensor")
    groups = lax.axis_size("fsdp")
    rank = lax.axis_index("tensor")
    micros, _, rows, width = tokens.shape
    seq_len = rows * ranks
    heads = w_query.shape[1] // HD
    span = heads * HD
    experts = ranks * expert_gate.shape[0]
    shared_units = shared_gate.shape[1]
    expert_units = expert_gate.shape[2]
    cut = expert_units // (2 * LANES) * LANES
    own_first = rank * rows
    local_pos = own_first + jnp.arange(rows, dtype=jnp.int32)

    per_device = norm1_gain.shape[0]
    small = jnp.concatenate(
        [
            norm1_gain,
            norm2_gain,
            shared_gate_vec,
            router.reshape(-1),
            b_query.reshape(-1),
            b_key.reshape(-1),
            b_value.reshape(-1),
        ]
    )
    attn_own = jnp.concatenate([w_query, w_key, w_value, w_out.T], axis=1)
    mesh_size = (ranks, groups)
    rows_a, attn_w, small_all = exchange(
        mesh_size,
        2,
        [
            ("gather", tokens, (0, 0)),
            ("cross_gather", attn_own),
            ("spread", packed(small, BF).reshape(-1, LANES)),
        ],
    )
    small_all = small_all.reshape(groups * ranks, -1)
    gain_one = small_all[:, :per_device].reshape(-1).astype(F32)
    gain_two = small_all[:, per_device : 2 * per_device].reshape(-1).astype(F32)
    gate_vec = small_all[:, 2 * per_device : 3 * per_device].reshape(-1)
    bias_at = per_device * (3 + experts)
    router_full = small_all[:, 3 * per_device : bias_at].reshape(width, experts)
    router_wide = padded_to(jnp.concatenate([router_full, gate_vec[:, None]], axis=1), LANES)
    own_bias = lax.dynamic_index_in_dim(
        small_all.reshape(groups, ranks, -1), rank, 1, False
    )[:, bias_at : small.shape[0]].reshape(groups, 3, heads, HD // groups)
    bias = own_bias.transpose(1, 2, 0, 3).reshape(1, 3 * span).astype(F32)

    def over_fsdp(packed_range):
        return lax.all_gather(packed_range, "fsdp", axis=0)

    low, high = pack(cut, expert_gate, expert_up, expert_down, [small_all])
    weights = [
        over_fsdp(jnp.stack([padded(shared_gate, 1), padded(shared_up, 1), padded(shared_down.T, 1)])),
        over_fsdp(low),
        over_fsdp(high),
    ]

    cosine, sine = rope_tables(seq_len)
    idle = Transfers(mesh_size)
    token_own = [tokens[m, 0] for m in range(micros)]
    grads_own = []
    for m in range(micros):
        inside = (local_pos < lengths[m, 0])[:, None]
        grads_own.append(jnp.where(inside, cotangent[m, 0], jnp.zeros((), BF)))

    def moving(ident, *moves, needed=()):
        return Transfers(mesh_size, ident, moves, needed)

    def attention(m, token_rows, transfers):
        return attend(lengths[m], token_rows, gain_one[None], attn_w, bias, cosine, sine, transfers)

    def second_norm(m, attended):
        hidden = token_own[m].astype(F32) + attended
        unit, inverse = normalize(hidden)
        return hidden, unit, inverse, (unit * gain_two).astype(BF)

    def second_norm_back(m, state, summed):
        grad_hidden, gain_part = norm_back(summed, state[1], state[2], gain_two)
        grad_hidden = grad_hidden + grads_own[m].astype(F32)
        return grad_hidden, grad_hidden.astype(BF), gain_part

    def first_norm_back(m, grad_hidden, summed):
        unit, inverse = normalize(token_own[m].astype(F32))
        grad_inputs, gain_part = norm_back(summed, unit, inverse, gain_one)
        return (grad_inputs + grad_hidden).astype(BF), gain_part

    def finished(m, hidden, moved):
        inside = (local_pos < lengths[m, 0]).astype(F32)[:, None]
        return (inside * (hidden + moved)).astype(BF)

    att_a, (rows_b,) = attention(0, rows_a, moving(3, ("gather", tokens, (1, 0))))
    grad_a, sum_a = exchange(
        mesh_size, 4, [("gather", cotangent, (0, 0)), ("scatter", att_a[3])]
    )
    norm_a = second_norm(0, sum_a)
    att_b, (two_a,) = attention(1, rows_b, moving(5, ("gather", norm_a[3])))

    def over_groups(grads):
        flat = grads.reshape(-1, grads.shape[-1])
        summed = lax.psum_scatter(flat, "fsdp", scatter_dimension=0, tiled=True)
        return with_layout_constraint(summed, Layout((0, 1))).reshape(grads.shape[1:])

    def grads_of(which, transfers, at=()):
        per_micro = []
        for key in range(micros):
            rows_two, grads = ((two_a, grad_a), (two_b, grad_b))[key]
            scaled, gate, up = act[which, key]
            more = [(acc_a, acc_b)[key][2]] if which == 2 else []
            per_micro.append([rows_two, grads, gate, up, scaled] + more)
        return ffn_grads(groups, per_micro, transfers, at)

    act = {}
    part = functools.partial(ffn, experts)
    single = ((0, 0), (1, 0), (2, 0), (3, 0))
    act[0, 0], acc_a, (grad_b, sum_b) = part(
        "first", two_a, grad_a, routes[0, 0], weights[0], [lengths[0]], router_wide,
        moving(6, ("gather", cotangent, (1, 0)), ("scatter", att_b[3])), ((0, 0), (1, 1), (3, 0)),
    )
    acc_a, route_a = acc_a[:3], acc_a[3]
    norm_b = second_norm(1, sum_b)
    act[1, 0], acc_a, (two_b,) = part(
        "next", two_a, grad_a, route_a, weights[1], acc_a, None,
        moving(7, ("gather", norm_b[3])), single,
    )
    act[0, 1], acc_b, _ = part(
        "first", two_b, grad_b, routes[1, 0], weights[0], [lengths[1]], router_wide, idle
    )
    acc_b, route_b = acc_b[:3], acc_b[3]
    (grads_0,), _ = grads_of(0, idle)
    range_0 = over_groups(grads_0)
    act[2, 0], acc_a, _ = part(
        "last", two_a, grad_a, route_a, weights[2], acc_a, router_wide, moving(0, needed=[grads_0])
    )
    act[1, 1], acc_b, (down_a,) = part(
        "next", two_b, grad_b, route_b, weights[1], acc_b, None,
        moving(8, ("scatter", acc_a[1])), single,
    )
    hid_a, send_a, gain_part_a = second_norm_back(0, norm_a, down_a)
    (grads_1,), (datt_a,) = grads_of(
        1, moving(9, ("gather", send_a)), ((0, 0), (1, 0), (2, 0), (3, 0))
    )
    range_1 = over_groups(grads_1)
    (grad_qkv_a, sums_a, first_a), _ = attend_back(
        lengths[0], datt_a, attn_w, att_a[1], cosine, sine, moving(0, needed=[grads_1])
    )
    act[2, 1], acc_b, (one_a,) = part(
        "last", two_b, grad_b, route_b, weights[2], acc_b, router_wide,
        moving(10, ("scatter", first_a)), single,
    )
    (grads_2, total_wide), (down_b,) = grads_of(
        2, moving(11, ("scatter", acc_b[1]), needed=[range_0]), ((0, 0), (1, 1), (2, 1), (3, 1))
    )
    range_2 = over_groups(grads_2)
    hid_b, send_b, gain_part_b = second_norm_back(1, norm_b, down_b)
    datt_b, moved_a = exchange(mesh_size, 12, [("gather", send_b), ("scatter", acc_a[0])])
    (grad_qkv_b, sums_b, first_b), _ = attend_back(
        lengths[1], datt_b, attn_w, att_b[1], cosine, sine, idle
    )
    attn_parts, (one_b,) = attention_grads(
        groups,
        [
            (att_a[0], datt_a, grad_qkv_a, att_a[2]),
            (att_b[0], datt_b, grad_qkv_b, att_b[2]),
        ],
        moving(13, ("scatter", first_b), needed=[range_1]),
    )

    grad_in_a, one_part_a = first_norm_back(0, hid_a, one_a)
    grad_in_b, one_part_b = first_norm_back(1, hid_b, one_b)

    devices = groups * ranks
    bias_part = (sums_a + sums_b).reshape(3, heads, groups, HD // groups).transpose(2, 0, 1, 3)
    bias_part = bias_part.reshape(groups, 1, -1)
    own_rank = (jnp.arange(ranks, dtype=jnp.int32) == rank).astype(F32)[None, :, None]
    parts = jnp.concatenate(
        [
            (one_part_a + one_part_b).reshape(devices, -1),
            (gain_part_a + gain_part_b).reshape(devices, -1),
            total_wide[:, : experts + 1].reshape(devices, -1),
            (bias_part * own_rank).reshape(devices, -1),
        ],
        axis=1,
    )
    moved_b, attn_g, shares = exchange(
        mesh_size,
        14,
        [
            ("scatter", acc_b[0]),
            ("cross_scatter", attn_parts),
            ("share", packed(parts, F32).reshape(devices, -1, LANES)),
        ],
        [range_2],
    )
    shares = shares.reshape(-1)
    wide_g = shares[2 * per_device : (3 + experts) * per_device].reshape(per_device, experts + 1)
    bias_g = shares[bias_at : parts.shape[1]].reshape(3, heads, HD // groups)

    shared_g = unpack([range_0], shared_units, (True, True, True))
    expert_g = unpack([range_1, range_2], expert_units, (False, False, True))
    return (
        jnp.stack([finished(0, norm_a[0], moved_a), finished(1, norm_b[0], moved_b)])[:, None],
        jnp.stack([grad_in_a, grad_in_b])[:, None],
        shares[:per_device],
        attn_g[:, :span],
        attn_g[:, span : 2 * span],
        attn_g[:, 2 * span : 3 * span],
        bias_g[0],
        bias_g[1],
        bias_g[2],
        attn_g[:, 3 * span :].T,
        shares[per_device : 2 * per_device],
        wide_g[:, :experts],
        wide_g[:, experts],
        shared_g[0].T,
        shared_g[1].T,
        shared_g[2],
        expert_g[0][None],
        expert_g[1][None],
        expert_g[2][None],
    )


def solution(mesh):
    in_specs = (
        P(None, "fsdp", "tensor", None),
        P(None, "fsdp"),
        P(None, "fsdp", None, None),
        P(("fsdp", "tensor")),
        P("fsdp", "tensor"),
        P("fsdp", "tensor"),
        P("fsdp", "tensor"),
        P("tensor", "fsdp"),
        P("tensor", "fsdp"),
        P("tensor", "fsdp"),
        P("tensor", "fsdp"),
        P(("fsdp", "tensor")),
        P(("fsdp", "tensor"), None),
        P(("fsdp", "tensor")),
        P("fsdp", "tensor"),
        P("fsdp", "tensor"),
        P("tensor", "fsdp"),
        P("tensor", "fsdp", None),
        P("tensor", "fsdp", None),
        P("tensor", None, "fsdp"),
        P(None, "fsdp", "tensor", None),
    )
    out_specs = (
        P(None, "fsdp", "tensor", None),
        P(None, "fsdp", "tensor", None),
        P(("fsdp", "tensor")),
        P("fsdp", "tensor"),
        P("fsdp", "tensor"),
        P("fsdp", "tensor"),
        P("tensor", "fsdp"),
        P("tensor", "fsdp"),
        P("tensor", "fsdp"),
        P("tensor", "fsdp"),
        P(("fsdp", "tensor")),
        P(("fsdp", "tensor"), None),
        P(("fsdp", "tensor")),
        P("fsdp", "tensor"),
        P("fsdp", "tensor"),
        P("tensor", "fsdp"),
        P("tensor", "fsdp", None),
        P("tensor", "fsdp", None),
        P("tensor", None, "fsdp"),
    )
    return jax.shard_map(local, mesh=mesh, in_specs=in_specs, out_specs=out_specs, check_vma=False)
```

```python
import functools

import jax
import jax.numpy as jnp
import numpy as np
from jax import lax
from jax.experimental import pallas as pl
from jax.experimental.layout import Layout, with_layout_constraint
from jax.experimental.pallas import tpu as pltpu
from jax.sharding import PartitionSpec as P

HD = 128
EPSILON = 1e-06
ROPE_BASE = 1000000.0
BF = jnp.bfloat16
F32 = jnp.float32
MESH = pl.DeviceIdType.MESH
QB = 256
LANES = 128
CHUNKS = 2
STRIP = 16
ROW_BLOCK = 256
VMEM_BYTES = 60 << 20


def dot(left, right, left_dims, right_dims):
    return lax.dot_general(
        left, right, ((left_dims, right_dims), ((), ())), preferred_element_type=F32
    )


def normalize(values):
    inverse = lax.rsqrt(jnp.mean(values * values, axis=-1, keepdims=True) + EPSILON)
    return (values * inverse, inverse)


def norm_back(grad_normed, unit, inverse, gain):
    grad_unit = grad_normed * gain
    grad_values = inverse * (grad_unit - unit * jnp.mean(grad_unit * unit, axis=-1, keepdims=True))
    return (grad_values, jnp.sum(grad_normed * unit, axis=0))


def remote(src, dst, sems, at, target):
    return pltpu.make_async_remote_copy(
        src_ref=src,
        dst_ref=dst,
        send_sem=sems[0].at[at],
        recv_sem=sems[1].at[at],
        device_id={"tensor": target},
        device_id_type=MESH,
    )


def gather_scratch(ranks):
    chips = ranks // 2
    pair = [pltpu.SemaphoreType.DMA((chips, CHUNKS))] * 2
    cross = [pltpu.SemaphoreType.DMA((2 * chips, CHUNKS))] * 2
    return [pltpu.SemaphoreType.DMA] + pair + pair + cross


def gather_steps(place, block, whole, local_sem, up_s, up_r, down_s, down_r, cross_s, cross_r):
    chips, chip, core = place.chips, place.chip, place.core
    rows = block.shape[0]
    part = rows // CHUNKS
    up, down, cross = (up_s, up_r), (down_s, down_r), (cross_s, cross_r)

    def at(owner, chunk):
        first = pl.multiple_of((2 * owner + core) * rows + chunk * part, part)
        return whole.at[pl.ds(first, part)]

    def theirs(owner, chunk):
        first = pl.multiple_of((2 * owner + 1 - core) * rows + chunk * part, part)
        return whole.at[pl.ds(first, part)]

    def own(chunk):
        return block.at[pl.ds(chunk * part, part)]

    def upward(step, chunk):
        source = own(chunk) if step == 0 else at(chip - step, chunk)
        return remote(source, at(chip - step, chunk), up, (step, chunk), place.above)

    def downward(step, chunk):
        source = own(chunk) if step == 0 else at(chip + step, chunk)
        return remote(source, at(chip + step, chunk), down, (step, chunk), place.below)

    def across(slot, owner, chunk):
        source = own(chunk) if slot == 0 else at(owner, chunk)
        return remote(source, at(owner, chunk), cross, (slot, chunk), place.partner)

    def arrived(slot, owner, chunk):
        return remote(theirs(owner, chunk), theirs(owner, chunk), cross, (slot, chunk), place.partner)

    def arrived_up(step, chunk):
        return remote(at(chip - step, chunk), at(chip - step, chunk), up, (step - 1, chunk), place.above)

    def arrived_down(step, chunk):
        return remote(at(chip + step, chunk), at(chip + step, chunk), down, (step - 1, chunk), place.below)

    both = range(CHUNKS)

    def mine():
        first = pl.multiple_of((2 * chip + core) * rows, rows)
        return pltpu.make_async_copy(block, whole.at[pl.ds(first, rows)], local_sem)

    def begin():
        for chunk in both:
            pl.when(place.not_top)(lambda: upward(0, chunk).start())
            pl.when(place.not_bottom)(lambda: downward(0, chunk).start())
        for chunk in both:
            across(0, chip, chunk).start()
        mine().start()

    def hop(step, chunk):
        @pl.when(chip >= step)
        def _():
            arrived_up(step, chunk).wait_recv()
            pl.when(place.not_top)(lambda: upward(step, chunk).start())
            across(2 * step - 1, chip - step, chunk).start()

        @pl.when(chip < chips - step)
        def _():
            arrived_down(step, chunk).wait_recv()
            pl.when(place.not_bottom)(lambda: downward(step, chunk).start())
            across(2 * step, chip + step, chunk).start()

    def end():
        mine().wait()
        for step in range(chips):
            for chunk in both:
                if step == 0:
                    arrived(0, chip, chunk).wait_recv()
                    across(0, chip, chunk).wait_send()
                else:

                    @pl.when(chip >= step)
                    def _():
                        arrived(2 * step - 1, chip - step, chunk).wait_recv()
                        across(2 * step - 1, chip - step, chunk).wait_send()

                    @pl.when(chip < chips - step)
                    def _():
                        arrived(2 * step, chip + step, chunk).wait_recv()
                        across(2 * step, chip + step, chunk).wait_send()

                @pl.when(place.not_top & (chip >= step))
                def _():
                    upward(step, chunk).wait_send()

                @pl.when(place.not_bottom & (chip < chips - step))
                def _():
                    downward(step, chunk).wait_send()

    hops = [functools.partial(hop, step, chunk) for step in range(1, chips) for chunk in both]
    return [begin] + hops + [end]


def scatter_scratch(ranks, rows, width):
    chips = ranks // 2
    line = [pltpu.SemaphoreType.DMA((chips, CHUNKS))] * 2
    buffers = [pltpu.VMEM((chips, rows, width), BF)] * 5
    return buffers + [pltpu.SemaphoreType.DMA((chips,))] + line * 3


def scatter_steps(
    place, partial, total, kept, pair, held, up_in, down_in, keep_sem,
    up_s, up_r, down_s, down_r, cross_s, cross_r,
):
    chips, chip, core = place.chips, place.chip, place.core
    rows = total.shape[0]
    part = rows // CHUNKS
    up, down, cross = (up_s, up_r), (down_s, down_r), (cross_s, cross_r)
    both = range(CHUNKS)

    def keep(k):
        first = pl.multiple_of((2 * k + core) * rows, rows)
        return pltpu.make_async_copy(partial.at[pl.ds(first, rows)], kept.at[k], keep_sem.at[k])

    def across(k, chunk):
        first = pl.multiple_of((2 * k + 1 - core) * rows + chunk * part, part)
        return remote(
            partial.at[pl.ds(first, part)],
            pair.at[k, pl.ds(chunk * part, part)],
            cross,
            (k, chunk),
            place.partner,
        )

    def upward(step, k, chunk):
        cut = pl.ds(chunk * part, part)
        return remote(held.at[k, cut], up_in.at[step, cut], up, (step, chunk), place.above)

    def downward(step, k, chunk):
        cut = pl.ds(chunk * part, part)
        return remote(held.at[k, cut], down_in.at[step, cut], down, (step, chunk), place.below)

    def add(k, chunk, target, others):
        def strip(i, carry):
            cut = pl.ds(chunk * part + i * STRIP, STRIP)
            value = kept[k, cut].astype(F32) + pair[k, cut].astype(F32)
            for ref, slot in others:
                value = value + ref[slot, cut].astype(F32)
            if target is None:
                total[cut] = value
            else:
                target[k, cut] = value.astype(BF)
            return carry

        lax.fori_loop(0, part // STRIP, strip, 0)

    order = []
    for i in range(chips):
        for k in (chips - 1 - i, i):
            if k not in order:
                order.append(k)
    def begin():
        for k in order:
            keep(k).start()
            for chunk in both:
                across(k, chunk).start()

    def hop(step, chunk):
        @pl.when(place.not_top & (chip <= step - 1))
        def _():
            k = chip + chips - step
            if chunk == 0:
                keep(k).wait()
            across(k, chunk).wait_recv()

            @pl.when(place.not_bottom)
            def _():
                upward(step - 1, k, chunk).wait_recv()
                add(k, chunk, held, [(up_in, step - 1)])

            pl.when(jnp.logical_not(place.not_bottom))(lambda: add(k, chunk, held, []))
            upward(step, k, chunk).start()

        @pl.when(place.not_bottom & (chip >= chips - step))
        def _():
            k = chip - (chips - step)
            if chunk == 0:
                keep(k).wait()
            across(k, chunk).wait_recv()

            @pl.when(place.not_top)
            def _():
                downward(step - 1, k, chunk).wait_recv()
                add(k, chunk, held, [(down_in, step - 1)])

            pl.when(jnp.logical_not(place.not_top))(lambda: add(k, chunk, held, []))
            downward(step, k, chunk).start()

    last = chips - 1

    def add_last(chunk):
        if chunk == 0:
            keep(chip).wait()
        across(chip, chunk).wait_recv()

        @pl.when(place.not_top & place.not_bottom)
        def _():
            upward(last, chip, chunk).wait_recv()
            downward(last, chip, chunk).wait_recv()
            add(chip, chunk, None, [(up_in, last), (down_in, last)])

        @pl.when(jnp.logical_not(place.not_top))
        def _():
            upward(last, chip, chunk).wait_recv()
            add(chip, chunk, None, [(up_in, last)])

        @pl.when(jnp.logical_not(place.not_bottom))
        def _():
            downward(last, chip, chunk).wait_recv()
            add(chip, chunk, None, [(down_in, last)])

    def end():
        for chunk in both:
            for k in range(chips):
                across(k, chunk).wait_send()
            for step in range(1, chips):

                @pl.when(place.not_top & (chip <= step - 1))
                def _():
                    upward(step, chip + chips - step, chunk).wait_send()

                @pl.when(place.not_bottom & (chip >= chips - step))
                def _():
                    downward(step, chip - (chips - step), chunk).wait_send()

    def first():
        begin()
        for chunk in both:
            hop(1, chunk)

    hops = [functools.partial(hop, step, chunk) for step in range(2, chips) for chunk in both]
    return [first] + hops + [functools.partial(add_last, chunk) for chunk in both] + [end]


class Place:
    def __init__(self, ranks, groups):
        rank, group = lax.axis_index("tensor"), lax.axis_index("fsdp")
        self.ranks, self.groups = ranks, groups
        self.chips = ranks // 2
        self.chip, self.core = rank // 2, rank % 2
        self.partner = rank + 1 - 2 * self.core
        self.above, self.below = rank + 2, rank - 2
        self.not_top = self.chip < self.chips - 1
        self.not_bottom = self.chip > 0
        self.rank, self.group = rank, group
        self.device = group * ranks + rank
        near, far = group % 2, group // 2
        self.beside = 2 * far + 1 - near
        self.across = 2 * (1 - far) + near
        self.opposite = 2 * (1 - far) + 1 - near
        self.square = groups == 4

    def name(self, device):
        return {"fsdp": device // self.ranks, "tensor": device % self.ranks}

    def meet(self, line, cross, everyone):
        barrier = pltpu.get_barrier_semaphore()

        def greet(name):
            pl.semaphore_signal(barrier, 1, device_id=name, device_id_type=MESH)

        if everyone:
            devices = self.groups * self.ranks

            def one(i, carry):
                greet(self.name(lax.rem(self.device + i, devices)))
                return carry

            lax.fori_loop(1, devices, one, 0)
            pl.semaphore_wait(barrier, devices - 1)
            return
        peers = 0
        if line:
            greet({"tensor": self.partner})
            pl.when(self.not_top)(lambda: greet({"tensor": self.above}))
            pl.when(self.not_bottom)(lambda: greet({"tensor": self.below}))
            peers = 1 + self.not_top.astype(jnp.int32) + self.not_bottom.astype(jnp.int32)
        if cross and self.square:
            greet({"fsdp": self.beside})
            greet({"fsdp": self.across})
            peers = peers + 2
        elif cross:
            for i in range(1, self.groups):
                greet({"fsdp": lax.rem(self.group + i, self.groups)})
            peers = peers + self.groups - 1
        pl.semaphore_wait(barrier, peers)


def to_group(src, dst, send, recv, at, target):
    return pltpu.make_async_remote_copy(
        src_ref=src,
        dst_ref=dst,
        send_sem=send.at[at],
        recv_sem=recv.at[at],
        device_id={"fsdp": target},
        device_id_type=MESH,
    )


def cross_gather_steps(place, block, whole, own_sem, send, recv):
    group = place.group
    half = block.shape[0] // 2

    def own():
        return pltpu.make_async_copy(block, whole.at[group], own_sem)

    if not place.square:

        def direct(i):
            target = lax.rem(group + i, place.groups)
            return to_group(block, whole.at[group], send, recv, i - 1, target)

        def begin_direct():
            own().start()
            for i in range(1, place.groups):
                direct(i).start()

        def end_direct():
            own().wait()
            for i in range(1, place.groups):
                source = lax.rem(group - i + place.groups, place.groups)
                to_group(block, whole.at[source], send, recv, i - 1, source).wait_recv()
                direct(i).wait_send()

        return [begin_direct, end_direct]

    def near(at):
        return to_group(block, whole.at[group], send, recv, at, (place.beside, place.across)[at])

    def came(at):
        source = (place.beside, place.across)[at]
        return to_group(whole.at[source], whole.at[source], send, recv, at, source)

    def forward(at):
        source, target = ((place.beside, place.across), (place.across, place.beside))[at]
        piece = whole.at[source, pl.ds(at * half, half)]
        return to_group(piece, piece, send, recv, 2 + at, target)

    def far(at):
        piece = whole.at[place.opposite, pl.ds(at * half, half)]
        return to_group(piece, piece, send, recv, 2 + at, place.opposite)

    def begin():
        for at in range(2):
            near(at).start()
        own().start()

    def pass_on():
        for at in range(2):
            came(at).wait_recv()
            forward(at).start()

    def end():
        own().wait()
        for at in range(2):
            far(at).wait_recv()
            near(at).wait_send()
            forward(at).wait_send()

    return [begin] + [nothing] * 5 + [pass_on, end]


def cross_scatter_steps(place, partial, total, mine, near_in, far_in, own_sem, send, recv):
    group = place.group
    rows = total.shape[0]
    half = rows // 2

    def own():
        return pltpu.make_async_copy(partial, mine, own_sem)

    def loop(count, body):
        def strip(i, carry):
            body(pl.ds(i * STRIP, STRIP))
            return carry

        lax.fori_loop(0, count // STRIP, strip, 0)

    if not place.square:

        def direct(i):
            target = lax.rem(group + i, place.groups)
            return to_group(partial.at[target], near_in.at[group], send, recv, i - 1, target)

        def begin_direct():
            own().start()
            for i in range(1, place.groups):
                direct(i).start()

        def sum_direct(cut):
            value = mine[group, cut].astype(F32)
            for i in range(1, place.groups):
                value = value + near_in[lax.rem(group + i, place.groups), cut].astype(F32)
            total[cut] = value

        def end_direct():
            own().wait()
            for i in range(1, place.groups):
                source = lax.rem(group - i + place.groups, place.groups)
                piece = partial.at[source]
                to_group(piece, near_in.at[source], send, recv, i - 1, source).wait_recv()
            loop(rows, sum_direct)
            for i in range(1, place.groups):
                direct(i).wait_send()

        return [begin_direct, end_direct]

    def first(at):
        target = (place.beside, place.across)[at]
        piece = partial.at[place.opposite, pl.ds(at * half, half)]
        return to_group(piece, far_in.at[at], send, recv, at, target)

    def second(at):
        target = (place.beside, place.across)[at]
        return to_group(mine.at[target], near_in.at[at], send, recv, 2 + at, target)

    def begin():
        own().start()
        for at in range(2):
            first(at).start()

    def join():
        own().wait()
        for at in range(2):
            target = (place.across, place.beside)[at]
            first(at).wait_recv()

            def one(cut, at=at, target=target):
                place_in = pl.ds(at * half + cut.start, STRIP)
                value = mine[target, place_in].astype(F32) + far_in[at, cut].astype(F32)
                mine[target, place_in] = value.astype(BF)

            loop(half, one)
            second(1 - at).start()

    def everything(cut):
        value = mine[group, cut].astype(F32) + near_in[0, cut].astype(F32)
        total[cut] = value + near_in[1, cut].astype(F32)

    def end():
        for at in range(2):
            second(at).wait_recv()
        loop(rows, everything)
        for at in range(2):
            first(at).wait_send()
            second(at).wait_send()

    return [begin, nothing, join, nothing, nothing, end]


def everyone_steps(place, piece_for, landing, own_sem, send, recv):
    devices = place.groups * place.ranks
    me = place.device

    def copy(i):
        target = lax.rem(me + i, devices)
        return pltpu.make_async_remote_copy(
            src_ref=piece_for(target),
            dst_ref=landing.at[me],
            send_sem=send.at[i],
            recv_sem=recv.at[i],
            device_id=place.name(target),
            device_id_type=MESH,
        )

    def arrival(i):
        source = lax.rem(me - i + devices, devices)
        return pltpu.make_async_remote_copy(
            src_ref=landing.at[source],
            dst_ref=landing.at[source],
            send_sem=send.at[i],
            recv_sem=recv.at[i],
            device_id=place.name(source),
            device_id_type=MESH,
        )

    def start(i, carry):
        copy(i).start()
        return carry

    def finish_one(i, carry):
        arrival(i).wait_recv()
        copy(i).wait_send()
        return carry

    def own():
        return pltpu.make_async_copy(piece_for(me), landing.at[me], own_sem)

    def begin():
        own().start()
        lax.fori_loop(1, devices, start, 0)

    def end():
        own().wait()
        lax.fori_loop(1, devices, finish_one, 0)

    return [begin, nothing, end]


def spread_steps(place, value, everyone, own_sem, send, recv):
    return everyone_steps(place, lambda target: value, everyone, own_sem, send, recv)


def share_steps(place, values, total, landing, own_sem, send, recv):
    phases = everyone_steps(place, lambda target: values.at[target], landing, own_sem, send, recv)

    def add_up():
        total[...] = jnp.sum(landing[...], axis=0)

    return phases + [add_up]


DMA = pltpu.SemaphoreType.DMA


class Transfers:
    def __init__(self, mesh_size, ident=0, moves=(), needed=()):
        self.ranks, self.groups = mesh_size
        self.ident = ident
        self.kinds = [move[0] for move in moves]
        self.parts = [move[2] if len(move) > 2 else None for move in moves]
        self.inputs = [move[1] for move in moves] + list(needed)
        self.moves = len(self.kinds)
        anywhere = pl.BlockSpec(memory_space=pl.ANY)
        vmem = pl.BlockSpec(memory_space=pltpu.VMEM)
        self.in_specs = [anywhere] * len(self.inputs)
        self.shapes, self.out_specs, self.scratch, self.counts = [], [], [], []
        for kind, array, *part in moves:
            shape, spec = array.shape[len(part[0]) :] if part else array.shape, anywhere
            if kind == "gather":
                shape, dtype = (self.ranks * shape[0], shape[1]), BF
                scratch = gather_scratch(self.ranks)
            elif kind == "scatter":
                shape, dtype, spec = (shape[0] // self.ranks, shape[1]), F32, vmem
                scratch = scatter_scratch(self.ranks, *shape)
            elif kind == "cross_gather":
                shape, dtype = (self.groups,) + shape, BF
                scratch = [DMA, DMA((max(4, self.groups),)), DMA((max(4, self.groups),))]
            elif kind == "cross_scatter":
                rest = shape[1:]
                square = self.groups == 4
                near = (2 if square else self.groups,) + rest
                scratch = [
                    pltpu.VMEM(shape, BF),
                    pltpu.VMEM(near, BF),
                    pltpu.VMEM((2, rest[0] // 2) + rest[1:], BF),
                    DMA,
                    DMA((max(4, self.groups),)),
                    DMA((max(4, self.groups),)),
                ]
                shape, dtype, spec = rest, F32, vmem
            elif kind == "share":
                devices = self.ranks * self.groups
                scratch = [pltpu.VMEM(shape, F32), DMA, DMA((devices,)), DMA((devices,))]
                shape, dtype, spec = shape[1:], F32, vmem
            else:
                devices = self.ranks * self.groups
                shape, dtype = (devices,) + shape, array.dtype
                scratch = [DMA, DMA((devices,)), DMA((devices,))]
            self.shapes.append(jax.ShapeDtypeStruct(shape, dtype))
            self.out_specs.append(spec)
            self.scratch += scratch
            self.counts.append(len(scratch))

    def params(self):
        if not self.moves:
            return pltpu.CompilerParams(vmem_limit_bytes=VMEM_BYTES)
        return pltpu.CompilerParams(
            collective_id=self.ident, has_side_effects=True, vmem_limit_bytes=VMEM_BYTES
        )

    def begin(self, inputs, outputs, scratch):
        if not self.moves:
            return []
        steps_of = {
            "gather": gather_steps,
            "scatter": scatter_steps,
            "cross_gather": cross_gather_steps,
            "cross_scatter": cross_scatter_steps,
            "spread": spread_steps,
            "share": share_steps,
        }
        place = Place(self.ranks, self.groups)
        scratch = list(scratch)
        lines = []
        for i, kind in enumerate(self.kinds):
            taken, scratch = scratch[: self.counts[i]], scratch[self.counts[i] :]
            given = inputs[i] if self.parts[i] is None else inputs[i].at[self.parts[i]]
            lines.append(steps_of[kind](place, given, outputs[i], *taken))

        def phase(number):
            if number == 0:
                kinds = set(self.kinds)
                place.meet(
                    bool(kinds & {"gather", "scatter"}),
                    bool(kinds & {"cross_gather", "cross_scatter"}),
                    bool(kinds & {"spread", "share"}),
                )
            for steps in lines:
                if number < len(steps):
                    steps[number]()

        return [functools.partial(phase, i) for i in range(max(map(len, lines)))]


def nothing():
    pass


def run_all(phases):
    for phase in phases:
        phase()


def exchange_kernel(transfers, *refs):
    count, moves = len(transfers.inputs), transfers.moves
    run_all(transfers.begin(refs[:moves], refs[count : count + moves], refs[count + moves :]))


def exchange(mesh_size, ident, moves, needed=()):
    transfers = Transfers(mesh_size, ident, moves, needed)
    return pl.pallas_call(
        functools.partial(exchange_kernel, transfers),
        out_shape=tuple(transfers.shapes),
        in_specs=transfers.in_specs,
        out_specs=tuple(transfers.out_specs),
        scratch_shapes=transfers.scratch,
        compiler_params=transfers.params(),
    )(*transfers.inputs)


def beside(phases, at, grid_steps, parts):
    step = pl.program_id(0)
    state = None
    for number, part in enumerate(parts):
        for phase, (when, ahead_of) in zip(phases, at):
            if ahead_of == number:
                pl.when(step == when)(phase)
        state = part(state)
    if phases:
        pl.when(step == grid_steps - 1)(lambda: run_all(phases[len(at) :]))


def column(values, at):
    lanes = lax.broadcasted_iota(jnp.int32, values.shape, 1)
    return jnp.sum(jnp.where(lanes == at, values, 0.0), axis=1, keepdims=True)


def routing(experts, length, first_row, rows, router, routes):
    rank = lax.axis_index("tensor")
    logits = dot(rows, router, (1,), (0,))
    lanes = lax.broadcasted_iota(jnp.int32, logits.shape, 1)
    inside = lanes < experts
    top = jnp.max(jnp.where(inside, logits, -1e30), axis=1, keepdims=True)
    exps = jnp.where(inside, jnp.exp(jnp.where(inside, logits, top) - top), 0.0)
    probs = exps / jnp.sum(exps, axis=1, keepdims=True)
    position = first_row + lax.broadcasted_iota(jnp.int32, (rows.shape[0], 1), 0)
    valid = jnp.where(position < length, 1.0, 0.0)
    gate = valid * jax.nn.sigmoid(column(logits, experts))
    chosen = valid * jnp.max(jnp.where(routes == rank, 1.0, 0.0), axis=1, keepdims=True)
    prob = column(probs, rank)
    out = jnp.where(lanes == experts, gate, probs)
    out = jnp.where(lanes == experts + 1, chosen * prob, out)
    out = jnp.where(lanes == experts + 2, chosen, out)
    return jnp.where(lanes == experts + 3, prob, out)


def routing_back(experts, route, shared_dot, expert_dot):
    rank = lax.axis_index("tensor")
    lanes = lax.broadcasted_iota(jnp.int32, route.shape, 1)
    gate, chosen, prob = [column(route, experts + i) for i in (0, 2, 3)]
    expert_grad = chosen * expert_dot
    logits = route * (jnp.where(lanes == rank, expert_grad, 0.0) - expert_grad * prob)
    gate_logit = shared_dot * gate * (1.0 - gate)
    return jnp.where(lanes < experts, logits, jnp.where(lanes == experts, gate_logit, 0.0))


def ffn_kernel(transfers, at, grid_steps, experts, kind, *refs):
    refs = list(refs)

    def take(count):
        taken = refs[:count]
        del refs[:count]
        return taken

    first, last = kind == "first", kind == "last"
    rows_ref, grad_ref, route_ref, w_ref = take(4)
    before = take(1) if first else take(3)
    router_ref = take(1)[0] if first or last else None
    sent = take(len(transfers.inputs))
    hidden_ref, gate_ref, up_ref, out_ref, back_ref, dots_ref = take(6)
    if first:
        made_ref = take(1)[0]
    landed = take(transfers.moves)
    w_vmem, w_sem = take(2)
    phases = transfers.begin(sent, landed, refs)
    step = pl.program_id(0)

    def weights():
        return pltpu.make_async_copy(w_ref, w_vmem, w_sem)

    pl.when(step == 0)(lambda: weights().start())

    def hidden_part(_):
        pl.when(step == 0)(lambda: weights().wait())
        groups, _, depth, units = w_vmem.shape
        gate_w, up_w, down_w = [w_vmem[:, i].reshape(groups * depth, units) for i in range(3)]
        rows, grad = rows_ref[...], grad_ref[...]
        if first:
            length = before[0][0]
            route = routing(experts, length, step * ROW_BLOCK, rows, router_ref[...], route_ref[...])
            made_ref[...] = route
        else:
            route = route_ref[...]
        scale = column(route, experts if first else experts + 1)
        gate_act = dot(rows, gate_w, (1,), (0,))
        up_act = dot(rows, up_w, (1,), (0,))
        back = dot(grad, down_w, (1,), (0,))
        sigmoid = 1.0 / (1.0 + jnp.exp(-gate_act))
        silu = gate_act * sigmoid
        hidden = (silu * up_act).astype(BF).astype(F32)
        dots = jnp.sum(hidden * back, axis=1, keepdims=True)
        scaled = (scale * hidden).astype(BF)
        hidden_ref[...] = scaled
        grad_hidden = scale * back
        grad_gate = (grad_hidden * up_act * (sigmoid * (1.0 + gate_act * (1.0 - sigmoid)))).astype(BF)
        gate_ref[...] = grad_gate
        grad_up = (grad_hidden * silu).astype(BF)
        up_ref[...] = grad_up
        return gate_w, up_w, down_w, scaled, grad_gate, grad_up, route, dots

    def outer_part(state):
        gate_w, up_w, down_w, scaled, grad_gate, grad_up, route, dots = state
        moved = dot(scaled, down_w, (1,), (1,))
        turned = dot(grad_gate, gate_w, (1,), (1,)) + dot(grad_up, up_w, (1,), (1,))
        lanes = lax.broadcasted_iota(jnp.int32, route.shape, 1)
        if first:
            dots_ref[...] = jnp.where(lanes == 0, dots, 0.0)
        else:
            moved = moved + before[0][...].astype(F32)
            turned = turned + before[1][...].astype(F32)
            earlier = before[2][...]
            if last:
                wide = routing_back(experts, route, column(earlier, 0), column(earlier, 1) + dots)
                wide = wide.astype(BF)
                dots_ref[...] = wide
                turned = turned + dot(wide, router_ref[...], (1,), (1,))
            else:
                dots_ref[...] = earlier + jnp.where(lanes == 1, dots, 0.0)
        out_ref[...] = moved.astype(BF)
        back_ref[...] = turned.astype(BF)

    beside(phases, at, grid_steps, [hidden_part, outer_part])


def ffn(experts, kind, rows, grads, route, weights, before, router, transfers, at=()):
    count, width = rows.shape
    units = weights.shape[3]
    first, last = kind == "first", kind == "last"
    steps = count // ROW_BLOCK

    def block(size):
        return pl.BlockSpec((ROW_BLOCK, size), lambda i: (i, 0))

    given = list(before)
    given_specs = [block(width), block(width), block(LANES)]
    if first:
        given_specs = [pl.BlockSpec(memory_space=pltpu.SMEM)]
    if first or last:
        given.append(router)
        given_specs.append(
            pl.BlockSpec(router.shape, lambda i: (0, 0), pipeline_mode=pl.Buffered(1))
        )
    narrow = [jax.ShapeDtypeStruct((count, units), BF)] * 3
    wide = [jax.ShapeDtypeStruct((count, width), BF)] * 2
    dots = [jax.ShapeDtypeStruct((count, LANES), BF if last else F32)]
    dots += [jax.ShapeDtypeStruct((count, LANES), F32)] * first
    results = pl.pallas_call(
        functools.partial(ffn_kernel, transfers, at, steps, experts, kind),
        grid=(steps,),
        in_specs=[block(width), block(width), block(route.shape[1]), pl.BlockSpec(memory_space=pl.ANY)]
        + given_specs
        + transfers.in_specs,
        out_specs=tuple(
            [block(units)] * 3
            + [block(width)] * 2
            + [block(LANES)] * len(dots)
            + transfers.out_specs
        ),
        out_shape=tuple(narrow + wide + dots + transfers.shapes),
        scratch_shapes=[pltpu.VMEM(weights.shape, BF), DMA] + transfers.scratch,
        compiler_params=transfers.params(),
        cost_estimate=pl.CostEstimate(
            flops=12 * count * width * units,
            bytes_accessed=2 * (3 * width * units + 4 * count * width + 3 * count * units),
            transcendentals=count * units,
        ),
    )(rows, grads, route, weights, *given, *transfers.inputs)
    made = 5 + len(dots)
    return results[:3], results[3:made], results[made:]


def ffn_grads_kernel(transfers, at, grid_steps, micros, last, *refs):
    refs = list(refs)

    def take(count):
        taken = refs[:count]
        del refs[:count]
        return taken

    per_micro = [take(6 if last else 5) for _ in range(micros)]
    sent = take(len(transfers.inputs))
    out_ref = take(1)[0]
    wide_ref = take(1)[0] if last else None
    landed = take(transfers.moves)
    phases = transfers.begin(sent, landed, refs)

    def summed(left, right):
        total = None
        for one in per_micro:
            product = dot(one[left][...], one[right][...], (0,), (0,))
            total = product if total is None else total + product
        return total

    def one_product(which):
        def part(_):
            out_ref[0, which] = summed((0, 0, 1)[which], 2 + which).astype(BF)
            if last and which == 2:
                wide_ref[...] = summed(0, 5)

        return part

    beside(phases, at, grid_steps, [one_product(which) for which in range(3)])


def ffn_grads(groups, per_micro, transfers, at=()):
    count, width = per_micro[0][0].shape
    units = per_micro[0][2].shape[1]
    last = len(per_micro[0]) == 6
    depth = width // groups
    columns = pl.BlockSpec((count, depth), lambda i: (0, i))

    def whole(size):
        return pl.BlockSpec((count, size), lambda i: (0, 0), pipeline_mode=pl.Buffered(1))

    shapes = [jax.ShapeDtypeStruct((groups, 3, depth, units), BF)]
    specs = [pl.BlockSpec((1, 3, depth, units), lambda i: (i, 0, 0, 0))]
    taken = [columns, columns] + [whole(units)] * 3
    if last:
        taken.append(whole(LANES))
        shapes.append(jax.ShapeDtypeStruct((width, LANES), F32))
        specs.append(pl.BlockSpec((depth, LANES), lambda i: (i, 0)))
    results = pl.pallas_call(
        functools.partial(ffn_grads_kernel, transfers, at, groups, len(per_micro), last),
        grid=(groups,),
        in_specs=taken * len(per_micro) + transfers.in_specs,
        out_specs=tuple(specs + transfers.out_specs),
        out_shape=tuple(shapes + transfers.shapes),
        scratch_shapes=transfers.scratch,
        compiler_params=transfers.params(),
        cost_estimate=pl.CostEstimate(
            flops=6 * len(per_micro) * count * width * units,
            bytes_accessed=2 * len(per_micro) * (2 * count * width + 3 * count * units)
            + 6 * width * units,
            transcendentals=0,
        ),
    )(*[array for one in per_micro for array in one], *transfers.inputs)
    return results[: len(shapes)], results[len(shapes) :]


def attention_grads_kernel(transfers, grid_steps, micros, *refs):
    refs = list(refs)

    def take(count):
        taken = refs[:count]
        del refs[:count]
        return taken

    per_micro = [take(4) for _ in range(micros)]
    sent = take(len(transfers.inputs))
    out_ref = take(1)[0]
    landed = take(transfers.moves)
    phases = transfers.begin(sent, landed, refs)

    def work(_):
        span = per_micro[0][2].shape[1]
        totals = [None, None]
        for one in per_micro:
            for which in range(2):
                product = dot(one[which][...], one[2 + which][...], (0,), (0,))
                totals[which] = product if totals[which] is None else totals[which] + product
        out_ref[0, :, :span] = totals[0].astype(BF)
        out_ref[0, :, span:] = totals[1].astype(BF)

    beside(phases, [(0, 0)], grid_steps, [work])


def attention_grads(groups, per_micro, transfers):
    count, width = per_micro[0][0].shape
    depth = width // groups
    spans = [per_micro[0][i].shape[1] for i in (2, 3)]
    columns = pl.BlockSpec((count, depth), lambda i: (0, i))
    whole = [
        pl.BlockSpec((count, size), lambda i: (0, 0), pipeline_mode=pl.Buffered(1)) for size in spans
    ]
    results = pl.pallas_call(
        functools.partial(attention_grads_kernel, transfers, groups, len(per_micro)),
        grid=(groups,),
        in_specs=([columns, columns] + whole) * len(per_micro) + transfers.in_specs,
        out_specs=tuple(
            [pl.BlockSpec((1, depth, sum(spans)), lambda i: (i, 0, 0))] + transfers.out_specs
        ),
        out_shape=tuple(
            [jax.ShapeDtypeStruct((groups, depth, sum(spans)), BF)] + transfers.shapes
        ),
        scratch_shapes=transfers.scratch,
        compiler_params=transfers.params(),
        cost_estimate=pl.CostEstimate(
            flops=2 * len(per_micro) * count * width * sum(spans),
            bytes_accessed=8 * len(per_micro) * count * width,
            transcendentals=0,
        ),
    )(*[array for one in per_micro for array in one], *transfers.inputs)
    return results[0], results[1:]


def opening_kernel(transfers, cut, *refs):
    refs = list(refs)

    def take(count):
        taken = refs[:count]
        del refs[:count]
        return taken

    sent, given = take(len(transfers.inputs)), take(6)
    landed, made = take(transfers.moves), take(3)
    held, packed_refs, in_sem, out_sem = take(6), take(3), take(1)[0], take(1)[0]
    phases = transfers.begin(sent, landed, refs)
    fetches = [
        pltpu.make_async_copy(source, target, in_sem.at[at])
        for at, (source, target) in enumerate(zip(given, held))
    ]
    gives = [
        pltpu.make_async_copy(source, target, out_sem.at[at])
        for at, (source, target) in enumerate(zip(packed_refs, made))
    ]
    for fetch in fetches:
        fetch.start()
    run_all(phases[:1])
    for fetch in fetches[:3]:
        fetch.wait()
    units = held[0].shape[0]
    packed_refs[0][...] = jnp.zeros_like(packed_refs[0])
    for which in range(3):
        packed_refs[0][which, :, :units] = held[which][...].T
    gives[0].start()
    for fetch in fetches[3:]:
        fetch.wait()
    for at, part in ((1, slice(0, cut)), (2, slice(cut, None))):
        packed_refs[at][0] = held[3][0, :, part]
        packed_refs[at][1] = held[4][0, :, part]
        packed_refs[at][2] = held[5][0, part, :].T
        gives[at].start()
    run_all(phases[1:])
    for give in gives:
        give.wait()


def opening(mesh_size, ident, moves, cut, shared, expert):
    transfers = Transfers(mesh_size, ident, moves)
    anywhere = pl.BlockSpec(memory_space=pl.ANY)
    units, depth = shared[0].shape
    sizes = (-(-units // LANES) * LANES, cut, expert[0].shape[2] - cut)
    shapes = [(3, depth, size) for size in sizes]
    results = pl.pallas_call(
        functools.partial(opening_kernel, transfers, cut),
        in_specs=transfers.in_specs + [anywhere] * 6,
        out_specs=tuple(transfers.out_specs + [anywhere] * 3),
        out_shape=tuple(transfers.shapes + [jax.ShapeDtypeStruct(shape, BF) for shape in shapes]),
        scratch_shapes=[pltpu.VMEM(array.shape, BF) for array in (*shared, *expert)]
        + [pltpu.VMEM(shape, BF) for shape in shapes]
        + [DMA((6,)), DMA((3,))]
        + transfers.scratch,
        compiler_params=transfers.params(),
    )(*transfers.inputs, *shared, *expert)
    return results[: transfers.moves], results[transfers.moves :]


def unpack_kernel(turned, *refs):
    count = len(refs) - 3
    for which, out_ref in enumerate(refs[count:]):
        first = 0
        for ref in refs[:count]:
            values = ref[which].astype(F32)
            if turned[which]:
                values = values.T
                size = min(values.shape[0], out_ref.shape[0] - first)
                out_ref[first : first + size, :] = values[:size]
            else:
                size = min(values.shape[1], out_ref.shape[1] - first)
                out_ref[:, first : first + size] = values[:, :size]
            first += size


def unpack(ranges, units, turned):
    depth = ranges[0].shape[1]
    vmem = pl.BlockSpec(memory_space=pltpu.VMEM)
    return pl.pallas_call(
        functools.partial(unpack_kernel, turned),
        in_specs=[vmem] * len(ranges),
        out_specs=(vmem,) * 3,
        out_shape=tuple(
            jax.ShapeDtypeStruct((units, depth) if turn else (depth, units), F32) for turn in turned
        ),
        compiler_params=pltpu.CompilerParams(vmem_limit_bytes=VMEM_BYTES),
        cost_estimate=pl.CostEstimate(flops=0, bytes_accessed=18 * depth * units, transcendentals=0),
    )(*ranges)


def rope_tables(seq_len):
    half = HD // 2
    frequency = np.float32(ROPE_BASE) ** (-(2.0 * np.arange(half, dtype=np.float32)) / HD)
    angles = np.arange(seq_len, dtype=np.float32)[:, None] * frequency[None, :].astype(np.float32)
    cosine, sine = np.cos(angles.astype(np.float64)), np.sin(angles.astype(np.float64))
    return (
        jnp.asarray(np.concatenate([cosine, cosine], axis=1).astype(np.float32)),
        jnp.asarray(np.concatenate([-sine, sine], axis=1).astype(np.float32)),
    )


def swap_halves(values):
    half = HD // 2
    return jnp.concatenate([values[:, half:], values[:, :half]], axis=1)


def block_scores(query, keys, first_row, length):
    scores = dot(query, keys, (1,), (1,)) * (HD ** (-0.5))
    rows = first_row + lax.broadcasted_iota(jnp.int32, scores.shape, 0)
    cols = lax.broadcasted_iota(jnp.int32, scores.shape, 1)
    return jnp.where((cols <= rows) & (cols < length), scores, -1e30)


def attend_kernel(heads, transfers, *refs):
    refs = list(refs)

    def take(count):
        taken = refs[:count]
        del refs[:count]
        return taken

    length_ref, x_ref, gain_ref, w_ref, bias_ref, cos_ref, sin_ref = take(7)
    sent = take(len(transfers.inputs))
    normed_ref, qkv_ref, mixed_ref, logs_ref, out_ref = take(5)
    landed = take(transfers.moves)
    rows_vmem, out_vmem, in_sem, normed_sem, out_sem = take(5)
    phases = transfers.begin(sent, landed, refs)
    seq_len, width = x_ref.shape
    groups, depth, columns = w_ref.shape
    span = heads * HD
    length = length_ref[0]
    blocks = [pl.ds(row, QB) for row in range(0, seq_len, QB)]

    def fetch(i):
        return pltpu.make_async_copy(x_ref.at[blocks[i]], rows_vmem.at[blocks[i]], in_sem.at[i])

    def keep(i):
        return pltpu.make_async_copy(rows_vmem.at[blocks[i]], normed_ref.at[blocks[i]], normed_sem.at[i])

    def give(i):
        return pltpu.make_async_copy(out_vmem.at[blocks[i]], out_ref.at[blocks[i]], out_sem.at[i])

    for i in range(len(blocks)):
        fetch(i).start()
    run_all(phases[:1])
    weights = w_ref[...].reshape(groups * depth, columns)
    qkv_w, out_w = weights[:, : 3 * span], weights[:, 3 * span :]
    for i in range(len(blocks)):
        row, end = i * QB, (i + 1) * QB
        if i >= 2:
            run_all(phases[i - 1 : i])
        fetch(i).wait()
        values = rows_vmem[row:end, :].astype(F32)
        normed = (normalize(values)[0] * gain_ref[...]).astype(BF)
        rows_vmem[row:end, :] = normed
        keep(i).start()
        pre = dot(normed, qkv_w, (1,), (0,)) + bias_ref[...]
        cosine, sine = cos_ref[row:end, :], sin_ref[row:end, :]
        for at in range(0, 3 * span, HD):
            part = pre[:, at : at + HD]
            if at < 2 * span:
                part = part * cosine + swap_halves(part) * sine
            qkv_ref[row:end, at : at + HD] = part.astype(BF)
        for head in range(heads):
            q_at, k_at, v_at = (head * HD, span + head * HD, 2 * span + head * HD)
            scores = block_scores(
                qkv_ref[row:end, q_at : q_at + HD], qkv_ref[:end, k_at : k_at + HD], row, length
            )
            top = jnp.max(scores, axis=1, keepdims=True)
            exps = jnp.exp(scores - top)
            totals = jnp.sum(exps, axis=1, keepdims=True)
            shares = exps * (1.0 / totals)
            logs_ref[row:end, head : head + 1] = top + jnp.log(totals)
            mixed = dot(shares.astype(BF), qkv_ref[:end, v_at : v_at + HD], (1,), (0,))
            mixed_ref[row:end, q_at : q_at + HD] = mixed.astype(BF)
        out_vmem[row:end, :] = dot(mixed_ref[row:end, :], out_w, (1,), (1,)).astype(BF)
        give(i).start()
    run_all(phases[max(1, len(blocks) - 1) :])
    for i in range(len(blocks)):
        keep(i).wait()
        give(i).wait()


def attend_back_kernel(heads, transfers, *refs):
    refs = list(refs)

    def take(count):
        taken = refs[:count]
        del refs[:count]
        return taken

    length_ref, datt_ref, w_ref, qkv_ref, logs_ref, cos_ref, sin_ref = take(7)
    sent = take(len(transfers.inputs))
    turned_ref, sums_ref, out_ref = take(3)
    landed = take(transfers.moves)
    rows_vmem, out_vmem, grad_vmem, key_acc, value_acc, in_sem, out_sem = take(7)
    phases = transfers.begin(sent, landed, refs)
    run_all(phases[:1])
    seq_len, width = datt_ref.shape
    groups, depth, columns = w_ref.shape
    span = heads * HD
    length = length_ref[0]
    scale = HD ** (-0.5)
    blocks = [pl.ds(row, QB) for row in range(0, seq_len, QB)]

    def fetch(i):
        return pltpu.make_async_copy(datt_ref.at[blocks[i]], rows_vmem.at[blocks[i]], in_sem.at[i])

    def give(i):
        return pltpu.make_async_copy(out_vmem.at[blocks[i]], out_ref.at[blocks[i]], out_sem.at[i])

    for i in range(len(blocks)):
        fetch(i).start()
    weights = w_ref[...].reshape(groups * depth, columns)
    qkv_w, out_w = weights[:, : 3 * span], weights[:, 3 * span :]
    key_acc[...] = jnp.zeros_like(key_acc)
    value_acc[...] = jnp.zeros_like(value_acc)
    query_sums = [jnp.zeros((1, HD), F32) for _ in range(heads)]
    for i in range(len(blocks)):
        row, end = i * QB, (i + 1) * QB
        fetch(i).wait()
        grad_vmem[row:end, :] = dot(rows_vmem[row:end, :], out_w, (1,), (0,)).astype(BF)
        for head in range(heads):
            q_at, k_at, v_at = (head * HD, span + head * HD, 2 * span + head * HD)
            query = qkv_ref[row:end, q_at : q_at + HD]
            keys = qkv_ref[:end, k_at : k_at + HD]
            grad = grad_vmem[row:end, q_at : q_at + HD]
            shares = jnp.exp(
                block_scores(query, keys, row, length) - logs_ref[row:end, head : head + 1]
            )
            grad_shares = dot(grad, qkv_ref[:end, v_at : v_at + HD], (1,), (1,))
            inner = jnp.sum(shares * grad_shares, axis=1, keepdims=True)
            grad_scores = (scale * shares * (grad_shares - inner)).astype(BF)
            turned = dot(grad_scores, keys, (1,), (0,))
            grad_query = (
                turned * cos_ref[row:end, :] - swap_halves(turned) * sin_ref[row:end, :]
            ).astype(BF)
            turned_ref[row:end, q_at : q_at + HD] = grad_query
            query_sums[head] += jnp.sum(grad_query.astype(F32), axis=0, keepdims=True)
            key_acc[:end, q_at : q_at + HD] += dot(grad_scores, query, (0,), (0,))
            value_acc[:end, q_at : q_at + HD] += dot(shares.astype(BF), grad, (0,), (0,))
    key_sums = [jnp.zeros((1, HD), F32) for _ in range(heads)]
    value_sums = [jnp.zeros((1, HD), F32) for _ in range(heads)]
    for i in range(len(blocks)):
        row, end = i * QB, (i + 1) * QB
        for head in range(heads):
            q_at, k_at, v_at = (head * HD, span + head * HD, 2 * span + head * HD)
            turned = key_acc[row:end, q_at : q_at + HD]
            grad_key = (
                turned * cos_ref[row:end, :] - swap_halves(turned) * sin_ref[row:end, :]
            ).astype(BF)
            grad_value = value_acc[row:end, q_at : q_at + HD].astype(BF)
            turned_ref[row:end, k_at : k_at + HD] = grad_key
            turned_ref[row:end, v_at : v_at + HD] = grad_value
            key_sums[head] += jnp.sum(grad_key.astype(F32), axis=0, keepdims=True)
            value_sums[head] += jnp.sum(grad_value.astype(F32), axis=0, keepdims=True)
        out_vmem[row:end, :] = dot(turned_ref[row:end, :], qkv_w, (1,), (1,)).astype(BF)
        give(i).start()
    for at, sums in enumerate(query_sums + key_sums + value_sums):
        sums_ref[:, at * HD : (at + 1) * HD] = sums
    for i in range(len(blocks)):
        give(i).wait()
    run_all(phases[1:])


def in_vmem(count):
    return [pl.BlockSpec(memory_space=pltpu.VMEM)] * count


def attend(length, rows, gain, weights, bias, cosine, sine, transfers):
    seq_len, width = rows.shape
    span = weights.shape[2] // 4
    heads, blocks = span // HD, seq_len // QB
    anywhere = pl.BlockSpec(memory_space=pl.ANY)
    results = pl.pallas_call(
        functools.partial(attend_kernel, heads, transfers),
        out_shape=tuple(
            [
                jax.ShapeDtypeStruct((seq_len, width), BF),
                jax.ShapeDtypeStruct((seq_len, 3 * span), BF),
                jax.ShapeDtypeStruct((seq_len, span), BF),
                jax.ShapeDtypeStruct((seq_len, heads), F32),
                jax.ShapeDtypeStruct((seq_len, width), BF),
            ]
            + transfers.shapes
        ),
        in_specs=[pl.BlockSpec(memory_space=pltpu.SMEM), anywhere] + in_vmem(5) + transfers.in_specs,
        out_specs=tuple([anywhere] + in_vmem(3) + [anywhere] + transfers.out_specs),
        scratch_shapes=[pltpu.VMEM((seq_len, width), BF)] * 2
        + [DMA((blocks,))] * 3
        + transfers.scratch,
        compiler_params=transfers.params(),
        cost_estimate=pl.CostEstimate(
            flops=8 * seq_len * width * span + 3 * span * seq_len * seq_len,
            bytes_accessed=8 * seq_len * width,
            transcendentals=heads * seq_len * seq_len,
        ),
    )(length, rows, gain, weights, bias, cosine, sine, *transfers.inputs)
    return results[:5], results[5:]


def attend_back(length, rows, weights, qkv, logs, cosine, sine, transfers):
    seq_len, width = rows.shape
    span = weights.shape[2] // 4
    heads, blocks = span // HD, seq_len // QB
    anywhere = pl.BlockSpec(memory_space=pl.ANY)
    results = pl.pallas_call(
        functools.partial(attend_back_kernel, heads, transfers),
        out_shape=tuple(
            [
                jax.ShapeDtypeStruct((seq_len, 3 * span), BF),
                jax.ShapeDtypeStruct((1, 3 * span), F32),
                jax.ShapeDtypeStruct((seq_len, width), BF),
            ]
            + transfers.shapes
        ),
        in_specs=[pl.BlockSpec(memory_space=pltpu.SMEM), anywhere] + in_vmem(5) + transfers.in_specs,
        out_specs=tuple(in_vmem(2) + [anywhere] + transfers.out_specs),
        scratch_shapes=[pltpu.VMEM((seq_len, width), BF)] * 2
        + [pltpu.VMEM((seq_len, span), BF)]
        + [pltpu.VMEM((seq_len, span), F32)] * 2
        + [DMA((blocks,))] * 2
        + transfers.scratch,
        compiler_params=transfers.params(),
        cost_estimate=pl.CostEstimate(
            flops=8 * seq_len * width * span + 8 * span * seq_len * seq_len,
            bytes_accessed=8 * seq_len * width,
            transcendentals=heads * seq_len * seq_len,
        ),
    )(length, rows, weights, qkv, logs, cosine, sine, *transfers.inputs)
    return results[:3], results[3:]


def padded(values, axis):
    size = values.shape[axis]
    more = -size % LANES
    if not more:
        return values
    return jnp.pad(values, [(0, more if i == axis else 0) for i in range(values.ndim)])


def packed(values, kind):
    tile = LANES * (16 if kind == BF else 8)
    values = values.astype(kind)
    return padded_to(values, -(-values.shape[-1] // tile) * tile)


def padded_to(values, size):
    more = size - values.shape[-1]
    return jnp.pad(values, [(0, 0)] * (values.ndim - 1) + [(0, more)])


def local(
    tokens,
    lengths,
    routes,
    norm1_gain,
    w_query,
    w_key,
    w_value,
    b_query,
    b_key,
    b_value,
    w_out,
    norm2_gain,
    router,
    shared_gate_vec,
    shared_gate,
    shared_up,
    shared_down,
    expert_gate,
    expert_up,
    expert_down,
    cotangent,
):
    ranks = lax.axis_size("tensor")
    groups = lax.axis_size("fsdp")
    rank = lax.axis_index("tensor")
    micros, _, rows, width = tokens.shape
    seq_len = rows * ranks
    heads = w_query.shape[1] // HD
    span = heads * HD
    experts = ranks * expert_gate.shape[0]
    shared_units = shared_gate.shape[1]
    expert_units = expert_gate.shape[2]
    cut = expert_units // (2 * LANES) * LANES
    own_first = rank * rows
    local_pos = own_first + jnp.arange(rows, dtype=jnp.int32)

    per_device = norm1_gain.shape[0]
    small = jnp.concatenate(
        [
            norm1_gain,
            norm2_gain,
            shared_gate_vec,
            router.reshape(-1),
            b_query.reshape(-1),
            b_key.reshape(-1),
            b_value.reshape(-1),
        ]
    )
    attn_own = jnp.concatenate([w_query, w_key, w_value, w_out.T], axis=1)
    mesh_size = (ranks, groups)
    (rows_a, attn_w, small_all), own_ranges = opening(
        mesh_size,
        2,
        [
            ("gather", tokens, (0, 0)),
            ("cross_gather", attn_own),
            ("spread", packed(small, BF).reshape(-1, LANES)),
        ],
        cut,
        (shared_gate.T, shared_up.T, shared_down),
        (expert_gate, expert_up, expert_down),
    )
    small_all = small_all.reshape(groups * ranks, -1)
    gain_one = small_all[:, :per_device].reshape(-1).astype(F32)
    gain_two = small_all[:, per_device : 2 * per_device].reshape(-1).astype(F32)
    gate_vec = small_all[:, 2 * per_device : 3 * per_device].reshape(-1)
    bias_at = per_device * (3 + experts)
    router_full = small_all[:, 3 * per_device : bias_at].reshape(width, experts)
    router_wide = padded_to(jnp.concatenate([router_full, gate_vec[:, None]], axis=1), LANES)
    own_bias = lax.dynamic_index_in_dim(
        small_all.reshape(groups, ranks, -1), rank, 1, False
    )[:, bias_at : small.shape[0]].reshape(groups, 3, heads, HD // groups)
    bias = own_bias.transpose(1, 2, 0, 3).reshape(1, 3 * span).astype(F32)

    weights = [lax.all_gather(own_range, "fsdp", axis=0) for own_range in own_ranges]

    cosine, sine = rope_tables(seq_len)
    idle = Transfers(mesh_size)
    token_own = [tokens[m, 0] for m in range(micros)]
    grads_own = []
    for m in range(micros):
        inside = (local_pos < lengths[m, 0])[:, None]
        grads_own.append(jnp.where(inside, cotangent[m, 0], jnp.zeros((), BF)))

    def moving(ident, *moves, needed=()):
        return Transfers(mesh_size, ident, moves, needed)

    def attention(m, token_rows, transfers):
        return attend(lengths[m], token_rows, gain_one[None], attn_w, bias, cosine, sine, transfers)

    def second_norm(m, attended):
        hidden = token_own[m].astype(F32) + attended
        unit, inverse = normalize(hidden)
        return hidden, unit, inverse, (unit * gain_two).astype(BF)

    def second_norm_back(m, state, summed):
        grad_hidden, gain_part = norm_back(summed, state[1], state[2], gain_two)
        grad_hidden = grad_hidden + grads_own[m].astype(F32)
        return grad_hidden, grad_hidden.astype(BF), gain_part

    def first_norm_back(m, grad_hidden, summed):
        unit, inverse = normalize(token_own[m].astype(F32))
        grad_inputs, gain_part = norm_back(summed, unit, inverse, gain_one)
        return (grad_inputs + grad_hidden).astype(BF), gain_part

    def finished(m, hidden, moved):
        inside = (local_pos < lengths[m, 0]).astype(F32)[:, None]
        return (inside * (hidden + moved)).astype(BF)

    att_a, (rows_b,) = attention(0, rows_a, moving(3, ("gather", tokens, (1, 0))))
    grad_a, sum_a = exchange(
        mesh_size, 4, [("gather", cotangent, (0, 0)), ("scatter", att_a[4])]
    )
    norm_a = second_norm(0, sum_a)
    att_b, (two_a,) = attention(1, rows_b, moving(5, ("gather", norm_a[3])))

    def over_groups(grads):
        flat = grads.reshape(-1, grads.shape[-1])
        summed = lax.psum_scatter(flat, "fsdp", scatter_dimension=0, tiled=True)
        return with_layout_constraint(summed, Layout((0, 1))).reshape(grads.shape[1:])

    def grads_of(which, transfers, at=()):
        per_micro = []
        for key in range(micros):
            rows_two, grads = ((two_a, grad_a), (two_b, grad_b))[key]
            scaled, gate, up = act[which, key]
            more = [(acc_a, acc_b)[key][2]] if which == 2 else []
            per_micro.append([rows_two, grads, gate, up, scaled] + more)
        return ffn_grads(groups, per_micro, transfers, at)

    act = {}
    part = functools.partial(ffn, experts)
    single = ((0, 0), (1, 0), (2, 0), (3, 0))
    act[0, 0], acc_a, (grad_b, sum_b) = part(
        "first", two_a, grad_a, routes[0, 0], weights[0], [lengths[0]], router_wide,
        moving(6, ("gather", cotangent, (1, 0)), ("scatter", att_b[4])), ((0, 0), (1, 1), (3, 0)),
    )
    acc_a, route_a = acc_a[:3], acc_a[3]
    norm_b = second_norm(1, sum_b)
    act[1, 0], acc_a, (two_b,) = part(
        "next", two_a, grad_a, route_a, weights[1], acc_a, None,
        moving(7, ("gather", norm_b[3])), single,
    )
    act[0, 1], acc_b, _ = part(
        "first", two_b, grad_b, routes[1, 0], weights[0], [lengths[1]], router_wide, idle
    )
    acc_b, route_b = acc_b[:3], acc_b[3]
    (grads_0,), _ = grads_of(0, idle)
    range_0 = over_groups(grads_0)
    act[2, 0], acc_a, _ = part(
        "last", two_a, grad_a, route_a, weights[2], acc_a, router_wide, moving(0, needed=[grads_0])
    )
    act[1, 1], acc_b, (down_a,) = part(
        "next", two_b, grad_b, route_b, weights[1], acc_b, None,
        moving(8, ("scatter", acc_a[1])), single,
    )
    hid_a, send_a, gain_part_a = second_norm_back(0, norm_a, down_a)
    (grads_1,), (datt_a,) = grads_of(
        1, moving(9, ("gather", send_a)), ((0, 0), (1, 0), (2, 0), (3, 0))
    )
    range_1 = over_groups(grads_1)
    (grad_qkv_a, sums_a, first_a), _ = attend_back(
        lengths[0], datt_a, attn_w, att_a[1], att_a[3], cosine, sine, moving(0, needed=[grads_1])
    )
    act[2, 1], acc_b, (one_a,) = part(
        "last", two_b, grad_b, route_b, weights[2], acc_b, router_wide,
        moving(10, ("scatter", first_a)), single,
    )
    (grads_2, total_wide), (down_b,) = grads_of(
        2, moving(11, ("scatter", acc_b[1]), needed=[range_0]), ((0, 0), (1, 1), (2, 1), (3, 1))
    )
    range_2 = over_groups(grads_2)
    hid_b, send_b, gain_part_b = second_norm_back(1, norm_b, down_b)
    datt_b, moved_a = exchange(mesh_size, 12, [("gather", send_b), ("scatter", acc_a[0])])
    (grad_qkv_b, sums_b, first_b), _ = attend_back(
        lengths[1], datt_b, attn_w, att_b[1], att_b[3], cosine, sine, idle
    )
    attn_parts, (one_b,) = attention_grads(
        groups,
        [
            (att_a[0], datt_a, grad_qkv_a, att_a[2]),
            (att_b[0], datt_b, grad_qkv_b, att_b[2]),
        ],
        moving(13, ("scatter", first_b), needed=[range_1]),
    )

    grad_in_a, one_part_a = first_norm_back(0, hid_a, one_a)
    grad_in_b, one_part_b = first_norm_back(1, hid_b, one_b)

    devices = groups * ranks
    bias_part = (sums_a + sums_b).reshape(3, heads, groups, HD // groups).transpose(2, 0, 1, 3)
    bias_part = bias_part.reshape(groups, 1, -1)
    own_rank = (jnp.arange(ranks, dtype=jnp.int32) == rank).astype(F32)[None, :, None]
    parts = jnp.concatenate(
        [
            (one_part_a + one_part_b).reshape(devices, -1),
            (gain_part_a + gain_part_b).reshape(devices, -1),
            total_wide[:, : experts + 1].reshape(devices, -1),
            (bias_part * own_rank).reshape(devices, -1),
        ],
        axis=1,
    )
    moved_b, attn_g, shares = exchange(
        mesh_size,
        14,
        [
            ("scatter", acc_b[0]),
            ("cross_scatter", attn_parts),
            ("share", packed(parts, F32).reshape(devices, -1, LANES)),
        ],
        [range_2],
    )
    shares = shares.reshape(-1)
    wide_g = shares[2 * per_device : (3 + experts) * per_device].reshape(per_device, experts + 1)
    bias_g = shares[bias_at : parts.shape[1]].reshape(3, heads, HD // groups)

    shared_g = unpack([range_0], shared_units, (True, True, True))
    expert_g = unpack([range_1, range_2], expert_units, (False, False, True))
    return (
        jnp.stack([finished(0, norm_a[0], moved_a), finished(1, norm_b[0], moved_b)])[:, None],
        jnp.stack([grad_in_a, grad_in_b])[:, None],
        shares[:per_device],
        attn_g[:, :span],
        attn_g[:, span : 2 * span],
        attn_g[:, 2 * span : 3 * span],
        bias_g[0],
        bias_g[1],
        bias_g[2],
        attn_g[:, 3 * span :].T,
        shares[per_device : 2 * per_device],
        wide_g[:, :experts],
        wide_g[:, experts],
        shared_g[0].T,
        shared_g[1].T,
        shared_g[2],
        expert_g[0][None],
        expert_g[1][None],
        expert_g[2][None],
    )


def solution(mesh):
    in_specs = (
        P(None, "fsdp", "tensor", None),
        P(None, "fsdp"),
        P(None, "fsdp", None, None),
        P(("fsdp", "tensor")),
        P("fsdp", "tensor"),
        P("fsdp", "tensor"),
        P("fsdp", "tensor"),
        P("tensor", "fsdp"),
        P("tensor", "fsdp"),
        P("tensor", "fsdp"),
        P("tensor", "fsdp"),
        P(("fsdp", "tensor")),
        P(("fsdp", "tensor"), None),
        P(("fsdp", "tensor")),
        P("fsdp", "tensor"),
        P("fsdp", "tensor"),
        P("tensor", "fsdp"),
        P("tensor", "fsdp", None),
        P("tensor", "fsdp", None),
        P("tensor", None, "fsdp"),
        P(None, "fsdp", "tensor", None),
    )
    out_specs = (
        P(None, "fsdp", "tensor", None),
        P(None, "fsdp", "tensor", None),
        P(("fsdp", "tensor")),
        P("fsdp", "tensor"),
        P("fsdp", "tensor"),
        P("fsdp", "tensor"),
        P("tensor", "fsdp"),
        P("tensor", "fsdp"),
        P("tensor", "fsdp"),
        P("tensor", "fsdp"),
        P(("fsdp", "tensor")),
        P(("fsdp", "tensor"), None),
        P(("fsdp", "tensor")),
        P("fsdp", "tensor"),
        P("fsdp", "tensor"),
        P("tensor", "fsdp"),
        P("tensor", "fsdp", None),
        P("tensor", "fsdp", None),
        P("tensor", None, "fsdp"),
    )
    return jax.shard_map(local, mesh=mesh, in_specs=in_specs, out_specs=out_specs, check_vma=False)
```

```python
import functools

import jax
import jax.numpy as jnp
import numpy as np
from jax import lax
from jax.experimental import pallas as pl
from jax.experimental.layout import Layout, with_layout_constraint
from jax.experimental.pallas import tpu as pltpu
from jax.sharding import PartitionSpec as P

HD = 128
EPSILON = 1e-06
ROPE_BASE = 1000000.0
BF = jnp.bfloat16
F32 = jnp.float32
MESH = pl.DeviceIdType.MESH
QB = 256
LANES = 128
CHUNKS = 2
STRIP = 16
ROW_BLOCK = 256
VMEM_BYTES = 60 << 20


def dot(left, right, left_dims, right_dims):
    return lax.dot_general(
        left, right, ((left_dims, right_dims), ((), ())), preferred_element_type=F32
    )


def normalize(values):
    inverse = lax.rsqrt(jnp.mean(values * values, axis=-1, keepdims=True) + EPSILON)
    return (values * inverse, inverse)


def norm_back(grad_normed, unit, inverse, gain):
    grad_unit = grad_normed * gain
    grad_values = inverse * (grad_unit - unit * jnp.mean(grad_unit * unit, axis=-1, keepdims=True))
    return (grad_values, jnp.sum(grad_normed * unit, axis=0))


def remote(src, dst, sems, at, target):
    return pltpu.make_async_remote_copy(
        src_ref=src,
        dst_ref=dst,
        send_sem=sems[0].at[at],
        recv_sem=sems[1].at[at],
        device_id={"tensor": target},
        device_id_type=MESH,
    )


def gather_scratch(ranks):
    chips = ranks // 2
    pair = [pltpu.SemaphoreType.DMA((chips, CHUNKS))] * 2
    cross = [pltpu.SemaphoreType.DMA((2 * chips, CHUNKS))] * 2
    return [pltpu.SemaphoreType.DMA] + pair + pair + cross


def gather_steps(place, block, whole, local_sem, up_s, up_r, down_s, down_r, cross_s, cross_r):
    chips, chip, core = place.chips, place.chip, place.core
    rows = block.shape[0]
    part = rows // CHUNKS
    up, down, cross = (up_s, up_r), (down_s, down_r), (cross_s, cross_r)

    def at(owner, chunk):
        first = pl.multiple_of((2 * owner + core) * rows + chunk * part, part)
        return whole.at[pl.ds(first, part)]

    def theirs(owner, chunk):
        first = pl.multiple_of((2 * owner + 1 - core) * rows + chunk * part, part)
        return whole.at[pl.ds(first, part)]

    def own(chunk):
        return block.at[pl.ds(chunk * part, part)]

    def upward(step, chunk):
        source = own(chunk) if step == 0 else at(chip - step, chunk)
        return remote(source, at(chip - step, chunk), up, (step, chunk), place.above)

    def downward(step, chunk):
        source = own(chunk) if step == 0 else at(chip + step, chunk)
        return remote(source, at(chip + step, chunk), down, (step, chunk), place.below)

    def across(slot, owner, chunk):
        source = own(chunk) if slot == 0 else at(owner, chunk)
        return remote(source, at(owner, chunk), cross, (slot, chunk), place.partner)

    def arrived(slot, owner, chunk):
        return remote(theirs(owner, chunk), theirs(owner, chunk), cross, (slot, chunk), place.partner)

    def arrived_up(step, chunk):
        return remote(at(chip - step, chunk), at(chip - step, chunk), up, (step - 1, chunk), place.above)

    def arrived_down(step, chunk):
        return remote(at(chip + step, chunk), at(chip + step, chunk), down, (step - 1, chunk), place.below)

    both = range(CHUNKS)

    def mine():
        first = pl.multiple_of((2 * chip + core) * rows, rows)
        return pltpu.make_async_copy(block, whole.at[pl.ds(first, rows)], local_sem)

    def begin():
        for chunk in both:
            pl.when(place.not_top)(lambda: upward(0, chunk).start())
            pl.when(place.not_bottom)(lambda: downward(0, chunk).start())
        for chunk in both:
            across(0, chip, chunk).start()
        mine().start()

    def hop(step, chunk):
        @pl.when(chip >= step)
        def _():
            arrived_up(step, chunk).wait_recv()
            pl.when(place.not_top)(lambda: upward(step, chunk).start())
            across(2 * step - 1, chip - step, chunk).start()

        @pl.when(chip < chips - step)
        def _():
            arrived_down(step, chunk).wait_recv()
            pl.when(place.not_bottom)(lambda: downward(step, chunk).start())
            across(2 * step, chip + step, chunk).start()

    def end():
        mine().wait()
        for step in range(chips):
            for chunk in both:
                if step == 0:
                    arrived(0, chip, chunk).wait_recv()
                    across(0, chip, chunk).wait_send()
                else:

                    @pl.when(chip >= step)
                    def _():
                        arrived(2 * step - 1, chip - step, chunk).wait_recv()
                        across(2 * step - 1, chip - step, chunk).wait_send()

                    @pl.when(chip < chips - step)
                    def _():
                        arrived(2 * step, chip + step, chunk).wait_recv()
                        across(2 * step, chip + step, chunk).wait_send()

                @pl.when(place.not_top & (chip >= step))
                def _():
                    upward(step, chunk).wait_send()

                @pl.when(place.not_bottom & (chip < chips - step))
                def _():
                    downward(step, chunk).wait_send()

    hops = [functools.partial(hop, step, chunk) for step in range(1, chips) for chunk in both]
    return [begin] + hops + [end]


def scatter_scratch(ranks, rows, width):
    chips = ranks // 2
    line = [pltpu.SemaphoreType.DMA((chips, CHUNKS))] * 2
    buffers = [pltpu.VMEM((chips, rows, width), BF)] * 5
    return buffers + [pltpu.SemaphoreType.DMA((chips,))] + line * 3


def scatter_steps(
    place, partial, total, kept, pair, held, up_in, down_in, keep_sem,
    up_s, up_r, down_s, down_r, cross_s, cross_r,
):
    chips, chip, core = place.chips, place.chip, place.core
    rows = total.shape[0]
    part = rows // CHUNKS
    up, down, cross = (up_s, up_r), (down_s, down_r), (cross_s, cross_r)
    both = range(CHUNKS)

    def keep(k):
        first = pl.multiple_of((2 * k + core) * rows, rows)
        return pltpu.make_async_copy(partial.at[pl.ds(first, rows)], kept.at[k], keep_sem.at[k])

    def across(k, chunk):
        first = pl.multiple_of((2 * k + 1 - core) * rows + chunk * part, part)
        return remote(
            partial.at[pl.ds(first, part)],
            pair.at[k, pl.ds(chunk * part, part)],
            cross,
            (k, chunk),
            place.partner,
        )

    def upward(step, k, chunk):
        cut = pl.ds(chunk * part, part)
        return remote(held.at[k, cut], up_in.at[step, cut], up, (step, chunk), place.above)

    def downward(step, k, chunk):
        cut = pl.ds(chunk * part, part)
        return remote(held.at[k, cut], down_in.at[step, cut], down, (step, chunk), place.below)

    def add(k, chunk, target, others):
        def strip(i, carry):
            cut = pl.ds(chunk * part + i * STRIP, STRIP)
            value = kept[k, cut].astype(F32) + pair[k, cut].astype(F32)
            for ref, slot in others:
                value = value + ref[slot, cut].astype(F32)
            if target is None:
                total[cut] = value
            else:
                target[k, cut] = value.astype(BF)
            return carry

        lax.fori_loop(0, part // STRIP, strip, 0)

    order = []
    for i in range(chips):
        for k in (chips - 1 - i, i):
            if k not in order:
                order.append(k)
    def begin():
        for k in order:
            keep(k).start()
            for chunk in both:
                across(k, chunk).start()

    def hop(step, chunk):
        @pl.when(place.not_top & (chip <= step - 1))
        def _():
            k = chip + chips - step
            if chunk == 0:
                keep(k).wait()
            across(k, chunk).wait_recv()

            @pl.when(place.not_bottom)
            def _():
                upward(step - 1, k, chunk).wait_recv()
                add(k, chunk, held, [(up_in, step - 1)])

            pl.when(jnp.logical_not(place.not_bottom))(lambda: add(k, chunk, held, []))
            upward(step, k, chunk).start()

        @pl.when(place.not_bottom & (chip >= chips - step))
        def _():
            k = chip - (chips - step)
            if chunk == 0:
                keep(k).wait()
            across(k, chunk).wait_recv()

            @pl.when(place.not_top)
            def _():
                downward(step - 1, k, chunk).wait_recv()
                add(k, chunk, held, [(down_in, step - 1)])

            pl.when(jnp.logical_not(place.not_top))(lambda: add(k, chunk, held, []))
            downward(step, k, chunk).start()

    last = chips - 1

    def add_last(chunk):
        if chunk == 0:
            keep(chip).wait()
        across(chip, chunk).wait_recv()

        @pl.when(place.not_top & place.not_bottom)
        def _():
            upward(last, chip, chunk).wait_recv()
            downward(last, chip, chunk).wait_recv()
            add(chip, chunk, None, [(up_in, last), (down_in, last)])

        @pl.when(jnp.logical_not(place.not_top))
        def _():
            upward(last, chip, chunk).wait_recv()
            add(chip, chunk, None, [(up_in, last)])

        @pl.when(jnp.logical_not(place.not_bottom))
        def _():
            downward(last, chip, chunk).wait_recv()
            add(chip, chunk, None, [(down_in, last)])

    def end():
        for chunk in both:
            for k in range(chips):
                across(k, chunk).wait_send()
            for step in range(1, chips):

                @pl.when(place.not_top & (chip <= step - 1))
                def _():
                    upward(step, chip + chips - step, chunk).wait_send()

                @pl.when(place.not_bottom & (chip >= chips - step))
                def _():
                    downward(step, chip - (chips - step), chunk).wait_send()

    def first():
        begin()
        for chunk in both:
            hop(1, chunk)

    hops = [functools.partial(hop, step, chunk) for step in range(2, chips) for chunk in both]
    return [first] + hops + [functools.partial(add_last, chunk) for chunk in both] + [end]


class Place:
    def __init__(self, ranks, groups):
        rank, group = lax.axis_index("tensor"), lax.axis_index("fsdp")
        self.ranks, self.groups = ranks, groups
        self.chips = ranks // 2
        self.chip, self.core = rank // 2, rank % 2
        self.partner = rank + 1 - 2 * self.core
        self.above, self.below = rank + 2, rank - 2
        self.not_top = self.chip < self.chips - 1
        self.not_bottom = self.chip > 0
        self.rank, self.group = rank, group
        self.device = group * ranks + rank
        near, far = group % 2, group // 2
        self.beside = 2 * far + 1 - near
        self.across = 2 * (1 - far) + near
        self.opposite = 2 * (1 - far) + 1 - near
        self.square = groups == 4

    def name(self, device):
        return {"fsdp": device // self.ranks, "tensor": device % self.ranks}

    def meet(self, line, cross, everyone):
        barrier = pltpu.get_barrier_semaphore()

        def greet(name):
            pl.semaphore_signal(barrier, 1, device_id=name, device_id_type=MESH)

        if everyone:
            devices = self.groups * self.ranks

            def one(i, carry):
                greet(self.name(lax.rem(self.device + i, devices)))
                return carry

            lax.fori_loop(1, devices, one, 0)
            pl.semaphore_wait(barrier, devices - 1)
            return
        peers = 0
        if line:
            greet({"tensor": self.partner})
            pl.when(self.not_top)(lambda: greet({"tensor": self.above}))
            pl.when(self.not_bottom)(lambda: greet({"tensor": self.below}))
            peers = 1 + self.not_top.astype(jnp.int32) + self.not_bottom.astype(jnp.int32)
        if cross and self.square:
            greet({"fsdp": self.beside})
            greet({"fsdp": self.across})
            peers = peers + 2
        elif cross:
            for i in range(1, self.groups):
                greet({"fsdp": lax.rem(self.group + i, self.groups)})
            peers = peers + self.groups - 1
        pl.semaphore_wait(barrier, peers)


def to_group(src, dst, send, recv, at, target):
    return pltpu.make_async_remote_copy(
        src_ref=src,
        dst_ref=dst,
        send_sem=send.at[at],
        recv_sem=recv.at[at],
        device_id={"fsdp": target},
        device_id_type=MESH,
    )


def cross_gather_steps(place, block, whole, own_sem, send, recv):
    group = place.group
    half = block.shape[0] // 2

    def own():
        return pltpu.make_async_copy(block, whole.at[group], own_sem)

    if not place.square:

        def direct(i):
            target = lax.rem(group + i, place.groups)
            return to_group(block, whole.at[group], send, recv, i - 1, target)

        def begin_direct():
            own().start()
            for i in range(1, place.groups):
                direct(i).start()

        def end_direct():
            own().wait()
            for i in range(1, place.groups):
                source = lax.rem(group - i + place.groups, place.groups)
                to_group(block, whole.at[source], send, recv, i - 1, source).wait_recv()
                direct(i).wait_send()

        return [begin_direct, end_direct]

    def near(at):
        return to_group(block, whole.at[group], send, recv, at, (place.beside, place.across)[at])

    def came(at):
        source = (place.beside, place.across)[at]
        return to_group(whole.at[source], whole.at[source], send, recv, at, source)

    def forward(at):
        source, target = ((place.beside, place.across), (place.across, place.beside))[at]
        piece = whole.at[source, pl.ds(at * half, half)]
        return to_group(piece, piece, send, recv, 2 + at, target)

    def far(at):
        piece = whole.at[place.opposite, pl.ds(at * half, half)]
        return to_group(piece, piece, send, recv, 2 + at, place.opposite)

    def begin():
        for at in range(2):
            near(at).start()
        own().start()

    def pass_on():
        for at in range(2):
            came(at).wait_recv()
            forward(at).start()

    def end():
        own().wait()
        for at in range(2):
            far(at).wait_recv()
            near(at).wait_send()
            forward(at).wait_send()

    return [begin] + [nothing] * 4 + [pass_on, nothing, end]


def cross_scatter_steps(place, partial, total, mine, near_in, far_in, own_sem, send, recv):
    group = place.group
    rows = total.shape[0]
    half = rows // 2

    def own():
        return pltpu.make_async_copy(partial, mine, own_sem)

    def loop(count, body):
        def strip(i, carry):
            body(pl.ds(i * STRIP, STRIP))
            return carry

        lax.fori_loop(0, count // STRIP, strip, 0)

    if not place.square:

        def direct(i):
            target = lax.rem(group + i, place.groups)
            return to_group(partial.at[target], near_in.at[group], send, recv, i - 1, target)

        def begin_direct():
            own().start()
            for i in range(1, place.groups):
                direct(i).start()

        def sum_direct(cut):
            value = mine[group, cut].astype(F32)
            for i in range(1, place.groups):
                value = value + near_in[lax.rem(group + i, place.groups), cut].astype(F32)
            total[cut] = value

        def end_direct():
            own().wait()
            for i in range(1, place.groups):
                source = lax.rem(group - i + place.groups, place.groups)
                piece = partial.at[source]
                to_group(piece, near_in.at[source], send, recv, i - 1, source).wait_recv()
            loop(rows, sum_direct)
            for i in range(1, place.groups):
                direct(i).wait_send()

        return [begin_direct, end_direct]

    def first(at):
        target = (place.beside, place.across)[at]
        piece = partial.at[place.opposite, pl.ds(at * half, half)]
        return to_group(piece, far_in.at[at], send, recv, at, target)

    def second(at):
        target = (place.beside, place.across)[at]
        return to_group(mine.at[target], near_in.at[at], send, recv, 2 + at, target)

    def begin():
        own().start()
        for at in range(2):
            first(at).start()

    def join():
        own().wait()
        for at in range(2):
            target = (place.across, place.beside)[at]
            first(at).wait_recv()

            def one(cut, at=at, target=target):
                place_in = pl.ds(at * half + cut.start, STRIP)
                value = mine[target, place_in].astype(F32) + far_in[at, cut].astype(F32)
                mine[target, place_in] = value.astype(BF)

            loop(half, one)
            second(1 - at).start()

    def everything(cut):
        value = mine[group, cut].astype(F32) + near_in[0, cut].astype(F32)
        total[cut] = value + near_in[1, cut].astype(F32)

    def end():
        for at in range(2):
            second(at).wait_recv()
        loop(rows, everything)
        for at in range(2):
            first(at).wait_send()
            second(at).wait_send()

    return [begin, nothing, join, nothing, nothing, end]


def everyone_steps(place, piece_for, landing, own_sem, send, recv):
    devices = place.groups * place.ranks
    me = place.device

    def copy(i):
        target = lax.rem(me + i, devices)
        return pltpu.make_async_remote_copy(
            src_ref=piece_for(target),
            dst_ref=landing.at[me],
            send_sem=send.at[i],
            recv_sem=recv.at[i],
            device_id=place.name(target),
            device_id_type=MESH,
        )

    def arrival(i):
        source = lax.rem(me - i + devices, devices)
        return pltpu.make_async_remote_copy(
            src_ref=landing.at[source],
            dst_ref=landing.at[source],
            send_sem=send.at[i],
            recv_sem=recv.at[i],
            device_id=place.name(source),
            device_id_type=MESH,
        )

    def start(i, carry):
        copy(i).start()
        return carry

    def finish_one(i, carry):
        arrival(i).wait_recv()
        copy(i).wait_send()
        return carry

    def own():
        return pltpu.make_async_copy(piece_for(me), landing.at[me], own_sem)

    def begin():
        own().start()
        lax.fori_loop(1, devices, start, 0)

    def end():
        own().wait()
        lax.fori_loop(1, devices, finish_one, 0)

    return [begin, nothing, end]


def spread_steps(place, value, everyone, own_sem, send, recv):
    return everyone_steps(place, lambda target: value, everyone, own_sem, send, recv)


def share_steps(place, values, total, landing, own_sem, send, recv):
    phases = everyone_steps(place, lambda target: values.at[target], landing, own_sem, send, recv)

    def add_up():
        total[...] = jnp.sum(landing[...], axis=0)

    return phases + [add_up]


DMA = pltpu.SemaphoreType.DMA


class Transfers:
    def __init__(self, mesh_size, ident=0, moves=(), needed=()):
        self.ranks, self.groups = mesh_size
        self.ident = ident
        self.kinds = [move[0] for move in moves]
        self.parts = [move[2] if len(move) > 2 else None for move in moves]
        self.inputs = [move[1] for move in moves] + list(needed)
        self.moves = len(self.kinds)
        anywhere = pl.BlockSpec(memory_space=pl.ANY)
        vmem = pl.BlockSpec(memory_space=pltpu.VMEM)
        self.in_specs = [anywhere] * len(self.inputs)
        self.shapes, self.out_specs, self.scratch, self.counts = [], [], [], []
        for kind, array, *part in moves:
            shape, spec = array.shape[len(part[0]) :] if part else array.shape, anywhere
            if kind == "gather":
                shape, dtype = (self.ranks * shape[0], shape[1]), BF
                scratch = gather_scratch(self.ranks)
            elif kind == "scatter":
                shape, dtype, spec = (shape[0] // self.ranks, shape[1]), F32, vmem
                scratch = scatter_scratch(self.ranks, *shape)
            elif kind == "cross_gather":
                shape, dtype = (self.groups,) + shape, BF
                scratch = [DMA, DMA((max(4, self.groups),)), DMA((max(4, self.groups),))]
            elif kind == "cross_scatter":
                rest = shape[1:]
                square = self.groups == 4
                near = (2 if square else self.groups,) + rest
                scratch = [
                    pltpu.VMEM(shape, BF),
                    pltpu.VMEM(near, BF),
                    pltpu.VMEM((2, rest[0] // 2) + rest[1:], BF),
                    DMA,
                    DMA((max(4, self.groups),)),
                    DMA((max(4, self.groups),)),
                ]
                shape, dtype, spec = rest, F32, vmem
            elif kind == "share":
                devices = self.ranks * self.groups
                scratch = [pltpu.VMEM(shape, F32), DMA, DMA((devices,)), DMA((devices,))]
                shape, dtype, spec = shape[1:], F32, vmem
            else:
                devices = self.ranks * self.groups
                shape, dtype = (devices,) + shape, array.dtype
                scratch = [DMA, DMA((devices,)), DMA((devices,))]
            self.shapes.append(jax.ShapeDtypeStruct(shape, dtype))
            self.out_specs.append(spec)
            self.scratch += scratch
            self.counts.append(len(scratch))

    def params(self):
        if not self.moves:
            return pltpu.CompilerParams(vmem_limit_bytes=VMEM_BYTES)
        return pltpu.CompilerParams(
            collective_id=self.ident, has_side_effects=True, vmem_limit_bytes=VMEM_BYTES
        )

    def begin(self, inputs, outputs, scratch):
        if not self.moves:
            return []
        steps_of = {
            "gather": gather_steps,
            "scatter": scatter_steps,
            "cross_gather": cross_gather_steps,
            "cross_scatter": cross_scatter_steps,
            "spread": spread_steps,
            "share": share_steps,
        }
        place = Place(self.ranks, self.groups)
        scratch = list(scratch)
        lines = []
        for i, kind in enumerate(self.kinds):
            taken, scratch = scratch[: self.counts[i]], scratch[self.counts[i] :]
            given = inputs[i] if self.parts[i] is None else inputs[i].at[self.parts[i]]
            lines.append(steps_of[kind](place, given, outputs[i], *taken))

        def phase(number):
            if number == 0:
                kinds = set(self.kinds)
                place.meet(
                    bool(kinds & {"gather", "scatter"}),
                    bool(kinds & {"cross_gather", "cross_scatter"}),
                    bool(kinds & {"spread", "share"}),
                )
            for steps in lines:
                if number < len(steps):
                    steps[number]()

        return [functools.partial(phase, i) for i in range(max(map(len, lines)))]


def nothing():
    pass


def run_all(phases):
    for phase in phases:
        phase()


def exchange_kernel(transfers, *refs):
    count, moves = len(transfers.inputs), transfers.moves
    run_all(transfers.begin(refs[:moves], refs[count : count + moves], refs[count + moves :]))


def exchange(mesh_size, ident, moves, needed=()):
    transfers = Transfers(mesh_size, ident, moves, needed)
    return pl.pallas_call(
        functools.partial(exchange_kernel, transfers),
        out_shape=tuple(transfers.shapes),
        in_specs=transfers.in_specs,
        out_specs=tuple(transfers.out_specs),
        scratch_shapes=transfers.scratch,
        compiler_params=transfers.params(),
    )(*transfers.inputs)


def beside(phases, at, grid_steps, parts):
    step = pl.program_id(0)
    state = None
    for number, part in enumerate(parts):
        for phase, (when, ahead_of) in zip(phases, at):
            if ahead_of == number:
                pl.when(step == when)(phase)
        state = part(state)
    if phases:
        pl.when(step == grid_steps - 1)(lambda: run_all(phases[len(at) :]))


def column(values, at):
    lanes = lax.broadcasted_iota(jnp.int32, values.shape, 1)
    return jnp.sum(jnp.where(lanes == at, values, 0.0), axis=1, keepdims=True)


def routing(experts, length, first_row, rows, router, routes):
    rank = lax.axis_index("tensor")
    logits = dot(rows, router, (1,), (0,))
    lanes = lax.broadcasted_iota(jnp.int32, logits.shape, 1)
    inside = lanes < experts
    top = jnp.max(jnp.where(inside, logits, -1e30), axis=1, keepdims=True)
    exps = jnp.where(inside, jnp.exp(jnp.where(inside, logits, top) - top), 0.0)
    probs = exps / jnp.sum(exps, axis=1, keepdims=True)
    position = first_row + lax.broadcasted_iota(jnp.int32, (rows.shape[0], 1), 0)
    valid = jnp.where(position < length, 1.0, 0.0)
    gate = valid * jax.nn.sigmoid(column(logits, experts))
    chosen = valid * jnp.max(jnp.where(routes == rank, 1.0, 0.0), axis=1, keepdims=True)
    prob = column(probs, rank)
    out = jnp.where(lanes == experts, gate, probs)
    out = jnp.where(lanes == experts + 1, chosen * prob, out)
    out = jnp.where(lanes == experts + 2, chosen, out)
    return jnp.where(lanes == experts + 3, prob, out)


def routing_back(experts, route, shared_dot, expert_dot):
    rank = lax.axis_index("tensor")
    lanes = lax.broadcasted_iota(jnp.int32, route.shape, 1)
    gate, chosen, prob = [column(route, experts + i) for i in (0, 2, 3)]
    expert_grad = chosen * expert_dot
    logits = route * (jnp.where(lanes == rank, expert_grad, 0.0) - expert_grad * prob)
    gate_logit = shared_dot * gate * (1.0 - gate)
    return jnp.where(lanes < experts, logits, jnp.where(lanes == experts, gate_logit, 0.0))


def ffn_kernel(transfers, at, grid_steps, experts, kind, *refs):
    refs = list(refs)

    def take(count):
        taken = refs[:count]
        del refs[:count]
        return taken

    first, last = kind == "first", kind == "last"
    rows_ref, grad_ref, route_ref, w_ref = take(4)
    before = take(1) if first else take(3)
    router_ref = take(1)[0] if first or last else None
    sent = take(len(transfers.inputs))
    hidden_ref, gate_ref, up_ref, out_ref, back_ref, dots_ref = take(6)
    if first:
        made_ref = take(1)[0]
    landed = take(transfers.moves)
    w_vmem, w_sem = take(2)
    phases = transfers.begin(sent, landed, refs)
    step = pl.program_id(0)

    def fetch(which):
        return pltpu.make_async_copy(w_ref.at[:, which], w_vmem.at[which], w_sem.at[which])

    @pl.when(step == 0)
    def _():
        for which in range(3):
            fetch(which).start()

    def weight(which):
        pl.when(step == 0)(lambda: fetch(which).wait())
        _, groups, depth, units = w_vmem.shape
        return w_vmem[which].reshape(groups * depth, units)

    def hidden_part(_):
        rows, grad = rows_ref[...], grad_ref[...]
        if first:
            length = before[0][0]
            route = routing(experts, length, step * ROW_BLOCK, rows, router_ref[...], route_ref[...])
            made_ref[...] = route
        else:
            route = route_ref[...]
        scale = column(route, experts if first else experts + 1)
        gate_w = weight(0)
        gate_act = dot(rows, gate_w, (1,), (0,))
        up_w = weight(1)
        up_act = dot(rows, up_w, (1,), (0,))
        down_w = weight(2)
        back = dot(grad, down_w, (1,), (0,))
        sigmoid = 1.0 / (1.0 + jnp.exp(-gate_act))
        silu = gate_act * sigmoid
        hidden = (silu * up_act).astype(BF).astype(F32)
        dots = jnp.sum(hidden * back, axis=1, keepdims=True)
        scaled = (scale * hidden).astype(BF)
        hidden_ref[...] = scaled
        grad_hidden = scale * back
        grad_gate = (grad_hidden * up_act * (sigmoid * (1.0 + gate_act * (1.0 - sigmoid)))).astype(BF)
        gate_ref[...] = grad_gate
        grad_up = (grad_hidden * silu).astype(BF)
        up_ref[...] = grad_up
        return gate_w, up_w, down_w, scaled, grad_gate, grad_up, route, dots

    def outer_part(state):
        gate_w, up_w, down_w, scaled, grad_gate, grad_up, route, dots = state
        moved = dot(scaled, down_w, (1,), (1,))
        turned = dot(grad_gate, gate_w, (1,), (1,)) + dot(grad_up, up_w, (1,), (1,))
        lanes = lax.broadcasted_iota(jnp.int32, route.shape, 1)
        if first:
            dots_ref[...] = jnp.where(lanes == 0, dots, 0.0)
        else:
            moved = moved + before[0][...].astype(F32)
            turned = turned + before[1][...].astype(F32)
            earlier = before[2][...]
            if last:
                wide = routing_back(experts, route, column(earlier, 0), column(earlier, 1) + dots)
                wide = wide.astype(BF)
                dots_ref[...] = wide
                turned = turned + dot(wide, router_ref[...], (1,), (1,))
            else:
                dots_ref[...] = earlier + jnp.where(lanes == 1, dots, 0.0)
        out_ref[...] = moved.astype(BF)
        back_ref[...] = turned.astype(BF)

    beside(phases, at, grid_steps, [hidden_part, outer_part])


def ffn(experts, kind, rows, grads, route, weights, before, router, transfers, at=()):
    count, width = rows.shape
    units = weights.shape[3]
    first, last = kind == "first", kind == "last"
    steps = count // ROW_BLOCK

    def block(size):
        return pl.BlockSpec((ROW_BLOCK, size), lambda i: (i, 0))

    given = list(before)
    given_specs = [block(width), block(width), block(LANES)]
    if first:
        given_specs = [pl.BlockSpec(memory_space=pltpu.SMEM)]
    if first or last:
        given.append(router)
        given_specs.append(
            pl.BlockSpec(router.shape, lambda i: (0, 0), pipeline_mode=pl.Buffered(1))
        )
    narrow = [jax.ShapeDtypeStruct((count, units), BF)] * 3
    wide = [jax.ShapeDtypeStruct((count, width), BF)] * 2
    dots = [jax.ShapeDtypeStruct((count, LANES), BF if last else F32)]
    dots += [jax.ShapeDtypeStruct((count, LANES), F32)] * first
    results = pl.pallas_call(
        functools.partial(ffn_kernel, transfers, at, steps, experts, kind),
        grid=(steps,),
        in_specs=[block(width), block(width), block(route.shape[1]), pl.BlockSpec(memory_space=pl.ANY)]
        + given_specs
        + transfers.in_specs,
        out_specs=tuple(
            [block(units)] * 3
            + [block(width)] * 2
            + [block(LANES)] * len(dots)
            + transfers.out_specs
        ),
        out_shape=tuple(narrow + wide + dots + transfers.shapes),
        scratch_shapes=[
            pltpu.VMEM((3, weights.shape[0]) + weights.shape[2:], BF),
            DMA((3,)),
        ]
        + transfers.scratch,
        compiler_params=transfers.params(),
        cost_estimate=pl.CostEstimate(
            flops=12 * count * width * units,
            bytes_accessed=2 * (3 * width * units + 4 * count * width + 3 * count * units),
            transcendentals=count * units,
        ),
    )(rows, grads, route, weights, *given, *transfers.inputs)
    made = 5 + len(dots)
    return results[:3], results[3:made], results[made:]


def ffn_grads_kernel(transfers, at, grid_steps, micros, last, *refs):
    refs = list(refs)

    def take(count):
        taken = refs[:count]
        del refs[:count]
        return taken

    per_micro = [take(6 if last else 5) for _ in range(micros)]
    sent = take(len(transfers.inputs))
    out_ref = take(1)[0]
    wide_ref = take(1)[0] if last else None
    landed = take(transfers.moves)
    phases = transfers.begin(sent, landed, refs)

    def summed(left, right):
        total = None
        for one in per_micro:
            product = dot(one[left][...], one[right][...], (0,), (0,))
            total = product if total is None else total + product
        return total

    def one_product(which):
        def part(_):
            out_ref[0, which] = summed((0, 0, 1)[which], 2 + which).astype(BF)
            if last and which == 2:
                wide_ref[...] = summed(0, 5)

        return part

    beside(phases, at, grid_steps, [one_product(which) for which in range(3)])


def ffn_grads(groups, per_micro, transfers, at=()):
    count, width = per_micro[0][0].shape
    units = per_micro[0][2].shape[1]
    last = len(per_micro[0]) == 6
    depth = width // groups
    columns = pl.BlockSpec((count, depth), lambda i: (0, i))

    def whole(size):
        return pl.BlockSpec((count, size), lambda i: (0, 0), pipeline_mode=pl.Buffered(1))

    shapes = [jax.ShapeDtypeStruct((groups, 3, depth, units), BF)]
    specs = [pl.BlockSpec((1, 3, depth, units), lambda i: (i, 0, 0, 0))]
    taken = [columns, columns] + [whole(units)] * 3
    if last:
        taken.append(whole(LANES))
        shapes.append(jax.ShapeDtypeStruct((width, LANES), F32))
        specs.append(pl.BlockSpec((depth, LANES), lambda i: (i, 0)))
    results = pl.pallas_call(
        functools.partial(ffn_grads_kernel, transfers, at, groups, len(per_micro), last),
        grid=(groups,),
        in_specs=taken * len(per_micro) + transfers.in_specs,
        out_specs=tuple(specs + transfers.out_specs),
        out_shape=tuple(shapes + transfers.shapes),
        scratch_shapes=transfers.scratch,
        compiler_params=transfers.params(),
        cost_estimate=pl.CostEstimate(
            flops=6 * len(per_micro) * count * width * units,
            bytes_accessed=2 * len(per_micro) * (2 * count * width + 3 * count * units)
            + 6 * width * units,
            transcendentals=0,
        ),
    )(*[array for one in per_micro for array in one], *transfers.inputs)
    return results[: len(shapes)], results[len(shapes) :]


def attention_grads_kernel(transfers, grid_steps, micros, *refs):
    refs = list(refs)

    def take(count):
        taken = refs[:count]
        del refs[:count]
        return taken

    per_micro = [take(4) for _ in range(micros)]
    sent = take(len(transfers.inputs))
    out_ref = take(1)[0]
    landed = take(transfers.moves)
    phases = transfers.begin(sent, landed, refs)

    def work(_):
        span = per_micro[0][2].shape[1]
        totals = [None, None]
        for one in per_micro:
            for which in range(2):
                product = dot(one[which][...], one[2 + which][...], (0,), (0,))
                totals[which] = product if totals[which] is None else totals[which] + product
        out_ref[0, :, :span] = totals[0].astype(BF)
        out_ref[0, :, span:] = totals[1].astype(BF)

    beside(phases, [(0, 0)], grid_steps, [work])


def attention_grads(groups, per_micro, transfers):
    count, width = per_micro[0][0].shape
    depth = width // groups
    spans = [per_micro[0][i].shape[1] for i in (2, 3)]
    columns = pl.BlockSpec((count, depth), lambda i: (0, i))
    whole = [
        pl.BlockSpec((count, size), lambda i: (0, 0), pipeline_mode=pl.Buffered(1)) for size in spans
    ]
    results = pl.pallas_call(
        functools.partial(attention_grads_kernel, transfers, groups, len(per_micro)),
        grid=(groups,),
        in_specs=([columns, columns] + whole) * len(per_micro) + transfers.in_specs,
        out_specs=tuple(
            [pl.BlockSpec((1, depth, sum(spans)), lambda i: (i, 0, 0))] + transfers.out_specs
        ),
        out_shape=tuple(
            [jax.ShapeDtypeStruct((groups, depth, sum(spans)), BF)] + transfers.shapes
        ),
        scratch_shapes=transfers.scratch,
        compiler_params=transfers.params(),
        cost_estimate=pl.CostEstimate(
            flops=2 * len(per_micro) * count * width * sum(spans),
            bytes_accessed=8 * len(per_micro) * count * width,
            transcendentals=0,
        ),
    )(*[array for one in per_micro for array in one], *transfers.inputs)
    return results[0], results[1:]


def opening_kernel(transfers, cut, *refs):
    refs = list(refs)

    def take(count):
        taken = refs[:count]
        del refs[:count]
        return taken

    sent, given = take(len(transfers.inputs)), take(6)
    landed, made = take(transfers.moves), take(3)
    held, packed_refs, in_sem, out_sem = take(6), take(3), take(1)[0], take(1)[0]
    phases = transfers.begin(sent, landed, refs)
    fetches = [
        pltpu.make_async_copy(source, target, in_sem.at[at])
        for at, (source, target) in enumerate(zip(given, held))
    ]
    gives = [
        pltpu.make_async_copy(source, target, out_sem.at[at])
        for at, (source, target) in enumerate(zip(packed_refs, made))
    ]
    for fetch in fetches:
        fetch.start()
    run_all(phases[:1])
    for fetch in fetches[:3]:
        fetch.wait()
    units = held[0].shape[0]
    packed_refs[0][...] = jnp.zeros_like(packed_refs[0])
    for which in range(3):
        packed_refs[0][which, :, :units] = held[which][...].T
    gives[0].start()
    for fetch in fetches[3:]:
        fetch.wait()
    for at, part in ((1, slice(0, cut)), (2, slice(cut, None))):
        packed_refs[at][0] = held[3][0, :, part]
        packed_refs[at][1] = held[4][0, :, part]
        packed_refs[at][2] = held[5][0, part, :].T
        gives[at].start()
    run_all(phases[1:])
    for give in gives:
        give.wait()


def opening(mesh_size, ident, moves, cut, shared, expert):
    transfers = Transfers(mesh_size, ident, moves)
    anywhere = pl.BlockSpec(memory_space=pl.ANY)
    units, depth = shared[0].shape
    sizes = (-(-units // LANES) * LANES, cut, expert[0].shape[2] - cut)
    shapes = [(3, depth, size) for size in sizes]
    results = pl.pallas_call(
        functools.partial(opening_kernel, transfers, cut),
        in_specs=transfers.in_specs + [anywhere] * 6,
        out_specs=tuple(transfers.out_specs + [anywhere] * 3),
        out_shape=tuple(transfers.shapes + [jax.ShapeDtypeStruct(shape, BF) for shape in shapes]),
        scratch_shapes=[pltpu.VMEM(array.shape, BF) for array in (*shared, *expert)]
        + [pltpu.VMEM(shape, BF) for shape in shapes]
        + [DMA((6,)), DMA((3,))]
        + transfers.scratch,
        compiler_params=transfers.params(),
    )(*transfers.inputs, *shared, *expert)
    return results[: transfers.moves], results[transfers.moves :]


def unpack_kernel(turned, *refs):
    count = len(refs) - 3
    for which, out_ref in enumerate(refs[count:]):
        first = 0
        for ref in refs[:count]:
            values = ref[which].astype(F32)
            if turned[which]:
                values = values.T
                size = min(values.shape[0], out_ref.shape[0] - first)
                out_ref[first : first + size, :] = values[:size]
            else:
                size = min(values.shape[1], out_ref.shape[1] - first)
                out_ref[:, first : first + size] = values[:, :size]
            first += size


def unpack(ranges, units, turned):
    depth = ranges[0].shape[1]
    vmem = pl.BlockSpec(memory_space=pltpu.VMEM)
    return pl.pallas_call(
        functools.partial(unpack_kernel, turned),
        in_specs=[vmem] * len(ranges),
        out_specs=(vmem,) * 3,
        out_shape=tuple(
            jax.ShapeDtypeStruct((units, depth) if turn else (depth, units), F32) for turn in turned
        ),
        compiler_params=pltpu.CompilerParams(vmem_limit_bytes=VMEM_BYTES),
        cost_estimate=pl.CostEstimate(flops=0, bytes_accessed=18 * depth * units, transcendentals=0),
    )(*ranges)


def rope_tables(seq_len):
    half = HD // 2
    frequency = np.float32(ROPE_BASE) ** (-(2.0 * np.arange(half, dtype=np.float32)) / HD)
    angles = np.arange(seq_len, dtype=np.float32)[:, None] * frequency[None, :].astype(np.float32)
    cosine, sine = np.cos(angles.astype(np.float64)), np.sin(angles.astype(np.float64))
    return (
        jnp.asarray(np.concatenate([cosine, cosine], axis=1).astype(np.float32)),
        jnp.asarray(np.concatenate([-sine, sine], axis=1).astype(np.float32)),
    )


def swap_halves(values):
    half = HD // 2
    return jnp.concatenate([values[:, half:], values[:, :half]], axis=1)


def block_scores(query, keys, first_row, length):
    scores = dot(query, keys, (1,), (1,)) * (HD ** (-0.5))
    rows = first_row + lax.broadcasted_iota(jnp.int32, scores.shape, 0)
    cols = lax.broadcasted_iota(jnp.int32, scores.shape, 1)
    return jnp.where((cols <= rows) & (cols < length), scores, -1e30)


def attend_kernel(heads, transfers, *refs):
    refs = list(refs)

    def take(count):
        taken = refs[:count]
        del refs[:count]
        return taken

    length_ref, x_ref, gain_ref, w_ref, bias_ref, cos_ref, sin_ref = take(7)
    sent = take(len(transfers.inputs))
    normed_ref, qkv_ref, mixed_ref, logs_ref, out_ref = take(5)
    landed = take(transfers.moves)
    rows_vmem, out_vmem, in_sem, normed_sem, out_sem = take(5)
    phases = transfers.begin(sent, landed, refs)
    seq_len, width = x_ref.shape
    groups, depth, columns = w_ref.shape
    span = heads * HD
    length = length_ref[0]
    blocks = [pl.ds(row, QB) for row in range(0, seq_len, QB)]

    def fetch(i):
        return pltpu.make_async_copy(x_ref.at[blocks[i]], rows_vmem.at[blocks[i]], in_sem.at[i])

    def keep(i):
        return pltpu.make_async_copy(rows_vmem.at[blocks[i]], normed_ref.at[blocks[i]], normed_sem.at[i])

    def give(i):
        return pltpu.make_async_copy(out_vmem.at[blocks[i]], out_ref.at[blocks[i]], out_sem.at[i])

    for i in range(len(blocks)):
        fetch(i).start()
    run_all(phases[:1])
    weights = w_ref[...].reshape(groups * depth, columns)
    qkv_w, out_w = weights[:, : 3 * span], weights[:, 3 * span :]
    for i in range(len(blocks)):
        row, end = i * QB, (i + 1) * QB
        if i >= 2:
            run_all(phases[i - 1 : i])
        fetch(i).wait()
        values = rows_vmem[row:end, :].astype(F32)
        normed = (normalize(values)[0] * gain_ref[...]).astype(BF)
        rows_vmem[row:end, :] = normed
        keep(i).start()
        pre = dot(normed, qkv_w, (1,), (0,)) + bias_ref[...]
        cosine, sine = cos_ref[row:end, :], sin_ref[row:end, :]
        for at in range(0, 3 * span, HD):
            part = pre[:, at : at + HD]
            if at < 2 * span:
                part = part * cosine + swap_halves(part) * sine
            qkv_ref[row:end, at : at + HD] = part.astype(BF)
        for head in range(heads):
            q_at, k_at, v_at = (head * HD, span + head * HD, 2 * span + head * HD)
            scores = block_scores(
                qkv_ref[row:end, q_at : q_at + HD], qkv_ref[:end, k_at : k_at + HD], row, length
            )
            top = jnp.max(scores, axis=1, keepdims=True)
            exps = jnp.exp(scores - top)
            totals = jnp.sum(exps, axis=1, keepdims=True)
            shares = exps * (1.0 / totals)
            logs_ref[row:end, head : head + 1] = top + jnp.log(totals)
            mixed = dot(shares.astype(BF), qkv_ref[:end, v_at : v_at + HD], (1,), (0,))
            mixed_ref[row:end, q_at : q_at + HD] = mixed.astype(BF)
        out_vmem[row:end, :] = dot(mixed_ref[row:end, :], out_w, (1,), (1,)).astype(BF)
        give(i).start()
    run_all(phases[max(1, len(blocks) - 1) :])
    for i in range(len(blocks)):
        keep(i).wait()
        give(i).wait()


def attend_back_kernel(heads, transfers, *refs):
    refs = list(refs)

    def take(count):
        taken = refs[:count]
        del refs[:count]
        return taken

    length_ref, datt_ref, w_ref, qkv_ref, logs_ref, cos_ref, sin_ref = take(7)
    sent = take(len(transfers.inputs))
    turned_ref, sums_ref, out_ref = take(3)
    landed = take(transfers.moves)
    rows_vmem, out_vmem, grad_vmem, key_acc, value_acc, in_sem, out_sem = take(7)
    phases = transfers.begin(sent, landed, refs)
    run_all(phases[:1])
    seq_len, width = datt_ref.shape
    groups, depth, columns = w_ref.shape
    span = heads * HD
    length = length_ref[0]
    scale = HD ** (-0.5)
    blocks = [pl.ds(row, QB) for row in range(0, seq_len, QB)]

    def fetch(i):
        return pltpu.make_async_copy(datt_ref.at[blocks[i]], rows_vmem.at[blocks[i]], in_sem.at[i])

    def give(i):
        return pltpu.make_async_copy(out_vmem.at[blocks[i]], out_ref.at[blocks[i]], out_sem.at[i])

    for i in range(len(blocks)):
        fetch(i).start()
    weights = w_ref[...].reshape(groups * depth, columns)
    qkv_w, out_w = weights[:, : 3 * span], weights[:, 3 * span :]
    key_acc[...] = jnp.zeros_like(key_acc)
    value_acc[...] = jnp.zeros_like(value_acc)
    query_sums = [jnp.zeros((1, HD), F32) for _ in range(heads)]
    for i in range(len(blocks)):
        row, end = i * QB, (i + 1) * QB
        fetch(i).wait()
        grad_vmem[row:end, :] = dot(rows_vmem[row:end, :], out_w, (1,), (0,)).astype(BF)
        for head in range(heads):
            q_at, k_at, v_at = (head * HD, span + head * HD, 2 * span + head * HD)
            query = qkv_ref[row:end, q_at : q_at + HD]
            keys = qkv_ref[:end, k_at : k_at + HD]
            grad = grad_vmem[row:end, q_at : q_at + HD]
            shares = jnp.exp(
                block_scores(query, keys, row, length) - logs_ref[row:end, head : head + 1]
            )
            grad_shares = dot(grad, qkv_ref[:end, v_at : v_at + HD], (1,), (1,))
            inner = jnp.sum(shares * grad_shares, axis=1, keepdims=True)
            grad_scores = (scale * shares * (grad_shares - inner)).astype(BF)
            turned = dot(grad_scores, keys, (1,), (0,))
            grad_query = (
                turned * cos_ref[row:end, :] - swap_halves(turned) * sin_ref[row:end, :]
            ).astype(BF)
            turned_ref[row:end, q_at : q_at + HD] = grad_query
            query_sums[head] += jnp.sum(grad_query.astype(F32), axis=0, keepdims=True)
            key_acc[:end, q_at : q_at + HD] += dot(grad_scores, query, (0,), (0,))
            value_acc[:end, q_at : q_at + HD] += dot(shares.astype(BF), grad, (0,), (0,))
    key_sums = [jnp.zeros((1, HD), F32) for _ in range(heads)]
    value_sums = [jnp.zeros((1, HD), F32) for _ in range(heads)]
    for i in range(len(blocks)):
        row, end = i * QB, (i + 1) * QB
        for head in range(heads):
            q_at, k_at, v_at = (head * HD, span + head * HD, 2 * span + head * HD)
            turned = key_acc[row:end, q_at : q_at + HD]
            grad_key = (
                turned * cos_ref[row:end, :] - swap_halves(turned) * sin_ref[row:end, :]
            ).astype(BF)
            grad_value = value_acc[row:end, q_at : q_at + HD].astype(BF)
            turned_ref[row:end, k_at : k_at + HD] = grad_key
            turned_ref[row:end, v_at : v_at + HD] = grad_value
            key_sums[head] += jnp.sum(grad_key.astype(F32), axis=0, keepdims=True)
            value_sums[head] += jnp.sum(grad_value.astype(F32), axis=0, keepdims=True)
        out_vmem[row:end, :] = dot(turned_ref[row:end, :], qkv_w, (1,), (1,)).astype(BF)
        give(i).start()
    for at, sums in enumerate(query_sums + key_sums + value_sums):
        sums_ref[:, at * HD : (at + 1) * HD] = sums
    for i in range(len(blocks)):
        give(i).wait()
    run_all(phases[1:])


def in_vmem(count):
    return [pl.BlockSpec(memory_space=pltpu.VMEM)] * count


def attend(length, rows, gain, weights, bias, cosine, sine, transfers):
    seq_len, width = rows.shape
    span = weights.shape[2] // 4
    heads, blocks = span // HD, seq_len // QB
    anywhere = pl.BlockSpec(memory_space=pl.ANY)
    results = pl.pallas_call(
        functools.partial(attend_kernel, heads, transfers),
        out_shape=tuple(
            [
                jax.ShapeDtypeStruct((seq_len, width), BF),
                jax.ShapeDtypeStruct((seq_len, 3 * span), BF),
                jax.ShapeDtypeStruct((seq_len, span), BF),
                jax.ShapeDtypeStruct((seq_len, heads), F32),
                jax.ShapeDtypeStruct((seq_len, width), BF),
            ]
            + transfers.shapes
        ),
        in_specs=[pl.BlockSpec(memory_space=pltpu.SMEM), anywhere] + in_vmem(5) + transfers.in_specs,
        out_specs=tuple([anywhere] + in_vmem(3) + [anywhere] + transfers.out_specs),
        scratch_shapes=[pltpu.VMEM((seq_len, width), BF)] * 2
        + [DMA((blocks,))] * 3
        + transfers.scratch,
        compiler_params=transfers.params(),
        cost_estimate=pl.CostEstimate(
            flops=8 * seq_len * width * span + 3 * span * seq_len * seq_len,
            bytes_accessed=8 * seq_len * width,
            transcendentals=heads * seq_len * seq_len,
        ),
    )(length, rows, gain, weights, bias, cosine, sine, *transfers.inputs)
    return results[:5], results[5:]


def attend_back(length, rows, weights, qkv, logs, cosine, sine, transfers):
    seq_len, width = rows.shape
    span = weights.shape[2] // 4
    heads, blocks = span // HD, seq_len // QB
    anywhere = pl.BlockSpec(memory_space=pl.ANY)
    results = pl.pallas_call(
        functools.partial(attend_back_kernel, heads, transfers),
        out_shape=tuple(
            [
                jax.ShapeDtypeStruct((seq_len, 3 * span), BF),
                jax.ShapeDtypeStruct((1, 3 * span), F32),
                jax.ShapeDtypeStruct((seq_len, width), BF),
            ]
            + transfers.shapes
        ),
        in_specs=[pl.BlockSpec(memory_space=pltpu.SMEM), anywhere] + in_vmem(5) + transfers.in_specs,
        out_specs=tuple(in_vmem(2) + [anywhere] + transfers.out_specs),
        scratch_shapes=[pltpu.VMEM((seq_len, width), BF)] * 2
        + [pltpu.VMEM((seq_len, span), BF)]
        + [pltpu.VMEM((seq_len, span), F32)] * 2
        + [DMA((blocks,))] * 2
        + transfers.scratch,
        compiler_params=transfers.params(),
        cost_estimate=pl.CostEstimate(
            flops=8 * seq_len * width * span + 8 * span * seq_len * seq_len,
            bytes_accessed=8 * seq_len * width,
            transcendentals=heads * seq_len * seq_len,
        ),
    )(length, rows, weights, qkv, logs, cosine, sine, *transfers.inputs)
    return results[:3], results[3:]


def padded(values, axis):
    size = values.shape[axis]
    more = -size % LANES
    if not more:
        return values
    return jnp.pad(values, [(0, more if i == axis else 0) for i in range(values.ndim)])


def packed(values, kind):
    tile = LANES * (16 if kind == BF else 8)
    values = values.astype(kind)
    return padded_to(values, -(-values.shape[-1] // tile) * tile)


def padded_to(values, size):
    more = size - values.shape[-1]
    return jnp.pad(values, [(0, 0)] * (values.ndim - 1) + [(0, more)])


def local(
    tokens,
    lengths,
    routes,
    norm1_gain,
    w_query,
    w_key,
    w_value,
    b_query,
    b_key,
    b_value,
    w_out,
    norm2_gain,
    router,
    shared_gate_vec,
    shared_gate,
    shared_up,
    shared_down,
    expert_gate,
    expert_up,
    expert_down,
    cotangent,
):
    ranks = lax.axis_size("tensor")
    groups = lax.axis_size("fsdp")
    rank = lax.axis_index("tensor")
    micros, _, rows, width = tokens.shape
    seq_len = rows * ranks
    heads = w_query.shape[1] // HD
    span = heads * HD
    experts = ranks * expert_gate.shape[0]
    shared_units = shared_gate.shape[1]
    expert_units = expert_gate.shape[2]
    cut = expert_units // (2 * LANES) * LANES
    own_first = rank * rows
    local_pos = own_first + jnp.arange(rows, dtype=jnp.int32)

    per_device = norm1_gain.shape[0]
    small = jnp.concatenate(
        [
            norm1_gain,
            norm2_gain,
            shared_gate_vec,
            router.reshape(-1),
            b_query.reshape(-1),
            b_key.reshape(-1),
            b_value.reshape(-1),
        ]
    )
    attn_own = jnp.concatenate([w_query, w_key, w_value, w_out.T], axis=1)
    mesh_size = (ranks, groups)
    (small_all, attn_w, rows_a), own_ranges = opening(
        mesh_size,
        2,
        [
            ("spread", packed(small, BF).reshape(-1, LANES)),
            ("cross_gather", attn_own),
            ("gather", tokens, (0, 0)),
        ],
        cut,
        (shared_gate.T, shared_up.T, shared_down),
        (expert_gate, expert_up, expert_down),
    )
    small_all = small_all.reshape(groups * ranks, -1)
    gain_one = small_all[:, :per_device].reshape(-1).astype(F32)
    gain_two = small_all[:, per_device : 2 * per_device].reshape(-1).astype(F32)
    gate_vec = small_all[:, 2 * per_device : 3 * per_device].reshape(-1)
    bias_at = per_device * (3 + experts)
    router_full = small_all[:, 3 * per_device : bias_at].reshape(width, experts)
    router_wide = padded_to(jnp.concatenate([router_full, gate_vec[:, None]], axis=1), LANES)
    own_bias = lax.dynamic_index_in_dim(
        small_all.reshape(groups, ranks, -1), rank, 1, False
    )[:, bias_at : small.shape[0]].reshape(groups, 3, heads, HD // groups)
    bias = own_bias.transpose(1, 2, 0, 3).reshape(1, 3 * span).astype(F32)

    weights = [lax.all_gather(own_range, "fsdp", axis=0) for own_range in own_ranges]

    cosine, sine = rope_tables(seq_len)
    idle = Transfers(mesh_size)
    token_own = [tokens[m, 0] for m in range(micros)]
    grads_own = []
    for m in range(micros):
        inside = (local_pos < lengths[m, 0])[:, None]
        grads_own.append(jnp.where(inside, cotangent[m, 0], jnp.zeros((), BF)))

    def moving(ident, *moves, needed=()):
        return Transfers(mesh_size, ident, moves, needed)

    def attention(m, token_rows, transfers):
        return attend(lengths[m], token_rows, gain_one[None], attn_w, bias, cosine, sine, transfers)

    def second_norm(m, attended):
        hidden = token_own[m].astype(F32) + attended
        unit, inverse = normalize(hidden)
        return hidden, unit, inverse, (unit * gain_two).astype(BF)

    def second_norm_back(m, state, summed):
        grad_hidden, gain_part = norm_back(summed, state[1], state[2], gain_two)
        grad_hidden = grad_hidden + grads_own[m].astype(F32)
        return grad_hidden, grad_hidden.astype(BF), gain_part

    def first_norm_back(m, grad_hidden, summed):
        unit, inverse = normalize(token_own[m].astype(F32))
        grad_inputs, gain_part = norm_back(summed, unit, inverse, gain_one)
        return (grad_inputs + grad_hidden).astype(BF), gain_part

    def finished(m, hidden, moved):
        inside = (local_pos < lengths[m, 0]).astype(F32)[:, None]
        return (inside * (hidden + moved)).astype(BF)

    att_a, (rows_b,) = attention(0, rows_a, moving(3, ("gather", tokens, (1, 0))))
    att_b, (grad_a, sum_a) = attention(
        1, rows_b, moving(4, ("gather", cotangent, (0, 0)), ("scatter", att_a[4]))
    )
    norm_a = second_norm(0, sum_a)
    two_a, sum_b = exchange(mesh_size, 5, [("gather", norm_a[3]), ("scatter", att_b[4])])
    norm_b = second_norm(1, sum_b)

    def over_groups(grads):
        flat = grads.reshape(-1, grads.shape[-1])
        summed = lax.psum_scatter(flat, "fsdp", scatter_dimension=0, tiled=True)
        return with_layout_constraint(summed, Layout((0, 1))).reshape(grads.shape[1:])

    def grads_of(which, transfers, at=()):
        per_micro = []
        for key in range(micros):
            rows_two, grads = ((two_a, grad_a), (two_b, grad_b))[key]
            scaled, gate, up = act[which, key]
            more = [(acc_a, acc_b)[key][2]] if which == 2 else []
            per_micro.append([rows_two, grads, gate, up, scaled] + more)
        return ffn_grads(groups, per_micro, transfers, at)

    act = {}
    part = functools.partial(ffn, experts)
    single = ((0, 0), (1, 0), (2, 0), (3, 0))
    act[0, 0], acc_a, (grad_b,) = part(
        "first", two_a, grad_a, routes[0, 0], weights[0], [lengths[0]], router_wide,
        moving(6, ("gather", cotangent, (1, 0))), single,
    )
    acc_a, route_a = acc_a[:3], acc_a[3]
    act[1, 0], acc_a, (two_b,) = part(
        "next", two_a, grad_a, route_a, weights[1], acc_a, None,
        moving(7, ("gather", norm_b[3])), single,
    )
    act[0, 1], acc_b, _ = part(
        "first", two_b, grad_b, routes[1, 0], weights[0], [lengths[1]], router_wide, idle
    )
    acc_b, route_b = acc_b[:3], acc_b[3]
    (grads_0,), _ = grads_of(0, idle)
    range_0 = over_groups(grads_0)
    act[2, 0], acc_a, _ = part(
        "last", two_a, grad_a, route_a, weights[2], acc_a, router_wide, moving(0, needed=[grads_0])
    )
    act[1, 1], acc_b, (down_a,) = part(
        "next", two_b, grad_b, route_b, weights[1], acc_b, None,
        moving(8, ("scatter", acc_a[1])), single,
    )
    hid_a, send_a, gain_part_a = second_norm_back(0, norm_a, down_a)
    (grads_1,), (datt_a,) = grads_of(
        1, moving(9, ("gather", send_a)), ((0, 0), (1, 0), (2, 0), (3, 0))
    )
    range_1 = over_groups(grads_1)
    act[2, 1], acc_b, (moved_a,) = part(
        "last", two_b, grad_b, route_b, weights[2], acc_b, router_wide,
        moving(10, ("scatter", acc_a[0]), needed=[grads_1]), single,
    )
    (grads_2, total_wide), (down_b,) = grads_of(
        2, moving(11, ("scatter", acc_b[1]), needed=[range_0]), ((0, 0), (1, 1), (2, 1), (3, 1))
    )
    range_2 = over_groups(grads_2)
    hid_b, send_b, gain_part_b = second_norm_back(1, norm_b, down_b)

    (grad_qkv_a, sums_a, first_a), (datt_b,) = attend_back(
        lengths[0], datt_a, attn_w, att_a[1], att_a[3], cosine, sine,
        moving(12, ("gather", send_b)),
    )
    (grad_qkv_b, sums_b, first_b), (one_a,) = attend_back(
        lengths[1], datt_b, attn_w, att_b[1], att_b[3], cosine, sine,
        moving(15, ("scatter", first_a), needed=[range_1]),
    )
    attn_parts, (one_b,) = attention_grads(
        groups,
        [
            (att_a[0], datt_a, grad_qkv_a, att_a[2]),
            (att_b[0], datt_b, grad_qkv_b, att_b[2]),
        ],
        moving(13, ("scatter", first_b)),
    )

    grad_in_a, one_part_a = first_norm_back(0, hid_a, one_a)
    grad_in_b, one_part_b = first_norm_back(1, hid_b, one_b)

    devices = groups * ranks
    bias_part = (sums_a + sums_b).reshape(3, heads, groups, HD // groups).transpose(2, 0, 1, 3)
    bias_part = bias_part.reshape(groups, 1, -1)
    own_rank = (jnp.arange(ranks, dtype=jnp.int32) == rank).astype(F32)[None, :, None]
    parts = jnp.concatenate(
        [
            (one_part_a + one_part_b).reshape(devices, -1),
            (gain_part_a + gain_part_b).reshape(devices, -1),
            total_wide[:, : experts + 1].reshape(devices, -1),
            (bias_part * own_rank).reshape(devices, -1),
        ],
        axis=1,
    )
    moved_b, attn_g, shares = exchange(
        mesh_size,
        14,
        [
            ("scatter", acc_b[0]),
            ("cross_scatter", attn_parts),
            ("share", packed(parts, F32).reshape(devices, -1, LANES)),
        ],
        [range_2],
    )
    shares = shares.reshape(-1)
    wide_g = shares[2 * per_device : (3 + experts) * per_device].reshape(per_device, experts + 1)
    bias_g = shares[bias_at : parts.shape[1]].reshape(3, heads, HD // groups)

    shared_g = unpack([range_0], shared_units, (True, True, True))
    expert_g = unpack([range_1, range_2], expert_units, (False, False, True))
    return (
        jnp.stack([finished(0, norm_a[0], moved_a), finished(1, norm_b[0], moved_b)])[:, None],
        jnp.stack([grad_in_a, grad_in_b])[:, None],
        shares[:per_device],
        attn_g[:, :span],
        attn_g[:, span : 2 * span],
        attn_g[:, 2 * span : 3 * span],
        bias_g[0],
        bias_g[1],
        bias_g[2],
        attn_g[:, 3 * span :].T,
        shares[per_device : 2 * per_device],
        wide_g[:, :experts],
        wide_g[:, experts],
        shared_g[0].T,
        shared_g[1].T,
        shared_g[2],
        expert_g[0][None],
        expert_g[1][None],
        expert_g[2][None],
    )


def solution(mesh):
    in_specs = (
        P(None, "fsdp", "tensor", None),
        P(None, "fsdp"),
        P(None, "fsdp", None, None),
        P(("fsdp", "tensor")),
        P("fsdp", "tensor"),
        P("fsdp", "tensor"),
        P("fsdp", "tensor"),
        P("tensor", "fsdp"),
        P("tensor", "fsdp"),
        P("tensor", "fsdp"),
        P("tensor", "fsdp"),
        P(("fsdp", "tensor")),
        P(("fsdp", "tensor"), None),
        P(("fsdp", "tensor")),
        P("fsdp", "tensor"),
        P("fsdp", "tensor"),
        P("tensor", "fsdp"),
        P("tensor", "fsdp", None),
        P("tensor", "fsdp", None),
        P("tensor", None, "fsdp"),
        P(None, "fsdp", "tensor", None),
    )
    out_specs = (
        P(None, "fsdp", "tensor", None),
        P(None, "fsdp", "tensor", None),
        P(("fsdp", "tensor")),
        P("fsdp", "tensor"),
        P("fsdp", "tensor"),
        P("fsdp", "tensor"),
        P("tensor", "fsdp"),
        P("tensor", "fsdp"),
        P("tensor", "fsdp"),
        P("tensor", "fsdp"),
        P(("fsdp", "tensor")),
        P(("fsdp", "tensor"), None),
        P(("fsdp", "tensor")),
        P("fsdp", "tensor"),
        P("fsdp", "tensor"),
        P("tensor", "fsdp"),
        P("tensor", "fsdp", None),
        P("tensor", "fsdp", None),
        P("tensor", None, "fsdp"),
    )
    return jax.shard_map(local, mesh=mesh, in_specs=in_specs, out_specs=out_specs, check_vma=False)
```

```python
import functools

import jax
import jax.numpy as jnp
import numpy as np
from jax import lax
from jax.experimental import pallas as pl
from jax.experimental.layout import Layout, with_layout_constraint
from jax.experimental.pallas import tpu as pltpu
from jax.sharding import PartitionSpec as P

HD = 128
EPSILON = 1e-06
ROPE_BASE = 1000000.0
BF = jnp.bfloat16
F32 = jnp.float32
MESH = pl.DeviceIdType.MESH
QB = 256
LANES = 128
CHUNKS = 2
STRIP = 16
ROW_BLOCK = 256
VMEM_BYTES = 60 << 20


def dot(left, right, left_dims, right_dims):
    return lax.dot_general(
        left, right, ((left_dims, right_dims), ((), ())), preferred_element_type=F32
    )


def normalize(values):
    inverse = lax.rsqrt(jnp.mean(values * values, axis=-1, keepdims=True) + EPSILON)
    return (values * inverse, inverse)


def norm_back(grad_normed, unit, inverse, gain):
    grad_unit = grad_normed * gain
    grad_values = inverse * (grad_unit - unit * jnp.mean(grad_unit * unit, axis=-1, keepdims=True))
    return (grad_values, jnp.sum(grad_normed * unit, axis=0))


def remote(src, dst, sems, at, target):
    return pltpu.make_async_remote_copy(
        src_ref=src,
        dst_ref=dst,
        send_sem=sems[0].at[at],
        recv_sem=sems[1].at[at],
        device_id={"tensor": target},
        device_id_type=MESH,
    )


def gather_scratch(ranks):
    chips = ranks // 2
    pair = [pltpu.SemaphoreType.DMA((chips, CHUNKS))] * 2
    cross = [pltpu.SemaphoreType.DMA((2 * chips, CHUNKS))] * 2
    return [pltpu.SemaphoreType.DMA] + pair + pair + cross


def gather_steps(place, block, whole, local_sem, up_s, up_r, down_s, down_r, cross_s, cross_r):
    chips, chip, core = place.chips, place.chip, place.core
    rows = block.shape[0]
    part = rows // CHUNKS
    up, down, cross = (up_s, up_r), (down_s, down_r), (cross_s, cross_r)

    def at(owner, chunk):
        first = pl.multiple_of((2 * owner + core) * rows + chunk * part, part)
        return whole.at[pl.ds(first, part)]

    def theirs(owner, chunk):
        first = pl.multiple_of((2 * owner + 1 - core) * rows + chunk * part, part)
        return whole.at[pl.ds(first, part)]

    def own(chunk):
        return block.at[pl.ds(chunk * part, part)]

    def upward(step, chunk):
        source = own(chunk) if step == 0 else at(chip - step, chunk)
        return remote(source, at(chip - step, chunk), up, (step, chunk), place.above)

    def downward(step, chunk):
        source = own(chunk) if step == 0 else at(chip + step, chunk)
        return remote(source, at(chip + step, chunk), down, (step, chunk), place.below)

    def across(slot, owner, chunk):
        source = own(chunk) if slot == 0 else at(owner, chunk)
        return remote(source, at(owner, chunk), cross, (slot, chunk), place.partner)

    def arrived(slot, owner, chunk):
        return remote(theirs(owner, chunk), theirs(owner, chunk), cross, (slot, chunk), place.partner)

    def arrived_up(step, chunk):
        return remote(at(chip - step, chunk), at(chip - step, chunk), up, (step - 1, chunk), place.above)

    def arrived_down(step, chunk):
        return remote(at(chip + step, chunk), at(chip + step, chunk), down, (step - 1, chunk), place.below)

    both = range(CHUNKS)

    def mine():
        first = pl.multiple_of((2 * chip + core) * rows, rows)
        return pltpu.make_async_copy(block, whole.at[pl.ds(first, rows)], local_sem)

    def begin():
        for chunk in both:
            pl.when(place.not_top)(lambda: upward(0, chunk).start())
            pl.when(place.not_bottom)(lambda: downward(0, chunk).start())
        for chunk in both:
            across(0, chip, chunk).start()
        mine().start()

    def hop(step, chunk):
        @pl.when(chip >= step)
        def _():
            arrived_up(step, chunk).wait_recv()
            pl.when(place.not_top)(lambda: upward(step, chunk).start())
            across(2 * step - 1, chip - step, chunk).start()

        @pl.when(chip < chips - step)
        def _():
            arrived_down(step, chunk).wait_recv()
            pl.when(place.not_bottom)(lambda: downward(step, chunk).start())
            across(2 * step, chip + step, chunk).start()

    def end():
        mine().wait()
        for step in range(chips):
            for chunk in both:
                if step == 0:
                    arrived(0, chip, chunk).wait_recv()
                    across(0, chip, chunk).wait_send()
                else:

                    @pl.when(chip >= step)
                    def _():
                        arrived(2 * step - 1, chip - step, chunk).wait_recv()
                        across(2 * step - 1, chip - step, chunk).wait_send()

                    @pl.when(chip < chips - step)
                    def _():
                        arrived(2 * step, chip + step, chunk).wait_recv()
                        across(2 * step, chip + step, chunk).wait_send()

                @pl.when(place.not_top & (chip >= step))
                def _():
                    upward(step, chunk).wait_send()

                @pl.when(place.not_bottom & (chip < chips - step))
                def _():
                    downward(step, chunk).wait_send()

    hops = [functools.partial(hop, step, chunk) for step in range(1, chips) for chunk in both]
    return [begin] + hops + [end]


def scatter_scratch(ranks, rows, width):
    chips = ranks // 2
    line = [pltpu.SemaphoreType.DMA((chips, CHUNKS))] * 2
    buffers = [pltpu.VMEM((chips, rows, width), BF)] * 5
    return buffers + [pltpu.SemaphoreType.DMA((chips,))] + line * 3


def scatter_steps(
    place, partial, total, kept, pair, held, up_in, down_in, keep_sem,
    up_s, up_r, down_s, down_r, cross_s, cross_r,
):
    chips, chip, core = place.chips, place.chip, place.core
    rows = total.shape[0]
    part = rows // CHUNKS
    up, down, cross = (up_s, up_r), (down_s, down_r), (cross_s, cross_r)
    both = range(CHUNKS)

    def keep(k):
        first = pl.multiple_of((2 * k + core) * rows, rows)
        return pltpu.make_async_copy(partial.at[pl.ds(first, rows)], kept.at[k], keep_sem.at[k])

    def across(k, chunk):
        first = pl.multiple_of((2 * k + 1 - core) * rows + chunk * part, part)
        return remote(
            partial.at[pl.ds(first, part)],
            pair.at[k, pl.ds(chunk * part, part)],
            cross,
            (k, chunk),
            place.partner,
        )

    def upward(step, k, chunk):
        cut = pl.ds(chunk * part, part)
        return remote(held.at[k, cut], up_in.at[step, cut], up, (step, chunk), place.above)

    def downward(step, k, chunk):
        cut = pl.ds(chunk * part, part)
        return remote(held.at[k, cut], down_in.at[step, cut], down, (step, chunk), place.below)

    def add(k, chunk, target, others):
        def strip(i, carry):
            cut = pl.ds(chunk * part + i * STRIP, STRIP)
            value = kept[k, cut].astype(F32) + pair[k, cut].astype(F32)
            for ref, slot in others:
                value = value + ref[slot, cut].astype(F32)
            if target is None:
                total[cut] = value
            else:
                target[k, cut] = value.astype(BF)
            return carry

        lax.fori_loop(0, part // STRIP, strip, 0)

    order = []
    for i in range(chips):
        for k in (chips - 1 - i, i):
            if k not in order:
                order.append(k)
    def begin():
        for k in order:
            keep(k).start()
            for chunk in both:
                across(k, chunk).start()

    def hop(step, chunk):
        @pl.when(place.not_top & (chip <= step - 1))
        def _():
            k = chip + chips - step
            if chunk == 0:
                keep(k).wait()
            across(k, chunk).wait_recv()

            @pl.when(place.not_bottom)
            def _():
                upward(step - 1, k, chunk).wait_recv()
                add(k, chunk, held, [(up_in, step - 1)])

            pl.when(jnp.logical_not(place.not_bottom))(lambda: add(k, chunk, held, []))
            upward(step, k, chunk).start()

        @pl.when(place.not_bottom & (chip >= chips - step))
        def _():
            k = chip - (chips - step)
            if chunk == 0:
                keep(k).wait()
            across(k, chunk).wait_recv()

            @pl.when(place.not_top)
            def _():
                downward(step - 1, k, chunk).wait_recv()
                add(k, chunk, held, [(down_in, step - 1)])

            pl.when(jnp.logical_not(place.not_top))(lambda: add(k, chunk, held, []))
            downward(step, k, chunk).start()

    last = chips - 1

    def add_last(chunk):
        if chunk == 0:
            keep(chip).wait()
        across(chip, chunk).wait_recv()

        @pl.when(place.not_top & place.not_bottom)
        def _():
            upward(last, chip, chunk).wait_recv()
            downward(last, chip, chunk).wait_recv()
            add(chip, chunk, None, [(up_in, last), (down_in, last)])

        @pl.when(jnp.logical_not(place.not_top))
        def _():
            upward(last, chip, chunk).wait_recv()
            add(chip, chunk, None, [(up_in, last)])

        @pl.when(jnp.logical_not(place.not_bottom))
        def _():
            downward(last, chip, chunk).wait_recv()
            add(chip, chunk, None, [(down_in, last)])

    def end():
        for chunk in both:
            for k in range(chips):
                across(k, chunk).wait_send()
            for step in range(1, chips):

                @pl.when(place.not_top & (chip <= step - 1))
                def _():
                    upward(step, chip + chips - step, chunk).wait_send()

                @pl.when(place.not_bottom & (chip >= chips - step))
                def _():
                    downward(step, chip - (chips - step), chunk).wait_send()

    def first():
        begin()
        for chunk in both:
            hop(1, chunk)

    hops = [functools.partial(hop, step, chunk) for step in range(2, chips) for chunk in both]
    return [first] + hops + [functools.partial(add_last, chunk) for chunk in both] + [end]


class Place:
    def __init__(self, ranks, groups):
        rank, group = lax.axis_index("tensor"), lax.axis_index("fsdp")
        self.ranks, self.groups = ranks, groups
        self.chips = ranks // 2
        self.chip, self.core = rank // 2, rank % 2
        self.partner = rank + 1 - 2 * self.core
        self.above, self.below = rank + 2, rank - 2
        self.not_top = self.chip < self.chips - 1
        self.not_bottom = self.chip > 0
        self.rank, self.group = rank, group
        self.device = group * ranks + rank
        near, far = group % 2, group // 2
        self.beside = 2 * far + 1 - near
        self.across = 2 * (1 - far) + near
        self.opposite = 2 * (1 - far) + 1 - near
        self.square = groups == 4

    def name(self, device):
        return {"fsdp": device // self.ranks, "tensor": device % self.ranks}

    def meet(self, line, cross, everyone):
        barrier = pltpu.get_barrier_semaphore()

        def greet(name):
            pl.semaphore_signal(barrier, 1, device_id=name, device_id_type=MESH)

        if everyone:
            devices = self.groups * self.ranks

            def one(i, carry):
                greet(self.name(lax.rem(self.device + i, devices)))
                return carry

            lax.fori_loop(1, devices, one, 0)
            pl.semaphore_wait(barrier, devices - 1)
            return
        peers = 0
        if line:
            greet({"tensor": self.partner})
            pl.when(self.not_top)(lambda: greet({"tensor": self.above}))
            pl.when(self.not_bottom)(lambda: greet({"tensor": self.below}))
            peers = 1 + self.not_top.astype(jnp.int32) + self.not_bottom.astype(jnp.int32)
        if cross and self.square:
            greet({"fsdp": self.beside})
            greet({"fsdp": self.across})
            peers = peers + 2
        elif cross:
            for i in range(1, self.groups):
                greet({"fsdp": lax.rem(self.group + i, self.groups)})
            peers = peers + self.groups - 1
        pl.semaphore_wait(barrier, peers)


def to_group(src, dst, send, recv, at, target):
    return pltpu.make_async_remote_copy(
        src_ref=src,
        dst_ref=dst,
        send_sem=send.at[at],
        recv_sem=recv.at[at],
        device_id={"fsdp": target},
        device_id_type=MESH,
    )


def cross_gather_steps(place, block, whole, own_sem, send, recv):
    group = place.group
    half = block.shape[0] // 2

    def own():
        return pltpu.make_async_copy(block, whole.at[group], own_sem)

    if not place.square:

        def direct(i):
            target = lax.rem(group + i, place.groups)
            return to_group(block, whole.at[group], send, recv, i - 1, target)

        def begin_direct():
            own().start()
            for i in range(1, place.groups):
                direct(i).start()

        def end_direct():
            own().wait()
            for i in range(1, place.groups):
                source = lax.rem(group - i + place.groups, place.groups)
                to_group(block, whole.at[source], send, recv, i - 1, source).wait_recv()
                direct(i).wait_send()

        return [begin_direct, end_direct]

    def near(at):
        return to_group(block, whole.at[group], send, recv, at, (place.beside, place.across)[at])

    def came(at):
        source = (place.beside, place.across)[at]
        return to_group(whole.at[source], whole.at[source], send, recv, at, source)

    def forward(at):
        source, target = ((place.beside, place.across), (place.across, place.beside))[at]
        piece = whole.at[source, pl.ds(at * half, half)]
        return to_group(piece, piece, send, recv, 2 + at, target)

    def far(at):
        piece = whole.at[place.opposite, pl.ds(at * half, half)]
        return to_group(piece, piece, send, recv, 2 + at, place.opposite)

    def begin():
        for at in range(2):
            near(at).start()
        own().start()

    def pass_on():
        for at in range(2):
            came(at).wait_recv()
            forward(at).start()

    def end():
        own().wait()
        for at in range(2):
            far(at).wait_recv()
            near(at).wait_send()
            forward(at).wait_send()

    return [begin] + [nothing] * 4 + [pass_on, nothing, end]


def cross_scatter_steps(place, partial, total, mine, near_in, far_in, own_sem, send, recv):
    group = place.group
    rows = total.shape[0]
    half = rows // 2

    def own():
        return pltpu.make_async_copy(partial, mine, own_sem)

    def loop(count, body):
        def strip(i, carry):
            body(pl.ds(i * STRIP, STRIP))
            return carry

        lax.fori_loop(0, count // STRIP, strip, 0)

    if not place.square:

        def direct(i):
            target = lax.rem(group + i, place.groups)
            return to_group(partial.at[target], near_in.at[group], send, recv, i - 1, target)

        def begin_direct():
            own().start()
            for i in range(1, place.groups):
                direct(i).start()

        def sum_direct(cut):
            value = mine[group, cut].astype(F32)
            for i in range(1, place.groups):
                value = value + near_in[lax.rem(group + i, place.groups), cut].astype(F32)
            total[cut] = value

        def end_direct():
            own().wait()
            for i in range(1, place.groups):
                source = lax.rem(group - i + place.groups, place.groups)
                piece = partial.at[source]
                to_group(piece, near_in.at[source], send, recv, i - 1, source).wait_recv()
            loop(rows, sum_direct)
            for i in range(1, place.groups):
                direct(i).wait_send()

        return [begin_direct, end_direct]

    def first(at):
        target = (place.beside, place.across)[at]
        piece = partial.at[place.opposite, pl.ds(at * half, half)]
        return to_group(piece, far_in.at[at], send, recv, at, target)

    def second(at):
        target = (place.beside, place.across)[at]
        return to_group(mine.at[target], near_in.at[at], send, recv, 2 + at, target)

    def begin():
        own().start()
        for at in range(2):
            first(at).start()

    def join():
        own().wait()
        for at in range(2):
            target = (place.across, place.beside)[at]
            first(at).wait_recv()

            def one(cut, at=at, target=target):
                place_in = pl.ds(at * half + cut.start, STRIP)
                value = mine[target, place_in].astype(F32) + far_in[at, cut].astype(F32)
                mine[target, place_in] = value.astype(BF)

            loop(half, one)
            second(1 - at).start()

    def everything(cut):
        value = mine[group, cut].astype(F32) + near_in[0, cut].astype(F32)
        total[cut] = value + near_in[1, cut].astype(F32)

    def end():
        for at in range(2):
            second(at).wait_recv()
        loop(rows, everything)
        for at in range(2):
            first(at).wait_send()
            second(at).wait_send()

    return [begin, nothing, join, nothing, nothing, end]


def everyone_steps(place, piece_for, landing, own_sem, send, recv):
    devices = place.groups * place.ranks
    me = place.device

    def copy(i):
        target = lax.rem(me + i, devices)
        return pltpu.make_async_remote_copy(
            src_ref=piece_for(target),
            dst_ref=landing.at[me],
            send_sem=send.at[i],
            recv_sem=recv.at[i],
            device_id=place.name(target),
            device_id_type=MESH,
        )

    def arrival(i):
        source = lax.rem(me - i + devices, devices)
        return pltpu.make_async_remote_copy(
            src_ref=landing.at[source],
            dst_ref=landing.at[source],
            send_sem=send.at[i],
            recv_sem=recv.at[i],
            device_id=place.name(source),
            device_id_type=MESH,
        )

    def start(i, carry):
        copy(i).start()
        return carry

    def finish_one(i, carry):
        arrival(i).wait_recv()
        copy(i).wait_send()
        return carry

    def own():
        return pltpu.make_async_copy(piece_for(me), landing.at[me], own_sem)

    def begin():
        own().start()
        lax.fori_loop(1, devices, start, 0)

    def end():
        own().wait()
        lax.fori_loop(1, devices, finish_one, 0)

    return [begin, nothing, end]


def spread_steps(place, value, everyone, own_sem, send, recv):
    return everyone_steps(place, lambda target: value, everyone, own_sem, send, recv)


def share_steps(place, values, total, landing, own_sem, send, recv):
    phases = everyone_steps(place, lambda target: values.at[target], landing, own_sem, send, recv)

    def add_up():
        total[...] = jnp.sum(landing[...], axis=0)

    return phases + [add_up]


DMA = pltpu.SemaphoreType.DMA


class Transfers:
    def __init__(self, mesh_size, ident=0, moves=(), needed=()):
        self.ranks, self.groups = mesh_size
        self.ident = ident
        self.kinds = [move[0] for move in moves]
        self.parts = [move[2] if len(move) > 2 else None for move in moves]
        self.inputs = [move[1] for move in moves] + list(needed)
        self.moves = len(self.kinds)
        anywhere = pl.BlockSpec(memory_space=pl.ANY)
        vmem = pl.BlockSpec(memory_space=pltpu.VMEM)
        self.in_specs = [anywhere] * len(self.inputs)
        self.shapes, self.out_specs, self.scratch, self.counts = [], [], [], []
        for kind, array, *part in moves:
            shape, spec = array.shape[len(part[0]) :] if part else array.shape, anywhere
            if kind == "gather":
                shape, dtype = (self.ranks * shape[0], shape[1]), BF
                scratch = gather_scratch(self.ranks)
            elif kind == "scatter":
                shape, dtype, spec = (shape[0] // self.ranks, shape[1]), F32, vmem
                scratch = scatter_scratch(self.ranks, *shape)
            elif kind == "cross_gather":
                shape, dtype = (self.groups,) + shape, BF
                scratch = [DMA, DMA((max(4, self.groups),)), DMA((max(4, self.groups),))]
            elif kind == "cross_scatter":
                rest = shape[1:]
                square = self.groups == 4
                near = (2 if square else self.groups,) + rest
                scratch = [
                    pltpu.VMEM(shape, BF),
                    pltpu.VMEM(near, BF),
                    pltpu.VMEM((2, rest[0] // 2) + rest[1:], BF),
                    DMA,
                    DMA((max(4, self.groups),)),
                    DMA((max(4, self.groups),)),
                ]
                shape, dtype, spec = rest, F32, vmem
            elif kind == "share":
                devices = self.ranks * self.groups
                scratch = [pltpu.VMEM(shape, F32), DMA, DMA((devices,)), DMA((devices,))]
                shape, dtype, spec = shape[1:], F32, vmem
            else:
                devices = self.ranks * self.groups
                shape, dtype = (devices,) + shape, array.dtype
                scratch = [DMA, DMA((devices,)), DMA((devices,))]
            self.shapes.append(jax.ShapeDtypeStruct(shape, dtype))
            self.out_specs.append(spec)
            self.scratch += scratch
            self.counts.append(len(scratch))

    def params(self):
        if not self.moves:
            return pltpu.CompilerParams(vmem_limit_bytes=VMEM_BYTES)
        return pltpu.CompilerParams(
            collective_id=self.ident, has_side_effects=True, vmem_limit_bytes=VMEM_BYTES
        )

    def begin(self, inputs, outputs, scratch):
        if not self.moves:
            return []
        steps_of = {
            "gather": gather_steps,
            "scatter": scatter_steps,
            "cross_gather": cross_gather_steps,
            "cross_scatter": cross_scatter_steps,
            "spread": spread_steps,
            "share": share_steps,
        }
        place = Place(self.ranks, self.groups)
        scratch = list(scratch)
        lines = []
        for i, kind in enumerate(self.kinds):
            taken, scratch = scratch[: self.counts[i]], scratch[self.counts[i] :]
            given = inputs[i] if self.parts[i] is None else inputs[i].at[self.parts[i]]
            lines.append(steps_of[kind](place, given, outputs[i], *taken))

        def phase(number):
            if number == 0:
                kinds = set(self.kinds)
                place.meet(
                    bool(kinds & {"gather", "scatter"}),
                    bool(kinds & {"cross_gather", "cross_scatter"}),
                    bool(kinds & {"spread", "share"}),
                )
            for steps in lines:
                if number < len(steps):
                    steps[number]()

        return [functools.partial(phase, i) for i in range(max(map(len, lines)))]


def nothing():
    pass


def run_all(phases):
    for phase in phases:
        phase()


def exchange_kernel(transfers, *refs):
    count, moves = len(transfers.inputs), transfers.moves
    run_all(transfers.begin(refs[:moves], refs[count : count + moves], refs[count + moves :]))


def exchange(mesh_size, ident, moves, needed=()):
    transfers = Transfers(mesh_size, ident, moves, needed)
    return pl.pallas_call(
        functools.partial(exchange_kernel, transfers),
        out_shape=tuple(transfers.shapes),
        in_specs=transfers.in_specs,
        out_specs=tuple(transfers.out_specs),
        scratch_shapes=transfers.scratch,
        compiler_params=transfers.params(),
    )(*transfers.inputs)


def beside(phases, at, grid_steps, parts):
    step = pl.program_id(0)
    state = None
    for number, part in enumerate(parts):
        for phase, (when, ahead_of) in zip(phases, at):
            if ahead_of == number:
                pl.when(step == when)(phase)
        state = part(state)
    if phases:
        pl.when(step == grid_steps - 1)(lambda: run_all(phases[len(at) :]))


def column(values, at):
    lanes = lax.broadcasted_iota(jnp.int32, values.shape, 1)
    return jnp.sum(jnp.where(lanes == at, values, 0.0), axis=1, keepdims=True)


def routing(experts, length, first_row, rows, router, routes):
    rank = lax.axis_index("tensor")
    logits = dot(rows, router, (1,), (0,))
    lanes = lax.broadcasted_iota(jnp.int32, logits.shape, 1)
    inside = lanes < experts
    top = jnp.max(jnp.where(inside, logits, -1e30), axis=1, keepdims=True)
    exps = jnp.where(inside, jnp.exp(jnp.where(inside, logits, top) - top), 0.0)
    probs = exps / jnp.sum(exps, axis=1, keepdims=True)
    position = first_row + lax.broadcasted_iota(jnp.int32, (rows.shape[0], 1), 0)
    valid = jnp.where(position < length, 1.0, 0.0)
    gate = valid * jax.nn.sigmoid(column(logits, experts))
    named = jnp.max(jnp.where(routes == rank, 1.0, 0.0), axis=0, keepdims=True)
    chosen = valid * jnp.broadcast_to(named, (8, rows.shape[0])).T[:, :1]
    prob = column(probs, rank)
    out = jnp.where(lanes == experts, gate, probs)
    out = jnp.where(lanes == experts + 1, chosen * prob, out)
    out = jnp.where(lanes == experts + 2, chosen, out)
    return jnp.where(lanes == experts + 3, prob, out)


def routing_back(experts, route, shared_dot, expert_dot):
    rank = lax.axis_index("tensor")
    lanes = lax.broadcasted_iota(jnp.int32, route.shape, 1)
    gate, chosen, prob = [column(route, experts + i) for i in (0, 2, 3)]
    expert_grad = chosen * expert_dot
    logits = route * (jnp.where(lanes == rank, expert_grad, 0.0) - expert_grad * prob)
    gate_logit = shared_dot * gate * (1.0 - gate)
    return jnp.where(lanes < experts, logits, jnp.where(lanes == experts, gate_logit, 0.0))


def ffn_kernel(transfers, at, grid_steps, experts, kind, *refs):
    refs = list(refs)

    def take(count):
        taken = refs[:count]
        del refs[:count]
        return taken

    first, last = kind == "first", kind == "last"
    rows_ref, grad_ref, route_ref, w_ref = take(4)
    before = take(1) if first else take(3)
    router_ref = take(1)[0] if first or last else None
    sent = take(len(transfers.inputs))
    hidden_ref, gate_ref, up_ref, out_ref, back_ref, dots_ref = take(6)
    if first:
        made_ref = take(1)[0]
    landed = take(transfers.moves)
    w_vmem, w_sem = take(2)
    phases = transfers.begin(sent, landed, refs)
    step = pl.program_id(0)

    def weights():
        return pltpu.make_async_copy(w_ref, w_vmem, w_sem)

    pl.when(step == 0)(lambda: weights().start())

    def hidden_part(_):
        pl.when(step == 0)(lambda: weights().wait())
        groups, _, depth, units = w_vmem.shape
        gate_w, up_w, down_w = [w_vmem[:, i].reshape(groups * depth, units) for i in range(3)]
        rows, grad = rows_ref[...], grad_ref[...]
        if first:
            length = before[0][0]
            route = routing(experts, length, step * ROW_BLOCK, rows, router_ref[...], route_ref[...])
            made_ref[...] = route
        else:
            route = route_ref[...]
        scale = column(route, experts if first else experts + 1)
        gate_act = dot(rows, gate_w, (1,), (0,))
        up_act = dot(rows, up_w, (1,), (0,))
        back = dot(grad, down_w, (1,), (0,))
        sigmoid = 1.0 / (1.0 + jnp.exp(-gate_act))
        silu = gate_act * sigmoid
        hidden = (silu * up_act).astype(BF).astype(F32)
        dots = jnp.sum(hidden * back, axis=1, keepdims=True)
        scaled = (scale * hidden).astype(BF)
        hidden_ref[...] = scaled
        grad_hidden = scale * back
        grad_gate = (grad_hidden * up_act * (sigmoid * (1.0 + gate_act * (1.0 - sigmoid)))).astype(BF)
        gate_ref[...] = grad_gate
        grad_up = (grad_hidden * silu).astype(BF)
        up_ref[...] = grad_up
        return gate_w, up_w, down_w, scaled, grad_gate, grad_up, route, dots

    def outer_part(state):
        gate_w, up_w, down_w, scaled, grad_gate, grad_up, route, dots = state
        moved = dot(scaled, down_w, (1,), (1,))
        turned = dot(grad_gate, gate_w, (1,), (1,)) + dot(grad_up, up_w, (1,), (1,))
        lanes = lax.broadcasted_iota(jnp.int32, route.shape, 1)
        if first:
            dots_ref[...] = jnp.where(lanes == 0, dots, 0.0)
        else:
            moved = moved + before[0][...].astype(F32)
            turned = turned + before[1][...].astype(F32)
            earlier = before[2][...]
            if last:
                wide = routing_back(experts, route, column(earlier, 0), column(earlier, 1) + dots)
                wide = wide.astype(BF)
                dots_ref[...] = wide
                turned = turned + dot(wide, router_ref[...], (1,), (1,))
            else:
                dots_ref[...] = earlier + jnp.where(lanes == 1, dots, 0.0)
        out_ref[...] = moved.astype(BF)
        back_ref[...] = turned.astype(BF)

    beside(phases, at, grid_steps, [hidden_part, outer_part])


def ffn(experts, kind, rows, grads, route, weights, before, router, transfers, at=()):
    count, width = rows.shape
    units = weights.shape[3]
    first, last = kind == "first", kind == "last"
    steps = count // ROW_BLOCK

    def block(size):
        return pl.BlockSpec((ROW_BLOCK, size), lambda i: (i, 0))

    given = list(before)
    given_specs = [block(width), block(width), block(LANES)]
    if first:
        given_specs = [pl.BlockSpec(memory_space=pltpu.SMEM)]
    if first or last:
        given.append(router)
        given_specs.append(
            pl.BlockSpec(router.shape, lambda i: (0, 0), pipeline_mode=pl.Buffered(1))
        )
    narrow = [jax.ShapeDtypeStruct((count, units), BF)] * 3
    wide = [jax.ShapeDtypeStruct((count, width), BF)] * 2
    dots = [jax.ShapeDtypeStruct((count, LANES), BF if last else F32)]
    dots += [jax.ShapeDtypeStruct((count, LANES), F32)] * first
    results = pl.pallas_call(
        functools.partial(ffn_kernel, transfers, at, steps, experts, kind),
        grid=(steps,),
        in_specs=[
            block(width),
            block(width),
            pl.BlockSpec((route.shape[0], ROW_BLOCK), lambda i: (0, i)) if first else block(LANES),
            pl.BlockSpec(memory_space=pl.ANY),
        ]
        + given_specs
        + transfers.in_specs,
        out_specs=tuple(
            [block(units)] * 3
            + [block(width)] * 2
            + [block(LANES)] * len(dots)
            + transfers.out_specs
        ),
        out_shape=tuple(narrow + wide + dots + transfers.shapes),
        scratch_shapes=[pltpu.VMEM(weights.shape, BF), DMA] + transfers.scratch,
        compiler_params=transfers.params(),
        cost_estimate=pl.CostEstimate(
            flops=12 * count * width * units,
            bytes_accessed=2 * (3 * width * units + 4 * count * width + 3 * count * units),
            transcendentals=count * units,
        ),
    )(rows, grads, route, weights, *given, *transfers.inputs)
    made = 5 + len(dots)
    return results[:3], results[3:made], results[made:]


def ffn_grads_kernel(transfers, at, grid_steps, micros, last, *refs):
    refs = list(refs)

    def take(count):
        taken = refs[:count]
        del refs[:count]
        return taken

    per_micro = [take(6 if last else 5) for _ in range(micros)]
    sent = take(len(transfers.inputs))
    out_ref = take(1)[0]
    wide_ref = take(1)[0] if last else None
    landed = take(transfers.moves)
    phases = transfers.begin(sent, landed, refs)

    def summed(left, right):
        total = None
        for one in per_micro:
            product = dot(one[left][...], one[right][...], (0,), (0,))
            total = product if total is None else total + product
        return total

    def one_product(which):
        def part(_):
            out_ref[0, which] = summed((0, 0, 1)[which], 2 + which).astype(BF)
            if last and which == 2:
                wide_ref[...] = summed(0, 5)

        return part

    beside(phases, at, grid_steps, [one_product(which) for which in range(3)])


def ffn_grads(groups, per_micro, transfers, at=()):
    count, width = per_micro[0][0].shape
    units = per_micro[0][2].shape[1]
    last = len(per_micro[0]) == 6
    depth = width // groups
    columns = pl.BlockSpec((count, depth), lambda i: (0, i))

    def whole(size):
        return pl.BlockSpec((count, size), lambda i: (0, 0), pipeline_mode=pl.Buffered(1))

    shapes = [jax.ShapeDtypeStruct((groups, 3, depth, units), BF)]
    specs = [pl.BlockSpec((1, 3, depth, units), lambda i: (i, 0, 0, 0))]
    taken = [columns, columns] + [whole(units)] * 3
    if last:
        taken.append(whole(LANES))
        shapes.append(jax.ShapeDtypeStruct((width, LANES), F32))
        specs.append(pl.BlockSpec((depth, LANES), lambda i: (i, 0)))
    results = pl.pallas_call(
        functools.partial(ffn_grads_kernel, transfers, at, groups, len(per_micro), last),
        grid=(groups,),
        in_specs=taken * len(per_micro) + transfers.in_specs,
        out_specs=tuple(specs + transfers.out_specs),
        out_shape=tuple(shapes + transfers.shapes),
        scratch_shapes=transfers.scratch,
        compiler_params=transfers.params(),
        cost_estimate=pl.CostEstimate(
            flops=6 * len(per_micro) * count * width * units,
            bytes_accessed=2 * len(per_micro) * (2 * count * width + 3 * count * units)
            + 6 * width * units,
            transcendentals=0,
        ),
    )(*[array for one in per_micro for array in one], *transfers.inputs)
    return results[: len(shapes)], results[len(shapes) :]


def attention_grads_kernel(transfers, grid_steps, micros, *refs):
    refs = list(refs)

    def take(count):
        taken = refs[:count]
        del refs[:count]
        return taken

    per_micro = [take(4) for _ in range(micros)]
    sent = take(len(transfers.inputs))
    out_ref = take(1)[0]
    landed = take(transfers.moves)
    phases = transfers.begin(sent, landed, refs)

    def work(_):
        span = per_micro[0][2].shape[1]
        totals = [None, None]
        for one in per_micro:
            for which in range(2):
                product = dot(one[which][...], one[2 + which][...], (0,), (0,))
                totals[which] = product if totals[which] is None else totals[which] + product
        out_ref[0, :, :span] = totals[0].astype(BF)
        out_ref[0, :, span:] = totals[1].astype(BF)

    beside(phases, [(0, 0), (grid_steps - 1, 0)], grid_steps, [work])


def attention_grads(groups, per_micro, transfers):
    count, width = per_micro[0][0].shape
    depth = width // groups
    spans = [per_micro[0][i].shape[1] for i in (2, 3)]
    columns = pl.BlockSpec((count, depth), lambda i: (0, i))
    whole = [
        pl.BlockSpec((count, size), lambda i: (0, 0), pipeline_mode=pl.Buffered(1)) for size in spans
    ]
    results = pl.pallas_call(
        functools.partial(attention_grads_kernel, transfers, groups, len(per_micro)),
        grid=(groups,),
        in_specs=([columns, columns] + whole) * len(per_micro) + transfers.in_specs,
        out_specs=tuple(
            [pl.BlockSpec((1, depth, sum(spans)), lambda i: (i, 0, 0))] + transfers.out_specs
        ),
        out_shape=tuple(
            [jax.ShapeDtypeStruct((groups, depth, sum(spans)), BF)] + transfers.shapes
        ),
        scratch_shapes=transfers.scratch,
        compiler_params=transfers.params(),
        cost_estimate=pl.CostEstimate(
            flops=2 * len(per_micro) * count * width * sum(spans),
            bytes_accessed=8 * len(per_micro) * count * width,
            transcendentals=0,
        ),
    )(*[array for one in per_micro for array in one], *transfers.inputs)
    return results[0], results[1:]


def opening_kernel(transfers, cut, *refs):
    refs = list(refs)

    def take(count):
        taken = refs[:count]
        del refs[:count]
        return taken

    sent, given = take(len(transfers.inputs)), take(6)
    landed, made = take(transfers.moves), take(3)
    held, packed_refs, in_sem, out_sem = take(6), take(3), take(1)[0], take(1)[0]
    phases = transfers.begin(sent, landed, refs)
    fetches = [
        pltpu.make_async_copy(source, target, in_sem.at[at])
        for at, (source, target) in enumerate(zip(given, held))
    ]
    gives = [
        pltpu.make_async_copy(source, target, out_sem.at[at])
        for at, (source, target) in enumerate(zip(packed_refs, made))
    ]
    for fetch in fetches:
        fetch.start()
    run_all(phases[:1])
    for fetch in fetches[:3]:
        fetch.wait()
    units = held[0].shape[0]
    packed_refs[0][...] = jnp.zeros_like(packed_refs[0])
    for which in range(3):
        packed_refs[0][which, :, :units] = held[which][...].T
    gives[0].start()
    for fetch in fetches[3:]:
        fetch.wait()
    for at, part in ((1, slice(0, cut)), (2, slice(cut, None))):
        packed_refs[at][0] = held[3][0, :, part]
        packed_refs[at][1] = held[4][0, :, part]
        packed_refs[at][2] = held[5][0, part, :].T
        gives[at].start()
    run_all(phases[1:])
    for give in gives:
        give.wait()


def opening(mesh_size, ident, moves, cut, shared, expert):
    transfers = Transfers(mesh_size, ident, moves)
    anywhere = pl.BlockSpec(memory_space=pl.ANY)
    units, depth = shared[0].shape
    sizes = (-(-units // LANES) * LANES, cut, expert[0].shape[2] - cut)
    shapes = [(3, depth, size) for size in sizes]
    results = pl.pallas_call(
        functools.partial(opening_kernel, transfers, cut),
        in_specs=transfers.in_specs + [anywhere] * 6,
        out_specs=tuple(transfers.out_specs + [anywhere] * 3),
        out_shape=tuple(transfers.shapes + [jax.ShapeDtypeStruct(shape, BF) for shape in shapes]),
        scratch_shapes=[pltpu.VMEM(array.shape, BF) for array in (*shared, *expert)]
        + [pltpu.VMEM(shape, BF) for shape in shapes]
        + [DMA((6,)), DMA((3,))]
        + transfers.scratch,
        compiler_params=transfers.params(),
    )(*transfers.inputs, *shared, *expert)
    return results[: transfers.moves], results[transfers.moves :]


def unpack_kernel(turned, *refs):
    count = len(refs) - 3
    for which, out_ref in enumerate(refs[count:]):
        first = 0
        for ref in refs[:count]:
            values = ref[which].astype(F32)
            if turned[which]:
                values = values.T
                size = min(values.shape[0], out_ref.shape[0] - first)
                out_ref[first : first + size, :] = values[:size]
            else:
                size = min(values.shape[1], out_ref.shape[1] - first)
                out_ref[:, first : first + size] = values[:, :size]
            first += size


def unpack(ranges, units, turned):
    depth = ranges[0].shape[1]
    rows = min(LANES, depth)
    shapes = [(units, depth) if turn else (depth, units) for turn in turned]
    return pl.pallas_call(
        functools.partial(unpack_kernel, turned),
        grid=(depth // rows,),
        in_specs=[pl.BlockSpec((3, rows, array.shape[2]), lambda i: (0, i, 0)) for array in ranges],
        out_specs=tuple(
            pl.BlockSpec((units, rows), lambda i: (0, i))
            if turn
            else pl.BlockSpec((rows, units), lambda i: (i, 0))
            for turn in turned
        ),
        out_shape=tuple(jax.ShapeDtypeStruct(shape, F32) for shape in shapes),
        compiler_params=pltpu.CompilerParams(vmem_limit_bytes=VMEM_BYTES),
        cost_estimate=pl.CostEstimate(flops=0, bytes_accessed=18 * depth * units, transcendentals=0),
    )(*ranges)


def rope_tables(seq_len):
    half = HD // 2
    frequency = np.float32(ROPE_BASE) ** (-(2.0 * np.arange(half, dtype=np.float32)) / HD)
    angles = np.arange(seq_len, dtype=np.float32)[:, None] * frequency[None, :].astype(np.float32)
    cosine, sine = np.cos(angles.astype(np.float64)), np.sin(angles.astype(np.float64))
    return (
        jnp.asarray(np.concatenate([cosine, cosine], axis=1).astype(np.float32)),
        jnp.asarray(np.concatenate([-sine, sine], axis=1).astype(np.float32)),
    )


def swap_halves(values):
    half = HD // 2
    return jnp.concatenate([values[:, half:], values[:, :half]], axis=1)


def block_scores(query, keys, first_row, length):
    scores = dot(query, keys, (1,), (1,)) * (HD ** (-0.5))
    rows = first_row + lax.broadcasted_iota(jnp.int32, scores.shape, 0)
    cols = lax.broadcasted_iota(jnp.int32, scores.shape, 1)
    return jnp.where((cols <= rows) & (cols < length), scores, -1e30)


def attend_kernel(heads, transfers, *refs):
    refs = list(refs)

    def take(count):
        taken = refs[:count]
        del refs[:count]
        return taken

    length_ref, x_ref, gain_ref, w_ref, bias_ref, cos_ref, sin_ref = take(7)
    sent = take(len(transfers.inputs))
    normed_ref, qkv_ref, mixed_ref, logs_ref, out_ref = take(5)
    landed = take(transfers.moves)
    rows_vmem, out_vmem, in_sem, normed_sem, out_sem = take(5)
    phases = transfers.begin(sent, landed, refs)
    seq_len, width = x_ref.shape
    groups, depth, columns = w_ref.shape
    span = heads * HD
    length = length_ref[0]
    blocks = [pl.ds(row, QB) for row in range(0, seq_len, QB)]

    def fetch(i):
        return pltpu.make_async_copy(x_ref.at[blocks[i]], rows_vmem.at[blocks[i]], in_sem.at[i])

    def keep(i):
        return pltpu.make_async_copy(rows_vmem.at[blocks[i]], normed_ref.at[blocks[i]], normed_sem.at[i])

    def give(i):
        return pltpu.make_async_copy(out_vmem.at[blocks[i]], out_ref.at[blocks[i]], out_sem.at[i])

    for i in range(len(blocks)):
        fetch(i).start()
    run_all(phases[:1])
    weights = w_ref[...].reshape(groups * depth, columns)
    qkv_w, out_w = weights[:, : 3 * span], weights[:, 3 * span :]
    for i in range(len(blocks)):
        row, end = i * QB, (i + 1) * QB
        if i >= 2:
            run_all(phases[i - 1 : i])
        fetch(i).wait()
        values = rows_vmem[row:end, :].astype(F32)
        normed = (normalize(values)[0] * gain_ref[...]).astype(BF)
        rows_vmem[row:end, :] = normed
        keep(i).start()
        pre = dot(normed, qkv_w, (1,), (0,)) + bias_ref[...]
        cosine, sine = cos_ref[row:end, :], sin_ref[row:end, :]
        for at in range(0, 3 * span, HD):
            part = pre[:, at : at + HD]
            if at < 2 * span:
                part = part * cosine + swap_halves(part) * sine
            qkv_ref[row:end, at : at + HD] = part.astype(BF)
        for head in range(heads):
            q_at, k_at, v_at = (head * HD, span + head * HD, 2 * span + head * HD)
            scores = block_scores(
                qkv_ref[row:end, q_at : q_at + HD], qkv_ref[:end, k_at : k_at + HD], row, length
            )
            top = jnp.max(scores, axis=1, keepdims=True)
            exps = jnp.exp(scores - top)
            totals = jnp.sum(exps, axis=1, keepdims=True)
            shares = exps * (1.0 / totals)
            logs_ref[row:end, head : head + 1] = top + jnp.log(totals)
            mixed = dot(shares.astype(BF), qkv_ref[:end, v_at : v_at + HD], (1,), (0,))
            mixed_ref[row:end, q_at : q_at + HD] = mixed.astype(BF)
        out_vmem[row:end, :] = dot(mixed_ref[row:end, :], out_w, (1,), (1,)).astype(BF)
        give(i).start()
    run_all(phases[max(1, len(blocks) - 1) :])
    for i in range(len(blocks)):
        keep(i).wait()
        give(i).wait()


def attend_back_kernel(heads, transfers, *refs):
    refs = list(refs)

    def take(count):
        taken = refs[:count]
        del refs[:count]
        return taken

    length_ref, datt_ref, w_ref, qkv_ref, logs_ref, cos_ref, sin_ref = take(7)
    sent = take(len(transfers.inputs))
    turned_ref, sums_ref, out_ref = take(3)
    landed = take(transfers.moves)
    rows_vmem, out_vmem, grad_vmem, key_acc, value_acc, in_sem, out_sem = take(7)
    phases = transfers.begin(sent, landed, refs)
    run_all(phases[:1])
    seq_len, width = datt_ref.shape
    groups, depth, columns = w_ref.shape
    span = heads * HD
    length = length_ref[0]
    scale = HD ** (-0.5)
    blocks = [pl.ds(row, QB) for row in range(0, seq_len, QB)]

    def fetch(i):
        return pltpu.make_async_copy(datt_ref.at[blocks[i]], rows_vmem.at[blocks[i]], in_sem.at[i])

    def give(i):
        return pltpu.make_async_copy(out_vmem.at[blocks[i]], out_ref.at[blocks[i]], out_sem.at[i])

    for i in range(len(blocks)):
        fetch(i).start()
    weights = w_ref[...].reshape(groups * depth, columns)
    qkv_w, out_w = weights[:, : 3 * span], weights[:, 3 * span :]
    key_acc[...] = jnp.zeros_like(key_acc)
    value_acc[...] = jnp.zeros_like(value_acc)
    query_sums = [jnp.zeros((1, HD), F32) for _ in range(heads)]
    for i in range(len(blocks)):
        row, end = i * QB, (i + 1) * QB
        if i >= 2:
            run_all(phases[i - 1 : i])
        fetch(i).wait()
        grad_vmem[row:end, :] = dot(rows_vmem[row:end, :], out_w, (1,), (0,)).astype(BF)
        for head in range(heads):
            q_at, k_at, v_at = (head * HD, span + head * HD, 2 * span + head * HD)
            query = qkv_ref[row:end, q_at : q_at + HD]
            keys = qkv_ref[:end, k_at : k_at + HD]
            grad = grad_vmem[row:end, q_at : q_at + HD]
            shares = jnp.exp(
                block_scores(query, keys, row, length) - logs_ref[row:end, head : head + 1]
            )
            grad_shares = dot(grad, qkv_ref[:end, v_at : v_at + HD], (1,), (1,))
            inner = jnp.sum(shares * grad_shares, axis=1, keepdims=True)
            grad_scores = (scale * shares * (grad_shares - inner)).astype(BF)
            turned = dot(grad_scores, keys, (1,), (0,))
            grad_query = (
                turned * cos_ref[row:end, :] - swap_halves(turned) * sin_ref[row:end, :]
            ).astype(BF)
            turned_ref[row:end, q_at : q_at + HD] = grad_query
            query_sums[head] += jnp.sum(grad_query.astype(F32), axis=0, keepdims=True)
            key_acc[:end, q_at : q_at + HD] += dot(grad_scores, query, (0,), (0,))
            value_acc[:end, q_at : q_at + HD] += dot(shares.astype(BF), grad, (0,), (0,))
    done = max(1, len(blocks) - 1)
    run_all(phases[done : done + 1])
    key_sums = [jnp.zeros((1, HD), F32) for _ in range(heads)]
    value_sums = [jnp.zeros((1, HD), F32) for _ in range(heads)]
    for i in range(len(blocks)):
        row, end = i * QB, (i + 1) * QB
        for head in range(heads):
            q_at, k_at, v_at = (head * HD, span + head * HD, 2 * span + head * HD)
            turned = key_acc[row:end, q_at : q_at + HD]
            grad_key = (
                turned * cos_ref[row:end, :] - swap_halves(turned) * sin_ref[row:end, :]
            ).astype(BF)
            grad_value = value_acc[row:end, q_at : q_at + HD].astype(BF)
            turned_ref[row:end, k_at : k_at + HD] = grad_key
            turned_ref[row:end, v_at : v_at + HD] = grad_value
            key_sums[head] += jnp.sum(grad_key.astype(F32), axis=0, keepdims=True)
            value_sums[head] += jnp.sum(grad_value.astype(F32), axis=0, keepdims=True)
        out_vmem[row:end, :] = dot(turned_ref[row:end, :], qkv_w, (1,), (1,)).astype(BF)
        give(i).start()
    for at, sums in enumerate(query_sums + key_sums + value_sums):
        sums_ref[:, at * HD : (at + 1) * HD] = sums
    for i in range(len(blocks)):
        give(i).wait()
    run_all(phases[done + 1 :])


def in_vmem(count):
    return [pl.BlockSpec(memory_space=pltpu.VMEM)] * count


def attend(length, rows, gain, weights, bias, cosine, sine, transfers):
    seq_len, width = rows.shape
    span = weights.shape[2] // 4
    heads, blocks = span // HD, seq_len // QB
    anywhere = pl.BlockSpec(memory_space=pl.ANY)
    results = pl.pallas_call(
        functools.partial(attend_kernel, heads, transfers),
        out_shape=tuple(
            [
                jax.ShapeDtypeStruct((seq_len, width), BF),
                jax.ShapeDtypeStruct((seq_len, 3 * span), BF),
                jax.ShapeDtypeStruct((seq_len, span), BF),
                jax.ShapeDtypeStruct((seq_len, heads), F32),
                jax.ShapeDtypeStruct((seq_len, width), BF),
            ]
            + transfers.shapes
        ),
        in_specs=[pl.BlockSpec(memory_space=pltpu.SMEM), anywhere] + in_vmem(5) + transfers.in_specs,
        out_specs=tuple([anywhere] + in_vmem(3) + [anywhere] + transfers.out_specs),
        scratch_shapes=[pltpu.VMEM((seq_len, width), BF)] * 2
        + [DMA((blocks,))] * 3
        + transfers.scratch,
        compiler_params=transfers.params(),
        cost_estimate=pl.CostEstimate(
            flops=8 * seq_len * width * span + 3 * span * seq_len * seq_len,
            bytes_accessed=8 * seq_len * width,
            transcendentals=heads * seq_len * seq_len,
        ),
    )(length, rows, gain, weights, bias, cosine, sine, *transfers.inputs)
    return results[:5], results[5:]


def attend_back(length, rows, weights, qkv, logs, cosine, sine, transfers):
    seq_len, width = rows.shape
    span = weights.shape[2] // 4
    heads, blocks = span // HD, seq_len // QB
    anywhere = pl.BlockSpec(memory_space=pl.ANY)
    results = pl.pallas_call(
        functools.partial(attend_back_kernel, heads, transfers),
        out_shape=tuple(
            [
                jax.ShapeDtypeStruct((seq_len, 3 * span), BF),
                jax.ShapeDtypeStruct((1, 3 * span), F32),
                jax.ShapeDtypeStruct((seq_len, width), BF),
            ]
            + transfers.shapes
        ),
        in_specs=[pl.BlockSpec(memory_space=pltpu.SMEM), anywhere] + in_vmem(5) + transfers.in_specs,
        out_specs=tuple(in_vmem(2) + [anywhere] + transfers.out_specs),
        scratch_shapes=[pltpu.VMEM((seq_len, width), BF)] * 2
        + [pltpu.VMEM((seq_len, span), BF)]
        + [pltpu.VMEM((seq_len, span), F32)] * 2
        + [DMA((blocks,))] * 2
        + transfers.scratch,
        compiler_params=transfers.params(),
        cost_estimate=pl.CostEstimate(
            flops=8 * seq_len * width * span + 8 * span * seq_len * seq_len,
            bytes_accessed=8 * seq_len * width,
            transcendentals=heads * seq_len * seq_len,
        ),
    )(length, rows, weights, qkv, logs, cosine, sine, *transfers.inputs)
    return results[:3], results[3:]


def padded(values, axis):
    size = values.shape[axis]
    more = -size % LANES
    if not more:
        return values
    return jnp.pad(values, [(0, more if i == axis else 0) for i in range(values.ndim)])


def packed(values, kind):
    tile = LANES * (16 if kind == BF else 8)
    values = values.astype(kind)
    return padded_to(values, -(-values.shape[-1] // tile) * tile)


def padded_to(values, size):
    more = size - values.shape[-1]
    return jnp.pad(values, [(0, 0)] * (values.ndim - 1) + [(0, more)])


def local(
    tokens,
    lengths,
    routes,
    norm1_gain,
    w_query,
    w_key,
    w_value,
    b_query,
    b_key,
    b_value,
    w_out,
    norm2_gain,
    router,
    shared_gate_vec,
    shared_gate,
    shared_up,
    shared_down,
    expert_gate,
    expert_up,
    expert_down,
    cotangent,
):
    ranks = lax.axis_size("tensor")
    groups = lax.axis_size("fsdp")
    rank = lax.axis_index("tensor")
    micros, _, rows, width = tokens.shape
    seq_len = rows * ranks
    heads = w_query.shape[1] // HD
    span = heads * HD
    experts = ranks * expert_gate.shape[0]
    shared_units = shared_gate.shape[1]
    expert_units = expert_gate.shape[2]
    cut = expert_units // (2 * LANES) * LANES
    own_first = rank * rows
    local_pos = own_first + jnp.arange(rows, dtype=jnp.int32)

    per_device = norm1_gain.shape[0]
    small = jnp.concatenate(
        [
            norm1_gain,
            norm2_gain,
            shared_gate_vec,
            router.reshape(-1),
            b_query.reshape(-1),
            b_key.reshape(-1),
            b_value.reshape(-1),
        ]
    )
    attn_own = jnp.concatenate([w_query, w_key, w_value, w_out.T], axis=1)
    mesh_size = (ranks, groups)
    (small_all, attn_w, rows_a), own_ranges = opening(
        mesh_size,
        2,
        [
            ("spread", packed(small, BF).reshape(-1, LANES)),
            ("cross_gather", attn_own),
            ("gather", tokens, (0, 0)),
        ],
        cut,
        (shared_gate.T, shared_up.T, shared_down),
        (expert_gate, expert_up, expert_down),
    )
    small_all = small_all.reshape(groups * ranks, -1)
    gain_one = small_all[:, :per_device].reshape(-1).astype(F32)
    gain_two = small_all[:, per_device : 2 * per_device].reshape(-1).astype(F32)
    gate_vec = small_all[:, 2 * per_device : 3 * per_device].reshape(-1)
    bias_at = per_device * (3 + experts)
    router_full = small_all[:, 3 * per_device : bias_at].reshape(width, experts)
    router_wide = padded_to(jnp.concatenate([router_full, gate_vec[:, None]], axis=1), LANES)
    own_bias = lax.dynamic_index_in_dim(
        small_all.reshape(groups, ranks, -1), rank, 1, False
    )[:, bias_at : small.shape[0]].reshape(groups, 3, heads, HD // groups)
    bias = own_bias.transpose(1, 2, 0, 3).reshape(1, 3 * span).astype(F32)

    weights = [lax.all_gather(own_range, "fsdp", axis=0) for own_range in own_ranges]

    cosine, sine = rope_tables(seq_len)
    idle = Transfers(mesh_size)
    token_own = [tokens[m, 0] for m in range(micros)]
    grads_own = []
    for m in range(micros):
        inside = (local_pos < lengths[m, 0])[:, None]
        grads_own.append(jnp.where(inside, cotangent[m, 0], jnp.zeros((), BF)))

    def moving(ident, *moves, needed=()):
        return Transfers(mesh_size, ident, moves, needed)

    def attention(m, token_rows, transfers):
        return attend(lengths[m], token_rows, gain_one[None], attn_w, bias, cosine, sine, transfers)

    def second_norm(m, attended):
        hidden = token_own[m].astype(F32) + attended
        unit, inverse = normalize(hidden)
        return hidden, unit, inverse, (unit * gain_two).astype(BF)

    def second_norm_back(m, state, summed):
        grad_hidden, gain_part = norm_back(summed, state[1], state[2], gain_two)
        grad_hidden = grad_hidden + grads_own[m].astype(F32)
        return grad_hidden, grad_hidden.astype(BF), gain_part

    def first_norm_back(m, grad_hidden, summed):
        unit, inverse = normalize(token_own[m].astype(F32))
        grad_inputs, gain_part = norm_back(summed, unit, inverse, gain_one)
        return (grad_inputs + grad_hidden).astype(BF), gain_part

    def finished(m, hidden, moved):
        inside = (local_pos < lengths[m, 0]).astype(F32)[:, None]
        return (inside * (hidden + moved)).astype(BF)

    att_a, (rows_b,) = attention(0, rows_a, moving(3, ("gather", tokens, (1, 0))))
    att_b, (grad_a, sum_a) = attention(
        1, rows_b, moving(4, ("gather", cotangent, (0, 0)), ("scatter", att_a[4]))
    )
    norm_a = second_norm(0, sum_a)
    two_a, sum_b = exchange(mesh_size, 5, [("gather", norm_a[3]), ("scatter", att_b[4])])
    norm_b = second_norm(1, sum_b)

    def over_groups(grads):
        flat = grads.reshape(-1, grads.shape[-1])
        summed = lax.psum_scatter(flat, "fsdp", scatter_dimension=0, tiled=True)
        return with_layout_constraint(summed, Layout((0, 1))).reshape(grads.shape[1:])

    def grads_of(which, transfers, at=()):
        per_micro = []
        for key in range(micros):
            rows_two, grads = ((two_a, grad_a), (two_b, grad_b))[key]
            scaled, gate, up = act[which, key]
            more = [(acc_a, acc_b)[key][2]] if which == 2 else []
            per_micro.append([rows_two, grads, gate, up, scaled] + more)
        return ffn_grads(groups, per_micro, transfers, at)

    act = {}
    part = functools.partial(ffn, experts)
    single = ((0, 0), (1, 0), (2, 0), (3, 0))
    act[0, 0], acc_a, (grad_b,) = part(
        "first", two_a, grad_a, routes[0, 0].T, weights[0], [lengths[0]], router_wide,
        moving(6, ("gather", cotangent, (1, 0))), single,
    )
    acc_a, route_a = acc_a[:3], acc_a[3]
    act[1, 0], acc_a, (two_b,) = part(
        "next", two_a, grad_a, route_a, weights[1], acc_a, None,
        moving(7, ("gather", norm_b[3])), single,
    )
    act[0, 1], acc_b, _ = part(
        "first", two_b, grad_b, routes[1, 0].T, weights[0], [lengths[1]], router_wide, idle
    )
    acc_b, route_b = acc_b[:3], acc_b[3]
    (grads_0,), _ = grads_of(0, idle)
    range_0 = over_groups(grads_0)
    act[2, 0], acc_a, _ = part(
        "last", two_a, grad_a, route_a, weights[2], acc_a, router_wide, moving(0, needed=[grads_0])
    )
    act[1, 1], acc_b, (down_a,) = part(
        "next", two_b, grad_b, route_b, weights[1], acc_b, None,
        moving(8, ("scatter", acc_a[1])), single,
    )
    hid_a, send_a, gain_part_a = second_norm_back(0, norm_a, down_a)
    (grads_1,), (datt_a,) = grads_of(
        1, moving(9, ("gather", send_a)), ((0, 0), (1, 0), (2, 0), (3, 0))
    )
    range_1 = over_groups(grads_1)
    act[2, 1], acc_b, (moved_a,) = part(
        "last", two_b, grad_b, route_b, weights[2], acc_b, router_wide,
        moving(10, ("scatter", acc_a[0]), needed=[grads_1]), single,
    )
    (grads_2, total_wide), (down_b,) = grads_of(
        2, moving(11, ("scatter", acc_b[1]), needed=[range_0]), ((0, 0), (1, 1), (2, 1), (3, 1))
    )
    range_2 = over_groups(grads_2)
    hid_b, send_b, gain_part_b = second_norm_back(1, norm_b, down_b)

    (grad_qkv_a, sums_a, first_a), (datt_b,) = attend_back(
        lengths[0], datt_a, attn_w, att_a[1], att_a[3], cosine, sine,
        moving(12, ("gather", send_b)),
    )
    (grad_qkv_b, sums_b, first_b), (one_a,) = attend_back(
        lengths[1], datt_b, attn_w, att_b[1], att_b[3], cosine, sine,
        moving(15, ("scatter", first_a), needed=[range_1]),
    )
    attn_parts, (one_b,) = attention_grads(
        groups,
        [
            (att_a[0], datt_a, grad_qkv_a, att_a[2]),
            (att_b[0], datt_b, grad_qkv_b, att_b[2]),
        ],
        moving(13, ("scatter", first_b)),
    )

    grad_in_a, one_part_a = first_norm_back(0, hid_a, one_a)
    grad_in_b, one_part_b = first_norm_back(1, hid_b, one_b)

    devices = groups * ranks
    bias_part = (sums_a + sums_b).reshape(3, heads, groups, HD // groups).transpose(2, 0, 1, 3)
    bias_part = bias_part.reshape(groups, 1, -1)
    own_rank = (jnp.arange(ranks, dtype=jnp.int32) == rank).astype(F32)[None, :, None]
    parts = jnp.concatenate(
        [
            (one_part_a + one_part_b).reshape(devices, -1),
            (gain_part_a + gain_part_b).reshape(devices, -1),
            total_wide[:, : experts + 1].reshape(devices, -1),
            (bias_part * own_rank).reshape(devices, -1),
        ],
        axis=1,
    )
    moved_b, attn_g, shares = exchange(
        mesh_size,
        14,
        [
            ("scatter", acc_b[0]),
            ("cross_scatter", attn_parts),
            ("share", packed(parts, F32).reshape(devices, -1, LANES)),
        ],
        [range_2],
    )
    shares = shares.reshape(-1)
    wide_g = shares[2 * per_device : (3 + experts) * per_device].reshape(per_device, experts + 1)
    bias_g = shares[bias_at : parts.shape[1]].reshape(3, heads, HD // groups)

    shared_g = unpack([range_0], shared_units, (True, True, True))
    expert_g = unpack([range_1, range_2], expert_units, (False, False, True))
    return (
        jnp.stack([finished(0, norm_a[0], moved_a), finished(1, norm_b[0], moved_b)])[:, None],
        jnp.stack([grad_in_a, grad_in_b])[:, None],
        shares[:per_device],
        attn_g[:, :span],
        attn_g[:, span : 2 * span],
        attn_g[:, 2 * span : 3 * span],
        bias_g[0],
        bias_g[1],
        bias_g[2],
        attn_g[:, 3 * span :].T,
        shares[per_device : 2 * per_device],
        wide_g[:, :experts],
        wide_g[:, experts],
        shared_g[0].T,
        shared_g[1].T,
        shared_g[2],
        expert_g[0][None],
        expert_g[1][None],
        expert_g[2][None],
    )


def solution(mesh):
    in_specs = (
        P(None, "fsdp", "tensor", None),
        P(None, "fsdp"),
        P(None, "fsdp", None, None),
        P(("fsdp", "tensor")),
        P("fsdp", "tensor"),
        P("fsdp", "tensor"),
        P("fsdp", "tensor"),
        P("tensor", "fsdp"),
        P("tensor", "fsdp"),
        P("tensor", "fsdp"),
        P("tensor", "fsdp"),
        P(("fsdp", "tensor")),
        P(("fsdp", "tensor"), None),
        P(("fsdp", "tensor")),
        P("fsdp", "tensor"),
        P("fsdp", "tensor"),
        P("tensor", "fsdp"),
        P("tensor", "fsdp", None),
        P("tensor", "fsdp", None),
        P("tensor", None, "fsdp"),
        P(None, "fsdp", "tensor", None),
    )
    out_specs = (
        P(None, "fsdp", "tensor", None),
        P(None, "fsdp", "tensor", None),
        P(("fsdp", "tensor")),
        P("fsdp", "tensor"),
        P("fsdp", "tensor"),
        P("fsdp", "tensor"),
        P("tensor", "fsdp"),
        P("tensor", "fsdp"),
        P("tensor", "fsdp"),
        P("tensor", "fsdp"),
        P(("fsdp", "tensor")),
        P(("fsdp", "tensor"), None),
        P(("fsdp", "tensor")),
        P("fsdp", "tensor"),
        P("fsdp", "tensor"),
        P("tensor", "fsdp"),
        P("tensor", "fsdp", None),
        P("tensor", "fsdp", None),
        P("tensor", None, "fsdp"),
    )
    return jax.shard_map(local, mesh=mesh, in_specs=in_specs, out_specs=out_specs, check_vma=False)
```

```python
import functools

import jax
import jax.numpy as jnp
import numpy as np
from jax import lax
from jax.experimental import pallas as pl
from jax.experimental.layout import Layout, with_layout_constraint
from jax.experimental.pallas import tpu as pltpu
from jax.sharding import PartitionSpec as P

HD = 128
EPSILON = 1e-06
ROPE_BASE = 1000000.0
BF = jnp.bfloat16
F32 = jnp.float32
MESH = pl.DeviceIdType.MESH
QB = 256
LANES = 128
CHUNKS = 2
STRIP = 16
ROW_BLOCK = 256
VMEM_BYTES = 60 << 20


def dot(left, right, left_dims, right_dims):
    return lax.dot_general(
        left, right, ((left_dims, right_dims), ((), ())), preferred_element_type=F32
    )


def normalize(values):
    inverse = lax.rsqrt(jnp.mean(values * values, axis=-1, keepdims=True) + EPSILON)
    return (values * inverse, inverse)


def norm_back(grad_normed, unit, inverse, gain):
    grad_unit = grad_normed * gain
    grad_values = inverse * (grad_unit - unit * jnp.mean(grad_unit * unit, axis=-1, keepdims=True))
    return (grad_values, jnp.sum(grad_normed * unit, axis=0))


def remote(src, dst, sems, at, target):
    return pltpu.make_async_remote_copy(
        src_ref=src,
        dst_ref=dst,
        send_sem=sems[0].at[at],
        recv_sem=sems[1].at[at],
        device_id={"tensor": target},
        device_id_type=MESH,
    )


def gather_scratch(ranks):
    chips = ranks // 2
    pair = [pltpu.SemaphoreType.DMA((chips, CHUNKS))] * 2
    cross = [pltpu.SemaphoreType.DMA((2 * chips, CHUNKS))] * 2
    return [pltpu.SemaphoreType.DMA] + pair + pair + cross


def gather_steps(place, block, whole, local_sem, up_s, up_r, down_s, down_r, cross_s, cross_r):
    chips, chip, core = place.chips, place.chip, place.core
    rows = block.shape[0]
    part = rows // CHUNKS
    up, down, cross = (up_s, up_r), (down_s, down_r), (cross_s, cross_r)

    def at(owner, chunk):
        first = pl.multiple_of((2 * owner + core) * rows + chunk * part, part)
        return whole.at[pl.ds(first, part)]

    def theirs(owner, chunk):
        first = pl.multiple_of((2 * owner + 1 - core) * rows + chunk * part, part)
        return whole.at[pl.ds(first, part)]

    def own(chunk):
        return block.at[pl.ds(chunk * part, part)]

    def upward(step, chunk):
        source = own(chunk) if step == 0 else at(chip - step, chunk)
        return remote(source, at(chip - step, chunk), up, (step, chunk), place.above)

    def downward(step, chunk):
        source = own(chunk) if step == 0 else at(chip + step, chunk)
        return remote(source, at(chip + step, chunk), down, (step, chunk), place.below)

    def across(slot, owner, chunk):
        source = own(chunk) if slot == 0 else at(owner, chunk)
        return remote(source, at(owner, chunk), cross, (slot, chunk), place.partner)

    def arrived(slot, owner, chunk):
        return remote(theirs(owner, chunk), theirs(owner, chunk), cross, (slot, chunk), place.partner)

    def arrived_up(step, chunk):
        return remote(at(chip - step, chunk), at(chip - step, chunk), up, (step - 1, chunk), place.above)

    def arrived_down(step, chunk):
        return remote(at(chip + step, chunk), at(chip + step, chunk), down, (step - 1, chunk), place.below)

    both = range(CHUNKS)

    def mine():
        first = pl.multiple_of((2 * chip + core) * rows, rows)
        return pltpu.make_async_copy(block, whole.at[pl.ds(first, rows)], local_sem)

    def begin():
        for chunk in both:
            pl.when(place.not_top)(lambda: upward(0, chunk).start())
            pl.when(place.not_bottom)(lambda: downward(0, chunk).start())
        for chunk in both:
            across(0, chip, chunk).start()
        mine().start()

    def hop(step, chunk):
        @pl.when(chip >= step)
        def _():
            arrived_up(step, chunk).wait_recv()
            pl.when(place.not_top)(lambda: upward(step, chunk).start())
            across(2 * step - 1, chip - step, chunk).start()

        @pl.when(chip < chips - step)
        def _():
            arrived_down(step, chunk).wait_recv()
            pl.when(place.not_bottom)(lambda: downward(step, chunk).start())
            across(2 * step, chip + step, chunk).start()

    def end():
        mine().wait()
        for step in range(chips):
            for chunk in both:
                if step == 0:
                    arrived(0, chip, chunk).wait_recv()
                    across(0, chip, chunk).wait_send()
                else:

                    @pl.when(chip >= step)
                    def _():
                        arrived(2 * step - 1, chip - step, chunk).wait_recv()
                        across(2 * step - 1, chip - step, chunk).wait_send()

                    @pl.when(chip < chips - step)
                    def _():
                        arrived(2 * step, chip + step, chunk).wait_recv()
                        across(2 * step, chip + step, chunk).wait_send()

                @pl.when(place.not_top & (chip >= step))
                def _():
                    upward(step, chunk).wait_send()

                @pl.when(place.not_bottom & (chip < chips - step))
                def _():
                    downward(step, chunk).wait_send()

    hops = [functools.partial(hop, step, chunk) for step in range(1, chips) for chunk in both]
    return [begin] + hops + [end]


def scatter_scratch(ranks, rows, width):
    chips = ranks // 2
    line = [pltpu.SemaphoreType.DMA((chips, CHUNKS))] * 2
    buffers = [pltpu.VMEM((chips, rows, width), BF)] * 5
    return buffers + [pltpu.SemaphoreType.DMA((chips,))] + line * 3


def scatter_steps(
    place, partial, total, kept, pair, held, up_in, down_in, keep_sem,
    up_s, up_r, down_s, down_r, cross_s, cross_r,
):
    chips, chip, core = place.chips, place.chip, place.core
    rows = total.shape[0]
    part = rows // CHUNKS
    up, down, cross = (up_s, up_r), (down_s, down_r), (cross_s, cross_r)
    both = range(CHUNKS)

    def keep(k):
        first = pl.multiple_of((2 * k + core) * rows, rows)
        return pltpu.make_async_copy(partial.at[pl.ds(first, rows)], kept.at[k], keep_sem.at[k])

    def across(k, chunk):
        first = pl.multiple_of((2 * k + 1 - core) * rows + chunk * part, part)
        return remote(
            partial.at[pl.ds(first, part)],
            pair.at[k, pl.ds(chunk * part, part)],
            cross,
            (k, chunk),
            place.partner,
        )

    def upward(step, k, chunk):
        cut = pl.ds(chunk * part, part)
        return remote(held.at[k, cut], up_in.at[step, cut], up, (step, chunk), place.above)

    def downward(step, k, chunk):
        cut = pl.ds(chunk * part, part)
        return remote(held.at[k, cut], down_in.at[step, cut], down, (step, chunk), place.below)

    def add(k, chunk, target, others):
        def strip(i, carry):
            cut = pl.ds(chunk * part + i * STRIP, STRIP)
            value = kept[k, cut].astype(F32) + pair[k, cut].astype(F32)
            for ref, slot in others:
                value = value + ref[slot, cut].astype(F32)
            if target is None:
                total[cut] = value
            else:
                target[k, cut] = value.astype(BF)
            return carry

        lax.fori_loop(0, part // STRIP, strip, 0)

    order = []
    for i in range(chips):
        for k in (chips - 1 - i, i):
            if k not in order:
                order.append(k)
    def begin():
        for k in order:
            keep(k).start()
            for chunk in both:
                across(k, chunk).start()

    def hop(step, chunk):
        @pl.when(place.not_top & (chip <= step - 1))
        def _():
            k = chip + chips - step
            if chunk == 0:
                keep(k).wait()
            across(k, chunk).wait_recv()

            @pl.when(place.not_bottom)
            def _():
                upward(step - 1, k, chunk).wait_recv()
                add(k, chunk, held, [(up_in, step - 1)])

            pl.when(jnp.logical_not(place.not_bottom))(lambda: add(k, chunk, held, []))
            upward(step, k, chunk).start()

        @pl.when(place.not_bottom & (chip >= chips - step))
        def _():
            k = chip - (chips - step)
            if chunk == 0:
                keep(k).wait()
            across(k, chunk).wait_recv()

            @pl.when(place.not_top)
            def _():
                downward(step - 1, k, chunk).wait_recv()
                add(k, chunk, held, [(down_in, step - 1)])

            pl.when(jnp.logical_not(place.not_top))(lambda: add(k, chunk, held, []))
            downward(step, k, chunk).start()

    last = chips - 1

    def add_last(chunk):
        if chunk == 0:
            keep(chip).wait()
        across(chip, chunk).wait_recv()

        @pl.when(place.not_top & place.not_bottom)
        def _():
            upward(last, chip, chunk).wait_recv()
            downward(last, chip, chunk).wait_recv()
            add(chip, chunk, None, [(up_in, last), (down_in, last)])

        @pl.when(jnp.logical_not(place.not_top))
        def _():
            upward(last, chip, chunk).wait_recv()
            add(chip, chunk, None, [(up_in, last)])

        @pl.when(jnp.logical_not(place.not_bottom))
        def _():
            downward(last, chip, chunk).wait_recv()
            add(chip, chunk, None, [(down_in, last)])

    def end():
        for chunk in both:
            for k in range(chips):
                across(k, chunk).wait_send()
            for step in range(1, chips):

                @pl.when(place.not_top & (chip <= step - 1))
                def _():
                    upward(step, chip + chips - step, chunk).wait_send()

                @pl.when(place.not_bottom & (chip >= chips - step))
                def _():
                    downward(step, chip - (chips - step), chunk).wait_send()

    def first():
        begin()
        for chunk in both:
            hop(1, chunk)

    hops = [functools.partial(hop, step, chunk) for step in range(2, chips) for chunk in both]
    return [first] + hops + [functools.partial(add_last, chunk) for chunk in both] + [end]


class Place:
    def __init__(self, ranks, groups):
        rank, group = lax.axis_index("tensor"), lax.axis_index("fsdp")
        self.ranks, self.groups = ranks, groups
        self.chips = ranks // 2
        self.chip, self.core = rank // 2, rank % 2
        self.partner = rank + 1 - 2 * self.core
        self.above, self.below = rank + 2, rank - 2
        self.not_top = self.chip < self.chips - 1
        self.not_bottom = self.chip > 0
        self.rank, self.group = rank, group
        self.device = group * ranks + rank
        near, far = group % 2, group // 2
        self.beside = 2 * far + 1 - near
        self.across = 2 * (1 - far) + near
        self.opposite = 2 * (1 - far) + 1 - near
        self.square = groups == 4

    def name(self, device):
        return {"fsdp": device // self.ranks, "tensor": device % self.ranks}

    def meet(self, line, cross, everyone):
        barrier = pltpu.get_barrier_semaphore()

        def greet(name):
            pl.semaphore_signal(barrier, 1, device_id=name, device_id_type=MESH)

        if everyone:
            devices = self.groups * self.ranks

            def one(i, carry):
                greet(self.name(lax.rem(self.device + i, devices)))
                return carry

            lax.fori_loop(1, devices, one, 0)
            pl.semaphore_wait(barrier, devices - 1)
            return
        peers = 0
        if line:
            greet({"tensor": self.partner})
            pl.when(self.not_top)(lambda: greet({"tensor": self.above}))
            pl.when(self.not_bottom)(lambda: greet({"tensor": self.below}))
            peers = 1 + self.not_top.astype(jnp.int32) + self.not_bottom.astype(jnp.int32)
        if cross and self.square:
            greet({"fsdp": self.beside})
            greet({"fsdp": self.across})
            peers = peers + 2
        elif cross:
            for i in range(1, self.groups):
                greet({"fsdp": lax.rem(self.group + i, self.groups)})
            peers = peers + self.groups - 1
        pl.semaphore_wait(barrier, peers)


def to_group(src, dst, send, recv, at, target):
    return pltpu.make_async_remote_copy(
        src_ref=src,
        dst_ref=dst,
        send_sem=send.at[at],
        recv_sem=recv.at[at],
        device_id={"fsdp": target},
        device_id_type=MESH,
    )


def cross_scatter_steps(place, partial, total, mine, near_in, far_in, own_sem, send, recv):
    group = place.group
    rows = total.shape[0]
    half = rows // 2

    def own():
        return pltpu.make_async_copy(partial, mine, own_sem)

    def loop(count, body):
        def strip(i, carry):
            body(pl.ds(i * STRIP, STRIP))
            return carry

        lax.fori_loop(0, count // STRIP, strip, 0)

    if not place.square:

        def direct(i):
            target = lax.rem(group + i, place.groups)
            return to_group(partial.at[target], near_in.at[group], send, recv, i - 1, target)

        def begin_direct():
            own().start()
            for i in range(1, place.groups):
                direct(i).start()

        def sum_direct(cut):
            value = mine[group, cut].astype(F32)
            for i in range(1, place.groups):
                value = value + near_in[lax.rem(group + i, place.groups), cut].astype(F32)
            total[cut] = value

        def end_direct():
            own().wait()
            for i in range(1, place.groups):
                source = lax.rem(group - i + place.groups, place.groups)
                piece = partial.at[source]
                to_group(piece, near_in.at[source], send, recv, i - 1, source).wait_recv()
            loop(rows, sum_direct)
            for i in range(1, place.groups):
                direct(i).wait_send()

        return [begin_direct, end_direct]

    def first(at):
        target = (place.beside, place.across)[at]
        piece = partial.at[place.opposite, pl.ds(at * half, half)]
        return to_group(piece, far_in.at[at], send, recv, at, target)

    def second(at, part):
        target = (place.beside, place.across)[at]
        cut = pl.ds(part * half, half)
        return to_group(
            mine.at[target, cut], near_in.at[at, cut], send, recv, 2 + 2 * at + part, target
        )

    def begin():
        own().start()
        for at in range(2):
            first(at).start()

    def plain():
        own().wait()
        for at in range(2):
            second(at, at).start()

    def join():
        for at in range(2):
            target = (place.across, place.beside)[at]
            first(at).wait_recv()

            def one(cut, at=at, target=target):
                place_in = pl.ds(at * half + cut.start, STRIP)
                value = mine[target, place_in].astype(F32) + far_in[at, cut].astype(F32)
                mine[target, place_in] = value.astype(BF)

            loop(half, one)
            second(1 - at, at).start()

    def everything(cut):
        value = mine[group, cut].astype(F32) + near_in[0, cut].astype(F32)
        total[cut] = value + near_in[1, cut].astype(F32)

    def end():
        for at in range(2):
            for part in range(2):
                second(at, part).wait_recv()
        loop(rows, everything)
        for at in range(2):
            first(at).wait_send()
            for part in range(2):
                second(at, part).wait_send()

    return [begin, plain, join, nothing, nothing, nothing, end]


def everyone_steps(place, piece_for, landing, own_sem, send, recv):
    devices = place.groups * place.ranks
    me = place.device

    def copy(i):
        target = lax.rem(me + i, devices)
        return pltpu.make_async_remote_copy(
            src_ref=piece_for(target),
            dst_ref=landing.at[me],
            send_sem=send.at[i],
            recv_sem=recv.at[i],
            device_id=place.name(target),
            device_id_type=MESH,
        )

    def arrival(i):
        source = lax.rem(me - i + devices, devices)
        return pltpu.make_async_remote_copy(
            src_ref=landing.at[source],
            dst_ref=landing.at[source],
            send_sem=send.at[i],
            recv_sem=recv.at[i],
            device_id=place.name(source),
            device_id_type=MESH,
        )

    def start(i, carry):
        copy(i).start()
        return carry

    def finish_one(i, carry):
        arrival(i).wait_recv()
        copy(i).wait_send()
        return carry

    def own():
        return pltpu.make_async_copy(piece_for(me), landing.at[me], own_sem)

    def begin():
        own().start()
        lax.fori_loop(1, devices, start, 0)

    def end():
        own().wait()
        lax.fori_loop(1, devices, finish_one, 0)

    return [begin, nothing, end]


def spread_steps(place, value, everyone, own_sem, send, recv):
    return everyone_steps(place, lambda target: value, everyone, own_sem, send, recv)


def share_steps(place, values, total, landing, own_sem, send, recv):
    phases = everyone_steps(place, lambda target: values.at[target], landing, own_sem, send, recv)

    def add_up():
        total[...] = jnp.sum(landing[...], axis=0)

    return phases + [add_up]


DMA = pltpu.SemaphoreType.DMA


class Transfers:
    def __init__(self, mesh_size, ident=0, moves=(), needed=()):
        self.ranks, self.groups = mesh_size
        self.ident = ident
        self.kinds = [move[0] for move in moves]
        self.parts = [move[2] if len(move) > 2 else None for move in moves]
        self.inputs = [move[1] for move in moves] + list(needed)
        self.moves = len(self.kinds)
        anywhere = pl.BlockSpec(memory_space=pl.ANY)
        vmem = pl.BlockSpec(memory_space=pltpu.VMEM)
        self.in_specs = [anywhere] * len(self.inputs)
        self.shapes, self.out_specs, self.scratch, self.counts = [], [], [], []
        for kind, array, *part in moves:
            shape, spec = array.shape[len(part[0]) :] if part else array.shape, anywhere
            if kind == "gather":
                shape, dtype = (self.ranks * shape[0], shape[1]), BF
                scratch = gather_scratch(self.ranks)
            elif kind == "scatter":
                shape, dtype, spec = (shape[0] // self.ranks, shape[1]), F32, vmem
                scratch = scatter_scratch(self.ranks, *shape)
            elif kind == "cross_scatter":
                rest = shape[1:]
                square = self.groups == 4
                near = (2 if square else self.groups,) + rest
                scratch = [
                    pltpu.VMEM(shape, BF),
                    pltpu.VMEM(near, BF),
                    pltpu.VMEM((2, rest[0] // 2) + rest[1:], BF),
                    DMA,
                    DMA((max(6, self.groups),)),
                    DMA((max(6, self.groups),)),
                ]
                shape, dtype, spec = rest, F32, vmem
            elif kind == "share":
                devices = self.ranks * self.groups
                scratch = [pltpu.VMEM(shape, F32), DMA, DMA((devices,)), DMA((devices,))]
                shape, dtype, spec = shape[1:], F32, vmem
            else:
                devices = self.ranks * self.groups
                shape, dtype = (devices,) + shape, array.dtype
                scratch = [DMA, DMA((devices,)), DMA((devices,))]
            self.shapes.append(jax.ShapeDtypeStruct(shape, dtype))
            self.out_specs.append(spec)
            self.scratch += scratch
            self.counts.append(len(scratch))

    def params(self):
        if not self.moves:
            return pltpu.CompilerParams(vmem_limit_bytes=VMEM_BYTES)
        return pltpu.CompilerParams(
            collective_id=self.ident, has_side_effects=True, vmem_limit_bytes=VMEM_BYTES
        )

    def begin(self, inputs, outputs, scratch):
        if not self.moves:
            return []
        steps_of = {
            "gather": gather_steps,
            "scatter": scatter_steps,
            "cross_scatter": cross_scatter_steps,
            "spread": spread_steps,
            "share": share_steps,
        }
        place = Place(self.ranks, self.groups)
        scratch = list(scratch)
        lines = []
        for i, kind in enumerate(self.kinds):
            taken, scratch = scratch[: self.counts[i]], scratch[self.counts[i] :]
            given = inputs[i] if self.parts[i] is None else inputs[i].at[self.parts[i]]
            lines.append(steps_of[kind](place, given, outputs[i], *taken))

        def phase(number):
            if number == 0:
                kinds = set(self.kinds)
                place.meet(
                    bool(kinds & {"gather", "scatter"}),
                    "cross_scatter" in kinds,
                    bool(kinds & {"spread", "share"}),
                )
            for steps in lines:
                if number < len(steps):
                    steps[number]()

        return [functools.partial(phase, i) for i in range(max(map(len, lines)))]


def nothing():
    pass


def run_all(phases):
    for phase in phases:
        phase()


def exchange_kernel(transfers, *refs):
    count, moves = len(transfers.inputs), transfers.moves
    run_all(transfers.begin(refs[:moves], refs[count : count + moves], refs[count + moves :]))


def exchange(mesh_size, ident, moves, needed=()):
    transfers = Transfers(mesh_size, ident, moves, needed)
    return pl.pallas_call(
        functools.partial(exchange_kernel, transfers),
        out_shape=tuple(transfers.shapes),
        in_specs=transfers.in_specs,
        out_specs=tuple(transfers.out_specs),
        scratch_shapes=transfers.scratch,
        compiler_params=transfers.params(),
    )(*transfers.inputs)


def beside(phases, at, grid_steps, parts):
    step = pl.program_id(0)
    state = None
    for number, part in enumerate(parts):
        for phase, (when, ahead_of) in zip(phases, at):
            if ahead_of == number:
                pl.when(step == when)(phase)
        state = part(state)
    if phases:
        pl.when(step == grid_steps - 1)(lambda: run_all(phases[len(at) :]))


def column(values, at):
    lanes = lax.broadcasted_iota(jnp.int32, values.shape, 1)
    return jnp.sum(jnp.where(lanes == at, values, 0.0), axis=1, keepdims=True)


def routing(experts, length, first_row, rows, router, routes):
    rank = lax.axis_index("tensor")
    logits = dot(rows, router, (1,), (0,))
    lanes = lax.broadcasted_iota(jnp.int32, logits.shape, 1)
    inside = lanes < experts
    top = jnp.max(jnp.where(inside, logits, -1e30), axis=1, keepdims=True)
    exps = jnp.where(inside, jnp.exp(jnp.where(inside, logits, top) - top), 0.0)
    probs = exps / jnp.sum(exps, axis=1, keepdims=True)
    position = first_row + lax.broadcasted_iota(jnp.int32, (rows.shape[0], 1), 0)
    valid = jnp.where(position < length, 1.0, 0.0)
    gate = valid * jax.nn.sigmoid(column(logits, experts))
    named = jnp.max(jnp.where(routes == rank, 1.0, 0.0), axis=0, keepdims=True)
    chosen = valid * jnp.broadcast_to(named, (8, rows.shape[0])).T[:, :1]
    prob = column(probs, rank)
    out = jnp.where(lanes == experts, gate, probs)
    out = jnp.where(lanes == experts + 1, chosen * prob, out)
    out = jnp.where(lanes == experts + 2, chosen, out)
    return jnp.where(lanes == experts + 3, prob, out)


def routing_back(experts, route, shared_dot, expert_dot):
    rank = lax.axis_index("tensor")
    lanes = lax.broadcasted_iota(jnp.int32, route.shape, 1)
    gate, chosen, prob = [column(route, experts + i) for i in (0, 2, 3)]
    expert_grad = chosen * expert_dot
    logits = route * (jnp.where(lanes == rank, expert_grad, 0.0) - expert_grad * prob)
    gate_logit = shared_dot * gate * (1.0 - gate)
    return jnp.where(lanes < experts, logits, jnp.where(lanes == experts, gate_logit, 0.0))


def ffn_kernel(transfers, at, grid_steps, experts, kind, *refs):
    refs = list(refs)

    def take(count):
        taken = refs[:count]
        del refs[:count]
        return taken

    first, last = kind == "first", kind == "last"
    rows_ref, grad_ref, route_ref, w_ref = take(4)
    before = take(1) if first else take(3)
    router_ref = take(1)[0] if first or last else None
    sent = take(len(transfers.inputs))
    hidden_ref, gate_ref, up_ref, out_ref, back_ref, dots_ref = take(6)
    if first:
        made_ref = take(1)[0]
    landed = take(transfers.moves)
    w_vmem, w_sem = take(2)
    phases = transfers.begin(sent, landed, refs)
    step = pl.program_id(0)

    def weights():
        return pltpu.make_async_copy(w_ref, w_vmem, w_sem)

    pl.when(step == 0)(lambda: weights().start())

    def hidden_part(_):
        pl.when(step == 0)(lambda: weights().wait())
        groups, _, depth, units = w_vmem.shape
        gate_w, up_w, down_w = [w_vmem[:, i].reshape(groups * depth, units) for i in range(3)]
        rows, grad = rows_ref[...], grad_ref[...]
        if first:
            length = before[0][0]
            route = routing(experts, length, step * ROW_BLOCK, rows, router_ref[...], route_ref[...])
            made_ref[...] = route
        else:
            route = route_ref[...]
        scale = column(route, experts if first else experts + 1)
        gate_act = dot(rows, gate_w, (1,), (0,))
        up_act = dot(rows, up_w, (1,), (0,))
        back = dot(grad, down_w, (1,), (0,))
        sigmoid = 1.0 / (1.0 + jnp.exp(-gate_act))
        silu = gate_act * sigmoid
        hidden = (silu * up_act).astype(BF).astype(F32)
        dots = jnp.sum(hidden * back, axis=1, keepdims=True)
        scaled = (scale * hidden).astype(BF)
        hidden_ref[...] = scaled
        grad_hidden = scale * back
        grad_gate = (grad_hidden * up_act * (sigmoid * (1.0 + gate_act * (1.0 - sigmoid)))).astype(BF)
        gate_ref[...] = grad_gate
        grad_up = (grad_hidden * silu).astype(BF)
        up_ref[...] = grad_up
        return gate_w, up_w, down_w, scaled, grad_gate, grad_up, route, dots

    def outer_part(state):
        gate_w, up_w, down_w, scaled, grad_gate, grad_up, route, dots = state
        moved = dot(scaled, down_w, (1,), (1,))
        turned = dot(grad_gate, gate_w, (1,), (1,)) + dot(grad_up, up_w, (1,), (1,))
        lanes = lax.broadcasted_iota(jnp.int32, route.shape, 1)
        if first:
            dots_ref[...] = jnp.where(lanes == 0, dots, 0.0)
        else:
            moved = moved + before[0][...].astype(F32)
            turned = turned + before[1][...].astype(F32)
            earlier = before[2][...]
            if last:
                wide = routing_back(experts, route, column(earlier, 0), column(earlier, 1) + dots)
                wide = wide.astype(BF)
                dots_ref[...] = wide
                turned = turned + dot(wide, router_ref[...], (1,), (1,))
            else:
                dots_ref[...] = earlier + jnp.where(lanes == 1, dots, 0.0)
        out_ref[...] = moved.astype(BF)
        back_ref[...] = turned.astype(BF)

    beside(phases, at, grid_steps, [hidden_part, outer_part])


def ffn(experts, kind, rows, grads, route, weights, before, router, transfers, at=()):
    count, width = rows.shape
    units = weights.shape[3]
    first, last = kind == "first", kind == "last"
    steps = count // ROW_BLOCK

    def block(size):
        return pl.BlockSpec((ROW_BLOCK, size), lambda i: (i, 0))

    given = list(before)
    given_specs = [block(width), block(width), block(LANES)]
    if first:
        given_specs = [pl.BlockSpec(memory_space=pltpu.SMEM)]
    if first or last:
        given.append(router)
        given_specs.append(
            pl.BlockSpec(router.shape, lambda i: (0, 0), pipeline_mode=pl.Buffered(1))
        )
    narrow = [jax.ShapeDtypeStruct((count, units), BF)] * 3
    wide = [jax.ShapeDtypeStruct((count, width), BF)] * 2
    dots = [jax.ShapeDtypeStruct((count, LANES), BF if last else F32)]
    dots += [jax.ShapeDtypeStruct((count, LANES), F32)] * first
    results = pl.pallas_call(
        functools.partial(ffn_kernel, transfers, at, steps, experts, kind),
        grid=(steps,),
        in_specs=[
            block(width),
            block(width),
            pl.BlockSpec((route.shape[0], ROW_BLOCK), lambda i: (0, i)) if first else block(LANES),
            pl.BlockSpec(memory_space=pl.ANY),
        ]
        + given_specs
        + transfers.in_specs,
        out_specs=tuple(
            [block(units)] * 3
            + [block(width)] * 2
            + [block(LANES)] * len(dots)
            + transfers.out_specs
        ),
        out_shape=tuple(narrow + wide + dots + transfers.shapes),
        scratch_shapes=[pltpu.VMEM(weights.shape, BF), DMA] + transfers.scratch,
        compiler_params=transfers.params(),
        cost_estimate=pl.CostEstimate(
            flops=12 * count * width * units,
            bytes_accessed=2 * (3 * width * units + 4 * count * width + 3 * count * units),
            transcendentals=count * units,
        ),
    )(rows, grads, route, weights, *given, *transfers.inputs)
    made = 5 + len(dots)
    return results[:3], results[3:made], results[made:]


def ffn_grads_kernel(transfers, at, grid_steps, micros, last, *refs):
    refs = list(refs)

    def take(count):
        taken = refs[:count]
        del refs[:count]
        return taken

    per_micro = [take(6 if last else 5) for _ in range(micros)]
    sent = take(len(transfers.inputs))
    out_ref = take(1)[0]
    wide_ref = take(1)[0] if last else None
    landed = take(transfers.moves)
    phases = transfers.begin(sent, landed, refs)

    def summed(left, right):
        total = None
        for one in per_micro:
            product = dot(one[left][...], one[right][...], (0,), (0,))
            total = product if total is None else total + product
        return total

    def one_product(which):
        def part(_):
            out_ref[0, which] = summed((0, 0, 1)[which], 2 + which).astype(BF)
            if last and which == 2:
                wide_ref[...] = summed(0, 5)

        return part

    beside(phases, at, grid_steps, [one_product(which) for which in range(3)])


def ffn_grads(groups, per_micro, transfers, at=()):
    count, width = per_micro[0][0].shape
    units = per_micro[0][2].shape[1]
    last = len(per_micro[0]) == 6
    depth = width // groups
    columns = pl.BlockSpec((count, depth), lambda i: (0, i))

    def whole(size):
        return pl.BlockSpec((count, size), lambda i: (0, 0), pipeline_mode=pl.Buffered(1))

    shapes = [jax.ShapeDtypeStruct((groups, 3, depth, units), BF)]
    specs = [pl.BlockSpec((1, 3, depth, units), lambda i: (i, 0, 0, 0))]
    taken = [columns, columns] + [whole(units)] * 3
    if last:
        taken.append(whole(LANES))
        shapes.append(jax.ShapeDtypeStruct((width, LANES), F32))
        specs.append(pl.BlockSpec((depth, LANES), lambda i: (i, 0)))
    results = pl.pallas_call(
        functools.partial(ffn_grads_kernel, transfers, at, groups, len(per_micro), last),
        grid=(groups,),
        in_specs=taken * len(per_micro) + transfers.in_specs,
        out_specs=tuple(specs + transfers.out_specs),
        out_shape=tuple(shapes + transfers.shapes),
        scratch_shapes=transfers.scratch,
        compiler_params=transfers.params(),
        cost_estimate=pl.CostEstimate(
            flops=6 * len(per_micro) * count * width * units,
            bytes_accessed=2 * len(per_micro) * (2 * count * width + 3 * count * units)
            + 6 * width * units,
            transcendentals=0,
        ),
    )(*[array for one in per_micro for array in one], *transfers.inputs)
    return results[: len(shapes)], results[len(shapes) :]


def attention_grads_kernel(transfers, grid_steps, micros, *refs):
    refs = list(refs)

    def take(count):
        taken = refs[:count]
        del refs[:count]
        return taken

    per_micro = [take(4) for _ in range(micros)]
    sent = take(len(transfers.inputs))
    out_ref = take(1)[0]
    landed = take(transfers.moves)
    phases = transfers.begin(sent, landed, refs)

    def work(_):
        span = per_micro[0][2].shape[1]
        totals = [None, None]
        for one in per_micro:
            for which in range(2):
                product = dot(one[which][...], one[2 + which][...], (0,), (0,))
                totals[which] = product if totals[which] is None else totals[which] + product
        out_ref[0, :, :span] = totals[0].astype(BF)
        out_ref[0, :, span:] = totals[1].astype(BF)

    beside(phases, [(0, 0), (grid_steps - 1, 0)], grid_steps, [work])


def attention_grads(groups, per_micro, transfers):
    count, width = per_micro[0][0].shape
    depth = width // groups
    spans = [per_micro[0][i].shape[1] for i in (2, 3)]
    columns = pl.BlockSpec((count, depth), lambda i: (0, i))
    whole = [
        pl.BlockSpec((count, size), lambda i: (0, 0), pipeline_mode=pl.Buffered(1)) for size in spans
    ]
    results = pl.pallas_call(
        functools.partial(attention_grads_kernel, transfers, groups, len(per_micro)),
        grid=(groups,),
        in_specs=([columns, columns] + whole) * len(per_micro) + transfers.in_specs,
        out_specs=tuple(
            [pl.BlockSpec((1, depth, sum(spans)), lambda i: (i, 0, 0))] + transfers.out_specs
        ),
        out_shape=tuple(
            [jax.ShapeDtypeStruct((groups, depth, sum(spans)), BF)] + transfers.shapes
        ),
        scratch_shapes=transfers.scratch,
        compiler_params=transfers.params(),
        cost_estimate=pl.CostEstimate(
            flops=2 * len(per_micro) * count * width * sum(spans),
            bytes_accessed=8 * len(per_micro) * count * width,
            transcendentals=0,
        ),
    )(*[array for one in per_micro for array in one], *transfers.inputs)
    return results[0], results[1:]


def opening_kernel(transfers, cut, *refs):
    refs = list(refs)

    def take(count):
        taken = refs[:count]
        del refs[:count]
        return taken

    sent, given = take(len(transfers.inputs)), take(6)
    landed, made = take(transfers.moves), take(3)
    held, packed_refs, in_sem, out_sem = take(6), take(3), take(1)[0], take(1)[0]
    phases = transfers.begin(sent, landed, refs)
    fetches = [
        pltpu.make_async_copy(source, target, in_sem.at[at])
        for at, (source, target) in enumerate(zip(given, held))
    ]
    gives = [
        pltpu.make_async_copy(source, target, out_sem.at[at])
        for at, (source, target) in enumerate(zip(packed_refs, made))
    ]
    for fetch in fetches:
        fetch.start()
    run_all(phases[:1])
    for fetch in fetches[:3]:
        fetch.wait()
    units = held[0].shape[0]
    packed_refs[0][...] = jnp.zeros_like(packed_refs[0])
    for which in range(3):
        packed_refs[0][which, :, :units] = held[which][...].T
    gives[0].start()
    for fetch in fetches[3:]:
        fetch.wait()
    for at, part in ((1, slice(0, cut)), (2, slice(cut, None))):
        packed_refs[at][0] = held[3][0, :, part]
        packed_refs[at][1] = held[4][0, :, part]
        packed_refs[at][2] = held[5][0, part, :].T
        gives[at].start()
    run_all(phases[1:])
    for give in gives:
        give.wait()


def opening(mesh_size, ident, moves, cut, shared, expert):
    transfers = Transfers(mesh_size, ident, moves)
    anywhere = pl.BlockSpec(memory_space=pl.ANY)
    units, depth = shared[0].shape
    sizes = (-(-units // LANES) * LANES, cut, expert[0].shape[2] - cut)
    shapes = [(3, depth, size) for size in sizes]
    results = pl.pallas_call(
        functools.partial(opening_kernel, transfers, cut),
        in_specs=transfers.in_specs + [anywhere] * 6,
        out_specs=tuple(transfers.out_specs + [anywhere] * 3),
        out_shape=tuple(transfers.shapes + [jax.ShapeDtypeStruct(shape, BF) for shape in shapes]),
        scratch_shapes=[pltpu.VMEM(array.shape, BF) for array in (*shared, *expert)]
        + [pltpu.VMEM(shape, BF) for shape in shapes]
        + [DMA((6,)), DMA((3,))]
        + transfers.scratch,
        compiler_params=transfers.params(),
    )(*transfers.inputs, *shared, *expert)
    return results[: transfers.moves], results[transfers.moves :]


def unpack_kernel(turned, *refs):
    count = len(refs) - 3
    for which, out_ref in enumerate(refs[count:]):
        first = 0
        for ref in refs[:count]:
            values = ref[which].astype(F32)
            if turned[which]:
                values = values.T
                size = min(values.shape[0], out_ref.shape[0] - first)
                out_ref[first : first + size, :] = values[:size]
            else:
                size = min(values.shape[1], out_ref.shape[1] - first)
                out_ref[:, first : first + size] = values[:, :size]
            first += size


def unpack(ranges, units, turned):
    depth = ranges[0].shape[1]
    rows = min(LANES, depth)
    shapes = [(units, depth) if turn else (depth, units) for turn in turned]
    return pl.pallas_call(
        functools.partial(unpack_kernel, turned),
        grid=(depth // rows,),
        in_specs=[pl.BlockSpec((3, rows, array.shape[2]), lambda i: (0, i, 0)) for array in ranges],
        out_specs=tuple(
            pl.BlockSpec((units, rows), lambda i: (0, i))
            if turn
            else pl.BlockSpec((rows, units), lambda i: (i, 0))
            for turn in turned
        ),
        out_shape=tuple(jax.ShapeDtypeStruct(shape, F32) for shape in shapes),
        compiler_params=pltpu.CompilerParams(vmem_limit_bytes=VMEM_BYTES),
        cost_estimate=pl.CostEstimate(flops=0, bytes_accessed=18 * depth * units, transcendentals=0),
    )(*ranges)


def rope_tables(seq_len):
    half = HD // 2
    frequency = np.float32(ROPE_BASE) ** (-(2.0 * np.arange(half, dtype=np.float32)) / HD)
    angles = np.arange(seq_len, dtype=np.float32)[:, None] * frequency[None, :].astype(np.float32)
    cosine, sine = np.cos(angles.astype(np.float64)), np.sin(angles.astype(np.float64))
    return (
        jnp.asarray(np.concatenate([cosine, cosine], axis=1).astype(np.float32)),
        jnp.asarray(np.concatenate([-sine, sine], axis=1).astype(np.float32)),
    )


def swap_halves(values):
    half = HD // 2
    return jnp.concatenate([values[:, half:], values[:, :half]], axis=1)


def block_scores(query, keys, first_row, length):
    scores = dot(query, keys, (1,), (1,)) * (HD ** (-0.5))
    rows = first_row + lax.broadcasted_iota(jnp.int32, scores.shape, 0)
    cols = lax.broadcasted_iota(jnp.int32, scores.shape, 1)
    return jnp.where((cols <= rows) & (cols < length), scores, -1e30)


def attend_kernel(heads, transfers, *refs):
    refs = list(refs)

    def take(count):
        taken = refs[:count]
        del refs[:count]
        return taken

    length_ref, x_ref, gain_ref, w_ref, bias_ref, cos_ref, sin_ref = take(7)
    sent = take(len(transfers.inputs))
    normed_ref, qkv_ref, mixed_ref, logs_ref, out_ref = take(5)
    landed = take(transfers.moves)
    rows_vmem, out_vmem, w_vmem, in_sem, normed_sem, out_sem, w_sem = take(7)
    phases = transfers.begin(sent, landed, refs)
    seq_len, width = x_ref.shape
    groups, depth, columns = w_ref.shape
    span = heads * HD
    length = length_ref[0]
    blocks = [pl.ds(row, QB) for row in range(0, seq_len, QB)]

    def fetch(i):
        return pltpu.make_async_copy(x_ref.at[blocks[i]], rows_vmem.at[blocks[i]], in_sem.at[i])

    def keep(i):
        return pltpu.make_async_copy(rows_vmem.at[blocks[i]], normed_ref.at[blocks[i]], normed_sem.at[i])

    def give(i):
        return pltpu.make_async_copy(out_vmem.at[blocks[i]], out_ref.at[blocks[i]], out_sem.at[i])

    fetch_w = pltpu.make_async_copy(w_ref, w_vmem, w_sem)
    fetch(0).start()
    fetch_w.start()
    run_all(phases[:1])
    for i in range(1, len(blocks)):
        fetch(i).start()
    fetch_w.wait()
    weights = w_vmem[...].reshape(groups * depth, columns)
    qkv_w, out_w = weights[:, : 3 * span], weights[:, 3 * span :]
    for i in range(len(blocks)):
        row, end = i * QB, (i + 1) * QB
        if i >= 2:
            run_all(phases[i - 1 : i])
        fetch(i).wait()
        values = rows_vmem[row:end, :].astype(F32)
        normed = (normalize(values)[0] * gain_ref[...]).astype(BF)
        rows_vmem[row:end, :] = normed
        keep(i).start()
        pre = dot(normed, qkv_w, (1,), (0,)) + bias_ref[...]
        cosine, sine = cos_ref[row:end, :], sin_ref[row:end, :]
        for at in range(0, 3 * span, HD):
            part = pre[:, at : at + HD]
            if at < 2 * span:
                part = part * cosine + swap_halves(part) * sine
            qkv_ref[row:end, at : at + HD] = part.astype(BF)
        for head in range(heads):
            q_at, k_at, v_at = (head * HD, span + head * HD, 2 * span + head * HD)
            scores = block_scores(
                qkv_ref[row:end, q_at : q_at + HD], qkv_ref[:end, k_at : k_at + HD], row, length
            )
            top = jnp.max(scores, axis=1, keepdims=True)
            exps = jnp.exp(scores - top)
            totals = jnp.sum(exps, axis=1, keepdims=True)
            shares = exps * (1.0 / totals)
            logs_ref[row:end, head : head + 1] = top + jnp.log(totals)
            mixed = dot(shares.astype(BF), qkv_ref[:end, v_at : v_at + HD], (1,), (0,))
            mixed_ref[row:end, q_at : q_at + HD] = mixed.astype(BF)
        out_vmem[row:end, :] = dot(mixed_ref[row:end, :], out_w, (1,), (1,)).astype(BF)
        give(i).start()
    run_all(phases[max(1, len(blocks) - 1) :])
    for i in range(len(blocks)):
        keep(i).wait()
        give(i).wait()


def attend_back_kernel(heads, transfers, *refs):
    refs = list(refs)

    def take(count):
        taken = refs[:count]
        del refs[:count]
        return taken

    length_ref, datt_ref, w_ref, qkv_ref, logs_ref, cos_ref, sin_ref = take(7)
    sent = take(len(transfers.inputs))
    turned_ref, sums_ref, out_ref = take(3)
    landed = take(transfers.moves)
    rows_vmem, out_vmem, w_vmem, grad_vmem, key_acc, value_acc, in_sem, out_sem, w_sem = take(9)
    phases = transfers.begin(sent, landed, refs)
    run_all(phases[:1])
    seq_len, width = datt_ref.shape
    groups, depth, columns = w_ref.shape
    span = heads * HD
    length = length_ref[0]
    scale = HD ** (-0.5)
    blocks = [pl.ds(row, QB) for row in range(0, seq_len, QB)]

    def fetch(i):
        return pltpu.make_async_copy(datt_ref.at[blocks[i]], rows_vmem.at[blocks[i]], in_sem.at[i])

    def give(i):
        return pltpu.make_async_copy(out_vmem.at[blocks[i]], out_ref.at[blocks[i]], out_sem.at[i])

    fetch_w = pltpu.make_async_copy(w_ref, w_vmem, w_sem)
    fetch_w.start()
    for i in range(len(blocks)):
        fetch(i).start()
    fetch_w.wait()
    weights = w_vmem[...].reshape(groups * depth, columns)
    qkv_w, out_w = weights[:, : 3 * span], weights[:, 3 * span :]
    key_acc[...] = jnp.zeros_like(key_acc)
    value_acc[...] = jnp.zeros_like(value_acc)
    query_sums = [jnp.zeros((1, HD), F32) for _ in range(heads)]
    for i in range(len(blocks)):
        row, end = i * QB, (i + 1) * QB
        if i >= 2:
            run_all(phases[i - 1 : i])
        fetch(i).wait()
        grad_vmem[row:end, :] = dot(rows_vmem[row:end, :], out_w, (1,), (0,)).astype(BF)
        for head in range(heads):
            q_at, k_at, v_at = (head * HD, span + head * HD, 2 * span + head * HD)
            query = qkv_ref[row:end, q_at : q_at + HD]
            keys = qkv_ref[:end, k_at : k_at + HD]
            grad = grad_vmem[row:end, q_at : q_at + HD]
            shares = jnp.exp(
                block_scores(query, keys, row, length) - logs_ref[row:end, head : head + 1]
            )
            grad_shares = dot(grad, qkv_ref[:end, v_at : v_at + HD], (1,), (1,))
            inner = jnp.sum(shares * grad_shares, axis=1, keepdims=True)
            grad_scores = (scale * shares * (grad_shares - inner)).astype(BF)
            turned = dot(grad_scores, keys, (1,), (0,))
            grad_query = (
                turned * cos_ref[row:end, :] - swap_halves(turned) * sin_ref[row:end, :]
            ).astype(BF)
            turned_ref[row:end, q_at : q_at + HD] = grad_query
            query_sums[head] += jnp.sum(grad_query.astype(F32), axis=0, keepdims=True)
            key_acc[:end, q_at : q_at + HD] += dot(grad_scores, query, (0,), (0,))
            value_acc[:end, q_at : q_at + HD] += dot(shares.astype(BF), grad, (0,), (0,))
    done = max(1, len(blocks) - 1)
    run_all(phases[done : done + 1])
    key_sums = [jnp.zeros((1, HD), F32) for _ in range(heads)]
    value_sums = [jnp.zeros((1, HD), F32) for _ in range(heads)]
    for i in range(len(blocks)):
        row, end = i * QB, (i + 1) * QB
        for head in range(heads):
            q_at, k_at, v_at = (head * HD, span + head * HD, 2 * span + head * HD)
            turned = key_acc[row:end, q_at : q_at + HD]
            grad_key = (
                turned * cos_ref[row:end, :] - swap_halves(turned) * sin_ref[row:end, :]
            ).astype(BF)
            grad_value = value_acc[row:end, q_at : q_at + HD].astype(BF)
            turned_ref[row:end, k_at : k_at + HD] = grad_key
            turned_ref[row:end, v_at : v_at + HD] = grad_value
            key_sums[head] += jnp.sum(grad_key.astype(F32), axis=0, keepdims=True)
            value_sums[head] += jnp.sum(grad_value.astype(F32), axis=0, keepdims=True)
        out_vmem[row:end, :] = dot(turned_ref[row:end, :], qkv_w, (1,), (1,)).astype(BF)
        give(i).start()
    for at, sums in enumerate(query_sums + key_sums + value_sums):
        sums_ref[:, at * HD : (at + 1) * HD] = sums
    for i in range(len(blocks)):
        give(i).wait()
    run_all(phases[done + 1 :])


def in_vmem(count):
    return [pl.BlockSpec(memory_space=pltpu.VMEM)] * count


def attend(length, rows, gain, weights, bias, cosine, sine, transfers):
    seq_len, width = rows.shape
    span = weights.shape[2] // 4
    heads, blocks = span // HD, seq_len // QB
    anywhere = pl.BlockSpec(memory_space=pl.ANY)
    results = pl.pallas_call(
        functools.partial(attend_kernel, heads, transfers),
        out_shape=tuple(
            [
                jax.ShapeDtypeStruct((seq_len, width), BF),
                jax.ShapeDtypeStruct((seq_len, 3 * span), BF),
                jax.ShapeDtypeStruct((seq_len, span), BF),
                jax.ShapeDtypeStruct((seq_len, heads), F32),
                jax.ShapeDtypeStruct((seq_len, width), BF),
            ]
            + transfers.shapes
        ),
        in_specs=[pl.BlockSpec(memory_space=pltpu.SMEM), anywhere]
        + in_vmem(1)
        + [anywhere]
        + in_vmem(3)
        + transfers.in_specs,
        out_specs=tuple([anywhere] + in_vmem(3) + [anywhere] + transfers.out_specs),
        scratch_shapes=[pltpu.VMEM((seq_len, width), BF)] * 2
        + [pltpu.VMEM(weights.shape, BF)]
        + [DMA((blocks,))] * 3
        + [DMA]
        + transfers.scratch,
        compiler_params=transfers.params(),
        cost_estimate=pl.CostEstimate(
            flops=8 * seq_len * width * span + 3 * span * seq_len * seq_len,
            bytes_accessed=8 * seq_len * width,
            transcendentals=heads * seq_len * seq_len,
        ),
    )(length, rows, gain, weights, bias, cosine, sine, *transfers.inputs)
    return results[:5], results[5:]


def attend_back(length, rows, weights, qkv, logs, cosine, sine, transfers):
    seq_len, width = rows.shape
    span = weights.shape[2] // 4
    heads, blocks = span // HD, seq_len // QB
    anywhere = pl.BlockSpec(memory_space=pl.ANY)
    results = pl.pallas_call(
        functools.partial(attend_back_kernel, heads, transfers),
        out_shape=tuple(
            [
                jax.ShapeDtypeStruct((seq_len, 3 * span), BF),
                jax.ShapeDtypeStruct((1, 3 * span), F32),
                jax.ShapeDtypeStruct((seq_len, width), BF),
            ]
            + transfers.shapes
        ),
        in_specs=[pl.BlockSpec(memory_space=pltpu.SMEM), anywhere, anywhere]
        + in_vmem(4)
        + transfers.in_specs,
        out_specs=tuple(in_vmem(2) + [anywhere] + transfers.out_specs),
        scratch_shapes=[pltpu.VMEM((seq_len, width), BF)] * 2
        + [pltpu.VMEM(weights.shape, BF), pltpu.VMEM((seq_len, span), BF)]
        + [pltpu.VMEM((seq_len, span), F32)] * 2
        + [DMA((blocks,))] * 2
        + [DMA]
        + transfers.scratch,
        compiler_params=transfers.params(),
        cost_estimate=pl.CostEstimate(
            flops=8 * seq_len * width * span + 8 * span * seq_len * seq_len,
            bytes_accessed=8 * seq_len * width,
            transcendentals=heads * seq_len * seq_len,
        ),
    )(length, rows, weights, qkv, logs, cosine, sine, *transfers.inputs)
    return results[:3], results[3:]


def padded(values, axis):
    size = values.shape[axis]
    more = -size % LANES
    if not more:
        return values
    return jnp.pad(values, [(0, more if i == axis else 0) for i in range(values.ndim)])


def packed(values, kind):
    tile = LANES * (16 if kind == BF else 8)
    values = values.astype(kind)
    return padded_to(values, -(-values.shape[-1] // tile) * tile)


def padded_to(values, size):
    more = size - values.shape[-1]
    return jnp.pad(values, [(0, 0)] * (values.ndim - 1) + [(0, more)])


def local(
    tokens,
    lengths,
    routes,
    norm1_gain,
    w_query,
    w_key,
    w_value,
    b_query,
    b_key,
    b_value,
    w_out,
    norm2_gain,
    router,
    shared_gate_vec,
    shared_gate,
    shared_up,
    shared_down,
    expert_gate,
    expert_up,
    expert_down,
    cotangent,
):
    ranks = lax.axis_size("tensor")
    groups = lax.axis_size("fsdp")
    rank = lax.axis_index("tensor")
    micros, _, rows, width = tokens.shape
    seq_len = rows * ranks
    heads = w_query.shape[1] // HD
    span = heads * HD
    experts = ranks * expert_gate.shape[0]
    shared_units = shared_gate.shape[1]
    expert_units = expert_gate.shape[2]
    cut = expert_units // (2 * LANES) * LANES
    own_first = rank * rows
    local_pos = own_first + jnp.arange(rows, dtype=jnp.int32)

    per_device = norm1_gain.shape[0]
    small = jnp.concatenate(
        [
            norm1_gain,
            norm2_gain,
            shared_gate_vec,
            router.reshape(-1),
            b_query.reshape(-1),
            b_key.reshape(-1),
            b_value.reshape(-1),
        ]
    )
    attn_own = jnp.concatenate([w_query, w_key, w_value, w_out.T], axis=1)
    mesh_size = (ranks, groups)
    attn_own = with_layout_constraint(attn_own, Layout((0, 1)))
    attn_w = lax.all_gather(attn_own, "fsdp", axis=0, tiled=True)
    attn_w = with_layout_constraint(attn_w, Layout((0, 1))).reshape((groups,) + attn_own.shape)
    (small_all, rows_a), own_ranges = opening(
        mesh_size,
        2,
        [
            ("spread", packed(small, BF).reshape(-1, LANES)),
            ("gather", tokens, (0, 0)),
        ],
        cut,
        (shared_gate.T, shared_up.T, shared_down),
        (expert_gate, expert_up, expert_down),
    )
    small_all = small_all.reshape(groups * ranks, -1)
    gain_one = small_all[:, :per_device].reshape(-1).astype(F32)
    gain_two = small_all[:, per_device : 2 * per_device].reshape(-1).astype(F32)
    gate_vec = small_all[:, 2 * per_device : 3 * per_device].reshape(-1)
    bias_at = per_device * (3 + experts)
    router_full = small_all[:, 3 * per_device : bias_at].reshape(width, experts)
    router_wide = padded_to(jnp.concatenate([router_full, gate_vec[:, None]], axis=1), LANES)
    own_bias = lax.dynamic_index_in_dim(
        small_all.reshape(groups, ranks, -1), rank, 1, False
    )[:, bias_at : small.shape[0]].reshape(groups, 3, heads, HD // groups)
    bias = own_bias.transpose(1, 2, 0, 3).reshape(1, 3 * span).astype(F32)

    weights = [lax.all_gather(own_range, "fsdp", axis=0) for own_range in own_ranges]

    cosine, sine = rope_tables(seq_len)
    idle = Transfers(mesh_size)
    token_own = [tokens[m, 0] for m in range(micros)]
    grads_own = []
    for m in range(micros):
        inside = (local_pos < lengths[m, 0])[:, None]
        grads_own.append(jnp.where(inside, cotangent[m, 0], jnp.zeros((), BF)))

    def moving(ident, *moves, needed=()):
        return Transfers(mesh_size, ident, moves, needed)

    def attention(m, token_rows, transfers):
        return attend(lengths[m], token_rows, gain_one[None], attn_w, bias, cosine, sine, transfers)

    def second_norm(m, attended):
        hidden = token_own[m].astype(F32) + attended
        unit, inverse = normalize(hidden)
        return hidden, unit, inverse, (unit * gain_two).astype(BF)

    def second_norm_back(m, state, summed):
        grad_hidden, gain_part = norm_back(summed, state[1], state[2], gain_two)
        grad_hidden = grad_hidden + grads_own[m].astype(F32)
        return grad_hidden, grad_hidden.astype(BF), gain_part

    def first_norm_back(m, grad_hidden, summed):
        unit, inverse = normalize(token_own[m].astype(F32))
        grad_inputs, gain_part = norm_back(summed, unit, inverse, gain_one)
        return (grad_inputs + grad_hidden).astype(BF), gain_part

    def finished(m, hidden, moved):
        inside = (local_pos < lengths[m, 0]).astype(F32)[:, None]
        return (inside * (hidden + moved)).astype(BF)

    att_a, (rows_b,) = attention(0, rows_a, moving(3, ("gather", tokens, (1, 0))))
    att_b, (grad_a, sum_a) = attention(
        1, rows_b, moving(4, ("gather", cotangent, (0, 0)), ("scatter", att_a[4]))
    )
    norm_a = second_norm(0, sum_a)
    two_a, sum_b = exchange(mesh_size, 5, [("gather", norm_a[3]), ("scatter", att_b[4])])
    norm_b = second_norm(1, sum_b)

    def over_groups(grads):
        flat = grads.reshape(-1, grads.shape[-1])
        summed = lax.psum_scatter(flat, "fsdp", scatter_dimension=0, tiled=True)
        return with_layout_constraint(summed, Layout((0, 1))).reshape(grads.shape[1:])

    def grads_of(which, transfers, at=()):
        per_micro = []
        for key in range(micros):
            rows_two, grads = ((two_a, grad_a), (two_b, grad_b))[key]
            scaled, gate, up = act[which, key]
            more = [(acc_a, acc_b)[key][2]] if which == 2 else []
            per_micro.append([rows_two, grads, gate, up, scaled] + more)
        return ffn_grads(groups, per_micro, transfers, at)

    act = {}
    part = functools.partial(ffn, experts)
    single = ((0, 0), (1, 0), (2, 0), (3, 0))
    act[0, 0], acc_a, (grad_b,) = part(
        "first", two_a, grad_a, routes[0, 0].T, weights[0], [lengths[0]], router_wide,
        moving(6, ("gather", cotangent, (1, 0))), single,
    )
    acc_a, route_a = acc_a[:3], acc_a[3]
    act[1, 0], acc_a, (two_b,) = part(
        "next", two_a, grad_a, route_a, weights[1], acc_a, None,
        moving(7, ("gather", norm_b[3])), single,
    )
    act[0, 1], acc_b, _ = part(
        "first", two_b, grad_b, routes[1, 0].T, weights[0], [lengths[1]], router_wide, idle
    )
    acc_b, route_b = acc_b[:3], acc_b[3]
    (grads_0,), _ = grads_of(0, idle)
    range_0 = over_groups(grads_0)
    act[2, 0], acc_a, _ = part(
        "last", two_a, grad_a, route_a, weights[2], acc_a, router_wide, moving(0, needed=[grads_0])
    )
    act[1, 1], acc_b, (down_a,) = part(
        "next", two_b, grad_b, route_b, weights[1], acc_b, None,
        moving(8, ("scatter", acc_a[1])), single,
    )
    hid_a, send_a, gain_part_a = second_norm_back(0, norm_a, down_a)
    (grads_1,), (datt_a,) = grads_of(
        1, moving(9, ("gather", send_a)), ((0, 0), (1, 0), (2, 0), (3, 0))
    )
    range_1 = over_groups(grads_1)
    act[2, 1], acc_b, (moved_a,) = part(
        "last", two_b, grad_b, route_b, weights[2], acc_b, router_wide,
        moving(10, ("scatter", acc_a[0]), needed=[grads_1]), single,
    )
    (grads_2, total_wide), (down_b,) = grads_of(
        2, moving(11, ("scatter", acc_b[1]), needed=[range_0]), ((0, 0), (1, 1), (2, 1), (3, 1))
    )
    range_2 = over_groups(grads_2)
    hid_b, send_b, gain_part_b = second_norm_back(1, norm_b, down_b)

    (grad_qkv_a, sums_a, first_a), (datt_b,) = attend_back(
        lengths[0], datt_a, attn_w, att_a[1], att_a[3], cosine, sine,
        moving(12, ("gather", send_b)),
    )
    (grad_qkv_b, sums_b, first_b), (one_a,) = attend_back(
        lengths[1], datt_b, attn_w, att_b[1], att_b[3], cosine, sine,
        moving(15, ("scatter", first_a), needed=[range_1]),
    )
    attn_parts, (one_b,) = attention_grads(
        groups,
        [
            (att_a[0], datt_a, grad_qkv_a, att_a[2]),
            (att_b[0], datt_b, grad_qkv_b, att_b[2]),
        ],
        moving(13, ("scatter", first_b)),
    )

    grad_in_a, one_part_a = first_norm_back(0, hid_a, one_a)
    grad_in_b, one_part_b = first_norm_back(1, hid_b, one_b)

    devices = groups * ranks
    bias_part = (sums_a + sums_b).reshape(3, heads, groups, HD // groups).transpose(2, 0, 1, 3)
    bias_part = bias_part.reshape(groups, 1, -1)
    own_rank = (jnp.arange(ranks, dtype=jnp.int32) == rank).astype(F32)[None, :, None]
    parts = jnp.concatenate(
        [
            (one_part_a + one_part_b).reshape(devices, -1),
            (gain_part_a + gain_part_b).reshape(devices, -1),
            total_wide[:, : experts + 1].reshape(devices, -1),
            (bias_part * own_rank).reshape(devices, -1),
        ],
        axis=1,
    )
    shares, attn_g, moved_b = exchange(
        mesh_size,
        14,
        [
            ("share", packed(parts, F32).reshape(devices, -1, LANES)),
            ("cross_scatter", attn_parts),
            ("scatter", acc_b[0]),
        ],
        [range_2],
    )
    shares = shares.reshape(-1)
    wide_g = shares[2 * per_device : (3 + experts) * per_device].reshape(per_device, experts + 1)
    bias_g = shares[bias_at : parts.shape[1]].reshape(3, heads, HD // groups)

    shared_g = unpack([range_0], shared_units, (True, True, True))
    expert_g = unpack([range_1, range_2], expert_units, (False, False, True))
    return (
        jnp.stack([finished(0, norm_a[0], moved_a), finished(1, norm_b[0], moved_b)])[:, None],
        jnp.stack([grad_in_a, grad_in_b])[:, None],
        shares[:per_device],
        attn_g[:, :span],
        attn_g[:, span : 2 * span],
        attn_g[:, 2 * span : 3 * span],
        bias_g[0],
        bias_g[1],
        bias_g[2],
        attn_g[:, 3 * span :].T,
        shares[per_device : 2 * per_device],
        wide_g[:, :experts],
        wide_g[:, experts],
        shared_g[0].T,
        shared_g[1].T,
        shared_g[2],
        expert_g[0][None],
        expert_g[1][None],
        expert_g[2][None],
    )


def solution(mesh):
    in_specs = (
        P(None, "fsdp", "tensor", None),
        P(None, "fsdp"),
        P(None, "fsdp", None, None),
        P(("fsdp", "tensor")),
        P("fsdp", "tensor"),
        P("fsdp", "tensor"),
        P("fsdp", "tensor"),
        P("tensor", "fsdp"),
        P("tensor", "fsdp"),
        P("tensor", "fsdp"),
        P("tensor", "fsdp"),
        P(("fsdp", "tensor")),
        P(("fsdp", "tensor"), None),
        P(("fsdp", "tensor")),
        P("fsdp", "tensor"),
        P("fsdp", "tensor"),
        P("tensor", "fsdp"),
        P("tensor", "fsdp", None),
        P("tensor", "fsdp", None),
        P("tensor", None, "fsdp"),
        P(None, "fsdp", "tensor", None),
    )
    out_specs = (
        P(None, "fsdp", "tensor", None),
        P(None, "fsdp", "tensor", None),
        P(("fsdp", "tensor")),
        P("fsdp", "tensor"),
        P("fsdp", "tensor"),
        P("fsdp", "tensor"),
        P("tensor", "fsdp"),
        P("tensor", "fsdp"),
        P("tensor", "fsdp"),
        P("tensor", "fsdp"),
        P(("fsdp", "tensor")),
        P(("fsdp", "tensor"), None),
        P(("fsdp", "tensor")),
        P("fsdp", "tensor"),
        P("fsdp", "tensor"),
        P("tensor", "fsdp"),
        P("tensor", "fsdp", None),
        P("tensor", "fsdp", None),
        P("tensor", None, "fsdp"),
    )
    return jax.shard_map(local, mesh=mesh, in_specs=in_specs, out_specs=out_specs, check_vma=False)
```

```python
import functools

import jax
import jax.numpy as jnp
import numpy as np
from jax import lax
from jax.experimental import pallas as pl
from jax.experimental.layout import Layout, with_layout_constraint
from jax.experimental.pallas import tpu as pltpu
from jax.sharding import PartitionSpec as P

HD = 128
EPSILON = 1e-06
ROPE_BASE = 1000000.0
BF = jnp.bfloat16
F32 = jnp.float32
MESH = pl.DeviceIdType.MESH
QB = 256
LANES = 128
CHUNKS = 2
STRIP = 16
ROW_BLOCK = 256
VMEM_BYTES = 60 << 20


def dot(left, right, left_dims, right_dims):
    return lax.dot_general(
        left, right, ((left_dims, right_dims), ((), ())), preferred_element_type=F32
    )


def normalize(values):
    inverse = lax.rsqrt(jnp.mean(values * values, axis=-1, keepdims=True) + EPSILON)
    return (values * inverse, inverse)


def norm_back(grad_normed, unit, inverse, gain):
    grad_unit = grad_normed * gain
    grad_values = inverse * (grad_unit - unit * jnp.mean(grad_unit * unit, axis=-1, keepdims=True))
    return (grad_values, jnp.sum(grad_normed * unit, axis=0))


def remote(src, dst, sems, at, target):
    return pltpu.make_async_remote_copy(
        src_ref=src,
        dst_ref=dst,
        send_sem=sems[0].at[at],
        recv_sem=sems[1].at[at],
        device_id={"tensor": target},
        device_id_type=MESH,
    )


def gather_scratch(ranks):
    chips = ranks // 2
    pair = [pltpu.SemaphoreType.DMA((chips, CHUNKS))] * 2
    cross = [pltpu.SemaphoreType.DMA((2 * chips, CHUNKS))] * 2
    return [pltpu.SemaphoreType.DMA] + pair + pair + cross


def gather_steps(place, block, whole, local_sem, up_s, up_r, down_s, down_r, cross_s, cross_r):
    chips, chip, core = place.chips, place.chip, place.core
    rows = block.shape[0]
    part = rows // CHUNKS
    up, down, cross = (up_s, up_r), (down_s, down_r), (cross_s, cross_r)

    def at(owner, chunk):
        first = pl.multiple_of((2 * owner + core) * rows + chunk * part, part)
        return whole.at[pl.ds(first, part)]

    def theirs(owner, chunk):
        first = pl.multiple_of((2 * owner + 1 - core) * rows + chunk * part, part)
        return whole.at[pl.ds(first, part)]

    def own(chunk):
        return block.at[pl.ds(chunk * part, part)]

    def upward(step, chunk):
        source = own(chunk) if step == 0 else at(chip - step, chunk)
        return remote(source, at(chip - step, chunk), up, (step, chunk), place.above)

    def downward(step, chunk):
        source = own(chunk) if step == 0 else at(chip + step, chunk)
        return remote(source, at(chip + step, chunk), down, (step, chunk), place.below)

    def across(slot, owner, chunk):
        source = own(chunk) if slot == 0 else at(owner, chunk)
        return remote(source, at(owner, chunk), cross, (slot, chunk), place.partner)

    def arrived(slot, owner, chunk):
        return remote(theirs(owner, chunk), theirs(owner, chunk), cross, (slot, chunk), place.partner)

    def arrived_up(step, chunk):
        return remote(at(chip - step, chunk), at(chip - step, chunk), up, (step - 1, chunk), place.partner)

    def arrived_down(step, chunk):
        return remote(at(chip + step, chunk), at(chip + step, chunk), down, (step - 1, chunk), place.partner)

    both = range(CHUNKS)

    def mine():
        first = pl.multiple_of((2 * chip + core) * rows, rows)
        return pltpu.make_async_copy(block, whole.at[pl.ds(first, rows)], local_sem)

    def begin():
        for chunk in both:
            pl.when(place.not_top)(lambda: upward(0, chunk).start())
            pl.when(place.not_bottom)(lambda: downward(0, chunk).start())
        for chunk in both:
            across(0, chip, chunk).start()
        mine().start()

    def hop(step, chunk):
        @pl.when(chip >= step)
        def _():
            arrived_up(step, chunk).wait_recv()
            pl.when(place.not_top)(lambda: upward(step, chunk).start())
            across(2 * step - 1, chip - step, chunk).start()

        @pl.when(chip < chips - step)
        def _():
            arrived_down(step, chunk).wait_recv()
            pl.when(place.not_bottom)(lambda: downward(step, chunk).start())
            across(2 * step, chip + step, chunk).start()

    def end():
        mine().wait()
        for step in range(chips):
            for chunk in both:
                if step == 0:
                    arrived(0, chip, chunk).wait_recv()
                    across(0, chip, chunk).wait_send()
                else:

                    @pl.when(chip >= step)
                    def _():
                        arrived(2 * step - 1, chip - step, chunk).wait_recv()
                        across(2 * step - 1, chip - step, chunk).wait_send()

                    @pl.when(chip < chips - step)
                    def _():
                        arrived(2 * step, chip + step, chunk).wait_recv()
                        across(2 * step, chip + step, chunk).wait_send()

                @pl.when(place.not_top & (chip >= step))
                def _():
                    upward(step, chunk).wait_send()

                @pl.when(place.not_bottom & (chip < chips - step))
                def _():
                    downward(step, chunk).wait_send()

    hops = [functools.partial(hop, step, chunk) for step in range(1, chips) for chunk in both]
    return [begin] + hops + [end]


def scatter_scratch(ranks, rows, width):
    chips = ranks // 2
    line = [pltpu.SemaphoreType.DMA((chips, CHUNKS))] * 2
    buffers = [pltpu.VMEM((chips, rows, width), BF)] * 5
    return buffers + [pltpu.SemaphoreType.DMA((chips,))] + line * 3


def scatter_steps(
    place, partial, total, kept, pair, held, up_in, down_in, keep_sem,
    up_s, up_r, down_s, down_r, cross_s, cross_r,
):
    chips, chip, core = place.chips, place.chip, place.core
    rows = total.shape[0]
    part = rows // CHUNKS
    up, down, cross = (up_s, up_r), (down_s, down_r), (cross_s, cross_r)
    both = range(CHUNKS)

    def keep(k):
        first = pl.multiple_of((2 * k + core) * rows, rows)
        return pltpu.make_async_copy(partial.at[pl.ds(first, rows)], kept.at[k], keep_sem.at[k])

    def across(k, chunk):
        first = pl.multiple_of((2 * k + 1 - core) * rows + chunk * part, part)
        return remote(
            partial.at[pl.ds(first, part)],
            pair.at[k, pl.ds(chunk * part, part)],
            cross,
            (k, chunk),
            place.partner,
        )

    def upward(step, k, chunk):
        cut = pl.ds(chunk * part, part)
        return remote(held.at[k, cut], up_in.at[step, cut], up, (step, chunk), place.above)

    def downward(step, k, chunk):
        cut = pl.ds(chunk * part, part)
        return remote(held.at[k, cut], down_in.at[step, cut], down, (step, chunk), place.below)

    def came(buffer, sems, step, chunk):
        piece = buffer.at[step, pl.ds(chunk * part, part)]
        return remote(piece, piece, sems, (step, chunk), place.partner)

    def add(k, chunk, target, others):
        def strip(i, carry):
            cut = pl.ds(chunk * part + i * STRIP, STRIP)
            value = kept[k, cut].astype(F32) + pair[k, cut].astype(F32)
            for ref, slot in others:
                value = value + ref[slot, cut].astype(F32)
            if target is None:
                total[cut] = value
            else:
                target[k, cut] = value.astype(BF)
            return carry

        lax.fori_loop(0, part // STRIP, strip, 0)

    order = []
    for i in range(chips):
        for k in (chips - 1 - i, i):
            if k not in order:
                order.append(k)
    def begin():
        for k in order:
            keep(k).start()
            for chunk in both:
                across(k, chunk).start()

    def hop(step, chunk):
        @pl.when(place.not_top & (chip <= step - 1))
        def _():
            k = chip + chips - step
            if chunk == 0:
                keep(k).wait()
            across(k, chunk).wait_recv()

            @pl.when(place.not_bottom)
            def _():
                came(up_in, up, step - 1, chunk).wait_recv()
                add(k, chunk, held, [(up_in, step - 1)])

            pl.when(jnp.logical_not(place.not_bottom))(lambda: add(k, chunk, held, []))
            upward(step, k, chunk).start()

        @pl.when(place.not_bottom & (chip >= chips - step))
        def _():
            k = chip - (chips - step)
            if chunk == 0:
                keep(k).wait()
            across(k, chunk).wait_recv()

            @pl.when(place.not_top)
            def _():
                came(down_in, down, step - 1, chunk).wait_recv()
                add(k, chunk, held, [(down_in, step - 1)])

            pl.when(jnp.logical_not(place.not_top))(lambda: add(k, chunk, held, []))
            downward(step, k, chunk).start()

    last = chips - 1

    def add_last(chunk):
        if chunk == 0:
            keep(chip).wait()
        across(chip, chunk).wait_recv()

        @pl.when(place.not_top & place.not_bottom)
        def _():
            came(up_in, up, last, chunk).wait_recv()
            came(down_in, down, last, chunk).wait_recv()
            add(chip, chunk, None, [(up_in, last), (down_in, last)])

        @pl.when(jnp.logical_not(place.not_top))
        def _():
            came(up_in, up, last, chunk).wait_recv()
            add(chip, chunk, None, [(up_in, last)])

        @pl.when(jnp.logical_not(place.not_bottom))
        def _():
            came(down_in, down, last, chunk).wait_recv()
            add(chip, chunk, None, [(down_in, last)])

    def end():
        for chunk in both:
            for k in range(chips):
                across(k, chunk).wait_send()
            for step in range(1, chips):

                @pl.when(place.not_top & (chip <= step - 1))
                def _():
                    upward(step, chip + chips - step, chunk).wait_send()

                @pl.when(place.not_bottom & (chip >= chips - step))
                def _():
                    downward(step, chip - (chips - step), chunk).wait_send()

    def first():
        begin()
        for chunk in both:
            hop(1, chunk)

    hops = [functools.partial(hop, step, chunk) for step in range(2, chips) for chunk in both]
    return [first] + hops + [functools.partial(add_last, chunk) for chunk in both] + [end]


class Place:
    def __init__(self, ranks, groups):
        rank, group = lax.axis_index("tensor"), lax.axis_index("fsdp")
        self.ranks, self.groups = ranks, groups
        self.chips = ranks // 2
        self.chip, self.core = rank // 2, rank % 2
        self.partner = rank + 1 - 2 * self.core
        self.above, self.below = rank + 2, rank - 2
        self.not_top = self.chip < self.chips - 1
        self.not_bottom = self.chip > 0
        self.rank, self.group = rank, group
        self.device = group * ranks + rank
        near, far = group % 2, group // 2
        self.beside = 2 * far + 1 - near
        self.across = 2 * (1 - far) + near
        self.opposite = 2 * (1 - far) + 1 - near
        self.square = groups == 4

    def name(self, device):
        return {"fsdp": device // self.ranks, "tensor": device % self.ranks}

    def meet(self, line, cross, everyone):
        barrier = pltpu.get_barrier_semaphore()

        def greet(name):
            pl.semaphore_signal(barrier, 1, device_id=name, device_id_type=MESH)

        if everyone:
            devices = self.groups * self.ranks

            def one(i, carry):
                greet(self.name(lax.rem(self.device + i, devices)))
                return carry

            lax.fori_loop(1, devices, one, 0)
            pl.semaphore_wait(barrier, devices - 1)
            return
        peers = 0
        if line:
            greet({"tensor": self.partner})
            pl.when(self.not_top)(lambda: greet({"tensor": self.above}))
            pl.when(self.not_bottom)(lambda: greet({"tensor": self.below}))
            peers = 1 + self.not_top.astype(jnp.int32) + self.not_bottom.astype(jnp.int32)
        if cross and self.square:
            greet({"fsdp": self.beside})
            greet({"fsdp": self.across})
            peers = peers + 2
        elif cross:
            for i in range(1, self.groups):
                greet({"fsdp": lax.rem(self.group + i, self.groups)})
            peers = peers + self.groups - 1
        pl.semaphore_wait(barrier, peers)


def to_group(src, dst, send, recv, at, target):
    return pltpu.make_async_remote_copy(
        src_ref=src,
        dst_ref=dst,
        send_sem=send.at[at],
        recv_sem=recv.at[at],
        device_id={"fsdp": target},
        device_id_type=MESH,
    )


def cross_scatter_steps(place, partial, total, mine, near_in, far_in, own_sem, send, recv):
    group = place.group
    rows = total.shape[0]
    half = rows // 2

    def own():
        return pltpu.make_async_copy(partial, mine, own_sem)

    def loop(count, body):
        def strip(i, carry):
            body(pl.ds(i * STRIP, STRIP))
            return carry

        lax.fori_loop(0, count // STRIP, strip, 0)

    if not place.square:

        def direct(i):
            target = lax.rem(group + i, place.groups)
            return to_group(partial.at[target], near_in.at[group], send, recv, i - 1, target)

        def begin_direct():
            own().start()
            for i in range(1, place.groups):
                direct(i).start()

        def sum_direct(cut):
            value = mine[group, cut].astype(F32)
            for i in range(1, place.groups):
                value = value + near_in[lax.rem(group + i, place.groups), cut].astype(F32)
            total[cut] = value

        def end_direct():
            own().wait()
            for i in range(1, place.groups):
                source = lax.rem(group - i + place.groups, place.groups)
                piece = partial.at[source]
                to_group(piece, near_in.at[source], send, recv, i - 1, source).wait_recv()
            loop(rows, sum_direct)
            for i in range(1, place.groups):
                direct(i).wait_send()

        return [begin_direct, end_direct]

    def first(at):
        target = (place.beside, place.across)[at]
        piece = partial.at[place.opposite, pl.ds(at * half, half)]
        return to_group(piece, far_in.at[at], send, recv, at, target)

    def second(at, part):
        target = (place.beside, place.across)[at]
        cut = pl.ds(part * half, half)
        return to_group(
            mine.at[target, cut], near_in.at[at, cut], send, recv, 2 + 2 * at + part, target
        )

    def begin():
        own().start()
        for at in range(2):
            first(at).start()

    def plain():
        own().wait()
        for at in range(2):
            second(at, at).start()

    def join():
        for at in range(2):
            target = (place.across, place.beside)[at]
            first(at).wait_recv()

            def one(cut, at=at, target=target):
                place_in = pl.ds(at * half + cut.start, STRIP)
                value = mine[target, place_in].astype(F32) + far_in[at, cut].astype(F32)
                mine[target, place_in] = value.astype(BF)

            loop(half, one)
            second(1 - at, at).start()

    def everything(cut):
        value = mine[group, cut].astype(F32) + near_in[0, cut].astype(F32)
        total[cut] = value + near_in[1, cut].astype(F32)

    def end():
        for at in range(2):
            for part in range(2):
                second(at, part).wait_recv()
        loop(rows, everything)
        for at in range(2):
            first(at).wait_send()
            for part in range(2):
                second(at, part).wait_send()

    return [begin, plain, join, nothing, nothing, nothing, end]


def everyone_steps(place, piece_for, landing, own_sem, send, recv):
    devices = place.groups * place.ranks
    me = place.device

    def copy(i):
        target = lax.rem(me + i, devices)
        return pltpu.make_async_remote_copy(
            src_ref=piece_for(target),
            dst_ref=landing.at[me],
            send_sem=send.at[i],
            recv_sem=recv.at[i],
            device_id=place.name(target),
            device_id_type=MESH,
        )

    def arrival(i):
        source = lax.rem(me - i + devices, devices)
        return pltpu.make_async_remote_copy(
            src_ref=landing.at[source],
            dst_ref=landing.at[source],
            send_sem=send.at[i],
            recv_sem=recv.at[i],
            device_id=place.name(source),
            device_id_type=MESH,
        )

    def start(i, carry):
        copy(i).start()
        return carry

    def finish_one(i, carry):
        arrival(i).wait_recv()
        copy(i).wait_send()
        return carry

    def own():
        return pltpu.make_async_copy(piece_for(me), landing.at[me], own_sem)

    def begin():
        own().start()
        lax.fori_loop(1, devices, start, 0)

    def end():
        own().wait()
        lax.fori_loop(1, devices, finish_one, 0)

    return [begin, nothing, end]


def spread_steps(place, value, everyone, own_sem, send, recv):
    return everyone_steps(place, lambda target: value, everyone, own_sem, send, recv)


def share_steps(place, values, total, landing, own_sem, send, recv):
    phases = everyone_steps(place, lambda target: values.at[target], landing, own_sem, send, recv)

    def add_up():
        total[...] = jnp.sum(landing[...], axis=0)

    return phases + [add_up]


DMA = pltpu.SemaphoreType.DMA


class Transfers:
    def __init__(self, mesh_size, ident=0, moves=(), needed=()):
        self.ranks, self.groups = mesh_size
        self.ident = ident
        self.kinds = [move[0] for move in moves]
        self.parts = [move[2] if len(move) > 2 else None for move in moves]
        self.inputs = [move[1] for move in moves] + list(needed)
        self.moves = len(self.kinds)
        anywhere = pl.BlockSpec(memory_space=pl.ANY)
        vmem = pl.BlockSpec(memory_space=pltpu.VMEM)
        self.in_specs = [anywhere] * len(self.inputs)
        self.shapes, self.out_specs, self.scratch, self.counts = [], [], [], []
        for kind, array, *part in moves:
            shape, spec = array.shape[len(part[0]) :] if part else array.shape, anywhere
            if kind == "gather":
                shape, dtype = (self.ranks * shape[0], shape[1]), BF
                scratch = gather_scratch(self.ranks)
            elif kind == "scatter":
                shape, dtype, spec = (shape[0] // self.ranks, shape[1]), F32, vmem
                scratch = scatter_scratch(self.ranks, *shape)
            elif kind == "cross_scatter":
                rest = shape[1:]
                square = self.groups == 4
                near = (2 if square else self.groups,) + rest
                scratch = [
                    pltpu.VMEM(shape, BF),
                    pltpu.VMEM(near, BF),
                    pltpu.VMEM((2, rest[0] // 2) + rest[1:], BF),
                    DMA,
                    DMA((max(6, self.groups),)),
                    DMA((max(6, self.groups),)),
                ]
                shape, dtype, spec = rest, F32, vmem
            elif kind == "share":
                devices = self.ranks * self.groups
                scratch = [pltpu.VMEM(shape, F32), DMA, DMA((devices,)), DMA((devices,))]
                shape, dtype, spec = shape[1:], F32, vmem
            else:
                devices = self.ranks * self.groups
                shape, dtype = (devices,) + shape, array.dtype
                scratch = [DMA, DMA((devices,)), DMA((devices,))]
            self.shapes.append(jax.ShapeDtypeStruct(shape, dtype))
            self.out_specs.append(spec)
            self.scratch += scratch
            self.counts.append(len(scratch))

    def params(self):
        if not self.moves:
            return pltpu.CompilerParams(vmem_limit_bytes=VMEM_BYTES)
        return pltpu.CompilerParams(
            collective_id=self.ident, has_side_effects=True, vmem_limit_bytes=VMEM_BYTES
        )

    def begin(self, inputs, outputs, scratch):
        if not self.moves:
            return []
        steps_of = {
            "gather": gather_steps,
            "scatter": scatter_steps,
            "cross_scatter": cross_scatter_steps,
            "spread": spread_steps,
            "share": share_steps,
        }
        place = Place(self.ranks, self.groups)
        scratch = list(scratch)
        lines = []
        for i, kind in enumerate(self.kinds):
            taken, scratch = scratch[: self.counts[i]], scratch[self.counts[i] :]
            given = inputs[i] if self.parts[i] is None else inputs[i].at[self.parts[i]]
            lines.append(steps_of[kind](place, given, outputs[i], *taken))

        def phase(number):
            if number == 0:
                kinds = set(self.kinds)
                place.meet(
                    bool(kinds & {"gather", "scatter"}),
                    "cross_scatter" in kinds,
                    bool(kinds & {"spread", "share"}),
                )
            for steps in lines:
                if number < len(steps):
                    steps[number]()

        return [functools.partial(phase, i) for i in range(max(map(len, lines)))]


def nothing():
    pass


def run_all(phases):
    for phase in phases:
        phase()


def exchange_kernel(transfers, *refs):
    count, moves = len(transfers.inputs), transfers.moves
    run_all(transfers.begin(refs[:moves], refs[count : count + moves], refs[count + moves :]))


def exchange(mesh_size, ident, moves, needed=()):
    transfers = Transfers(mesh_size, ident, moves, needed)
    return pl.pallas_call(
        functools.partial(exchange_kernel, transfers),
        out_shape=tuple(transfers.shapes),
        in_specs=transfers.in_specs,
        out_specs=tuple(transfers.out_specs),
        scratch_shapes=transfers.scratch,
        compiler_params=transfers.params(),
    )(*transfers.inputs)


def beside(phases, at, grid_steps, parts):
    step = pl.program_id(0)
    state = None
    for number, part in enumerate(parts):
        for phase, (when, ahead_of) in zip(phases, at):
            if ahead_of == number:
                pl.when(step == when)(phase)
        state = part(state)
    if phases:
        pl.when(step == grid_steps - 1)(lambda: run_all(phases[len(at) :]))


def column(values, at):
    lanes = lax.broadcasted_iota(jnp.int32, values.shape, 1)
    return jnp.sum(jnp.where(lanes == at, values, 0.0), axis=1, keepdims=True)


def routing(experts, length, first_row, rows, router, routes):
    rank = lax.axis_index("tensor")
    logits = dot(rows, router, (1,), (0,))
    lanes = lax.broadcasted_iota(jnp.int32, logits.shape, 1)
    inside = lanes < experts
    top = jnp.max(jnp.where(inside, logits, -1e30), axis=1, keepdims=True)
    exps = jnp.where(inside, jnp.exp(jnp.where(inside, logits, top) - top), 0.0)
    probs = exps / jnp.sum(exps, axis=1, keepdims=True)
    position = first_row + lax.broadcasted_iota(jnp.int32, (rows.shape[0], 1), 0)
    valid = jnp.where(position < length, 1.0, 0.0)
    gate = valid * jax.nn.sigmoid(column(logits, experts))
    named = jnp.max(jnp.where(routes == rank, 1.0, 0.0), axis=0, keepdims=True)
    chosen = valid * jnp.broadcast_to(named, (8, rows.shape[0])).T[:, :1]
    prob = column(probs, rank)
    out = jnp.where(lanes == experts, gate, probs)
    out = jnp.where(lanes == experts + 1, chosen * prob, out)
    out = jnp.where(lanes == experts + 2, chosen, out)
    return jnp.where(lanes == experts + 3, prob, out)


def routing_back(experts, route, shared_dot, expert_dot):
    rank = lax.axis_index("tensor")
    lanes = lax.broadcasted_iota(jnp.int32, route.shape, 1)
    gate, chosen, prob = [column(route, experts + i) for i in (0, 2, 3)]
    expert_grad = chosen * expert_dot
    logits = route * (jnp.where(lanes == rank, expert_grad, 0.0) - expert_grad * prob)
    gate_logit = shared_dot * gate * (1.0 - gate)
    return jnp.where(lanes < experts, logits, jnp.where(lanes == experts, gate_logit, 0.0))


def ffn_kernel(transfers, at, grid_steps, experts, kind, *refs):
    refs = list(refs)

    def take(count):
        taken = refs[:count]
        del refs[:count]
        return taken

    first, last = kind == "first", kind == "last"
    rows_ref, grad_ref, route_ref, w_ref = take(4)
    before = take(1) if first else take(3)
    router_ref = take(1)[0] if first or last else None
    sent = take(len(transfers.inputs))
    hidden_ref, gate_ref, up_ref, out_ref, back_ref, dots_ref = take(6)
    if first:
        made_ref = take(1)[0]
    landed = take(transfers.moves)
    w_vmem, w_sem = take(2)
    phases = transfers.begin(sent, landed, refs)
    step = pl.program_id(0)

    def weights():
        return pltpu.make_async_copy(w_ref, w_vmem, w_sem)

    pl.when(step == 0)(lambda: weights().start())

    def hidden_part(_):
        pl.when(step == 0)(lambda: weights().wait())
        groups, _, depth, units = w_vmem.shape
        gate_w, up_w, down_w = [w_vmem[:, i].reshape(groups * depth, units) for i in range(3)]
        rows, grad = rows_ref[...], grad_ref[...]
        if first:
            length = before[0][0]
            route = routing(experts, length, step * ROW_BLOCK, rows, router_ref[...], route_ref[...])
            made_ref[...] = route
        else:
            route = route_ref[...]
        scale = column(route, experts if first else experts + 1)
        gate_act = dot(rows, gate_w, (1,), (0,))
        up_act = dot(rows, up_w, (1,), (0,))
        back = dot(grad, down_w, (1,), (0,))
        sigmoid = 1.0 / (1.0 + jnp.exp(-gate_act))
        silu = gate_act * sigmoid
        hidden = (silu * up_act).astype(BF).astype(F32)
        dots = jnp.sum(hidden * back, axis=1, keepdims=True)
        scaled = (scale * hidden).astype(BF)
        hidden_ref[...] = scaled
        grad_hidden = scale * back
        grad_gate = (grad_hidden * up_act * (sigmoid * (1.0 + gate_act * (1.0 - sigmoid)))).astype(BF)
        gate_ref[...] = grad_gate
        grad_up = (grad_hidden * silu).astype(BF)
        up_ref[...] = grad_up
        return gate_w, up_w, down_w, scaled, grad_gate, grad_up, route, dots

    def outer_part(state):
        gate_w, up_w, down_w, scaled, grad_gate, grad_up, route, dots = state
        moved = dot(scaled, down_w, (1,), (1,))
        turned = dot(grad_gate, gate_w, (1,), (1,)) + dot(grad_up, up_w, (1,), (1,))
        lanes = lax.broadcasted_iota(jnp.int32, route.shape, 1)
        if first:
            dots_ref[...] = jnp.where(lanes == 0, dots, 0.0)
        else:
            moved = moved + before[0][...].astype(F32)
            turned = turned + before[1][...].astype(F32)
            earlier = before[2][...]
            if last:
                wide = routing_back(experts, route, column(earlier, 0), column(earlier, 1) + dots)
                wide = wide.astype(BF)
                dots_ref[...] = wide
                turned = turned + dot(wide, router_ref[...], (1,), (1,))
            else:
                dots_ref[...] = earlier + jnp.where(lanes == 1, dots, 0.0)
        out_ref[...] = moved.astype(BF)
        back_ref[...] = turned.astype(BF)

    beside(phases, at, grid_steps, [hidden_part, outer_part])


def ffn(experts, kind, rows, grads, route, weights, before, router, transfers, at=()):
    count, width = rows.shape
    units = weights.shape[3]
    first, last = kind == "first", kind == "last"
    steps = count // ROW_BLOCK

    def block(size):
        return pl.BlockSpec((ROW_BLOCK, size), lambda i: (i, 0))

    given = list(before)
    given_specs = [block(width), block(width), block(LANES)]
    if first:
        given_specs = [pl.BlockSpec(memory_space=pltpu.SMEM)]
    if first or last:
        given.append(router)
        given_specs.append(
            pl.BlockSpec(router.shape, lambda i: (0, 0), pipeline_mode=pl.Buffered(1))
        )
    narrow = [jax.ShapeDtypeStruct((count, units), BF)] * 3
    wide = [jax.ShapeDtypeStruct((count, width), BF)] * 2
    dots = [jax.ShapeDtypeStruct((count, LANES), BF if last else F32)]
    dots += [jax.ShapeDtypeStruct((count, LANES), F32)] * first
    results = pl.pallas_call(
        functools.partial(ffn_kernel, transfers, at, steps, experts, kind),
        grid=(steps,),
        in_specs=[
            block(width),
            block(width),
            pl.BlockSpec((route.shape[0], ROW_BLOCK), lambda i: (0, i)) if first else block(LANES),
            pl.BlockSpec(memory_space=pl.ANY),
        ]
        + given_specs
        + transfers.in_specs,
        out_specs=tuple(
            [block(units)] * 3
            + [block(width)] * 2
            + [block(LANES)] * len(dots)
            + transfers.out_specs
        ),
        out_shape=tuple(narrow + wide + dots + transfers.shapes),
        scratch_shapes=[pltpu.VMEM(weights.shape, BF), DMA] + transfers.scratch,
        compiler_params=transfers.params(),
        cost_estimate=pl.CostEstimate(
            flops=12 * count * width * units,
            bytes_accessed=2 * (3 * width * units + 4 * count * width + 3 * count * units),
            transcendentals=count * units,
        ),
    )(rows, grads, route, weights, *given, *transfers.inputs)
    made = 5 + len(dots)
    return results[:3], results[3:made], results[made:]


def ffn_grads_kernel(transfers, at, grid_steps, micros, last, *refs):
    refs = list(refs)

    def take(count):
        taken = refs[:count]
        del refs[:count]
        return taken

    per_micro = [take(6 if last else 5) for _ in range(micros)]
    sent = take(len(transfers.inputs))
    out_ref = take(1)[0]
    wide_ref = take(1)[0] if last else None
    landed = take(transfers.moves)
    phases = transfers.begin(sent, landed, refs)

    def summed(left, right):
        total = None
        for one in per_micro:
            product = dot(one[left][...], one[right][...], (0,), (0,))
            total = product if total is None else total + product
        return total

    def one_product(which):
        def part(_):
            out_ref[0, which] = summed((0, 0, 1)[which], 2 + which).astype(BF)
            if last and which == 2:
                wide_ref[...] = summed(0, 5)

        return part

    beside(phases, at, grid_steps, [one_product(which) for which in range(3)])


def ffn_grads(groups, per_micro, transfers, at=()):
    count, width = per_micro[0][0].shape
    units = per_micro[0][2].shape[1]
    last = len(per_micro[0]) == 6
    depth = width // groups
    columns = pl.BlockSpec((count, depth), lambda i: (0, i))

    def whole(size):
        return pl.BlockSpec((count, size), lambda i: (0, 0), pipeline_mode=pl.Buffered(1))

    shapes = [jax.ShapeDtypeStruct((groups, 3, depth, units), BF)]
    specs = [pl.BlockSpec((1, 3, depth, units), lambda i: (i, 0, 0, 0))]
    taken = [columns, columns] + [whole(units)] * 3
    if last:
        taken.append(whole(LANES))
        shapes.append(jax.ShapeDtypeStruct((width, LANES), F32))
        specs.append(pl.BlockSpec((depth, LANES), lambda i: (i, 0)))
    results = pl.pallas_call(
        functools.partial(ffn_grads_kernel, transfers, at, groups, len(per_micro), last),
        grid=(groups,),
        in_specs=taken * len(per_micro) + transfers.in_specs,
        out_specs=tuple(specs + transfers.out_specs),
        out_shape=tuple(shapes + transfers.shapes),
        scratch_shapes=transfers.scratch,
        compiler_params=transfers.params(),
        cost_estimate=pl.CostEstimate(
            flops=6 * len(per_micro) * count * width * units,
            bytes_accessed=2 * len(per_micro) * (2 * count * width + 3 * count * units)
            + 6 * width * units,
            transcendentals=0,
        ),
    )(*[array for one in per_micro for array in one], *transfers.inputs)
    return results[: len(shapes)], results[len(shapes) :]


def attention_grads_kernel(transfers, grid_steps, micros, *refs):
    refs = list(refs)

    def take(count):
        taken = refs[:count]
        del refs[:count]
        return taken

    per_micro = [take(4) for _ in range(micros)]
    sent = take(len(transfers.inputs))
    out_ref = take(1)[0]
    landed = take(transfers.moves)
    phases = transfers.begin(sent, landed, refs)

    def work(_):
        span = per_micro[0][2].shape[1]
        totals = [None, None]
        for one in per_micro:
            for which in range(2):
                product = dot(one[which][...], one[2 + which][...], (0,), (0,))
                totals[which] = product if totals[which] is None else totals[which] + product
        out_ref[0, :, :span] = totals[0].astype(BF)
        out_ref[0, :, span:] = totals[1].astype(BF)

    beside(phases, [(0, 0), (grid_steps - 1, 0)], grid_steps, [work])


def attention_grads(groups, per_micro, transfers):
    count, width = per_micro[0][0].shape
    depth = width // groups
    spans = [per_micro[0][i].shape[1] for i in (2, 3)]
    columns = pl.BlockSpec((count, depth), lambda i: (0, i))
    whole = [
        pl.BlockSpec((count, size), lambda i: (0, 0), pipeline_mode=pl.Buffered(1)) for size in spans
    ]
    results = pl.pallas_call(
        functools.partial(attention_grads_kernel, transfers, groups, len(per_micro)),
        grid=(groups,),
        in_specs=([columns, columns] + whole) * len(per_micro) + transfers.in_specs,
        out_specs=tuple(
            [pl.BlockSpec((1, depth, sum(spans)), lambda i: (i, 0, 0))] + transfers.out_specs
        ),
        out_shape=tuple(
            [jax.ShapeDtypeStruct((groups, depth, sum(spans)), BF)] + transfers.shapes
        ),
        scratch_shapes=transfers.scratch,
        compiler_params=transfers.params(),
        cost_estimate=pl.CostEstimate(
            flops=2 * len(per_micro) * count * width * sum(spans),
            bytes_accessed=8 * len(per_micro) * count * width,
            transcendentals=0,
        ),
    )(*[array for one in per_micro for array in one], *transfers.inputs)
    return results[0], results[1:]


def opening_kernel(transfers, cut, *refs):
    refs = list(refs)

    def take(count):
        taken = refs[:count]
        del refs[:count]
        return taken

    sent, given = take(len(transfers.inputs)), take(6)
    landed, made = take(transfers.moves), take(3)
    held, packed_refs, in_sem, out_sem = take(6), take(3), take(1)[0], take(1)[0]
    phases = transfers.begin(sent, landed, refs)
    fetches = [
        pltpu.make_async_copy(source, target, in_sem.at[at])
        for at, (source, target) in enumerate(zip(given, held))
    ]
    gives = [
        pltpu.make_async_copy(source, target, out_sem.at[at])
        for at, (source, target) in enumerate(zip(packed_refs, made))
    ]
    for fetch in fetches:
        fetch.start()
    run_all(phases[:1])
    for fetch in fetches[:3]:
        fetch.wait()
    units = held[0].shape[0]
    packed_refs[0][...] = jnp.zeros_like(packed_refs[0])
    for which in range(3):
        packed_refs[0][which, :, :units] = held[which][...].T
    gives[0].start()
    for fetch in fetches[3:]:
        fetch.wait()
    for at, part in ((1, slice(0, cut)), (2, slice(cut, None))):
        packed_refs[at][0] = held[3][0, :, part]
        packed_refs[at][1] = held[4][0, :, part]
        packed_refs[at][2] = held[5][0, part, :].T
        gives[at].start()
    run_all(phases[1:])
    for give in gives:
        give.wait()


def opening(mesh_size, ident, moves, cut, shared, expert):
    transfers = Transfers(mesh_size, ident, moves)
    anywhere = pl.BlockSpec(memory_space=pl.ANY)
    units, depth = shared[0].shape
    sizes = (-(-units // LANES) * LANES, cut, expert[0].shape[2] - cut)
    shapes = [(3, depth, size) for size in sizes]
    results = pl.pallas_call(
        functools.partial(opening_kernel, transfers, cut),
        in_specs=transfers.in_specs + [anywhere] * 6,
        out_specs=tuple(transfers.out_specs + [anywhere] * 3),
        out_shape=tuple(transfers.shapes + [jax.ShapeDtypeStruct(shape, BF) for shape in shapes]),
        scratch_shapes=[pltpu.VMEM(array.shape, BF) for array in (*shared, *expert)]
        + [pltpu.VMEM(shape, BF) for shape in shapes]
        + [DMA((6,)), DMA((3,))]
        + transfers.scratch,
        compiler_params=transfers.params(),
    )(*transfers.inputs, *shared, *expert)
    return results[: transfers.moves], results[transfers.moves :]


def unpack_kernel(turned, *refs):
    count = len(refs) - 3
    for which, out_ref in enumerate(refs[count:]):
        first = 0
        for ref in refs[:count]:
            values = ref[which].astype(F32)
            if turned[which]:
                values = values.T
                size = min(values.shape[0], out_ref.shape[0] - first)
                out_ref[first : first + size, :] = values[:size]
            else:
                size = min(values.shape[1], out_ref.shape[1] - first)
                out_ref[:, first : first + size] = values[:, :size]
            first += size


def unpack(ranges, units, turned):
    depth = ranges[0].shape[1]
    rows = min(LANES, depth)
    shapes = [(units, depth) if turn else (depth, units) for turn in turned]
    return pl.pallas_call(
        functools.partial(unpack_kernel, turned),
        grid=(depth // rows,),
        in_specs=[pl.BlockSpec((3, rows, array.shape[2]), lambda i: (0, i, 0)) for array in ranges],
        out_specs=tuple(
            pl.BlockSpec((units, rows), lambda i: (0, i))
            if turn
            else pl.BlockSpec((rows, units), lambda i: (i, 0))
            for turn in turned
        ),
        out_shape=tuple(jax.ShapeDtypeStruct(shape, F32) for shape in shapes),
        compiler_params=pltpu.CompilerParams(vmem_limit_bytes=VMEM_BYTES),
        cost_estimate=pl.CostEstimate(flops=0, bytes_accessed=18 * depth * units, transcendentals=0),
    )(*ranges)


def rope_tables(seq_len):
    half = HD // 2
    frequency = np.float32(ROPE_BASE) ** (-(2.0 * np.arange(half, dtype=np.float32)) / HD)
    angles = np.arange(seq_len, dtype=np.float32)[:, None] * frequency[None, :].astype(np.float32)
    cosine, sine = np.cos(angles.astype(np.float64)), np.sin(angles.astype(np.float64))
    return (
        jnp.asarray(np.concatenate([cosine, cosine], axis=1).astype(np.float32)),
        jnp.asarray(np.concatenate([-sine, sine], axis=1).astype(np.float32)),
    )


def swap_halves(values):
    half = HD // 2
    return jnp.concatenate([values[:, half:], values[:, :half]], axis=1)


def block_scores(query, keys, first_row, length):
    scores = dot(query, keys, (1,), (1,)) * (HD ** (-0.5))
    rows = first_row + lax.broadcasted_iota(jnp.int32, scores.shape, 0)
    cols = lax.broadcasted_iota(jnp.int32, scores.shape, 1)
    return jnp.where((cols <= rows) & (cols < length), scores, -1e30)


def attend_kernel(heads, transfers, *refs):
    refs = list(refs)

    def take(count):
        taken = refs[:count]
        del refs[:count]
        return taken

    length_ref, x_ref, gain_ref, w_ref, bias_ref, cos_ref, sin_ref = take(7)
    sent = take(len(transfers.inputs))
    normed_ref, qkv_ref, mixed_ref, logs_ref, out_ref = take(5)
    landed = take(transfers.moves)
    rows_vmem, out_vmem, w_vmem, in_sem, normed_sem, out_sem, w_sem = take(7)
    phases = transfers.begin(sent, landed, refs)
    seq_len, width = x_ref.shape
    groups, depth, columns = w_ref.shape
    span = heads * HD
    length = length_ref[0]
    blocks = [pl.ds(row, QB) for row in range(0, seq_len, QB)]

    def fetch(i):
        return pltpu.make_async_copy(x_ref.at[blocks[i]], rows_vmem.at[blocks[i]], in_sem.at[i])

    def keep(i):
        return pltpu.make_async_copy(rows_vmem.at[blocks[i]], normed_ref.at[blocks[i]], normed_sem.at[i])

    def give(i):
        return pltpu.make_async_copy(out_vmem.at[blocks[i]], out_ref.at[blocks[i]], out_sem.at[i])

    fetch_w = pltpu.make_async_copy(w_ref, w_vmem, w_sem)
    fetch(0).start()
    fetch_w.start()
    run_all(phases[:1])
    for i in range(1, len(blocks)):
        fetch(i).start()
    fetch_w.wait()
    weights = w_vmem[...].reshape(groups * depth, columns)
    qkv_w, out_w = weights[:, : 3 * span], weights[:, 3 * span :]
    for i in range(len(blocks)):
        row, end = i * QB, (i + 1) * QB
        if i >= 2:
            run_all(phases[i - 1 : i])
        fetch(i).wait()
        values = rows_vmem[row:end, :].astype(F32)
        normed = (normalize(values)[0] * gain_ref[...]).astype(BF)
        rows_vmem[row:end, :] = normed
        keep(i).start()
        pre = dot(normed, qkv_w, (1,), (0,)) + bias_ref[...]
        cosine, sine = cos_ref[row:end, :], sin_ref[row:end, :]
        for at in range(0, 3 * span, HD):
            part = pre[:, at : at + HD]
            if at < 2 * span:
                part = part * cosine + swap_halves(part) * sine
            qkv_ref[row:end, at : at + HD] = part.astype(BF)
        for head in range(heads):
            q_at, k_at, v_at = (head * HD, span + head * HD, 2 * span + head * HD)
            scores = block_scores(
                qkv_ref[row:end, q_at : q_at + HD], qkv_ref[:end, k_at : k_at + HD], row, length
            )
            top = jnp.max(scores, axis=1, keepdims=True)
            exps = jnp.exp(scores - top)
            totals = jnp.sum(exps, axis=1, keepdims=True)
            shares = exps * (1.0 / totals)
            logs_ref[row:end, head : head + 1] = top + jnp.log(totals)
            mixed = dot(shares.astype(BF), qkv_ref[:end, v_at : v_at + HD], (1,), (0,))
            mixed_ref[row:end, q_at : q_at + HD] = mixed.astype(BF)
        out_vmem[row:end, :] = dot(mixed_ref[row:end, :], out_w, (1,), (1,)).astype(BF)
        give(i).start()
    run_all(phases[max(1, len(blocks) - 1) :])
    for i in range(len(blocks)):
        keep(i).wait()
        give(i).wait()


def attend_back_kernel(heads, transfers, *refs):
    refs = list(refs)

    def take(count):
        taken = refs[:count]
        del refs[:count]
        return taken

    length_ref, datt_ref, w_ref, qkv_ref, logs_ref, cos_ref, sin_ref = take(7)
    sent = take(len(transfers.inputs))
    turned_ref, sums_ref, out_ref = take(3)
    landed = take(transfers.moves)
    rows_vmem, out_vmem, w_vmem, grad_vmem, key_acc, value_acc, in_sem, out_sem, w_sem = take(9)
    phases = transfers.begin(sent, landed, refs)
    run_all(phases[:1])
    seq_len, width = datt_ref.shape
    groups, depth, columns = w_ref.shape
    span = heads * HD
    length = length_ref[0]
    scale = HD ** (-0.5)
    blocks = [pl.ds(row, QB) for row in range(0, seq_len, QB)]

    def fetch(i):
        return pltpu.make_async_copy(datt_ref.at[blocks[i]], rows_vmem.at[blocks[i]], in_sem.at[i])

    def give(i):
        return pltpu.make_async_copy(out_vmem.at[blocks[i]], out_ref.at[blocks[i]], out_sem.at[i])

    fetch_w = pltpu.make_async_copy(w_ref, w_vmem, w_sem)
    fetch_w.start()
    for i in range(len(blocks)):
        fetch(i).start()
    fetch_w.wait()
    weights = w_vmem[...].reshape(groups * depth, columns)
    qkv_w, out_w = weights[:, : 3 * span], weights[:, 3 * span :]
    key_acc[...] = jnp.zeros_like(key_acc)
    value_acc[...] = jnp.zeros_like(value_acc)
    query_sums = [jnp.zeros((1, HD), F32) for _ in range(heads)]
    for i in range(len(blocks)):
        row, end = i * QB, (i + 1) * QB
        if i >= 2:
            run_all(phases[i - 1 : i])
        fetch(i).wait()
        grad_vmem[row:end, :] = dot(rows_vmem[row:end, :], out_w, (1,), (0,)).astype(BF)
        for head in range(heads):
            q_at, k_at, v_at = (head * HD, span + head * HD, 2 * span + head * HD)
            query = qkv_ref[row:end, q_at : q_at + HD]
            keys = qkv_ref[:end, k_at : k_at + HD]
            grad = grad_vmem[row:end, q_at : q_at + HD]
            shares = jnp.exp(
                block_scores(query, keys, row, length) - logs_ref[row:end, head : head + 1]
            )
            grad_shares = dot(grad, qkv_ref[:end, v_at : v_at + HD], (1,), (1,))
            inner = jnp.sum(shares * grad_shares, axis=1, keepdims=True)
            grad_scores = (scale * shares * (grad_shares - inner)).astype(BF)
            turned = dot(grad_scores, keys, (1,), (0,))
            grad_query = (
                turned * cos_ref[row:end, :] - swap_halves(turned) * sin_ref[row:end, :]
            ).astype(BF)
            turned_ref[row:end, q_at : q_at + HD] = grad_query
            query_sums[head] += jnp.sum(grad_query.astype(F32), axis=0, keepdims=True)
            key_acc[:end, q_at : q_at + HD] += dot(grad_scores, query, (0,), (0,))
            value_acc[:end, q_at : q_at + HD] += dot(shares.astype(BF), grad, (0,), (0,))
    done = max(1, len(blocks) - 1)
    run_all(phases[done : done + 1])
    key_sums = [jnp.zeros((1, HD), F32) for _ in range(heads)]
    value_sums = [jnp.zeros((1, HD), F32) for _ in range(heads)]
    for i in range(len(blocks)):
        row, end = i * QB, (i + 1) * QB
        for head in range(heads):
            q_at, k_at, v_at = (head * HD, span + head * HD, 2 * span + head * HD)
            turned = key_acc[row:end, q_at : q_at + HD]
            grad_key = (
                turned * cos_ref[row:end, :] - swap_halves(turned) * sin_ref[row:end, :]
            ).astype(BF)
            grad_value = value_acc[row:end, q_at : q_at + HD].astype(BF)
            turned_ref[row:end, k_at : k_at + HD] = grad_key
            turned_ref[row:end, v_at : v_at + HD] = grad_value
            key_sums[head] += jnp.sum(grad_key.astype(F32), axis=0, keepdims=True)
            value_sums[head] += jnp.sum(grad_value.astype(F32), axis=0, keepdims=True)
        out_vmem[row:end, :] = dot(turned_ref[row:end, :], qkv_w, (1,), (1,)).astype(BF)
        give(i).start()
    for at, sums in enumerate(query_sums + key_sums + value_sums):
        sums_ref[:, at * HD : (at + 1) * HD] = sums
    for i in range(len(blocks)):
        give(i).wait()
    run_all(phases[done + 1 :])


def in_vmem(count):
    return [pl.BlockSpec(memory_space=pltpu.VMEM)] * count


def attend(length, rows, gain, weights, bias, cosine, sine, transfers):
    seq_len, width = rows.shape
    span = weights.shape[2] // 4
    heads, blocks = span // HD, seq_len // QB
    anywhere = pl.BlockSpec(memory_space=pl.ANY)
    results = pl.pallas_call(
        functools.partial(attend_kernel, heads, transfers),
        out_shape=tuple(
            [
                jax.ShapeDtypeStruct((seq_len, width), BF),
                jax.ShapeDtypeStruct((seq_len, 3 * span), BF),
                jax.ShapeDtypeStruct((seq_len, span), BF),
                jax.ShapeDtypeStruct((seq_len, heads), F32),
                jax.ShapeDtypeStruct((seq_len, width), BF),
            ]
            + transfers.shapes
        ),
        in_specs=[pl.BlockSpec(memory_space=pltpu.SMEM), anywhere]
        + in_vmem(1)
        + [anywhere]
        + in_vmem(3)
        + transfers.in_specs,
        out_specs=tuple([anywhere] + in_vmem(3) + [anywhere] + transfers.out_specs),
        scratch_shapes=[pltpu.VMEM((seq_len, width), BF)] * 2
        + [pltpu.VMEM(weights.shape, BF)]
        + [DMA((blocks,))] * 3
        + [DMA]
        + transfers.scratch,
        compiler_params=transfers.params(),
        cost_estimate=pl.CostEstimate(
            flops=8 * seq_len * width * span + 3 * span * seq_len * seq_len,
            bytes_accessed=8 * seq_len * width,
            transcendentals=heads * seq_len * seq_len,
        ),
    )(length, rows, gain, weights, bias, cosine, sine, *transfers.inputs)
    return results[:5], results[5:]


def attend_back(length, rows, weights, qkv, logs, cosine, sine, transfers):
    seq_len, width = rows.shape
    span = weights.shape[2] // 4
    heads, blocks = span // HD, seq_len // QB
    anywhere = pl.BlockSpec(memory_space=pl.ANY)
    results = pl.pallas_call(
        functools.partial(attend_back_kernel, heads, transfers),
        out_shape=tuple(
            [
                jax.ShapeDtypeStruct((seq_len, 3 * span), BF),
                jax.ShapeDtypeStruct((1, 3 * span), F32),
                jax.ShapeDtypeStruct((seq_len, width), BF),
            ]
            + transfers.shapes
        ),
        in_specs=[pl.BlockSpec(memory_space=pltpu.SMEM), anywhere, anywhere]
        + in_vmem(4)
        + transfers.in_specs,
        out_specs=tuple(in_vmem(2) + [anywhere] + transfers.out_specs),
        scratch_shapes=[pltpu.VMEM((seq_len, width), BF)] * 2
        + [pltpu.VMEM(weights.shape, BF), pltpu.VMEM((seq_len, span), BF)]
        + [pltpu.VMEM((seq_len, span), F32)] * 2
        + [DMA((blocks,))] * 2
        + [DMA]
        + transfers.scratch,
        compiler_params=transfers.params(),
        cost_estimate=pl.CostEstimate(
            flops=8 * seq_len * width * span + 8 * span * seq_len * seq_len,
            bytes_accessed=8 * seq_len * width,
            transcendentals=heads * seq_len * seq_len,
        ),
    )(length, rows, weights, qkv, logs, cosine, sine, *transfers.inputs)
    return results[:3], results[3:]


def padded(values, axis):
    size = values.shape[axis]
    more = -size % LANES
    if not more:
        return values
    return jnp.pad(values, [(0, more if i == axis else 0) for i in range(values.ndim)])


def packed(values, kind):
    tile = LANES * (16 if kind == BF else 8)
    values = values.astype(kind)
    return padded_to(values, -(-values.shape[-1] // tile) * tile)


def padded_to(values, size):
    more = size - values.shape[-1]
    return jnp.pad(values, [(0, 0)] * (values.ndim - 1) + [(0, more)])


def local(
    tokens,
    lengths,
    routes,
    norm1_gain,
    w_query,
    w_key,
    w_value,
    b_query,
    b_key,
    b_value,
    w_out,
    norm2_gain,
    router,
    shared_gate_vec,
    shared_gate,
    shared_up,
    shared_down,
    expert_gate,
    expert_up,
    expert_down,
    cotangent,
):
    ranks = lax.axis_size("tensor")
    groups = lax.axis_size("fsdp")
    rank = lax.axis_index("tensor")
    micros, _, rows, width = tokens.shape
    seq_len = rows * ranks
    heads = w_query.shape[1] // HD
    span = heads * HD
    experts = ranks * expert_gate.shape[0]
    shared_units = shared_gate.shape[1]
    expert_units = expert_gate.shape[2]
    cut = expert_units // (2 * LANES) * LANES
    own_first = rank * rows
    local_pos = own_first + jnp.arange(rows, dtype=jnp.int32)

    per_device = norm1_gain.shape[0]
    small = jnp.concatenate(
        [
            norm1_gain,
            norm2_gain,
            shared_gate_vec,
            router.reshape(-1),
            b_query.reshape(-1),
            b_key.reshape(-1),
            b_value.reshape(-1),
        ]
    )
    attn_own = jnp.concatenate([w_query, w_key, w_value, w_out.T], axis=1)
    mesh_size = (ranks, groups)
    attn_own = with_layout_constraint(attn_own, Layout((0, 1)))
    attn_w = lax.all_gather(attn_own, "fsdp", axis=0, tiled=True)
    attn_w = with_layout_constraint(attn_w, Layout((0, 1))).reshape((groups,) + attn_own.shape)
    (small_all, rows_a), own_ranges = opening(
        mesh_size,
        2,
        [
            ("spread", packed(small, BF).reshape(-1, LANES)),
            ("gather", tokens, (0, 0)),
        ],
        cut,
        (shared_gate.T, shared_up.T, shared_down),
        (expert_gate, expert_up, expert_down),
    )
    small_all = small_all.reshape(groups * ranks, -1)
    gain_one = small_all[:, :per_device].reshape(-1).astype(F32)
    gain_two = small_all[:, per_device : 2 * per_device].reshape(-1).astype(F32)
    gate_vec = small_all[:, 2 * per_device : 3 * per_device].reshape(-1)
    bias_at = per_device * (3 + experts)
    router_full = small_all[:, 3 * per_device : bias_at].reshape(width, experts)
    router_wide = padded_to(jnp.concatenate([router_full, gate_vec[:, None]], axis=1), LANES)
    own_bias = lax.dynamic_index_in_dim(
        small_all.reshape(groups, ranks, -1), rank, 1, False
    )[:, bias_at : small.shape[0]].reshape(groups, 3, heads, HD // groups)
    bias = own_bias.transpose(1, 2, 0, 3).reshape(1, 3 * span).astype(F32)

    weights = [lax.all_gather(own_range, "fsdp", axis=0) for own_range in own_ranges]

    cosine, sine = rope_tables(seq_len)
    idle = Transfers(mesh_size)
    token_own = [tokens[m, 0] for m in range(micros)]
    grads_own = []
    for m in range(micros):
        inside = (local_pos < lengths[m, 0])[:, None]
        grads_own.append(jnp.where(inside, cotangent[m, 0], jnp.zeros((), BF)))

    def moving(ident, *moves, needed=()):
        return Transfers(mesh_size, ident, moves, needed)

    def attention(m, token_rows, transfers):
        return attend(lengths[m], token_rows, gain_one[None], attn_w, bias, cosine, sine, transfers)

    def second_norm(m, attended):
        hidden = token_own[m].astype(F32) + attended
        unit, inverse = normalize(hidden)
        return hidden, unit, inverse, (unit * gain_two).astype(BF)

    def second_norm_back(m, state, summed):
        grad_hidden, gain_part = norm_back(summed, state[1], state[2], gain_two)
        grad_hidden = grad_hidden + grads_own[m].astype(F32)
        return grad_hidden, grad_hidden.astype(BF), gain_part

    def first_norm_back(m, grad_hidden, summed):
        unit, inverse = normalize(token_own[m].astype(F32))
        grad_inputs, gain_part = norm_back(summed, unit, inverse, gain_one)
        return (grad_inputs + grad_hidden).astype(BF), gain_part

    def finished(m, hidden, moved):
        inside = (local_pos < lengths[m, 0]).astype(F32)[:, None]
        return (inside * (hidden + moved)).astype(BF)

    att_a, (rows_b,) = attention(0, rows_a, moving(3, ("gather", tokens, (1, 0))))
    att_b, (grad_a, sum_a) = attention(
        1, rows_b, moving(4, ("gather", cotangent, (0, 0)), ("scatter", att_a[4]))
    )
    norm_a = second_norm(0, sum_a)
    two_a, sum_b = exchange(mesh_size, 5, [("gather", norm_a[3]), ("scatter", att_b[4])])
    norm_b = second_norm(1, sum_b)

    def over_groups(grads):
        flat = grads.reshape(-1, grads.shape[-1])
        summed = lax.psum_scatter(flat, "fsdp", scatter_dimension=0, tiled=True)
        return with_layout_constraint(summed, Layout((0, 1))).reshape(grads.shape[1:])

    def grads_of(which, transfers, at=()):
        per_micro = []
        for key in range(micros):
            rows_two, grads = ((two_a, grad_a), (two_b, grad_b))[key]
            scaled, gate, up = act[which, key]
            more = [(acc_a, acc_b)[key][2]] if which == 2 else []
            per_micro.append([rows_two, grads, gate, up, scaled] + more)
        return ffn_grads(groups, per_micro, transfers, at)

    act = {}
    part = functools.partial(ffn, experts)
    single = ((0, 0), (1, 0), (2, 0), (3, 0))
    act[0, 0], acc_a, (grad_b,) = part(
        "first", two_a, grad_a, routes[0, 0].T, weights[0], [lengths[0]], router_wide,
        moving(6, ("gather", cotangent, (1, 0))), single,
    )
    acc_a, route_a = acc_a[:3], acc_a[3]
    act[1, 0], acc_a, (two_b,) = part(
        "next", two_a, grad_a, route_a, weights[1], acc_a, None,
        moving(7, ("gather", norm_b[3])), single,
    )
    act[0, 1], acc_b, _ = part(
        "first", two_b, grad_b, routes[1, 0].T, weights[0], [lengths[1]], router_wide, idle
    )
    acc_b, route_b = acc_b[:3], acc_b[3]
    (grads_0,), _ = grads_of(0, idle)
    range_0 = over_groups(grads_0)
    act[2, 0], acc_a, _ = part(
        "last", two_a, grad_a, route_a, weights[2], acc_a, router_wide, moving(0, needed=[grads_0])
    )
    act[1, 1], acc_b, (down_a,) = part(
        "next", two_b, grad_b, route_b, weights[1], acc_b, None,
        moving(8, ("scatter", acc_a[1])), single,
    )
    hid_a, send_a, gain_part_a = second_norm_back(0, norm_a, down_a)
    (grads_1,), (datt_a,) = grads_of(
        1, moving(9, ("gather", send_a)), ((0, 0), (1, 0), (2, 0), (3, 0))
    )
    range_1 = over_groups(grads_1)
    act[2, 1], acc_b, (moved_a,) = part(
        "last", two_b, grad_b, route_b, weights[2], acc_b, router_wide,
        moving(10, ("scatter", acc_a[0]), needed=[grads_1]), single,
    )
    (grads_2, total_wide), (down_b,) = grads_of(
        2, moving(11, ("scatter", acc_b[1]), needed=[range_0]), ((0, 0), (1, 1), (2, 1), (3, 1))
    )
    range_2 = over_groups(grads_2)
    hid_b, send_b, gain_part_b = second_norm_back(1, norm_b, down_b)

    (grad_qkv_a, sums_a, first_a), (datt_b,) = attend_back(
        lengths[0], datt_a, attn_w, att_a[1], att_a[3], cosine, sine,
        moving(12, ("gather", send_b)),
    )
    (grad_qkv_b, sums_b, first_b), (one_a,) = attend_back(
        lengths[1], datt_b, attn_w, att_b[1], att_b[3], cosine, sine,
        moving(15, ("scatter", first_a), needed=[range_1]),
    )
    attn_parts, (one_b,) = attention_grads(
        groups,
        [
            (att_a[0], datt_a, grad_qkv_a, att_a[2]),
            (att_b[0], datt_b, grad_qkv_b, att_b[2]),
        ],
        moving(13, ("scatter", first_b)),
    )

    grad_in_a, one_part_a = first_norm_back(0, hid_a, one_a)
    grad_in_b, one_part_b = first_norm_back(1, hid_b, one_b)

    devices = groups * ranks
    bias_part = (sums_a + sums_b).reshape(3, heads, groups, HD // groups).transpose(2, 0, 1, 3)
    bias_part = bias_part.reshape(groups, 1, -1)
    own_rank = (jnp.arange(ranks, dtype=jnp.int32) == rank).astype(F32)[None, :, None]
    parts = jnp.concatenate(
        [
            (one_part_a + one_part_b).reshape(devices, -1),
            (gain_part_a + gain_part_b).reshape(devices, -1),
            total_wide[:, : experts + 1].reshape(devices, -1),
            (bias_part * own_rank).reshape(devices, -1),
        ],
        axis=1,
    )
    shares, attn_g, moved_b = exchange(
        mesh_size,
        14,
        [
            ("share", packed(parts, F32).reshape(devices, -1, LANES)),
            ("cross_scatter", attn_parts),
            ("scatter", acc_b[0]),
        ],
        [range_2],
    )
    shares = shares.reshape(-1)
    wide_g = shares[2 * per_device : (3 + experts) * per_device].reshape(per_device, experts + 1)
    bias_g = shares[bias_at : parts.shape[1]].reshape(3, heads, HD // groups)

    shared_g = unpack([range_0], shared_units, (True, True, True))
    expert_g = unpack([range_1, range_2], expert_units, (False, False, True))
    return (
        jnp.stack([finished(0, norm_a[0], moved_a), finished(1, norm_b[0], moved_b)])[:, None],
        jnp.stack([grad_in_a, grad_in_b])[:, None],
        shares[:per_device],
        attn_g[:, :span],
        attn_g[:, span : 2 * span],
        attn_g[:, 2 * span : 3 * span],
        bias_g[0],
        bias_g[1],
        bias_g[2],
        attn_g[:, 3 * span :].T,
        shares[per_device : 2 * per_device],
        wide_g[:, :experts],
        wide_g[:, experts],
        shared_g[0].T,
        shared_g[1].T,
        shared_g[2],
        expert_g[0][None],
        expert_g[1][None],
        expert_g[2][None],
    )


def solution(mesh):
    in_specs = (
        P(None, "fsdp", "tensor", None),
        P(None, "fsdp"),
        P(None, "fsdp", None, None),
        P(("fsdp", "tensor")),
        P("fsdp", "tensor"),
        P("fsdp", "tensor"),
        P("fsdp", "tensor"),
        P("tensor", "fsdp"),
        P("tensor", "fsdp"),
        P("tensor", "fsdp"),
        P("tensor", "fsdp"),
        P(("fsdp", "tensor")),
        P(("fsdp", "tensor"), None),
        P(("fsdp", "tensor")),
        P("fsdp", "tensor"),
        P("fsdp", "tensor"),
        P("tensor", "fsdp"),
        P("tensor", "fsdp", None),
        P("tensor", "fsdp", None),
        P("tensor", None, "fsdp"),
        P(None, "fsdp", "tensor", None),
    )
    out_specs = (
        P(None, "fsdp", "tensor", None),
        P(None, "fsdp", "tensor", None),
        P(("fsdp", "tensor")),
        P("fsdp", "tensor"),
        P("fsdp", "tensor"),
        P("fsdp", "tensor"),
        P("tensor", "fsdp"),
        P("tensor", "fsdp"),
        P("tensor", "fsdp"),
        P("tensor", "fsdp"),
        P(("fsdp", "tensor")),
        P(("fsdp", "tensor"), None),
        P(("fsdp", "tensor")),
        P("fsdp", "tensor"),
        P("fsdp", "tensor"),
        P("tensor", "fsdp"),
        P("tensor", "fsdp", None),
        P("tensor", "fsdp", None),
        P("tensor", None, "fsdp"),
    )
    return jax.shard_map(local, mesh=mesh, in_specs=in_specs, out_specs=out_specs, check_vma=False)
```
